32 devices in a mesh: ens: 2 (over x), gy: 16 (over z, y, core).
Axes of the slice: x: 2, y: 2, z: 4, core: 2. Of those that a mesh axis runs over, the one named last changes fastest.
Arguments:
- flow_state: float32 [5, 32, 128, 128], P(None, 'ens', 'gy'), parts along dimension 1, may hold values from -0.05 to 1.1, as said below
- section_cotangent: float32 [5, 32, 128, 128], P(None, 'ens', 'gy'), parts along dimension 1, may hold values from -6 to 6
- face_flags: int32 [3, 32, 128, 128], P(None, 'ens', 'gy'), parts along dimension 1, may hold values from 0 to 15
- conv_kernel: float32 [16, 135], replicated, may hold values from -0.5 to 0.5
- head_weights: float32 [5, 16], replicated, may hold values from -1.5 to 1.5
Outputs:
- flow_adjoint: float32 [5, 32, 128, 128], P(None, 'ens', 'gy'), parts along dimension 1
- kernel_adjoint: float32 [32, 135], P('ens'), parts along dimension 0
- head_adjoint: float32 [10, 16], P('ens'), parts along dimension 0
The draws below stay inside these ranges and needn't reach their ends.
There are 2 independent parts, one for each index of `ens`. The reference program is written for one: setup_inputs(seed, part) draws one part's arguments, and reference() takes and returns one part's arrays. A program takes and returns all parts, laid end to end along the dimension named above; an argument that names none is the same for every part. Nothing has to cross between parts.
Inputs may be any that keep to these rules, and one draw needn't show every extreme that they name: `flow_state`: components 0 and 4 (density, pressure) lie within 0.9 to 1.1, components 1 to 3 (velocities) within -0.05 to 0.05. `face_flags`: entry [d, i] belongs to the face between cell i and cell i+1 along direction d; its value mod 4 is the HLLC region, its value div 4 the reconstruction choice.
All inputs are finite; a program needn't handle non-finite values.
Results may differ from the reference program's by a relative error of at most 0.0003.
Values sent between devices are 32-bit elements; how exact they have to be, the bound alone decides.
No kernel may reach another device: no remote copies, remote signals or barrier semaphores. Data moves between devices by JAX's collectives and lax.ppermute only.
A program may use at most 128 MiB of HBM per device.

```python
from functools import partial
import jax
import jax.numpy as jnp
from jax import lax

X = 16
CY = 8
Z = 128
CH = 16
TAPS = 135
NY = 128
N_GY = 16


def draw_flow_state(key, part):
    key = jax.random.fold_in(key, 11)
    mean_level = jnp.array([1.0, 0.0, 0.0, 0.0, 1.0], jnp.float32).reshape(5, 1, 1, 1)
    spread = jnp.array([0.1, 0.05, 0.05, 0.05, 0.1], jnp.float32).reshape(5, 1, 1, 1)
    rough_part = jax.random.uniform(key, (5, X, NY, Z), jnp.float32, -1.0, 1.0)
    return mean_level + spread * rough_part


def with_ends(values, stream_key, least, high):
    place = [jax.random.randint(jax.random.fold_in(stream_key, axis), (), 0, length) for axis, length in enumerate(values.shape)]
    main_axis = values.shape.index(max(values.shape))
    beside = place[:main_axis] + [(place[main_axis] + 1) % values.shape[main_axis]] + place[main_axis + 1:]
    return values.at[tuple(place)].set(least).at[tuple(beside)].set(high)


def levels(key, extent, shards, low, high):
    def one(axis_at, shards_of):
        steps = jax.random.uniform(jax.random.fold_in(jax.random.fold_in(key, 6), axis_at), (shards_of,), jnp.float32, low / len(shards), high / len(shards))
        return jnp.repeat(jnp.exp(steps), extent[axis_at] // shards_of).reshape((-1,) + (1,) * (len(extent) - axis_at - 1))

    loudness = one(*shards[0])
    for cut in shards[1:]:
        loudness = loudness * one(*cut)
    return loudness


def noise(own_key, dims, deviation, limit, split=(), kind=jnp.bfloat16):
    level = levels(own_key, dims, split, -0.22, 0.18) if split else 1.0
    values = jax.random.normal(own_key, dims, jnp.float32) * deviation * level
    return jnp.minimum(jnp.maximum(values, -limit), limit).astype(kind)


def setup_inputs(seed: int = 0, part: int = 0) -> dict:
    key_of = jax.random.split(jax.random.key(seed), 6)
    part_splits = jax.random.split(jax.random.fold_in(key_of[5], part), 6)
    flow_state = draw_flow_state(jax.random.fold_in(jax.random.fold_in(key_of[5], part), 71), part)
    section_cotangent = noise(part_splits[1], (5, X, NY, Z), 1.0, 6.0, ((2, 16),), jnp.float32)
    face_flags = with_ends(jax.random.randint(part_splits[2], (3, X, NY, Z), 0, 16), jax.random.fold_in(part_splits[2], 1), 0, 15).astype(jnp.int32)
    conv_kernel = noise(key_of[3], (CH, TAPS), TAPS ** -0.5, 0.5, (), jnp.float32)
    head_weights = noise(key_of[4], (5, CH), CH ** -0.5, 1.5, (), jnp.float32)
    return dict(flow_state=flow_state, section_cotangent=section_cotangent, face_flags=face_flags, conv_kernel=conv_kernel, head_weights=head_weights)


heat_ratio = 1.4
step_ratio = 0.3
weno_floor = 0.01

def weno_value(far_low, near_low, center, near_high, far_high, stencil):
    candidate_low = (2.0 * far_low - 7.0 * near_low + 11.0 * center) / 6.0
    candidate_mid = (-near_low + 5.0 * center + 2.0 * near_high) / 6.0
    candidate_high = (2.0 * center + 5.0 * near_high - far_high) / 6.0
    rough_low = 13.0 / 12.0 * (far_low - 2.0 * near_low + center) ** 2 + 0.25 * (far_low - 4.0 * near_low + 3.0 * center) ** 2
    rough_mid = 13.0 / 12.0 * (near_low - 2.0 * center + near_high) ** 2 + 0.25 * (near_low - near_high) ** 2
    rough_high = 13.0 / 12.0 * (center - 2.0 * near_high + far_high) ** 2 + 0.25 * (3.0 * center - 4.0 * near_high + far_high) ** 2
    alpha_low = 0.1 / (weno_floor + rough_low) ** 2
    alpha_mid = 0.6 / (weno_floor + rough_mid) ** 2
    alpha_high = 0.3 / (weno_floor + rough_high) ** 2
    blended = (alpha_low * candidate_low + alpha_mid * candidate_mid + alpha_high * candidate_high) / (alpha_low + alpha_mid + alpha_high)
    choose = stencil[None]
    return (choose == 0).astype(jnp.float32) * blended + (choose == 1).astype(jnp.float32) * candidate_low + (choose == 2).astype(jnp.float32) * candidate_mid + (choose == 3).astype(jnp.float32) * candidate_high

def euler_terms(primitive, normal):
    density = primitive[0]
    velocity = [primitive[1], primitive[2], primitive[3]]
    pressure = primitive[4]
    energy = pressure / (heat_ratio - 1.0) + 0.5 * density * (velocity[0] ** 2 + velocity[1] ** 2 + velocity[2] ** 2)
    normal_speed = velocity[normal]
    conserved_list = [density, density * velocity[0], density * velocity[1], density * velocity[2], energy]
    flux_list = [density * normal_speed]
    for component in range(3):
        term = density * normal_speed * velocity[component]
        if component == normal:
            term = term + pressure
        flux_list.append(term)
    flux_list.append(normal_speed * (energy + pressure))
    return (conserved_list, flux_list, normal_speed, energy)

def hllc_flux(left_state, right_state, normal, region):
    cons_left, flux_left, speed_left, energy_left = euler_terms(left_state, normal)
    cons_right, flux_right, speed_right, energy_right = euler_terms(right_state, normal)
    sound_left = jnp.sqrt(heat_ratio * left_state[4] / left_state[0])
    sound_right = jnp.sqrt(heat_ratio * right_state[4] / right_state[0])
    mean_speed = 0.5 * (speed_left + speed_right)
    mean_sound = 0.5 * (sound_left + sound_right)
    mean_density = 0.5 * (left_state[0] + right_state[0])
    wave_low = mean_speed - mean_sound
    wave_high = mean_speed + mean_sound
    contact = mean_speed + 0.5 * (left_state[4] - right_state[4]) / (mean_density * mean_sound)

    def star_state(primitive, normal_speed, energy, wave_speed):
        factor = primitive[0] * (wave_speed - normal_speed) / (wave_speed - contact)
        moment = []
        for component in range(3):
            if component == normal:
                moment.append(factor * contact)
            else:
                moment.append(factor * primitive[1 + component])
        total_energy = factor * (energy / primitive[0] + (contact - normal_speed) * (contact + primitive[4] / (primitive[0] * (wave_speed - normal_speed))))
        return [factor] + moment + [total_energy]
    star_left = star_state(left_state, speed_left, energy_left, wave_low)
    star_right = star_state(right_state, speed_right, energy_right, wave_high)
    level_masks = [(region == region_level).astype(jnp.float32) for region_level in range(4)]
    result = []
    for component in range(5):
        result.append(level_masks[0] * flux_left[component] + level_masks[1] * (flux_left[component] + wave_low * (star_left[component] - cons_left[component])) + level_masks[2] * (flux_right[component] + wave_high * (star_right[component] - cons_right[component])) + level_masks[3] * flux_right[component])
    return jnp.stack(result)

def flux_change(padded_state, padded_flags, axis_index, margin):
    row_count = padded_state.shape[2] - 2 * margin
    if axis_index == 1:

        def neighbour(offset):
            return padded_state[:, :, margin - 1 + offset:margin + row_count + offset, :]
        flag_rows = padded_flags[1, :, margin - 1:margin + row_count, :]
    else:
        interior = padded_state[:, :, margin:margin + row_count, :]

        def neighbour(offset):
            return jnp.roll(interior, -offset, axis=axis_index + 1)
        flag_rows = padded_flags[axis_index, :, margin:margin + row_count, :]
    region = flag_rows % 4
    stencil = flag_rows // 4
    left_state = weno_value(neighbour(-2), neighbour(-1), neighbour(0), neighbour(1), neighbour(2), stencil)
    right_state = weno_value(neighbour(3), neighbour(2), neighbour(1), neighbour(0), neighbour(-1), stencil)
    face_flux = hllc_flux(left_state, right_state, axis_index, region)
    if axis_index == 1:
        return face_flux[:, :, 1:] - face_flux[:, :, :-1]
    return face_flux - jnp.roll(face_flux, 1, axis=axis_index + 1)

def closure_term(padded_state, conv_kernel, head_weights, margin):
    row_count = padded_state.shape[2] - 2 * margin
    cells_x = padded_state.shape[1]
    cells_z = padded_state.shape[3]
    hidden_sum = jnp.zeros((conv_kernel.shape[0], cells_x * row_count * cells_z), jnp.float32)
    tap_index = 0
    for shift_y in (-1, 0, 1):
        row_block = padded_state[:, :, margin + shift_y:margin + shift_y + row_count, :]
        for shift_x in (-1, 0, 1):
            moved_x = jnp.roll(row_block, -shift_x, axis=1)
            for shift_z in (-1, 0, 1):
                shifted = jnp.roll(moved_x, -shift_z, axis=3).reshape(5, -1)
                weights = conv_kernel[:, tap_index * 5:tap_index * 5 + 5]
                hidden_sum = hidden_sum + jnp.dot(weights, shifted, precision=lax.Precision.HIGHEST, preferred_element_type=jnp.float32)
                tap_index += 1
    hidden = jnp.tanh(hidden_sum)
    closure_out = jnp.dot(head_weights, hidden, precision=lax.Precision.HIGHEST, preferred_element_type=jnp.float32)
    return closure_out.reshape(5, cells_x, row_count, cells_z)

def conserved(padded_state, margin):
    interior = padded_state[:, :, margin:padded_state.shape[2] - margin, :]
    density = interior[0]
    energy = interior[4] / (heat_ratio - 1.0) + 0.5 * density * (interior[1] ** 2 + interior[2] ** 2 + interior[3] ** 2)
    return jnp.stack([density, density * interior[1], density * interior[2], density * interior[3], energy])

def section_piece(piece_index, padded_flags, margin, padded_state, conv_kernel, head_weights):
    if piece_index < 3:
        return -step_ratio * flux_change(padded_state, padded_flags, piece_index, margin)
    if piece_index == 3:
        return step_ratio * closure_term(padded_state, conv_kernel, head_weights, margin)
    return conserved(padded_state, margin)

def piece_grads(padded_state, padded_flags, conv_kernel, head_weights, margin, upstream):
    state_sum = jnp.zeros_like(padded_state)
    kernel_sum = jnp.zeros_like(conv_kernel)
    head_sum = jnp.zeros_like(head_weights)
    for piece_index in range(5):
        _, pullback = jax.vjp(partial(section_piece, piece_index, padded_flags, margin), padded_state, conv_kernel, head_weights)
        grad_state, grad_kernel, grad_head = pullback(upstream)
        state_sum = state_sum + grad_state
        kernel_sum = kernel_sum + grad_kernel
        head_sum = head_sum + grad_head
    return (state_sum, kernel_sum, head_sum)

def block_grads(state_window, flag_window, upstream_window, conv_kernel, head_weights):
    row_count = state_window.shape[2] - 12
    state_sum, _, _ = piece_grads(state_window, flag_window, conv_kernel, head_weights, 3, upstream_window)
    own_rows = state_sum[:, :, 6:6 + row_count]
    _, pullback = jax.vjp(partial(section_piece, 3, flag_window, 1, state_window[:, :, 5:7 + row_count]), conv_kernel, head_weights)
    grad_kernel, grad_head = pullback(upstream_window[:, :, 3:3 + row_count])
    return (own_rows, grad_kernel, grad_head)

def reference(flow_state, section_cotangent, face_flags, conv_kernel, head_weights):
    wide_state = jnp.concatenate([flow_state[:, :, -6:], flow_state, flow_state[:, :, :6]], axis=2)
    wide_flags = jnp.concatenate([face_flags[:, :, -6:], face_flags, face_flags[:, :, :6]], axis=2)
    wide_upstream = jnp.concatenate([section_cotangent[:, :, -3:], section_cotangent, section_cotangent[:, :, :3]], axis=2)

    def one_block(totals, block_index):
        first_row = (block_index * CY).astype(jnp.int32)
        state_window = lax.dynamic_slice_in_dim(wide_state, first_row, CY + 12, 2)
        flag_window = lax.dynamic_slice_in_dim(wide_flags, first_row, CY + 12, 2)
        upstream_window = lax.dynamic_slice_in_dim(wide_upstream, first_row, CY + 6, 2)
        own_rows, grad_kernel, grad_head = block_grads(state_window, flag_window, upstream_window, conv_kernel, head_weights)
        return ((totals[0] + grad_kernel, totals[1] + grad_head), own_rows)
    start_totals = (jnp.zeros(conv_kernel.shape, jnp.float32), jnp.zeros(head_weights.shape, jnp.float32))
    final_totals, blocks = lax.scan(one_block, start_totals, jnp.arange(N_GY, dtype=jnp.int32))
    flow_adjoint = jnp.transpose(blocks, (1, 2, 0, 3, 4)).reshape(5, X, NY, Z)
    grad_scale = float(X * NY * Z) ** (-0.5)
    return (flow_adjoint, final_totals[0] * grad_scale, final_totals[1] * grad_scale)
```

```python
import functools

import jax
import jax.numpy as jnp
import numpy as np
from jax import lax
from jax.experimental import pallas as pl
from jax.experimental.pallas import tpu as pltpu
from jax.sharding import PartitionSpec as P

STEP = 0.3
FLOOR = 0.01
BELOW, ABOVE = 2, 3
SLABS = 2
VMEM = 48 * 1024 * 1024
F32 = jnp.float32
BF16 = jnp.bfloat16


def rcp(x):
    return pl.reciprocal(x, approx=True)


def shared_terms(v):
    p = [v[i + 1] - v[i] for i in range(5)]
    d = [p[i + 1] - p[i] for i in range(4)]
    h = [(4.0 / 3.0) * x for x in d]
    k = [h[i] * d[i] + FLOOR for i in range(4)]
    g = [x + x for x in h]
    t = [d[i + 1] - d[i] for i in range(3)]
    return p, d, k, g, t


def side_value(pa, pm, pm2, ka, kb, kc, m0, m2, td, t1, smooth, c0, c2):
    i0 = rcp(ka + pa * m0)
    i1 = rcp(kb + pa * pm)
    i2 = rcp(kc + pm * m2)
    w0 = i0 * i0
    w1 = 6.0 * (i1 * i1)
    w2 = 3.0 * (i2 * i2)
    r = rcp(w0 + w1 + w2)
    o0 = jnp.where(smooth, w0 * r, c0)
    o2 = jnp.where(smooth, w2 * r, c2)
    u = o0 * td + o2 * t1
    return (pa + pm2) - u, (i0, i1, i2, w0, w1, w2, r, o0, o2, u)


def side_pull(mu, pa, pm, m0, m2, td, t1, smooth, saved):
    i0, i1, i2, w0, w1, w2, r, o0, o2, u = saved
    mu2 = mu + mu
    rm = jnp.where(smooth, mu2, 0.0) * r
    s0 = (w0 * i0) * rm * (td - u)
    s1 = (w1 * i1) * rm * u
    s2 = (w2 * i2) * rm * (t1 - u)
    pa_bar = s0 * (m0 + pa) - s1 * pm + mu
    pm_bar = s2 * (m2 + pm) - s1 * pa + mu2
    return s0, s1, s2, pa_bar, pm_bar, o0 * mu2, o2 * mu


def hllc_pull(left, right, normal, flags, cot):
    region = flags & 3
    is_right = region >= 2
    star = ((region + 1) & 2) != 0
    n_at = 1 + normal
    tang = [1 + i for i in range(3) if i != normal]
    rl, rr_, pl_, pr_, nl, nr = left[0], right[0], left[4], right[4], left[n_at], right[n_at]

    def sound(r, p):
        inv = rcp(r)
        t = 1.4 * p * inv
        inv_c = lax.rsqrt(t)
        return inv, inv_c, t * inv_c

    inv_rl, inv_cl, cl = sound(rl, pl_)
    inv_rr, inv_cr, cr = sound(rr_, pr_)
    c = 0.5 * (cl + cr)
    r2 = rl + rr_
    inv = rcp(r2 * c)
    nm = 0.5 * (nl + nr)
    gap = (pl_ - pr_) * inv
    sm = nm + gap
    sc = jnp.where(is_right, c, -c)
    s = nm + sc
    pick = [jnp.where(is_right, right[i], left[i]) for i in range(5)]
    r, un, u1, u2, p = pick[0], pick[n_at], pick[tang[0]], pick[tang[1]], pick[4]
    a = s - un
    dl = sm - un
    si = jnp.where(star, rcp(sc - gap), 0.0)
    j = s * si
    kap = j * dl
    g0, gn, g1, g2, ge = cot[0], cot[n_at], cot[tang[0]], cot[tang[1]], cot[4]
    w = un + kap
    half_q = 0.5 * (un * un + u1 * u1 + u2 * u2)
    enthalpy = 3.5 * p + r * half_q
    b = g0 + u1 * g1 + u2 * g2 + un * gn
    m = r * b + enthalpy * ge
    n = gn + sm * ge
    rkap = r * kap
    f_kap = m + r * a * n
    f_a = rkap * n
    si2 = si * si
    s_bar = f_a - f_kap * (dl * sm * si2)
    sm_bar = f_kap * (s * a * si2) + rkap * a * ge
    wr = w * r
    k_bar = [None] * 5
    k_bar[0] = w * (b + half_q * ge) + kap * a * n
    k_bar[n_at] = m + wr * (gn + un * ge) - f_kap * j - f_a
    k_bar[tang[0]] = wr * (g1 + u1 * ge)
    k_bar[tang[1]] = wr * (g2 + u2 * ge)
    k_bar[4] = 3.5 * (w * ge) + gn
    e = sm_bar * inv
    eg = e * gap
    c_half = 0.5 * (jnp.where(is_right, s_bar, -s_bar) - eg * r2)
    n_half = 0.5 * (s_bar + sm_bar)
    r_both = -(eg * c)
    xl = c_half * inv_rl
    xr = c_half * inv_rr
    base_l = {0: r_both - 0.5 * (xl * cl), n_at: n_half, 4: 0.7 * (xl * inv_cl) + e}
    base_r = {0: r_both - 0.5 * (xr * cr), n_at: n_half, 4: 0.7 * (xr * inv_cr) - e}
    l_bar, r_bar = [], []
    for i in range(5):
        kr = jnp.where(is_right, k_bar[i], 0.0)
        kl = k_bar[i] - kr
        l_bar.append(base_l[i] + kl if i in base_l else kl)
        r_bar.append(base_r[i] + kr if i in base_r else kr)
    return l_bar, r_bar


def face_pull(cells, cot, flags, normal):
    stencil = flags >> 2
    smooth = stencil == 0
    c0 = jnp.where(stencil == 1, 1.0, 0.0)
    c2 = jnp.where(stencil == 3, 1.0, 0.0)
    left, right, kept = [], [], []
    for v in cells:
        p, d, k, g, t = shared_terms(v)
        pm2 = p[2] + p[2]
        args_l = (p[1], p[2], p[1] + d[0], p[2] - d[2], t[0] + t[0], t[1])
        args_r = (p[3], p[2], p[3] - d[3], p[2] + d[1], t[2] + t[2], t[1])
        hl, saved_l = side_value(
            p[1], p[2], pm2, k[0], k[1], k[2], *args_l[2:], smooth, c0, c2
        )
        hr, saved_r = side_value(
            p[3], p[2], pm2, k[3], k[2], k[1], *args_r[2:], smooth, c0, c2
        )
        left.append(v[2] + hl * (1.0 / 6.0))
        right.append(v[3] - hr * (1.0 / 6.0))
        kept.append((p, g, args_l, args_r, saved_l, saved_r))
    l_bar, r_bar = hllc_pull(left, right, normal, flags, cot)
    out = []
    for i in range(5):
        p, g, args_l, args_r, saved_l, saved_r = kept[i]
        a0, a1, a2, pa_l, pm_l, x0, x2 = side_pull(
            l_bar[i] * (1.0 / 6.0), *args_l, smooth, saved_l
        )
        b0, b1, b2, pa_r, pm_r, y0, y2 = side_pull(
            r_bar[i] * (-1.0 / 6.0), *args_r, smooth, saved_r
        )
        d0 = a0 * (g[0] + p[1]) + x0
        d1 = (b2 * (g[1] + p[2]) - a1 * g[1]) + (x2 - x0) + y2
        d2 = (a2 * (g[2] - p[2]) - b1 * g[2]) + (y0 - y2) - x2
        d3 = b0 * (g[3] - p[3]) - y0
        p2 = pa_l + (d0 - d1)
        p3 = pm_l + pm_r + (d1 - d2)
        p4 = pa_r + (d2 - d3)
        out.append([d0, -d0 - p2, l_bar[i] + (p2 - p3), r_bar[i] + (p3 - p4), p4 - d3, d3])
    return out


def conserved_pull(s, g):
    half_q = 0.5 * (s[1] * s[1] + s[2] * s[2] + s[3] * s[3])
    return [
        g[0] + s[1] * g[1] + s[2] * g[2] + s[3] * g[3] + half_q * g[4],
        s[0] * (g[1] + s[1] * g[4]),
        s[0] * (g[2] + s[2] * g[4]),
        s[0] * (g[3] + s[3] * g[4]),
        2.5 * g[4],
    ]


def x_kernel(state, cot, flags, kernel, pick, mass, out, w_rows, w_cols, bias, pad, gpad, acc, wide):
    nx = state.shape[1]
    for v in range(5):
        pad[v, pl.ds(2, nx)] = state[v]
        pad[v, pl.ds(0, 2)] = state[v, pl.ds(nx - 2, 2)]
        pad[v, pl.ds(nx + 2, 3)] = state[v, pl.ds(0, 3)]
        gpad[v, pl.ds(0, nx)] = cot[v]
        gpad[v, pl.ds(nx, 1)] = cot[v, pl.ds(0, 1)]
    acc[...] = jnp.zeros_like(acc)

    def step(i, carry):
        x = i * SLABS
        cells = [[pad[v, pl.ds(x + k, SLABS)] for k in range(6)] for v in range(5)]
        g = [gpad[v, pl.ds(x, SLABS)] for v in range(5)]
        face = [STEP * (gpad[v, pl.ds(x + 1, SLABS)] - g[v]) for v in range(5)]
        terms = face_pull(cells, face, flags[0, pl.ds(x, SLABS)], 0)
        own = conserved_pull([cells[v][2] for v in range(5)], g)
        for v in range(5):
            terms[v][2] = terms[v][2] + own[v]
            for s in range(SLABS + 5):
                total = None
                for k in range(6):
                    if 0 <= s - k < SLABS:
                        part = terms[v][k][s - k]
                        total = part if total is None else total + part
                acc[v, x + s] = acc[v, x + s] + total
        return carry

    lax.fori_loop(0, nx // SLABS, step, 0)
    for v in range(5):
        acc[v, pl.ds(nx, 2)] = acc[v, pl.ds(nx, 2)] + acc[v, pl.ds(0, 2)]
        acc[v, pl.ds(2, 3)] = acc[v, pl.ds(2, 3)] + acc[v, pl.ds(nx + 2, 3)]
        out[v] = acc[v, pl.ds(2, nx)]

    ch, taps = kernel.shape
    rows = pick.shape[1] // 512
    w = kernel[...]
    hi = w.astype(BF16)
    lo = (w - hi.astype(F32)).astype(BF16)
    wide[...] = jnp.zeros_like(wide)
    wide[pl.ds(0, ch), pl.ds(0, taps)] = hi.astype(F32)
    wide[pl.ds(ch, ch), pl.ds(0, taps)] = lo.astype(F32)
    both = wide[...].astype(BF16)
    band = jnp.dot(both, pick[...], preferred_element_type=F32)
    top = [band[:ch, y * 512 : (y + 1) * 512] for y in range(rows)]
    low = [band[ch:, y * 512 : (y + 1) * 512] for y in range(rows)]
    full = jnp.concatenate(top + low, axis=0)
    w_rows[...] = full.astype(BF16)
    w_cols[...] = full.T.astype(BF16)
    total = jnp.sum(w * mass[...], axis=1, keepdims=True)
    total = jnp.broadcast_to(total, (ch, 128))
    bias[...] = jnp.concatenate([total] * rows, axis=0)


def y_kernel(state, cot, flags, above, below, own, rim, out, up, down, halo, ghalo, back):
    nx = state.shape[1]
    for v in range(5):
        base = v * nx * 8
        for r in range(BELOW):
            halo[pl.ds(base + 8 - BELOW + r, nx, stride=8), :] = below[r, v]
        for r in range(ABOVE):
            halo[pl.ds(base + r, nx, stride=8), :] = above[r, v]
        ghalo[pl.ds(base, nx, stride=8), :] = above[ABOVE, v]
    row = lax.broadcasted_iota(jnp.int32, (SLABS, 8, 128), 1)
    inside = {}
    for k in (-2, -1, 1, 2, 3):
        inside[k] = (row < 8 + k) if k < 0 else (row >= k)

    def step(i, carry):
        x = i * SLABS
        cells, face = [], []
        for v in range(5):
            at = pl.multiple_of((v * nx + x) * 8, 8)
            rim_rows = halo[pl.ds(at, 8 * SLABS), :].reshape(SLABS, 8, 128)
            mid = state[v, pl.ds(x, SLABS)]
            line = []
            for k in range(-2, 4):
                if k == 0:
                    line.append(mid)
                else:
                    line.append(pltpu.roll(jnp.where(inside[k], mid, rim_rows), (-k) % 8, 1))
            cells.append(line)
            g = cot[v, pl.ds(x, SLABS)]
            g_rim = ghalo[pl.ds(at, 8 * SLABS), :].reshape(SLABS, 8, 128)
            face.append(STEP * (pltpu.roll(jnp.where(inside[1], g, g_rim), 7, 1) - g))
        terms = face_pull(cells, face, flags[1, pl.ds(x, SLABS)], 1)
        for v in range(5):
            at = pl.multiple_of((v * nx + x) * 8, 8)
            mine = own[v, pl.ds(x, SLABS)] + terms[v][2]
            outer = None
            for k in (-2, -1, 1, 2, 3):
                moved = pltpu.roll(terms[v][k + 2], k % 8, 1)
                kept = jnp.where(inside[k], moved, 0.0)
                mine = mine + kept
                left = moved - kept
                outer = left if outer is None else outer + left
            out[v, pl.ds(x, SLABS)] = mine
            back[pl.ds(at, 8 * SLABS), :] = outer.reshape(8 * SLABS, 128)
        return carry

    lax.fori_loop(0, nx // SLABS, step, 0)
    for v in range(5):
        base = v * nx * 8
        for r in range(BELOW):
            rows = back[pl.ds(base + 8 - BELOW + r, nx, stride=8), :]
            if r == BELOW - 1:
                rows = rows + rim[pl.ds(v, nx, stride=16), :]
            down[r, v] = rows
        for r in range(ABOVE):
            rows = back[pl.ds(base + r, nx, stride=8), :]
            if r == 0:
                rows = rows + rim[pl.ds(5 + v, nx, stride=16), :]
            up[r, v] = rows


def z_faces(state, cot, flags, x):
    cells, face = [], []
    for v in range(5):
        mid = state[v, pl.ds(x, SLABS)]
        cells.append([mid if k == 0 else pltpu.roll(mid, (-k) % 128, 2) for k in range(-2, 4)])
        g = cot[v, pl.ds(x, SLABS)]
        face.append(STEP * (pltpu.roll(g, 127, 2) - g))
    terms = face_pull(cells, face, flags[2, pl.ds(x, SLABS)], 2)
    total = []
    for v in range(5):
        t = terms[v][2]
        for k in (-2, -1, 1, 2, 3):
            t = t + pltpu.roll(terms[v][k + 2], k % 128, 2)
        total.append(t)
    return total


def z_kernel(state, cot, flags, first, out):
    half = out.shape[1]

    def step(i, carry):
        x = i * SLABS
        total = z_faces(state, cot, flags, x)
        for v in range(5):
            out[v, pl.ds(x, SLABS)] = first[v, pl.ds(x, SLABS)] + total[v]
        return carry

    lax.fori_loop(0, half // SLABS, step, 0)


def last_kernel(scale, state, cot, flags, first, second, done, from_below, from_above, parts, out, k_out, h_out, halo):
    nx = state.shape[1]
    half = done.shape[1]
    for v in range(5):
        base = v * nx * 8
        for r in range(8):
            if r < ABOVE:
                rows = from_below[r, v]
            elif r >= 8 - BELOW:
                rows = from_above[r - (8 - BELOW), v]
            else:
                rows = jnp.zeros((nx, 128), F32)
            halo[pl.ds(base + r, nx, stride=8), :] = rows

    def put(x, v, value):
        at = pl.multiple_of((v * nx + x) * 8, 8)
        rim = halo[pl.ds(at, 8 * SLABS), :].reshape(SLABS, 8, 128)
        out[v, pl.ds(x, SLABS)] = value + second[v, pl.ds(x, SLABS)] + rim

    def step(i, carry):
        x = i * SLABS
        total = z_faces(state, cot, flags, half + x)
        for v in range(5):
            put(half + x, v, first[v, pl.ds(half + x, SLABS)] + total[v])
            put(x, v, done[v, pl.ds(x, SLABS)])
        return carry

    lax.fori_loop(0, half // SLABS, step, 0)
    total = parts[0]
    for i in range(1, parts.shape[0]):
        total = total + parts[i]
    total = total * scale
    k_out[...] = total[:, : k_out.shape[1]]
    ch = total.shape[0]
    pick = (
        lax.broadcasted_iota(jnp.int32, (8, 128), 1)
        == lax.broadcasted_iota(jnp.int32, (8, 128), 0) + 16
    ).astype(F32)
    heads = lax.dot_general(
        pick,
        total[:, 128:],
        (((1,), (1,)), ((), ())),
        precision=lax.Precision.HIGHEST,
        preferred_element_type=F32,
    )
    h_out[...] = heads[: h_out.shape[0], :ch]


def split(x):
    hi = x.astype(BF16)
    return hi, (x - hi.astype(F32)).astype(BF16)


def over_lanes(a, b):
    return lax.dot_general(a, b, (((1,), (1,)), ((), ())), preferred_element_type=F32)


def c_kernel(
    state, cot, above, below, heads, pick, mass, w_rows, w_cols, bias,
    own, rim, parts,
    t, acc, edge, kg, hg, dsum,
):
    nx = state.shape[1]
    ch = heads.shape[1]
    block, slot = 56, 168

    edge[...] = jnp.zeros_like(edge)
    for v in range(5):
        level = 1.0 if v in (0, 4) else 0.0
        edge[pl.ds(v, nx, stride=16), :] = below[BELOW - 1, v] - level
        edge[pl.ds(5 + v, nx, stride=16), :] = above[0, v] - level

    def fill(x, carry):
        rows = [state[v, x] - (1.0 if v in (0, 4) else 0.0) for v in range(5)]
        rows.append(edge[pl.ds(pl.multiple_of(x * 16, 16), 16), :])
        mid = jnp.concatenate(rows, axis=0)
        at = pl.multiple_of((x + 1) * slot, 8)
        t[pl.ds(at, block), :] = pltpu.roll(mid, 1, 1)
        t[pl.ds(at + block, block), :] = mid
        t[pl.ds(at + 2 * block, block), :] = pltpu.roll(mid, 127, 1)
        return carry

    lax.fori_loop(0, nx, fill, 0)
    t[pl.ds(0, slot), :] = t[pl.ds(nx * slot, slot), :]
    t[pl.ds((nx + 1) * slot, slot), :] = t[pl.ds(slot, slot), :]
    t[pl.ds((nx + 2) * slot, 8), :] = jnp.zeros((8, 128), F32)
    acc[...] = jnp.zeros_like(acc)
    kg[...] = jnp.zeros_like(kg)
    hg[...] = jnp.zeros_like(hg)
    dsum[...] = jnp.zeros_like(dsum)

    r = lax.broadcasted_iota(jnp.int32, (8 * ch, ch), 0)
    q = lax.broadcasted_iota(jnp.int32, (8 * ch, ch), 1)
    spread = ((r & (ch - 1)) == q).astype(F32)
    high = dict(precision=lax.Precision.HIGHEST, preferred_element_type=F32)
    h5 = lax.dot_general(spread, heads[...], (((1,), (1,)), ((), ())), **high)
    e_of = lax.broadcasted_iota(jnp.int32, (5, 40), 0)
    c_of = lax.broadcasted_iota(jnp.int32, (5, 40), 1)
    h40 = jnp.dot(h5, ((c_of >> 3) == e_of).astype(F32), **high)
    y_row = lax.broadcasted_iota(jnp.int32, (8 * ch, 40), 0)
    y_col = lax.broadcasted_iota(jnp.int32, (8 * ch, 40), 1) & 7
    same_y = (y_row >= y_col * ch) & (y_row < (y_col + 1) * ch)
    h_hi, h_lo = split(jnp.where(same_y, STEP * h40, 0.0))
    wide_head = jnp.concatenate(
        [h_hi.astype(F32), h_lo.astype(F32), h_hi.astype(F32)], axis=1
    ).astype(BF16)

    def step(i, carry):
        x = i * 2
        at0 = pl.multiple_of(x * slot, 8)
        at1 = pl.multiple_of((x + 1) * slot, 8)
        s = jnp.concatenate([t[pl.ds(at0, 512), :], t[pl.ds(at1, 512), :]], axis=1).astype(BF16)
        z2 = jnp.dot(w_rows[...], s, preferred_element_type=F32)
        b = bias[...]
        z = z2[: 8 * ch] + z2[8 * ch :] + jnp.concatenate([b, b], axis=1)
        hidden = jnp.tanh(z)
        g = jnp.concatenate(
            [jnp.concatenate([cot[v, x + j] for v in range(5)], axis=0) for j in range(2)], axis=1
        )
        g_hi, g_lo = split(g)
        g_hi32, g_lo32 = g_hi.astype(F32), g_lo.astype(F32)
        g3 = jnp.concatenate([g_hi32, g_hi32, g_lo32], axis=0).astype(BF16)
        d = (1.0 - hidden * hidden) * jnp.dot(wide_head, g3, preferred_element_type=F32)
        hid_hi, hid_lo = split(hidden)
        hid2 = jnp.concatenate([hid_hi, hid_lo], axis=0)
        g2 = jnp.concatenate([g_hi32, g_lo32], axis=0).astype(BF16)
        hg[...] = hg[...] + over_lanes(hid2, g2)
        d_hi, d_lo = split(d)
        d2 = jnp.concatenate([d_hi, d_lo], axis=0)
        k2 = over_lanes(d2, s)
        kg[...] = kg[...] + (k2[: 8 * ch] + k2[8 * ch :])
        dsum[...] = dsum[...] + (d[:, :128] + d[:, 128:])
        wc_hi = w_cols[:, : 8 * ch]
        wc2 = jnp.concatenate([wc_hi, wc_hi], axis=1)
        back = jnp.dot(wc2, d2, preferred_element_type=F32) + jnp.dot(
            w_cols[:, 8 * ch :], d_hi, preferred_element_type=F32
        )
        acc[pl.ds(at0, 504), :] = acc[pl.ds(at0, 504), :] + back[:504, :128]
        acc[pl.ds(at1, 504), :] = acc[pl.ds(at1, 504), :] + back[:504, 128:]
        return carry

    lax.fori_loop(0, nx // 2, step, 0)
    acc[pl.ds(nx * slot, slot), :] = acc[pl.ds(nx * slot, slot), :] + acc[pl.ds(0, slot), :]
    acc[pl.ds(slot, slot), :] = acc[pl.ds(slot, slot), :] + acc[pl.ds((nx + 1) * slot, slot), :]

    def drain(x, carry):
        at = pl.multiple_of((x + 1) * slot, 8)
        total = (
            acc[pl.ds(at + block, block), :]
            + pltpu.roll(acc[pl.ds(at, block), :], 127, 1)
            + pltpu.roll(acc[pl.ds(at + 2 * block, block), :], 1, 1)
        )
        for v in range(5):
            own[v, x] = total[8 * v : 8 * v + 8]
        rim[pl.ds(pl.multiple_of(x * 16, 16), 16), :] = total[40:56]
        return carry

    lax.fori_loop(0, nx, drain, 0)

    grads = jnp.zeros((2 * ch, pick.shape[0]), F32)
    level_sum = jnp.zeros((ch, 1), F32)
    head_sum = jnp.zeros((ch, 40), F32)
    sums = jnp.sum(dsum[...], axis=1, keepdims=True)
    h2 = hg[...]
    h_all = (h2[: 8 * ch, :40] + h2[8 * ch :, :40]) + (h2[: 8 * ch, 40:80] + h2[8 * ch :, 40:80])
    h_all = jnp.where(same_y, h_all, 0.0)
    for y in range(8):
        rows = kg[pl.ds(y * ch, ch), :]
        hi, lo = split(rows)
        pair = jnp.concatenate([hi, lo], axis=0)
        grads = grads + over_lanes(pair, pick[:, y * 512 : (y + 1) * 512])
        level_sum = level_sum + sums[y * ch : (y + 1) * ch]
        head_sum = head_sum + h_all[y * ch : (y + 1) * ch]
    taps = mass.shape[1]
    n_pick = pick.shape[0]
    parts[...] = jnp.zeros_like(parts)
    parts[:, pl.ds(0, n_pick)] = grads[:ch] + grads[ch:]
    parts[:, pl.ds(0, taps)] = parts[:, pl.ds(0, taps)] + level_sum * mass[...]
    e_row = lax.broadcasted_iota(jnp.int32, (40, 128), 0) >> 3
    e_col = lax.broadcasted_iota(jnp.int32, (40, 128), 1) - 16
    head_out = jnp.dot(head_sum * STEP, (e_row == e_col).astype(F32), **high)
    parts[:, pl.ds(128, 128)] = parts[:, pl.ds(128, 128)] + head_out


def band_pick():
    pick = np.zeros((144, 8, 512), np.float32)
    for ox in range(3):
        for oz in range(3):
            for v in range(5):
                for y in range(8):
                    for oy in range(3):
                        row = y + oy - 1
                        if row < 0:
                            at = 40 + v
                        elif row > 7:
                            at = 45 + v
                        else:
                            at = v * 8 + row
                        pick[(oy * 9 + ox * 3 + oz) * 5 + v, y, (ox * 3 + oz) * 56 + at] = 1.0
    return pick.reshape(144, 8 * 512)


def call(kernel, outs, scratch, flops, moved):
    return pl.pallas_call(
        kernel,
        out_shape=outs,
        scratch_shapes=scratch,
        compiler_params=pltpu.CompilerParams(vmem_limit_bytes=VMEM),
        cost_estimate=pl.CostEstimate(flops=flops, bytes_accessed=moved, transcendentals=0),
    )


def body(pick, mass, state, cot, flags, kernel, heads):
    _, nx, ny, nz = state.shape
    ch, taps = kernel.shape
    count = lax.axis_size("gy")
    cells = nx * ny * nz
    shape = lambda *dims: jax.ShapeDtypeStruct(dims, F32)
    full = shape(5, nx, ny, nz)
    up = [(i, (i + 1) % count) for i in range(count)]
    down = [((i + 1) % count, i) for i in range(count)]
    pick = jnp.asarray(pick, BF16)
    mass = jnp.asarray(mass)

    rows = lambda a, lo, hi: jnp.transpose(a[:, :, lo:hi], (2, 0, 1, 3))
    head = jnp.concatenate([rows(state, 0, ABOVE), rows(cot, 0, 1)], axis=0)
    above = lax.ppermute(head, "gy", down)
    below = lax.ppermute(rows(state, ny - BELOW, ny), "gy", up)

    vm = pltpu.VMEM
    first, w_rows, w_cols, bias = call(
        x_kernel,
        (
            full,
            jax.ShapeDtypeStruct((16 * ch, 512), BF16),
            jax.ShapeDtypeStruct((512, 16 * ch), BF16),
            shape(8 * ch, 128),
        ),
        [
            vm((5, nx + 5, ny, nz), F32),
            vm((5, nx + 1, ny, nz), F32),
            vm((5, nx + 5, ny, nz), F32),
            vm((2 * ch, pick.shape[0]), F32),
        ],
        1000 * cells,
        1 << 22,
    )(state, cot, flags, kernel, pick, mass)
    own, rim, parts = call(
        c_kernel,
        (full, shape(16 * nx, nz), shape(ch, 256)),
        [
            vm(((nx + 2) * 168 + 8, nz), F32),
            vm(((nx + 2) * 168 + 8, nz), F32),
            vm((16 * nx, nz), F32),
            vm((8 * ch, 512), F32),
            vm((16 * ch, 80), F32),
            vm((8 * ch, 128), F32),
        ],
        1000 * cells,
        1 << 22,
    )(state, cot, above, below, heads, pick, mass, w_rows, w_cols, bias)
    gathered = lax.all_gather(parts, "gy")
    second, give_up, give_down = call(
        y_kernel,
        (full, shape(ABOVE, 5, nx, nz), shape(BELOW, 5, nx, nz)),
        [vm((5 * nx * 8, nz), F32)] * 3,
        1000 * cells,
        1 << 22,
    )(state, cot, flags, above, below, own, rim)
    from_below = lax.ppermute(give_up, "gy", up)
    from_above = lax.ppermute(give_down, "gy", down)
    done = call(z_kernel, shape(5, nx // 2, ny, nz), [], 500 * cells, 1 << 22)(
        state, cot, flags, first
    )
    scale = float(cells * count) ** (-0.5)
    return call(
        functools.partial(last_kernel, scale),
        (full, shape(ch, taps), shape(5, ch)),
        [vm((5 * nx * 8, nz), F32)],
        500 * cells,
        1 << 22,
    )(state, cot, flags, first, second, done, from_below, from_above, gathered)


def solution(mesh):
    pick = band_pick()
    mass = np.zeros((16, 135), np.float32)
    mass[:, 0::5] = 1.0
    mass[:, 4::5] = 1.0
    split_y = P(None, "ens", "gy", None)
    return jax.shard_map(
        functools.partial(body, pick, mass),
        mesh=mesh,
        in_specs=(split_y, split_y, split_y, P(), P()),
        out_specs=(split_y, P("ens", None), P("ens", None)),
        check_vma=False,
    )
```

```python
import functools

import jax
import jax.numpy as jnp
import numpy as np
from jax import lax
from jax.experimental import pallas as pl
from jax.experimental.pallas import tpu as pltpu
from jax.sharding import PartitionSpec as P

STEP = 0.3
FLOOR = 0.01
BELOW, ABOVE = 2, 3
SLABS = 2
WIDE = 4
VMEM = 48 * 1024 * 1024
F32 = jnp.float32
BF16 = jnp.bfloat16


def rcp(x):
    return pl.reciprocal(x, approx=True)


def shared_terms(v):
    p = [v[i + 1] - v[i] for i in range(5)]
    d = [p[i + 1] - p[i] for i in range(4)]
    h = [(4.0 / 3.0) * x for x in d]
    k = [h[i] * d[i] + FLOOR for i in range(4)]
    g = [x + x for x in h]
    t = [d[i + 1] - d[i] for i in range(3)]
    return p, d, k, g, t


def side_value(pa, pm, pm2, ka, kb, kc, m0, m2, td, t1, smooth, c0, c2):
    i0 = rcp(ka + pa * m0)
    i1 = rcp(kb + pa * pm)
    i2 = rcp(kc + pm * m2)
    w0 = i0 * i0
    w1 = 6.0 * (i1 * i1)
    w2 = 3.0 * (i2 * i2)
    r = rcp(w0 + w1 + w2)
    o0 = jnp.where(smooth, w0 * r, c0)
    o2 = jnp.where(smooth, w2 * r, c2)
    u = o0 * td + o2 * t1
    return (pa + pm2) - u, (i0, i1, i2, w0, w1, w2, r, o0, o2, u)


def side_pull(mu, pa, pm, m0, m2, td, t1, smooth, saved):
    i0, i1, i2, w0, w1, w2, r, o0, o2, u = saved
    mu2 = mu + mu
    rm = jnp.where(smooth, mu2, 0.0) * r
    s0 = (w0 * i0) * rm * (td - u)
    s1 = (w1 * i1) * rm * u
    s2 = (w2 * i2) * rm * (t1 - u)
    pa_bar = s0 * (m0 + pa) - s1 * pm + mu
    pm_bar = s2 * (m2 + pm) - s1 * pa + mu2
    return s0, s1, s2, pa_bar, pm_bar, o0 * mu2, o2 * mu


def hllc_pull(left, right, normal, flags, cot):
    region = flags & 3
    is_right = region >= 2
    star = ((region + 1) & 2) != 0
    n_at = 1 + normal
    tang = [1 + i for i in range(3) if i != normal]
    rl, rr_, pl_, pr_, nl, nr = left[0], right[0], left[4], right[4], left[n_at], right[n_at]

    def sound(r, p):
        inv = rcp(r)
        t = 1.4 * p * inv
        inv_c = lax.rsqrt(t)
        return inv, inv_c, t * inv_c

    inv_rl, inv_cl, cl = sound(rl, pl_)
    inv_rr, inv_cr, cr = sound(rr_, pr_)
    c = 0.5 * (cl + cr)
    r2 = rl + rr_
    inv = rcp(r2 * c)
    nm = 0.5 * (nl + nr)
    gap = (pl_ - pr_) * inv
    sm = nm + gap
    sc = jnp.where(is_right, c, -c)
    s = nm + sc
    pick = [jnp.where(is_right, right[i], left[i]) for i in range(5)]
    r, un, u1, u2, p = pick[0], pick[n_at], pick[tang[0]], pick[tang[1]], pick[4]
    a = s - un
    dl = sm - un
    si = jnp.where(star, rcp(sc - gap), 0.0)
    j = s * si
    kap = j * dl
    g0, gn, g1, g2, ge = cot[0], cot[n_at], cot[tang[0]], cot[tang[1]], cot[4]
    w = un + kap
    half_q = 0.5 * (un * un + u1 * u1 + u2 * u2)
    enthalpy = 3.5 * p + r * half_q
    b = g0 + u1 * g1 + u2 * g2 + un * gn
    m = r * b + enthalpy * ge
    n = gn + sm * ge
    rkap = r * kap
    f_kap = m + r * a * n
    f_a = rkap * n
    si2 = si * si
    s_bar = f_a - f_kap * (dl * sm * si2)
    sm_bar = f_kap * (s * a * si2) + rkap * a * ge
    wr = w * r
    k_bar = [None] * 5
    k_bar[0] = w * (b + half_q * ge) + kap * a * n
    k_bar[n_at] = m + wr * (gn + un * ge) - f_kap * j - f_a
    k_bar[tang[0]] = wr * (g1 + u1 * ge)
    k_bar[tang[1]] = wr * (g2 + u2 * ge)
    k_bar[4] = 3.5 * (w * ge) + gn
    e = sm_bar * inv
    eg = e * gap
    c_half = 0.5 * (jnp.where(is_right, s_bar, -s_bar) - eg * r2)
    n_half = 0.5 * (s_bar + sm_bar)
    r_both = -(eg * c)
    xl = c_half * inv_rl
    xr = c_half * inv_rr
    base_l = {0: r_both - 0.5 * (xl * cl), n_at: n_half, 4: 0.7 * (xl * inv_cl) + e}
    base_r = {0: r_both - 0.5 * (xr * cr), n_at: n_half, 4: 0.7 * (xr * inv_cr) - e}
    l_bar, r_bar = [], []
    for i in range(5):
        kr = jnp.where(is_right, k_bar[i], 0.0)
        kl = k_bar[i] - kr
        l_bar.append(base_l[i] + kl if i in base_l else kl)
        r_bar.append(base_r[i] + kr if i in base_r else kr)
    return l_bar, r_bar


def face_pull(cells, cot, flags, normal):
    stencil = flags >> 2
    smooth = stencil == 0
    c0 = jnp.where(stencil == 1, 1.0, 0.0)
    c2 = jnp.where(stencil == 3, 1.0, 0.0)
    left, right, kept = [], [], []
    for v in cells:
        p, d, k, g, t = shared_terms(v)
        pm2 = p[2] + p[2]
        args_l = (p[1], p[2], p[1] + d[0], p[2] - d[2], t[0] + t[0], t[1])
        args_r = (p[3], p[2], p[3] - d[3], p[2] + d[1], t[2] + t[2], t[1])
        hl, saved_l = side_value(
            p[1], p[2], pm2, k[0], k[1], k[2], *args_l[2:], smooth, c0, c2
        )
        hr, saved_r = side_value(
            p[3], p[2], pm2, k[3], k[2], k[1], *args_r[2:], smooth, c0, c2
        )
        left.append(v[2] + hl * (1.0 / 6.0))
        right.append(v[3] - hr * (1.0 / 6.0))
        kept.append((p, g, args_l, args_r, saved_l, saved_r))
    l_bar, r_bar = hllc_pull(left, right, normal, flags, cot)
    out = []
    for i in range(5):
        p, g, args_l, args_r, saved_l, saved_r = kept[i]
        a0, a1, a2, pa_l, pm_l, x0, x2 = side_pull(
            l_bar[i] * (1.0 / 6.0), *args_l, smooth, saved_l
        )
        b0, b1, b2, pa_r, pm_r, y0, y2 = side_pull(
            r_bar[i] * (-1.0 / 6.0), *args_r, smooth, saved_r
        )
        d0 = a0 * (g[0] + p[1]) + x0
        d1 = (b2 * (g[1] + p[2]) - a1 * g[1]) + (x2 - x0) + y2
        d2 = (a2 * (g[2] - p[2]) - b1 * g[2]) + (y0 - y2) - x2
        d3 = b0 * (g[3] - p[3]) - y0
        p2 = pa_l + (d0 - d1)
        p3 = pm_l + pm_r + (d1 - d2)
        p4 = pa_r + (d2 - d3)
        out.append([d0, -d0 - p2, l_bar[i] + (p2 - p3), r_bar[i] + (p3 - p4), p4 - d3, d3])
    return out


def conserved_pull(s, g):
    half_q = 0.5 * (s[1] * s[1] + s[2] * s[2] + s[3] * s[3])
    return [
        g[0] + s[1] * g[1] + s[2] * g[2] + s[3] * g[3] + half_q * g[4],
        s[0] * (g[1] + s[1] * g[4]),
        s[0] * (g[2] + s[2] * g[4]),
        s[0] * (g[3] + s[3] * g[4]),
        2.5 * g[4],
    ]


def is_even():
    return lax.rem(lax.axis_index("gy"), 2) == 0


def pack_kernel(state, cot, twin, other):
    even = is_even()
    nx = twin.shape[2]
    for v in range(5):
        base = v * nx * 8
        for r in range(ABOVE + 1):
            if r < ABOVE:
                low = state[pl.ds(base + r, nx, stride=8), :]
            else:
                low = cot[pl.ds(base, nx, stride=8), :]
            if r < BELOW:
                top = state[pl.ds(base + 8 - BELOW + r, nx, stride=8), :]
            else:
                top = low
            twin[r, v] = jnp.where(even, top, low)
            other[r, v] = jnp.where(even, low, top)


def x_kernel(state, cot, flags, kernel, pick, code, mass, out, w_rows, w_cols, bias, pad, gpad, acc, wide):
    nx = state.shape[1]
    for v in range(5):
        pad[v, pl.ds(2, nx)] = state[v]
        pad[v, pl.ds(0, 2)] = state[v, pl.ds(nx - 2, 2)]
        pad[v, pl.ds(nx + 2, 3)] = state[v, pl.ds(0, 3)]
        gpad[v, pl.ds(0, nx)] = cot[v]
        gpad[v, pl.ds(nx, 1)] = cot[v, pl.ds(0, 1)]
    acc[...] = jnp.zeros_like(acc)

    def step(i, carry):
        x = i * SLABS
        cells = [[pad[v, pl.ds(x + k, SLABS)] for k in range(6)] for v in range(5)]
        g = [gpad[v, pl.ds(x, SLABS)] for v in range(5)]
        face = [STEP * (gpad[v, pl.ds(x + 1, SLABS)] - g[v]) for v in range(5)]
        terms = face_pull(cells, face, flags[0, pl.ds(x, SLABS)], 0)
        own = conserved_pull([cells[v][2] for v in range(5)], g)
        for v in range(5):
            terms[v][2] = terms[v][2] + own[v]
            for s in range(SLABS + 5):
                total = None
                for k in range(6):
                    if 0 <= s - k < SLABS:
                        part = terms[v][k][s - k]
                        total = part if total is None else total + part
                acc[v, x + s] = acc[v, x + s] + total
        return carry

    lax.fori_loop(0, nx // SLABS, step, 0)
    for v in range(5):
        acc[v, pl.ds(nx, 2)] = acc[v, pl.ds(nx, 2)] + acc[v, pl.ds(0, 2)]
        acc[v, pl.ds(2, 3)] = acc[v, pl.ds(2, 3)] + acc[v, pl.ds(nx + 2, 3)]
        out[v] = acc[v, pl.ds(2, nx)]

    ch, taps = kernel.shape
    w = kernel[...]
    hi, lo = split(w)
    wide[...] = jnp.zeros_like(wide)
    wide[pl.ds(0, ch), pl.ds(0, taps)] = hi.astype(F32)
    wide[pl.ds(ch, ch), pl.ds(0, taps)] = lo.astype(F32)
    base = jnp.dot(wide[...].astype(BF16), pick[...], preferred_element_type=F32)
    kind = jnp.broadcast_to(code[0:1], base.shape)
    main = jnp.where(kind < 3, base, 0.0)
    bands = []
    for y in range(8):
        rows = main
        if y == 0:
            rows = jnp.where(kind == 0, 0.0, rows)
        if y == 7:
            rows = jnp.where(kind == 2, 0.0, rows)
        if y != 1:
            rows = pltpu.roll(rows, (y - 1) % 512, 1)
        if y == 0:
            rows = rows + jnp.where(kind == 8, base, 0.0)
        if y == 7:
            rows = rows + jnp.where(kind == 9, base, 0.0)
        bands.append(rows)
    full = jnp.concatenate([b[:ch] for b in bands] + [b[ch:] for b in bands], axis=0)
    w_rows[...] = full.astype(BF16)
    cols = full.T.astype(BF16)
    w_cols[...] = jnp.concatenate([cols[:, : 8 * ch], cols], axis=1)
    total = jnp.sum(w * mass[...], axis=1, keepdims=True)
    total = jnp.broadcast_to(total, (ch, 128))
    bias[...] = jnp.concatenate([total] * 8, axis=0)


def y_faces(x0, state, cot, flags, twin, other, own, first, out, halo, ghalo, back):
    part = out.shape[1]
    even = is_even()
    for v in range(5):
        base = v * part * 8
        for r in range(ABOVE + 1):
            a, b = twin[r, v, pl.ds(x0, part)], other[r, v, pl.ds(x0, part)]
            above = jnp.where(even, a, b)
            if r < ABOVE:
                halo[pl.ds(base + r, part, stride=8), :] = above
            else:
                ghalo[pl.ds(base, part, stride=8), :] = above
            if r < BELOW:
                halo[pl.ds(base + 8 - BELOW + r, part, stride=8), :] = jnp.where(even, b, a)
    row = lax.broadcasted_iota(jnp.int32, (SLABS, 8, 128), 1)
    inside = {}
    for k in (-2, -1, 1, 2, 3):
        inside[k] = (row < 8 + k) if k < 0 else (row >= k)

    def step(i, carry):
        x = i * SLABS
        cells, face = [], []
        for v in range(5):
            at = pl.multiple_of((v * part + x) * 8, 8)
            rim_rows = halo[pl.ds(at, 8 * SLABS), :].reshape(SLABS, 8, 128)
            mid = state[v, pl.ds(x0 + x, SLABS)]
            line = []
            for k in range(-2, 4):
                if k == 0:
                    line.append(mid)
                else:
                    line.append(pltpu.roll(jnp.where(inside[k], mid, rim_rows), (-k) % 8, 1))
            cells.append(line)
            g = cot[v, pl.ds(x0 + x, SLABS)]
            g_rim = ghalo[pl.ds(at, 8 * SLABS), :].reshape(SLABS, 8, 128)
            face.append(STEP * (pltpu.roll(jnp.where(inside[1], g, g_rim), 7, 1) - g))
        terms = face_pull(cells, face, flags[1, pl.ds(x0 + x, SLABS)], 1)
        for v in range(5):
            at = pl.multiple_of((v * part + x) * 8, 8)
            mine = own[v, pl.ds(x0 + x, SLABS)] + first[v, pl.ds(x0 + x, SLABS)] + terms[v][2]
            outer = None
            for k in (-2, -1, 1, 2, 3):
                moved = pltpu.roll(terms[v][k + 2], k % 8, 1)
                kept = jnp.where(inside[k], moved, 0.0)
                mine = mine + kept
                left = moved - kept
                outer = left if outer is None else outer + left
            out[v, pl.ds(x, SLABS)] = mine
            back[pl.ds(at, 8 * SLABS), :] = outer.reshape(8 * SLABS, 128)
        return carry

    lax.fori_loop(0, part // SLABS, step, 0)


def y_kernel(state, cot, flags, twin, other, own, first, out, back, halo, ghalo):
    y_faces(0, state, cot, flags, twin, other, own, first, out, halo, ghalo, back)


def y_last_kernel(state, cot, flags, twin, other, own, first, back0, rim, order, out, give_twin, give_other, halo, ghalo, back1):
    del order
    nx = state.shape[1]
    part = out.shape[1]
    y_faces(nx - part, state, cot, flags, twin, other, own, first, out, halo, ghalo, back1)
    even = is_even()
    for v in range(5):
        base = v * part * 8
        for r in range(ABOVE):
            for h, back in ((0, back0), (1, back1)):
                rows = back[pl.ds(base + r, part, stride=8), :]
                if r == 0:
                    rows = rows + rim[pl.ds(h * part * 16 + 5 + v, part, stride=16), :]
                up = rows
                if r < BELOW:
                    rows = back[pl.ds(base + 8 - BELOW + r, part, stride=8), :]
                    if r == BELOW - 1:
                        rows = rows + rim[pl.ds(h * part * 16 + v, part, stride=16), :]
                give_twin[r, v, pl.ds(h * part, part)] = jnp.where(even, up, rows)
                give_other[r, v, pl.ds(h * part, part)] = jnp.where(even, rows, up)


def z_faces(state, cot, flags, x):
    cells, face = [], []
    for v in range(5):
        mid = state[v, pl.ds(x, SLABS)]
        cells.append([mid if k == 0 else pltpu.roll(mid, (-k) % 128, 2) for k in range(-2, 4)])
        g = cot[v, pl.ds(x, SLABS)]
        face.append(STEP * (pltpu.roll(g, 127, 2) - g))
    terms = face_pull(cells, face, flags[2, pl.ds(x, SLABS)], 2)
    total = []
    for v in range(5):
        t = terms[v][2]
        for k in (-2, -1, 1, 2, 3):
            t = t + pltpu.roll(terms[v][k + 2], k % 128, 2)
        total.append(t)
    return total


def z_kernel(state, cot, flags, before, order, order2, out):
    del order, order2
    half = out.shape[1]

    def step(i, carry):
        x = i * SLABS
        total = z_faces(state, cot, flags, x)
        for v in range(5):
            out[v, pl.ds(x, SLABS)] = before[v, pl.ds(x, SLABS)] + total[v]
        return carry

    lax.fori_loop(0, half // SLABS, step, 0)


def z_last_kernel(state, cot, flags, done, before, twin, other, order, out, halo):
    del order
    nx = state.shape[1]
    half = done.shape[1]
    even = is_even()
    for v in range(5):
        base = v * nx * 8
        for r in range(8):
            if r < ABOVE:
                rows = jnp.where(even, other[r, v], twin[r, v])
            elif r >= 8 - BELOW:
                q = r - (8 - BELOW)
                rows = jnp.where(even, twin[q, v], other[q, v])
            else:
                rows = jnp.zeros((nx, 128), F32)
            halo[pl.ds(base + r, nx, stride=8), :] = rows

    def put(x, v, value):
        at = pl.multiple_of((v * nx + x) * 8, 8)
        out[v, pl.ds(x, SLABS)] = value + halo[pl.ds(at, 8 * SLABS), :].reshape(SLABS, 8, 128)

    def step(i, carry):
        x = i * SLABS
        total = z_faces(state, cot, flags, half + x)
        for v in range(5):
            put(half + x, v, before[v, pl.ds(x, SLABS)] + total[v])
            put(x, v, done[v, pl.ds(x, SLABS)])
        return carry

    lax.fori_loop(0, half // SLABS, step, 0)


def sum_kernel(scale, mine, theirs, k_out, h_out):
    total = (mine[...] + theirs[...]) * scale
    k_out[...] = total[:, : k_out.shape[1]]
    ch = total.shape[0]
    pick = (
        lax.broadcasted_iota(jnp.int32, (8, 128), 1)
        == lax.broadcasted_iota(jnp.int32, (8, 128), 0) + 16
    ).astype(F32)
    heads = lax.dot_general(
        pick,
        total[:, 128:],
        (((1,), (1,)), ((), ())),
        precision=lax.Precision.HIGHEST,
        preferred_element_type=F32,
    )
    h_out[...] = heads[: h_out.shape[0], :ch]


def split(x):
    hi = x.astype(BF16)
    return hi, (x - hi.astype(F32)).astype(BF16)


def over_lanes(a, b):
    return lax.dot_general(a, b, (((1,), (1,)), ((), ())), preferred_element_type=F32)


def c_kernel(
    state, cot, twin, other, heads, pick, code, mass, w_rows, w_cols, bias,
    own, rim, parts,
    t, acc, edge, kg, hg, dsum,
):
    nx = state.shape[1]
    ch = heads.shape[1]
    block, slot = 56, 168

    even = is_even()
    edge[...] = jnp.zeros_like(edge)
    for v in range(5):
        level = 1.0 if v in (0, 4) else 0.0
        below = jnp.where(even, other[BELOW - 1, v], twin[BELOW - 1, v])
        above = jnp.where(even, twin[0, v], other[0, v])
        edge[pl.ds(v, nx, stride=16), :] = below - level
        edge[pl.ds(5 + v, nx, stride=16), :] = above - level

    def fill(x, carry):
        rows = [state[v, x] - (1.0 if v in (0, 4) else 0.0) for v in range(5)]
        rows.append(edge[pl.ds(pl.multiple_of(x * 16, 16), 16), :])
        mid = jnp.concatenate(rows, axis=0)
        at = pl.multiple_of((x + 1) * slot, 8)
        t[pl.ds(at, block), :] = pltpu.roll(mid, 1, 1)
        t[pl.ds(at + block, block), :] = mid
        t[pl.ds(at + 2 * block, block), :] = pltpu.roll(mid, 127, 1)
        return carry

    lax.fori_loop(0, nx, fill, 0)
    t[pl.ds(0, slot), :] = t[pl.ds(nx * slot, slot), :]
    t[pl.ds((nx + 1) * slot, slot), :] = t[pl.ds(slot, slot), :]
    t[pl.ds((nx + 2) * slot, 8), :] = jnp.zeros((8, 128), F32)
    acc[...] = jnp.zeros_like(acc)
    kg[...] = jnp.zeros_like(kg)
    hg[...] = jnp.zeros_like(hg)
    dsum[...] = jnp.zeros_like(dsum)

    r = lax.broadcasted_iota(jnp.int32, (8 * ch, ch), 0)
    q = lax.broadcasted_iota(jnp.int32, (8 * ch, ch), 1)
    spread = ((r & (ch - 1)) == q).astype(F32)
    high = dict(precision=lax.Precision.HIGHEST, preferred_element_type=F32)
    h5 = lax.dot_general(spread, heads[...], (((1,), (1,)), ((), ())), **high)
    e_of = lax.broadcasted_iota(jnp.int32, (5, 40), 0)
    c_of = lax.broadcasted_iota(jnp.int32, (5, 40), 1)
    h40 = jnp.dot(h5, ((c_of >> 3) == e_of).astype(F32), **high)
    y_row = lax.broadcasted_iota(jnp.int32, (8 * ch, 40), 0)
    y_col = lax.broadcasted_iota(jnp.int32, (8 * ch, 40), 1) & 7
    same_y = (y_row >= y_col * ch) & (y_row < (y_col + 1) * ch)
    h_hi, h_lo = split(jnp.where(same_y, STEP * h40, 0.0))
    wide_head = jnp.concatenate(
        [h_hi.astype(F32), h_lo.astype(F32), h_hi.astype(F32)], axis=1
    ).astype(BF16)

    def step(i, carry):
        x = i * WIDE
        at = [pl.multiple_of((x + j) * slot, 8) for j in range(WIDE)]
        s = jnp.concatenate([t[pl.ds(a, 512), :] for a in at], axis=1).astype(BF16)
        z2 = jnp.dot(w_rows[...], s, preferred_element_type=F32)
        z = z2[: 8 * ch] + z2[8 * ch :] + jnp.concatenate([bias[...]] * WIDE, axis=1)
        hidden = jnp.tanh(z)
        g = jnp.concatenate(
            [jnp.concatenate([cot[v, x + j] for v in range(5)], axis=0) for j in range(WIDE)], axis=1
        )
        g_hi, g_lo = split(g)
        g_hi32, g_lo32 = g_hi.astype(F32), g_lo.astype(F32)
        g3 = jnp.concatenate([g_hi32, g_hi32, g_lo32], axis=0).astype(BF16)
        d = (1.0 - hidden * hidden) * jnp.dot(wide_head, g3, preferred_element_type=F32)
        d_hi, d_lo = split(d)
        back = jnp.dot(
            w_cols[...], jnp.concatenate([d_hi, d_lo, d_hi], axis=0), preferred_element_type=F32
        )
        k2 = over_lanes(jnp.concatenate([d_hi, d_lo], axis=0), s)
        hid2 = jnp.concatenate(split(hidden), axis=0)
        g2 = jnp.concatenate([g_hi32, g_lo32], axis=0).astype(BF16)
        hg[...] = hg[...] + over_lanes(hid2, g2)
        kg[...] = kg[...] + (k2[: 8 * ch] + k2[8 * ch :])
        level = d[:, :128]
        for j in range(1, WIDE):
            level = level + d[:, 128 * j : 128 * (j + 1)]
        dsum[...] = dsum[...] + level
        for m in range(WIDE + 2):
            total = None
            for j in range(WIDE):
                if 0 <= m - j < 3:
                    q = m - j
                    piece = back[q * slot : (q + 1) * slot, 128 * j : 128 * (j + 1)]
                    total = piece if total is None else total + piece
            here = pl.multiple_of((x + m) * slot, 8)
            acc[pl.ds(here, slot), :] = acc[pl.ds(here, slot), :] + total
        return carry

    lax.fori_loop(0, nx // WIDE, step, 0)
    acc[pl.ds(nx * slot, slot), :] = acc[pl.ds(nx * slot, slot), :] + acc[pl.ds(0, slot), :]
    acc[pl.ds(slot, slot), :] = acc[pl.ds(slot, slot), :] + acc[pl.ds((nx + 1) * slot, slot), :]

    def drain(x, carry):
        at = pl.multiple_of((x + 1) * slot, 8)
        total = (
            acc[pl.ds(at + block, block), :]
            + pltpu.roll(acc[pl.ds(at, block), :], 127, 1)
            + pltpu.roll(acc[pl.ds(at + 2 * block, block), :], 1, 1)
        )
        for v in range(5):
            own[v, x] = total[8 * v : 8 * v + 8]
        rim[pl.ds(pl.multiple_of(x * 16, 16), 16), :] = total[40:56]
        return carry

    lax.fori_loop(0, nx, drain, 0)

    sums = jnp.sum(dsum[...], axis=1, keepdims=True)
    h2 = hg[...]
    h_all = (h2[: 8 * ch, :40] + h2[8 * ch :, :40]) + (h2[: 8 * ch, 40:80] + h2[8 * ch :, 40:80])
    h_all = jnp.where(same_y, h_all, 0.0)
    level_sum = jnp.zeros((ch, 1), F32)
    head_sum = jnp.zeros((ch, 40), F32)
    kind = jnp.broadcast_to(code[0:1], (ch, 512))
    total = jnp.zeros((ch, 512), F32)
    for y in range(8):
        rows = kg[pl.ds(y * ch, ch), :]
        moved = rows if y == 1 else pltpu.roll(rows, (1 - y) % 512, 1)
        keep = kind < 3
        if y == 0:
            keep = (kind == 1) | (kind == 2)
            total = total + jnp.where(kind == 8, rows, 0.0)
        if y == 7:
            keep = kind < 2
            total = total + jnp.where(kind == 9, rows, 0.0)
        total = total + jnp.where(keep, moved, 0.0)
        level_sum = level_sum + sums[y * ch : (y + 1) * ch]
        head_sum = head_sum + h_all[y * ch : (y + 1) * ch]
    grads = over_lanes(jnp.concatenate(split(total), axis=0), pick[...])
    taps = mass.shape[1]
    n_pick = pick.shape[0]
    parts[...] = jnp.zeros_like(parts)
    parts[:, pl.ds(0, n_pick)] = grads[:ch] + grads[ch:]
    parts[:, pl.ds(0, taps)] = parts[:, pl.ds(0, taps)] + level_sum * mass[...]
    e_row = lax.broadcasted_iota(jnp.int32, (40, 128), 0) >> 3
    e_col = lax.broadcasted_iota(jnp.int32, (40, 128), 1) - 16
    head_out = jnp.dot(head_sum * STEP, (e_row == e_col).astype(F32), **high)
    parts[:, pl.ds(128, 128)] = parts[:, pl.ds(128, 128)] + head_out


def band_pick():
    pick = np.zeros((144, 512), np.float32)
    code = np.full((8, 512), 10, np.int32)
    for ox in range(3):
        for oz in range(3):
            for v in range(5):
                at = (ox * 3 + oz) * 56
                tap = [(oy * 9 + ox * 3 + oz) * 5 + v for oy in range(3)]
                for k in range(8):
                    code[:, at + v * 8 + k] = k if k < 3 else 7
                for oy in range(3):
                    pick[tap[oy], at + v * 8 + oy] = 1.0
                pick[tap[0], at + 40 + v] = 1.0
                pick[tap[2], at + 45 + v] = 1.0
                code[:, at + 40 + v] = 8
                code[:, at + 45 + v] = 9
    return pick, code


def call(kernel, outs, scratch, us, n_in, order=0):
    spec = pl.BlockSpec(memory_space=pltpu.VMEM)
    return pl.pallas_call(
        kernel,
        out_shape=outs,
        in_specs=[spec] * n_in + [pl.BlockSpec(memory_space=pl.ANY)] * order,
        scratch_shapes=scratch,
        compiler_params=pltpu.CompilerParams(vmem_limit_bytes=VMEM),
        cost_estimate=pl.CostEstimate(
            flops=0, bytes_accessed=int(us * 3.69e6), transcendentals=0
        ),
    )


def body(pick, code, mass, state, cot, flags, kernel, heads):
    _, nx, ny, nz = state.shape
    ch, taps = kernel.shape
    count = lax.axis_size("gy")
    cells = nx * ny * nz
    half = nx // 2
    shape = lambda *dims: jax.ShapeDtypeStruct(dims, F32)
    full, part = shape(5, nx, ny, nz), shape(5, half, ny, nz)
    with_twin = [(i, i ^ 1) for i in range(count)]
    with_other = [(i, (i + 1) % count if i % 2 else (i - 1) % count) for i in range(count)]
    pick = jnp.asarray(pick, BF16)
    code = jnp.asarray(code)
    mass = jnp.asarray(mass)
    vm = pltpu.VMEM

    rows = shape(ABOVE + 1, 5, nx, nz)
    to_twin, to_other = call(pack_kernel, (rows, rows), [], 1.0, 2)(
        state.reshape(5 * nx * ny, nz), cot.reshape(5 * nx * ny, nz)
    )
    twin = lax.ppermute(to_twin, "gy", with_twin)
    other = lax.ppermute(to_other, "gy", with_other)

    first, w_rows, w_cols, bias = call(
        x_kernel,
        (
            full,
            jax.ShapeDtypeStruct((16 * ch, 512), BF16),
            jax.ShapeDtypeStruct((512, 24 * ch), BF16),
            shape(8 * ch, 128),
        ),
        [
            vm((5, nx + 5, ny, nz), F32),
            vm((5, nx + 1, ny, nz), F32),
            vm((5, nx + 5, ny, nz), F32),
            vm((2 * ch, pick.shape[0]), F32),
        ],
        3.2,
        7,
    )(state, cot, flags, kernel, pick, code, mass)
    own, rim, parts = call(
        c_kernel,
        (full, shape(16 * nx, nz), shape(ch, 256)),
        [
            vm(((nx + 2) * 168 + 8, nz), F32),
            vm(((nx + 2) * 168 + 8, nz), F32),
            vm((16 * nx, nz), F32),
            vm((8 * ch, 512), F32),
            vm((16 * ch, 80), F32),
            vm((8 * ch, 128), F32),
        ],
        5.0,
        11,
    )(state, cot, twin, other, heads, pick, code, mass, w_rows, w_cols, bias)

    def exchanged(value, bit):
        return lax.ppermute(value, "gy", [(i, i ^ bit) for i in range(count)])

    bits = [1 << b for b in range(count.bit_length() - 1)]
    late = bits[3:]
    sums = parts
    got = exchanged(sums, bits[0])
    halos = [vm((5 * half * ny, nz), F32)] * 2
    y0, back0 = call(
        y_kernel, (part, shape(5 * half * ny, nz)), halos, 1.6, 7
    )(state, cot, flags, twin, other, own, first)
    sums = sums + got
    got = exchanged(sums, bits[1])
    y1, give_twin, give_other = call(
        y_last_kernel,
        (part, shape(ABOVE, 5, nx, nz), shape(ABOVE, 5, nx, nz)),
        [*halos, halos[0]],
        1.8,
        9,
        1,
    )(state, cot, flags, twin, other, own, first, back0, rim, sums)
    sums = sums + got
    back_twin = lax.ppermute(give_twin, "gy", with_twin)
    back_other = lax.ppermute(give_other, "gy", with_other)
    got = exchanged(sums, bits[2])
    z0 = call(z_kernel, part, [], 1.8, 4, 2)(state, cot, flags, y0, give_twin, sums)
    sums = sums + got
    for bit in late[:-1]:
        sums = sums + exchanged(sums, bit)
    got = exchanged(sums, late[-1])
    flow = call(z_last_kernel, full, [vm((5 * nx * ny, nz), F32)], 2.6, 7, 1)(
        state, cot, flags, z0, y1, back_twin, back_other, sums
    )
    scale = float(cells * count) ** (-0.5)
    k_out, h_out = call(
        functools.partial(sum_kernel, scale), (shape(ch, taps), shape(5, ch)), [], 0.5, 2
    )(sums, got)
    return flow, k_out, h_out


def solution(mesh):
    pick, code = band_pick()
    mass = np.zeros((16, 135), np.float32)
    mass[:, 0::5] = 1.0
    mass[:, 4::5] = 1.0
    split_y = P(None, "ens", "gy", None)
    return jax.shard_map(
        functools.partial(body, pick, code, mass),
        mesh=mesh,
        in_specs=(split_y, split_y, split_y, P(), P()),
        out_specs=(split_y, P("ens", None), P("ens", None)),
        check_vma=False,
    )
```

```python
import functools

import jax
import jax.numpy as jnp
import numpy as np
from jax import lax
from jax.experimental import pallas as pl
from jax.experimental.pallas import tpu as pltpu
from jax.sharding import PartitionSpec as P

STEP = 0.3
FLOOR = 0.01
BELOW, ABOVE = 2, 3
SLABS = 2
WIDE = 4
VMEM = 48 * 1024 * 1024
F32 = jnp.float32
BF16 = jnp.bfloat16


def rcp(x):
    return pl.reciprocal(x, approx=True)


def shared_terms(v):
    p = [v[i + 1] - v[i] for i in range(5)]
    d = [p[i + 1] - p[i] for i in range(4)]
    h = [(4.0 / 3.0) * x for x in d]
    k = [h[i] * d[i] + FLOOR for i in range(4)]
    g = [x + x for x in h]
    t = [d[i + 1] - d[i] for i in range(3)]
    return p, d, k, g, t


def side_value(pa, pm, pm2, ka, kb, kc, m0, m2, td, t1, smooth, c0, c2):
    i0 = rcp(ka + pa * m0)
    i1 = rcp(kb + pa * pm)
    i2 = rcp(kc + pm * m2)
    w0 = i0 * i0
    w1 = 6.0 * (i1 * i1)
    w2 = 3.0 * (i2 * i2)
    r = rcp(w0 + w1 + w2)
    o0 = jnp.where(smooth, w0 * r, c0)
    o2 = jnp.where(smooth, w2 * r, c2)
    u = o0 * td + o2 * t1
    return (pa + pm2) - u, (i0, i1, i2, w0, w1, w2, r, o0, o2, u)


def side_pull(mu, pa, pm, m0, m2, td, t1, smooth, saved):
    i0, i1, i2, w0, w1, w2, r, o0, o2, u = saved
    mu2 = mu + mu
    rm = jnp.where(smooth, mu2, 0.0) * r
    s0 = (w0 * i0) * rm * (td - u)
    s1 = (w1 * i1) * rm * u
    s2 = (w2 * i2) * rm * (t1 - u)
    pa_bar = s0 * (m0 + pa) - s1 * pm + mu
    pm_bar = s2 * (m2 + pm) - s1 * pa + mu2
    return s0, s1, s2, pa_bar, pm_bar, o0 * mu2, o2 * mu


def hllc_pull(left, right, normal, flags, cot):
    region = flags & 3
    is_right = region >= 2
    star = ((region + 1) & 2) != 0
    n_at = 1 + normal
    tang = [1 + i for i in range(3) if i != normal]
    rl, rr_, pl_, pr_, nl, nr = left[0], right[0], left[4], right[4], left[n_at], right[n_at]

    def sound(r, p):
        inv = rcp(r)
        t = 1.4 * p * inv
        inv_c = lax.rsqrt(t)
        return inv, inv_c, t * inv_c

    inv_rl, inv_cl, cl = sound(rl, pl_)
    inv_rr, inv_cr, cr = sound(rr_, pr_)
    c = 0.5 * (cl + cr)
    r2 = rl + rr_
    inv = rcp(r2 * c)
    nm = 0.5 * (nl + nr)
    gap = (pl_ - pr_) * inv
    sm = nm + gap
    sc = jnp.where(is_right, c, -c)
    s = nm + sc
    pick = [jnp.where(is_right, right[i], left[i]) for i in range(5)]
    r, un, u1, u2, p = pick[0], pick[n_at], pick[tang[0]], pick[tang[1]], pick[4]
    a = s - un
    dl = sm - un
    si = jnp.where(star, rcp(sc - gap), 0.0)
    j = s * si
    kap = j * dl
    g0, gn, g1, g2, ge = cot[0], cot[n_at], cot[tang[0]], cot[tang[1]], cot[4]
    w = un + kap
    half_q = 0.5 * (un * un + u1 * u1 + u2 * u2)
    enthalpy = 3.5 * p + r * half_q
    b = g0 + u1 * g1 + u2 * g2 + un * gn
    m = r * b + enthalpy * ge
    n = gn + sm * ge
    rkap = r * kap
    f_kap = m + r * a * n
    f_a = rkap * n
    si2 = si * si
    s_bar = f_a - f_kap * (dl * sm * si2)
    sm_bar = f_kap * (s * a * si2) + rkap * a * ge
    wr = w * r
    k_bar = [None] * 5
    k_bar[0] = w * (b + half_q * ge) + kap * a * n
    k_bar[n_at] = m + wr * (gn + un * ge) - f_kap * j - f_a
    k_bar[tang[0]] = wr * (g1 + u1 * ge)
    k_bar[tang[1]] = wr * (g2 + u2 * ge)
    k_bar[4] = 3.5 * (w * ge) + gn
    e = sm_bar * inv
    eg = e * gap
    c_half = 0.5 * (jnp.where(is_right, s_bar, -s_bar) - eg * r2)
    n_half = 0.5 * (s_bar + sm_bar)
    r_both = -(eg * c)
    xl = c_half * inv_rl
    xr = c_half * inv_rr
    base_l = {0: r_both - 0.5 * (xl * cl), n_at: n_half, 4: 0.7 * (xl * inv_cl) + e}
    base_r = {0: r_both - 0.5 * (xr * cr), n_at: n_half, 4: 0.7 * (xr * inv_cr) - e}
    l_bar, r_bar = [], []
    for i in range(5):
        kr = jnp.where(is_right, k_bar[i], 0.0)
        kl = k_bar[i] - kr
        l_bar.append(base_l[i] + kl if i in base_l else kl)
        r_bar.append(base_r[i] + kr if i in base_r else kr)
    return l_bar, r_bar


def face_pull(cells, cot, flags, normal):
    stencil = flags >> 2
    smooth = stencil == 0
    c0 = jnp.where(stencil == 1, 1.0, 0.0)
    c2 = jnp.where(stencil == 3, 1.0, 0.0)
    left, right, kept = [], [], []
    for v in cells:
        p, d, k, g, t = shared_terms(v)
        pm2 = p[2] + p[2]
        args_l = (p[1], p[2], p[1] + d[0], p[2] - d[2], t[0] + t[0], t[1])
        args_r = (p[3], p[2], p[3] - d[3], p[2] + d[1], t[2] + t[2], t[1])
        hl, saved_l = side_value(
            p[1], p[2], pm2, k[0], k[1], k[2], *args_l[2:], smooth, c0, c2
        )
        hr, saved_r = side_value(
            p[3], p[2], pm2, k[3], k[2], k[1], *args_r[2:], smooth, c0, c2
        )
        left.append(v[2] + hl * (1.0 / 6.0))
        right.append(v[3] - hr * (1.0 / 6.0))
        kept.append((p, g, args_l, args_r, saved_l, saved_r))
    l_bar, r_bar = hllc_pull(left, right, normal, flags, cot)
    out = []
    for i in range(5):
        p, g, args_l, args_r, saved_l, saved_r = kept[i]
        a0, a1, a2, pa_l, pm_l, x0, x2 = side_pull(
            l_bar[i] * (1.0 / 6.0), *args_l, smooth, saved_l
        )
        b0, b1, b2, pa_r, pm_r, y0, y2 = side_pull(
            r_bar[i] * (-1.0 / 6.0), *args_r, smooth, saved_r
        )
        d0 = a0 * (g[0] + p[1]) + x0
        d1 = (b2 * (g[1] + p[2]) - a1 * g[1]) + (x2 - x0) + y2
        d2 = (a2 * (g[2] - p[2]) - b1 * g[2]) + (y0 - y2) - x2
        d3 = b0 * (g[3] - p[3]) - y0
        p2 = pa_l + (d0 - d1)
        p3 = pm_l + pm_r + (d1 - d2)
        p4 = pa_r + (d2 - d3)
        out.append([d0, -d0 - p2, l_bar[i] + (p2 - p3), r_bar[i] + (p3 - p4), p4 - d3, d3])
    return out


def conserved_pull(s, g):
    half_q = 0.5 * (s[1] * s[1] + s[2] * s[2] + s[3] * s[3])
    return [
        g[0] + s[1] * g[1] + s[2] * g[2] + s[3] * g[3] + half_q * g[4],
        s[0] * (g[1] + s[1] * g[4]),
        s[0] * (g[2] + s[2] * g[4]),
        s[0] * (g[3] + s[3] * g[4]),
        2.5 * g[4],
    ]


REACH_STATE, REACH_COT, REACH_FLAGS = 5, 3, 3
COT_AT = 5 * REACH_STATE
FLAGS_AT = COT_AT + 5 * REACH_COT
SENT = FLAGS_AT + REACH_FLAGS


def pack_kernel(state, cot, flags, twin, other, s, g, f, sem):
    rows_in = f.shape[0]
    copies = [
        pltpu.make_async_copy(state, s, sem.at[0]),
        pltpu.make_async_copy(cot, g, sem.at[1]),
        pltpu.make_async_copy(flags.at[pl.ds(rows_in, rows_in)], f, sem.at[2]),
    ]
    for copy in copies:
        copy.start()
    for copy in copies:
        copy.wait()
    even = is_even()
    nx = twin.shape[1]

    def put(at, low, top):
        twin[at] = jnp.where(even, top, low)
        other[at] = jnp.where(even, low, top)

    for v in range(5):
        base = v * nx * 8
        for ref, reach, at in ((s, REACH_STATE, 0), (g, REACH_COT, COT_AT)):
            for r in range(reach):
                put(
                    at + r * 5 + v,
                    ref[pl.ds(base + r, nx, stride=8), :],
                    ref[pl.ds(base + 8 - reach + r, nx, stride=8), :],
                )
    for r in range(REACH_FLAGS):
        low = f[pl.ds(r, nx, stride=8), :]
        top = f[pl.ds(8 - REACH_FLAGS + r, nx, stride=8), :]
        put(FLAGS_AT + r, low.astype(F32), top.astype(F32))


def from_rims(twin, other):
    even = is_even()

    def read(row, reach, at, v):
        if row < 0:
            i = at + (reach + row) * 5 + v
            return jnp.where(even, other[i], twin[i])
        i = at + (row - 8) * 5 + v
        return jnp.where(even, twin[i], other[i])

    def state(row, v):
        return read(row, REACH_STATE, 0, v)

    def cot(row, v):
        return read(row, REACH_COT, COT_AT, v)

    def flags(row):
        if row < 0:
            i = FLAGS_AT + REACH_FLAGS + row
            return jnp.where(even, other[i], twin[i])
        i = FLAGS_AT + row - 8
        return jnp.where(even, twin[i], other[i])

    return state, cot, flags


def xz_kernel(state, cot, flags, kernel, heads, pick, pick2, code, mass, out, w_rows, w_cols, w_head, bias, pad, gpad, acc, wide):
    nx = state.shape[1]
    for v in range(5):
        pad[v, pl.ds(2, nx)] = state[v]
        pad[v, pl.ds(0, 2)] = state[v, pl.ds(nx - 2, 2)]
        pad[v, pl.ds(nx + 2, 3)] = state[v, pl.ds(0, 3)]
        gpad[v, pl.ds(0, nx)] = cot[v]
        gpad[v, pl.ds(nx, 1)] = cot[v, pl.ds(0, 1)]
    acc[...] = jnp.zeros_like(acc)

    def step(i, carry):
        x = i * SLABS
        cells = [[pad[v, pl.ds(x + k, SLABS)] for k in range(6)] for v in range(5)]
        g = [gpad[v, pl.ds(x, SLABS)] for v in range(5)]
        face = [STEP * (gpad[v, pl.ds(x + 1, SLABS)] - g[v]) for v in range(5)]
        terms = face_pull(cells, face, flags[0, pl.ds(x, SLABS)], 0)
        own = conserved_pull([cells[v][2] for v in range(5)], g)
        for v in range(5):
            terms[v][2] = terms[v][2] + own[v]
            for s in range(SLABS + 5):
                total = None
                for k in range(6):
                    if 0 <= s - k < SLABS:
                        part = terms[v][k][s - k]
                        total = part if total is None else total + part
                acc[v, x + s] = acc[v, x + s] + total
        return carry

    lax.fori_loop(0, nx // SLABS, step, 0)
    for v in range(5):
        acc[v, pl.ds(nx, 2)] = acc[v, pl.ds(nx, 2)] + acc[v, pl.ds(0, 2)]
        acc[v, pl.ds(2, 3)] = acc[v, pl.ds(2, 3)] + acc[v, pl.ds(nx + 2, 3)]

    def z_step(i, carry):
        x = i * SLABS
        cells, face = [], []
        for v in range(5):
            mid = state[v, pl.ds(x, SLABS)]
            cells.append([mid if k == 0 else pltpu.roll(mid, (-k) % 128, 2) for k in range(-2, 4)])
            g = cot[v, pl.ds(x, SLABS)]
            face.append(STEP * (pltpu.roll(g, 127, 2) - g))
        terms = face_pull(cells, face, flags[2, pl.ds(x, SLABS)], 2)
        for v in range(5):
            t = acc[v, pl.ds(x + 2, SLABS)] + terms[v][2]
            for k in (-2, -1, 1, 2, 3):
                t = t + pltpu.roll(terms[v][k + 2], k % 128, 2)
            out[v, pl.ds(x, SLABS)] = t
        return carry

    lax.fori_loop(0, nx // SLABS, z_step, 0)

    ch, taps = kernel.shape
    w = kernel[...]
    hi, lo = split(w)
    wide[...] = jnp.zeros_like(wide)
    wide[pl.ds(0, ch), pl.ds(0, taps)] = hi.astype(F32)
    wide[pl.ds(ch, ch), pl.ds(0, taps)] = lo.astype(F32)
    both = wide[...].astype(BF16)
    base = jnp.dot(both, pick[...], preferred_element_type=F32)
    rim = jnp.dot(both, pick2[...], preferred_element_type=F32)
    n = base.shape[1]
    kind = jnp.broadcast_to(code[0:1], base.shape)
    main = jnp.where(kind < 3, base, 0.0)
    bands = []
    for y in range(8):
        rows = main
        if y == 0:
            rows = jnp.where(kind == 0, 0.0, rows)
        if y == 7:
            rows = jnp.where(kind == 2, 0.0, rows)
        if y != 1:
            rows = pltpu.roll(rows, (y - 1) % n, 1)
        if y == 0:
            rows = rows + jnp.where(kind == 9, base, 0.0)
        if y == 7:
            rows = rows + jnp.where(kind == 10, base, 0.0)
        bands.append(rows)
    bands.append(jnp.where((kind == 0) | (kind == 8) | (kind == 9), rim, 0.0))
    bands.append(jnp.where((kind == 7) | (kind == 10) | (kind == 11), rim, 0.0))
    full = jnp.concatenate([b[:ch] for b in bands] + [b[ch:] for b in bands], axis=0)
    w_rows[...] = full.astype(BF16)
    kept = full.shape[0] // 2
    cols = jnp.concatenate([full[:kept], full[:kept], full[kept:]], axis=0)
    cols = jnp.concatenate([cols, jnp.zeros((512 - 3 * kept, n), F32)], axis=0)
    own_cols = []
    for q in range(3):
        own_cols += [cols[:, (3 * q + o) * BLOCK : (3 * q + o) * BLOCK + 40] for o in range(3)]
        own_cols.append(jnp.zeros((512, 8), F32))
    w_cols[...] = jnp.concatenate(own_cols, axis=1).T.astype(BF16)
    total = jnp.sum(w * mass[...], axis=1, keepdims=True)
    total = jnp.broadcast_to(total, (ch, 128))
    bias[...] = jnp.concatenate([total] * 10, axis=0)

    h_hi, h_lo = split(STEP * heads[...])
    none = jnp.zeros((3, ch), F32)
    pair = jnp.concatenate([h_hi.astype(F32), none, h_lo.astype(F32), none], axis=0).astype(BF16)
    r = lax.broadcasted_iota(jnp.int32, (kept, ch), 0)
    q = lax.broadcasted_iota(jnp.int32, (kept, ch), 1)
    spread = jnp.where((r & (ch - 1)) == q, 1.0, 0.0).astype(BF16)
    picked = over_lanes(pair, spread)
    y_of = lax.broadcasted_iota(jnp.int32, (8, kept), 0)
    col = lax.broadcasted_iota(jnp.int32, (8, kept), 1)
    same = (col >= y_of * ch) & (col < (y_of + 1) * ch)
    split_heads = []
    for at in (0, 8):
        rows = [
            jnp.where(same, jnp.broadcast_to(picked[at + e : at + e + 1], (8, kept)), 0.0)
            for e in range(5)
        ]
        five = picked[at : at + 8]
        rows.append(jnp.where((col >= 8 * ch) & (col < 9 * ch), five, 0.0))
        rows.append(jnp.where(col >= 9 * ch, five, 0.0))
        rows.append(jnp.zeros((8, kept), F32))
        split_heads.append(jnp.concatenate(rows, axis=0))
    three = jnp.concatenate([split_heads[0], split_heads[1], split_heads[0]], axis=0)
    w_head[...] = three.T.astype(BF16)


def e_kernel(state, cot, twin, other, order, out):
    del order
    nx = twin.shape[1]
    rim_state, rim_cot, rim_flags = from_rims(twin, other)

    def own(ref, row, v):
        return ref[pl.ds(v * nx * 8 + row, nx, stride=8), :]

    state_rows, cot_rows = {}, {}
    for v in range(5):
        for row in (*range(-5, 3), *range(6, 13)):
            inside = 0 <= row < 8
            state_rows[row, v] = own(state, row, v) if inside else rim_state(row, v)
        for row in (-3, -2, -1, 0, 8, 9, 10):
            inside = 0 <= row < 8
            cot_rows[row, v] = own(cot, row, v) if inside else rim_cot(row, v)
    sums = {}
    for j in (-3, -2, -1, 8, 9):
        cells = [[state_rows[j + k, v] for k in range(-2, 4)] for v in range(5)]
        face = [STEP * (cot_rows[j + 1, v] - cot_rows[j, v]) for v in range(5)]
        terms = face_pull(cells, face, rim_flags(j).astype(jnp.int32), 1)
        for v in range(5):
            for k in range(-2, 4):
                if 0 <= j + k < 8:
                    t = terms[v][k + 2]
                    sums[j + k, v] = sums[j + k, v] + t if (j + k, v) in sums else t
    for v in range(5):
        for row in range(8):
            value = sums[row, v] if (row, v) in sums else jnp.zeros((nx, 128), F32)
            out[pl.ds(v * nx * 8 + row, nx, stride=8), :] = value


def y_faces(x0, state, cot, flags, twin, other, own, first, rim, put, part, halo, ghalo):
    rim_state, rim_cot, _ = from_rims(twin, other)
    nx = state.shape[1]
    for v in range(5):
        base = v * nx * 8
        for r in range(ABOVE):
            halo[pl.ds(base + r, nx, stride=8), :] = rim_state(8 + r, v)
        for r in range(BELOW):
            halo[pl.ds(base + 8 - BELOW + r, nx, stride=8), :] = rim_state(r - BELOW, v)
        ghalo[pl.ds(base, nx, stride=8), :] = rim_cot(8, v)
    row = lax.broadcasted_iota(jnp.int32, (SLABS, 8, 128), 1)
    inside = {}
    for k in (-2, -1, 1, 2, 3):
        inside[k] = (row < 8 + k) if k < 0 else (row >= k)

    def step(i, carry):
        x = x0 + i * SLABS
        cells, face = [], []
        for v in range(5):
            at = pl.multiple_of((v * nx + x) * 8, 8)
            rim_rows = halo[pl.ds(at, 8 * SLABS), :].reshape(SLABS, 8, 128)
            mid = state[v, pl.ds(x, SLABS)]
            line = []
            for k in range(-2, 4):
                if k == 0:
                    line.append(mid)
                else:
                    line.append(pltpu.roll(jnp.where(inside[k], mid, rim_rows), (-k) % 8, 1))
            cells.append(line)
            g = cot[v, pl.ds(x, SLABS)]
            g_rim = ghalo[pl.ds(at, 8 * SLABS), :].reshape(SLABS, 8, 128)
            face.append(STEP * (pltpu.roll(jnp.where(inside[1], g, g_rim), 7, 1) - g))
        terms = face_pull(cells, face, flags[1, pl.ds(x, SLABS)], 1)
        for v in range(5):
            at = pl.multiple_of((v * nx + x) * 8, 8)
            total = own[v, pl.ds(x, SLABS)] + first[v, pl.ds(x, SLABS)] + terms[v][2]
            total = total + rim[pl.ds(at, 8 * SLABS), :].reshape(SLABS, 8, 128)
            for k in (-2, -1, 1, 2, 3):
                moved = pltpu.roll(terms[v][k + 2], k % 8, 1)
                total = total + jnp.where(inside[k], moved, 0.0)
            put(i, x, v, total)
        return carry

    lax.fori_loop(0, part // SLABS, step, 0)


def y_kernel(state, cot, flags, twin, other, own, first, rim, order, out, halo, ghalo):
    del order
    part = out.shape[1]

    def put(i, x, v, total):
        out[v, pl.ds(x, SLABS)] = total

    y_faces(0, state, cot, flags, twin, other, own, first, rim, put, part, halo, ghalo)


def y_last_kernel(state, cot, flags, twin, other, own, first, rim, done, order, out, halo, ghalo):
    del order
    part = done.shape[1]
    half = out.shape[1] - part

    def put(i, x, v, total):
        out[v, pl.ds(x, SLABS)] = total
        out[v, pl.ds(i * SLABS, SLABS)] = done[v, pl.ds(i * SLABS, SLABS)]

    y_faces(half, state, cot, flags, twin, other, own, first, rim, put, part, halo, ghalo)


def sum_kernel(scale, mine, theirs, k_out, h_out):
    total = (mine[...] + theirs[...]) * scale
    k_out[...] = total[:, : k_out.shape[1]]
    ch = total.shape[0]
    pick = (
        lax.broadcasted_iota(jnp.int32, (8, 128), 1)
        == lax.broadcasted_iota(jnp.int32, (8, 128), 0) + 16
    ).astype(F32)
    heads = lax.dot_general(
        pick,
        total[:, 128:],
        (((1,), (1,)), ((), ())),
        precision=lax.Precision.HIGHEST,
        preferred_element_type=F32,
    )
    h_out[...] = heads[: h_out.shape[0], :ch]


BLOCK = 64
SLOT = 3 * BLOCK


def split(x):
    hi = x.astype(BF16)
    return hi, (x - hi.astype(F32)).astype(BF16)


def over_lanes(a, b):
    return lax.dot_general(a, b, (((1,), (1,)), ((), ())), preferred_element_type=F32)


def is_even():
    return lax.rem(lax.axis_index("gy"), 2) == 0


def c_kernel(
    state, cot, twin, other, pick, code, mass, w_rows, w_cols, w_head, bias,
    own, parts,
    t, acc, edge, gedge,
):
    nx = state.shape[1]
    ch, taps = mass.shape
    rim_state, rim_cot, _ = from_rims(twin, other)

    for v in range(5):
        level = 1.0 if v in (0, 4) else 0.0
        for q, row in enumerate((-2, -1, 8, 9)):
            edge[pl.ds(5 * q + v, nx, stride=24), :] = rim_state(row, v) - level
        gedge[pl.ds(v, nx, stride=16), :] = rim_cot(-1, v)
        gedge[pl.ds(8 + v, nx, stride=16), :] = rim_cot(8, v)
    for q in range(20, 24):
        edge[pl.ds(q, nx, stride=24), :] = jnp.zeros((nx, 128), F32)
    for q in (5, 6, 7):
        gedge[pl.ds(q, nx, stride=16), :] = jnp.zeros((nx, 128), F32)
        gedge[pl.ds(8 + q, nx, stride=16), :] = jnp.zeros((nx, 128), F32)
    for x in range(nx):
        rows = [state[v, x] - (1.0 if v in (0, 4) else 0.0) for v in range(5)]
        rows.append(edge[pl.ds(x * 24, 24), :])
        mid = jnp.concatenate(rows, axis=0)
        at = (x + 1) * SLOT
        t[pl.ds(at, BLOCK), :] = pltpu.roll(mid, 1, 1).astype(BF16)
        t[pl.ds(at + BLOCK, BLOCK), :] = mid.astype(BF16)
        t[pl.ds(at + 2 * BLOCK, BLOCK), :] = pltpu.roll(mid, 127, 1).astype(BF16)
    t[pl.ds(0, SLOT), :] = t[pl.ds(nx * SLOT, SLOT), :]
    t[pl.ds((nx + 1) * SLOT, SLOT), :] = t[pl.ds(SLOT, SLOT), :]

    kept = 8 * ch
    kg = hg = dsum = None
    zeros8 = jnp.zeros((8, 128 * WIDE), F32)
    written = set()
    for x in range(0, nx, WIDE):
        s = jnp.concatenate([t[pl.ds((x + j) * SLOT, 3 * SLOT), :] for j in range(WIDE)], axis=1)
        z2 = jnp.dot(w_rows[...], s, preferred_element_type=F32)
        rows = z2.shape[0] // 2
        z = z2[:rows] + z2[rows:] + jnp.concatenate([bias[...]] * WIDE, axis=1)
        hidden = jnp.tanh(z)
        g = jnp.concatenate(
            [
                jnp.concatenate(
                    [cot[v, x + j] for v in range(5)] + [gedge[pl.ds((x + j) * 16, 16), :]], axis=0
                )
                for j in range(WIDE)
            ],
            axis=1,
        )
        g_hi, g_lo = split(g)
        g_hi32, g_lo32 = g_hi.astype(F32), g_lo.astype(F32)
        g3 = jnp.concatenate(
            [g_hi32, zeros8, g_hi32, zeros8, g_lo32, zeros8], axis=0
        ).astype(BF16)
        d = (1.0 - hidden * hidden) * jnp.dot(w_head[...], g3, preferred_element_type=F32)
        d_hi, d_lo = split(d)
        zeros = jnp.zeros((512 - 3 * rows, 128 * WIDE), BF16)
        back = jnp.dot(
            w_cols[...],
            jnp.concatenate([d_hi, d_lo, d_hi, zeros], axis=0),
            preferred_element_type=F32,
        )
        k2 = over_lanes(jnp.concatenate([d_hi[:kept], d_lo[:kept]], axis=0), s)
        k2 = k2[:kept] + k2[kept:]
        kg = k2 if kg is None else kg + k2
        hid2 = jnp.concatenate(split(hidden[:kept]), axis=0)
        g2 = jnp.concatenate([g_hi32[:40], g_lo32[:40]], axis=0).astype(BF16)
        h2 = over_lanes(hid2, g2)
        hg = h2 if hg is None else hg + h2
        for j in range(WIDE):
            level = d[:kept, 128 * j : 128 * (j + 1)]
            dsum = level if dsum is None else dsum + level
        for m in range(WIDE + 2):
            total = None
            for j in range(WIDE):
                if 0 <= m - j < 3:
                    q = m - j
                    piece = back[q * 128 : q * 128 + 120, 128 * j : 128 * (j + 1)]
                    total = piece if total is None else total + piece
            here = (x + m - 1) % nx
            if here in written:
                total = total + acc[pl.ds(here * 120, 120), :]
            written.add(here)
            acc[pl.ds(here * 120, 120), :] = total
    for x in range(nx):
        at = x * 120
        total = (
            acc[pl.ds(at + 40, 40), :]
            + pltpu.roll(acc[pl.ds(at, 40), :], 127, 1)
            + pltpu.roll(acc[pl.ds(at + 80, 40), :], 1, 1)
        )
        for v in range(5):
            own[v, x] = total[8 * v : 8 * v + 8]

    sums = jnp.sum(dsum, axis=1, keepdims=True)
    y_row = lax.broadcasted_iota(jnp.int32, (kept, 40), 0)
    y_col = lax.broadcasted_iota(jnp.int32, (kept, 40), 1) & 7
    same_y = (y_row >= y_col * ch) & (y_row < (y_col + 1) * ch)
    h_all = (hg[:kept, :40] + hg[kept:, :40]) + (hg[:kept, 40:80] + hg[kept:, 40:80])
    h_all = jnp.where(same_y, h_all, 0.0)
    level_sum = jnp.zeros((ch, 1), F32)
    head_sum = jnp.zeros((ch, 40), F32)
    n = kg.shape[1]
    kind = jnp.broadcast_to(code[0:1], (ch, n))
    total = jnp.zeros((ch, n), F32)
    for y in range(8):
        rows = kg[y * ch : (y + 1) * ch]
        moved = rows if y == 1 else pltpu.roll(rows, (1 - y) % n, 1)
        keep = kind < 3
        if y == 0:
            keep = (kind == 1) | (kind == 2)
            total = total + jnp.where(kind == 9, rows, 0.0)
        if y == 7:
            keep = kind < 2
            total = total + jnp.where(kind == 10, rows, 0.0)
        total = total + jnp.where(keep, moved, 0.0)
        level_sum = level_sum + sums[y * ch : (y + 1) * ch]
        head_sum = head_sum + h_all[y * ch : (y + 1) * ch]
    grads = over_lanes(jnp.concatenate(split(total), axis=0), pick[...])
    n_pick = pick.shape[0]
    parts[...] = jnp.zeros_like(parts)
    parts[:, pl.ds(0, n_pick)] = grads[:ch] + grads[ch:]
    parts[:, pl.ds(0, taps)] = parts[:, pl.ds(0, taps)] + level_sum * mass[...]
    e_row = lax.broadcasted_iota(jnp.int32, (40, 128), 0) >> 3
    e_col = lax.broadcasted_iota(jnp.int32, (40, 128), 1) - 16
    to_col = jnp.where(e_row == e_col, 1.0, 0.0).astype(BF16)
    head_out = jnp.dot(
        jnp.concatenate(split(head_sum * STEP), axis=0), to_col, preferred_element_type=F32
    )
    parts[:, pl.ds(128, 128)] = parts[:, pl.ds(128, 128)] + (head_out[:ch] + head_out[ch:])


def band_pick():
    n = 9 * BLOCK
    pick = np.zeros((144, n), np.float32)
    pick2 = np.zeros((144, n), np.float32)
    code = np.full((8, n), 12, np.int32)
    for o in range(9):
        for v in range(5):
            at = o * BLOCK
            tap = [(oy * 9 + o) * 5 + v for oy in range(3)]
            for k in range(8):
                code[:, at + v * 8 + k] = k
            for q in range(4):
                code[:, at + 40 + 5 * q + v] = 8 + q
            for oy in range(3):
                pick[tap[oy], at + v * 8 + oy] = 1.0
            pick[tap[0], at + 45 + v] = 1.0
            pick[tap[2], at + 50 + v] = 1.0
            pick2[tap[0], at + 40 + v] = 1.0
            pick2[tap[1], at + 45 + v] = 1.0
            pick2[tap[2], at + v * 8] = 1.0
            pick2[tap[0], at + v * 8 + 7] = 1.0
            pick2[tap[1], at + 50 + v] = 1.0
            pick2[tap[2], at + 55 + v] = 1.0
    return pick, pick2, code


def call(kernel, outs, scratch, us, n_in, order=0, space=pl.ANY, limit=VMEM):
    spec = pl.BlockSpec(memory_space=pltpu.VMEM)
    return pl.pallas_call(
        kernel,
        out_shape=outs,
        in_specs=[spec] * n_in + [pl.BlockSpec(memory_space=space)] * order,
        scratch_shapes=scratch,
        compiler_params=pltpu.CompilerParams(vmem_limit_bytes=limit),
        cost_estimate=pl.CostEstimate(
            flops=0, bytes_accessed=int(us * 3.69e6), transcendentals=0
        ),
    )


def body(pick, pick2, code, mass, state, cot, flags, kernel, heads):
    _, nx, ny, nz = state.shape
    ch, taps = kernel.shape
    count = lax.axis_size("gy")
    cells = nx * ny * nz
    half = nx // 2
    shape = lambda *dims: jax.ShapeDtypeStruct(dims, F32)
    half_shape = lambda *dims: jax.ShapeDtypeStruct(dims, BF16)
    full, part = shape(5, nx, ny, nz), shape(5, half, ny, nz)
    with_twin = [(i, i ^ 1) for i in range(count)]
    with_other = [(i, (i + 1) % count if i % 2 else (i - 1) % count) for i in range(count)]
    pick, pick2 = jnp.asarray(pick, BF16), jnp.asarray(pick2, BF16)
    code = jnp.asarray(code)
    mass = jnp.asarray(mass)
    vm = pltpu.VMEM
    lines = 5 * nx * ny
    flat_state, flat_cot = state.reshape(lines, nz), cot.reshape(lines, nz)

    sent = shape(SENT, nx, nz)
    to_twin, to_other = call(
        pack_kernel,
        (sent, sent),
        [
            vm((lines, nz), F32),
            vm((lines, nz), F32),
            vm((nx * ny, nz), jnp.int32),
            pltpu.SemaphoreType.DMA((3,)),
        ],
        1.0,
        0,
        3,
        pltpu.HBM,
        64 * 1024 * 1024 - 256 * 1024,
    )(flat_state, flat_cot, flags.reshape(3 * nx * ny, nz))
    twin = lax.ppermute(to_twin, "gy", with_twin)
    other = lax.ppermute(to_other, "gy", with_other)

    first, w_rows, w_cols, w_head, bias = call(
        xz_kernel,
        (
            full,
            half_shape(20 * ch, 9 * BLOCK),
            half_shape(384, 512),
            half_shape(10 * ch, SLOT),
            shape(10 * ch, 128),
        ),
        [
            vm((5, nx + 5, ny, nz), F32),
            vm((5, nx + 1, ny, nz), F32),
            vm((5, nx + 5, ny, nz), F32),
            vm((2 * ch, pick.shape[0]), F32),
        ],
        6.6,
        9,
    )(state, cot, flags, kernel, heads, pick, pick2, code, mass)
    own, parts = call(
        c_kernel,
        (full, shape(ch, 256)),
        [
            vm(((nx + 2) * SLOT, nz), BF16),
            vm((nx * 120, nz), F32),
            vm((24 * nx, nz), F32),
            vm((16 * nx, nz), F32),
        ],
        5.0,
        11,
    )(state, cot, twin, other, pick, code, mass, w_rows, w_cols, w_head, bias)

    def exchanged(value, bit):
        return lax.ppermute(value, "gy", [(i, i ^ bit) for i in range(count)])

    bits = [1 << b for b in range(count.bit_length() - 1)]
    sums = parts
    for bit in bits[:-3]:
        sums = sums + exchanged(sums, bit)
    halos = [vm((lines, nz), F32)] * 2
    got = exchanged(sums, bits[-3])
    rim = call(e_kernel, shape(lines, nz), [], 2.0, 4, 1)(
        flat_state, flat_cot, twin, other, sums
    )
    got, rim = lax.optimization_barrier((got, rim))
    sums = sums + got
    got = exchanged(sums, bits[-2])
    y0 = call(y_kernel, part, halos, 1.6, 8, 1)(
        state, cot, flags, twin, other, own, first, rim, sums
    )
    got, y0 = lax.optimization_barrier((got, y0))
    sums = sums + got
    got = exchanged(sums, bits[-1])
    flow = call(y_last_kernel, full, halos, 2.0, 9, 1)(
        state, cot, flags, twin, other, own, first, rim, y0, sums
    )
    scale = float(cells * count) ** (-0.5)
    k_out, h_out = call(
        functools.partial(sum_kernel, scale), (shape(ch, taps), shape(5, ch)), [], 0.5, 2
    )(sums, got)
    return flow, k_out, h_out


def solution(mesh):
    picks = band_pick()
    mass = np.zeros((16, 135), np.float32)
    mass[:, 0::5] = 1.0
    mass[:, 4::5] = 1.0
    split_y = P(None, "ens", "gy", None)
    return jax.shard_map(
        functools.partial(body, *picks, mass),
        mesh=mesh,
        in_specs=(split_y, split_y, split_y, P(), P()),
        out_specs=(split_y, P("ens", None), P("ens", None)),
        check_vma=False,
    )
```

```python
import functools

import jax
import jax.numpy as jnp
from jax import lax
from jax.experimental import pallas as pl
from jax.experimental.pallas import tpu as pltpu
from jax.sharding import PartitionSpec as P

STEP = 0.3
FLOOR = 0.01
BELOW, ABOVE = 2, 3
SLABS = 2
WIDE = 4
VMEM = 48 * 1024 * 1024
F32 = jnp.float32
BF16 = jnp.bfloat16


def rcp(x):
    return pl.reciprocal(x, approx=True)


def shared_terms(v):
    p = [v[i + 1] - v[i] for i in range(5)]
    d = [p[i + 1] - p[i] for i in range(4)]
    h = [(4.0 / 3.0) * x for x in d]
    k = [h[i] * d[i] + FLOOR for i in range(4)]
    g = [x + x for x in h]
    t = [d[i + 1] - d[i] for i in range(3)]
    return p, d, k, g, t


def side_value(pa, pm, pm2, ka, kb, kc, m0, m2, td, t1, smooth, c0, c2):
    i0 = rcp(ka + pa * m0)
    i1 = rcp(kb + pa * pm)
    i2 = rcp(kc + pm * m2)
    w0 = i0 * i0
    w1 = 6.0 * (i1 * i1)
    w2 = 3.0 * (i2 * i2)
    r = rcp(w0 + w1 + w2)
    o0 = jnp.where(smooth, w0 * r, c0)
    o2 = jnp.where(smooth, w2 * r, c2)
    u = o0 * td + o2 * t1
    return (pa + pm2) - u, (i0, i1, i2, w0, w1, w2, r, o0, o2, u)


def side_pull(mu, pa, pm, m0, m2, td, t1, smooth, saved):
    i0, i1, i2, w0, w1, w2, r, o0, o2, u = saved
    mu2 = mu + mu
    rm = jnp.where(smooth, mu2, 0.0) * r
    s0 = (w0 * i0) * rm * (td - u)
    s1 = (w1 * i1) * rm * u
    s2 = (w2 * i2) * rm * (t1 - u)
    pa_bar = s0 * (m0 + pa) - s1 * pm + mu
    pm_bar = s2 * (m2 + pm) - s1 * pa + mu2
    return s0, s1, s2, pa_bar, pm_bar, o0 * mu2, o2 * mu


def hllc_pull(left, right, normal, flags, cot):
    region = flags & 3
    is_right = region >= 2
    star = ((region + 1) & 2) != 0
    n_at = 1 + normal
    tang = [1 + i for i in range(3) if i != normal]
    rl, rr_, pl_, pr_, nl, nr = left[0], right[0], left[4], right[4], left[n_at], right[n_at]

    def sound(r, p):
        inv = rcp(r)
        t = 1.4 * p * inv
        inv_c = lax.rsqrt(t)
        return inv, inv_c, t * inv_c

    inv_rl, inv_cl, cl = sound(rl, pl_)
    inv_rr, inv_cr, cr = sound(rr_, pr_)
    c = 0.5 * (cl + cr)
    r2 = rl + rr_
    inv = rcp(r2 * c)
    nm = 0.5 * (nl + nr)
    gap = (pl_ - pr_) * inv
    sm = nm + gap
    sc = jnp.where(is_right, c, -c)
    s = nm + sc
    pick = [jnp.where(is_right, right[i], left[i]) for i in range(5)]
    r, un, u1, u2, p = pick[0], pick[n_at], pick[tang[0]], pick[tang[1]], pick[4]
    a = s - un
    dl = sm - un
    si = jnp.where(star, rcp(sc - gap), 0.0)
    j = s * si
    kap = j * dl
    g0, gn, g1, g2, ge = cot[0], cot[n_at], cot[tang[0]], cot[tang[1]], cot[4]
    w = un + kap
    half_q = 0.5 * (un * un + u1 * u1 + u2 * u2)
    enthalpy = 3.5 * p + r * half_q
    b = g0 + u1 * g1 + u2 * g2 + un * gn
    m = r * b + enthalpy * ge
    n = gn + sm * ge
    rkap = r * kap
    f_kap = m + r * a * n
    f_a = rkap * n
    si2 = si * si
    s_bar = f_a - f_kap * (dl * sm * si2)
    sm_bar = f_kap * (s * a * si2) + rkap * a * ge
    wr = w * r
    k_bar = [None] * 5
    k_bar[0] = w * (b + half_q * ge) + kap * a * n
    k_bar[n_at] = m + wr * (gn + un * ge) - f_kap * j - f_a
    k_bar[tang[0]] = wr * (g1 + u1 * ge)
    k_bar[tang[1]] = wr * (g2 + u2 * ge)
    k_bar[4] = 3.5 * (w * ge) + gn
    e = sm_bar * inv
    eg = e * gap
    c_half = 0.5 * (jnp.where(is_right, s_bar, -s_bar) - eg * r2)
    n_half = 0.5 * (s_bar + sm_bar)
    r_both = -(eg * c)
    xl = c_half * inv_rl
    xr = c_half * inv_rr
    base_l = {0: r_both - 0.5 * (xl * cl), n_at: n_half, 4: 0.7 * (xl * inv_cl) + e}
    base_r = {0: r_both - 0.5 * (xr * cr), n_at: n_half, 4: 0.7 * (xr * inv_cr) - e}
    l_bar, r_bar = [], []
    for i in range(5):
        kr = jnp.where(is_right, k_bar[i], 0.0)
        kl = k_bar[i] - kr
        l_bar.append(base_l[i] + kl if i in base_l else kl)
        r_bar.append(base_r[i] + kr if i in base_r else kr)
    return l_bar, r_bar


def face_pull(cells, cot, flags, normal):
    stencil = flags >> 2
    smooth = stencil == 0
    c0 = jnp.where(stencil == 1, 1.0, 0.0)
    c2 = jnp.where(stencil == 3, 1.0, 0.0)
    left, right, kept = [], [], []
    for v in cells:
        p, d, k, g, t = shared_terms(v)
        pm2 = p[2] + p[2]
        args_l = (p[1], p[2], p[1] + d[0], p[2] - d[2], t[0] + t[0], t[1])
        args_r = (p[3], p[2], p[3] - d[3], p[2] + d[1], t[2] + t[2], t[1])
        hl, saved_l = side_value(
            p[1], p[2], pm2, k[0], k[1], k[2], *args_l[2:], smooth, c0, c2
        )
        hr, saved_r = side_value(
            p[3], p[2], pm2, k[3], k[2], k[1], *args_r[2:], smooth, c0, c2
        )
        left.append(v[2] + hl * (1.0 / 6.0))
        right.append(v[3] - hr * (1.0 / 6.0))
        kept.append((p, g, args_l, args_r, saved_l, saved_r))
    l_bar, r_bar = hllc_pull(left, right, normal, flags, cot)
    out = []
    for i in range(5):
        p, g, args_l, args_r, saved_l, saved_r = kept[i]
        a0, a1, a2, pa_l, pm_l, x0, x2 = side_pull(
            l_bar[i] * (1.0 / 6.0), *args_l, smooth, saved_l
        )
        b0, b1, b2, pa_r, pm_r, y0, y2 = side_pull(
            r_bar[i] * (-1.0 / 6.0), *args_r, smooth, saved_r
        )
        d0 = a0 * (g[0] + p[1]) + x0
        d1 = (b2 * (g[1] + p[2]) - a1 * g[1]) + (x2 - x0) + y2
        d2 = (a2 * (g[2] - p[2]) - b1 * g[2]) + (y0 - y2) - x2
        d3 = b0 * (g[3] - p[3]) - y0
        p2 = pa_l + (d0 - d1)
        p3 = pm_l + pm_r + (d1 - d2)
        p4 = pa_r + (d2 - d3)
        out.append([d0, -d0 - p2, l_bar[i] + (p2 - p3), r_bar[i] + (p3 - p4), p4 - d3, d3])
    return out


def conserved_pull(s, g):
    half_q = 0.5 * (s[1] * s[1] + s[2] * s[2] + s[3] * s[3])
    return [
        g[0] + s[1] * g[1] + s[2] * g[2] + s[3] * g[3] + half_q * g[4],
        s[0] * (g[1] + s[1] * g[4]),
        s[0] * (g[2] + s[2] * g[4]),
        s[0] * (g[3] + s[3] * g[4]),
        2.5 * g[4],
    ]


REACH_STATE, REACH_COT, REACH_FLAGS = 5, 3, 3
COT_AT = 5 * REACH_STATE
FLAGS_AT = COT_AT + 5 * REACH_COT
SENT = FLAGS_AT + REACH_FLAGS


def views(fields):
    n = fields.shape[0] // 13
    return (
        fields.at[pl.ds(0, 5 * n)],
        fields.at[pl.ds(5 * n, 5 * n)],
        fields.at[pl.ds(10 * n, 3 * n)],
    )


def pack_kernel(fields, twin, other):
    s, g, f = views(fields)
    rows_in = f.shape[0] // 3
    even = is_even()
    nx = twin.shape[1]

    def put(at, low, top):
        twin[at] = jnp.where(even, top, low)
        other[at] = jnp.where(even, low, top)

    for v in range(5):
        base = v * nx * 8
        for ref, reach, at in ((s, REACH_STATE, 0), (g, REACH_COT, COT_AT)):
            for r in range(reach):
                put(
                    at + r * 5 + v,
                    ref[pl.ds(base + r, nx, stride=8), :],
                    ref[pl.ds(base + 8 - reach + r, nx, stride=8), :],
                )
    for r in range(REACH_FLAGS):
        low = f[pl.ds(rows_in + r, nx, stride=8), :]
        top = f[pl.ds(rows_in + 8 - REACH_FLAGS + r, nx, stride=8), :]
        put(FLAGS_AT + r, low, top)


def from_rims(twin, other):
    even = is_even()

    def read(row, reach, at, v):
        if row < 0:
            i = at + (reach + row) * 5 + v
            return jnp.where(even, other[i], twin[i])
        i = at + (row - 8) * 5 + v
        return jnp.where(even, twin[i], other[i])

    def state(row, v):
        return read(row, REACH_STATE, 0, v)

    def cot(row, v):
        return read(row, REACH_COT, COT_AT, v)

    def flags(row):
        if row < 0:
            i = FLAGS_AT + REACH_FLAGS + row
            return jnp.where(even, other[i], twin[i])
        i = FLAGS_AT + row - 8
        return jnp.where(even, twin[i], other[i])

    return state, cot, flags


def x_kernel(fields, out, pad, gpad, acc):
    state, cot, flags = views(fields)
    nx = state.shape[1]
    for v in range(5):
        pad[v, pl.ds(2, nx)] = state[v]
        pad[v, pl.ds(0, 2)] = state[v, pl.ds(nx - 2, 2)]
        pad[v, pl.ds(nx + 2, 3)] = state[v, pl.ds(0, 3)]
        gpad[v, pl.ds(0, nx)] = cot[v]
        gpad[v, pl.ds(nx, 1)] = cot[v, pl.ds(0, 1)]
    acc[...] = jnp.zeros_like(acc)

    def step(i, carry):
        x = i * SLABS
        cells = [[pad[v, pl.ds(x + k, SLABS)] for k in range(6)] for v in range(5)]
        g = [gpad[v, pl.ds(x, SLABS)] for v in range(5)]
        face = [STEP * (gpad[v, pl.ds(x + 1, SLABS)] - g[v]) for v in range(5)]
        terms = face_pull(cells, face, flags[0, pl.ds(x, SLABS)].astype(jnp.int32), 0)
        own = conserved_pull([cells[v][2] for v in range(5)], g)
        for v in range(5):
            terms[v][2] = terms[v][2] + own[v]
            for s in range(SLABS + 5):
                total = None
                for k in range(6):
                    if 0 <= s - k < SLABS:
                        part = terms[v][k][s - k]
                        total = part if total is None else total + part
                acc[v, x + s] = acc[v, x + s] + total
        return carry

    lax.fori_loop(0, nx // SLABS, step, 0)
    for v in range(5):
        acc[v, pl.ds(nx, 2)] = acc[v, pl.ds(nx, 2)] + acc[v, pl.ds(0, 2)]
        acc[v, pl.ds(2, 3)] = acc[v, pl.ds(2, 3)] + acc[v, pl.ds(nx + 2, 3)]

    for v in range(5):
        out[v] = acc[v, pl.ds(2, nx)]


def z_kernel(fields, first, order, out):
    del order
    state, cot, flags = views(fields)
    nx = state.shape[1]

    def z_step(i, carry):
        x = i * SLABS
        cells, face = [], []
        for v in range(5):
            mid = state[v, pl.ds(x, SLABS)]
            cells.append([mid if k == 0 else pltpu.roll(mid, (-k) % 128, 2) for k in range(-2, 4)])
            g = cot[v, pl.ds(x, SLABS)]
            face.append(STEP * (pltpu.roll(g, 127, 2) - g))
        terms = face_pull(cells, face, flags[2, pl.ds(x, SLABS)].astype(jnp.int32), 2)
        for v in range(5):
            t = first[v, pl.ds(x, SLABS)] + terms[v][2]
            for k in (-2, -1, 1, 2, 3):
                t = t + pltpu.roll(terms[v][k + 2], k % 128, 2)
            out[v, pl.ds(x, SLABS)] = t
        return carry

    lax.fori_loop(0, nx // SLABS, z_step, 0)


def e_kernel(fields, twin, other, order, out):
    del order
    state, cot, _ = views(fields)
    nx = twin.shape[1]
    rim_state, rim_cot, rim_flags = from_rims(twin, other)

    def own(ref, row, v):
        return ref[pl.ds(v * nx * 8 + row, nx, stride=8), :]

    state_rows, cot_rows = {}, {}
    for v in range(5):
        for row in (*range(-5, 3), *range(6, 13)):
            inside = 0 <= row < 8
            state_rows[row, v] = own(state, row, v) if inside else rim_state(row, v)
        for row in (-3, -2, -1, 0, 8, 9, 10):
            inside = 0 <= row < 8
            cot_rows[row, v] = own(cot, row, v) if inside else rim_cot(row, v)
    sums = {}
    for j in (-3, -2, -1, 8, 9):
        cells = [[state_rows[j + k, v] for k in range(-2, 4)] for v in range(5)]
        face = [STEP * (cot_rows[j + 1, v] - cot_rows[j, v]) for v in range(5)]
        terms = face_pull(cells, face, rim_flags(j).astype(jnp.int32), 1)
        for v in range(5):
            for k in range(-2, 4):
                if 0 <= j + k < 8:
                    t = terms[v][k + 2]
                    sums[j + k, v] = sums[j + k, v] + t if (j + k, v) in sums else t
    for v in range(5):
        for row in range(8):
            value = sums[row, v] if (row, v) in sums else jnp.zeros((nx, 128), F32)
            out[pl.ds(v * nx * 8 + row, nx, stride=8), :] = value


def y_faces(x0, fields, twin, other, own, first, rim, put, part, halo, ghalo):
    rim_state, rim_cot, _ = from_rims(twin, other)
    state, cot, flags = views(fields)
    nx = state.shape[1]
    for v in range(5):
        base = v * nx * 8
        for r in range(ABOVE):
            halo[pl.ds(base + r, nx, stride=8), :] = rim_state(8 + r, v)
        for r in range(BELOW):
            halo[pl.ds(base + 8 - BELOW + r, nx, stride=8), :] = rim_state(r - BELOW, v)
        ghalo[pl.ds(base, nx, stride=8), :] = rim_cot(8, v)
    row = lax.broadcasted_iota(jnp.int32, (SLABS, 8, 128), 1)
    inside = {}
    for k in (-2, -1, 1, 2, 3):
        inside[k] = (row < 8 + k) if k < 0 else (row >= k)

    def step(i, carry):
        x = x0 + i * SLABS
        cells, face = [], []
        for v in range(5):
            at = pl.multiple_of((v * nx + x) * 8, 8)
            rim_rows = halo[pl.ds(at, 8 * SLABS), :].reshape(SLABS, 8, 128)
            mid = state[v, pl.ds(x, SLABS)]
            line = []
            for k in range(-2, 4):
                if k == 0:
                    line.append(mid)
                else:
                    line.append(pltpu.roll(jnp.where(inside[k], mid, rim_rows), (-k) % 8, 1))
            cells.append(line)
            g = cot[v, pl.ds(x, SLABS)]
            g_rim = ghalo[pl.ds(at, 8 * SLABS), :].reshape(SLABS, 8, 128)
            face.append(STEP * (pltpu.roll(jnp.where(inside[1], g, g_rim), 7, 1) - g))
        terms = face_pull(cells, face, flags[1, pl.ds(x, SLABS)].astype(jnp.int32), 1)
        for v in range(5):
            at = pl.multiple_of((v * nx + x) * 8, 8)
            total = own[v, pl.ds(x, SLABS)] + first[v, pl.ds(x, SLABS)] + terms[v][2]
            total = total + rim[pl.ds(at, 8 * SLABS), :].reshape(SLABS, 8, 128)
            for k in (-2, -1, 1, 2, 3):
                moved = pltpu.roll(terms[v][k + 2], k % 8, 1)
                total = total + jnp.where(inside[k], moved, 0.0)
            put(i, x, v, total)
        return carry

    lax.fori_loop(0, part // SLABS, step, 0)


def y_kernel(fields, twin, other, own, first, rim, order, out, halo, ghalo):
    del order
    part = out.shape[1]

    def put(i, x, v, total):
        out[v, pl.ds(x, SLABS)] = total

    y_faces(0, fields, twin, other, own, first, rim, put, part, halo, ghalo)


def y_last_kernel(fields, twin, other, own, first, rim, done, order, out, halo, ghalo):
    del order
    part = done.shape[1]
    half = out.shape[1] - part

    def put(i, x, v, total):
        out[v, pl.ds(x, SLABS)] = total
        out[v, pl.ds(i * SLABS, SLABS)] = done[v, pl.ds(i * SLABS, SLABS)]

    y_faces(half, fields, twin, other, own, first, rim, put, part, halo, ghalo)


def sum_kernel(scale, mine, theirs, k_out, h_out):
    total = (mine[...] + theirs[...]) * scale
    k_out[...] = total[:, : k_out.shape[1]]
    ch = total.shape[0]
    pick = (
        lax.broadcasted_iota(jnp.int32, (8, 128), 1)
        == lax.broadcasted_iota(jnp.int32, (8, 128), 0) + 16
    ).astype(F32)
    heads = lax.dot_general(
        pick,
        total[:, 128:],
        (((1,), (1,)), ((), ())),
        precision=lax.Precision.HIGHEST,
        preferred_element_type=F32,
    )
    h_out[...] = heads[: h_out.shape[0], :ch]


BLOCK = 64
SLOT = 3 * BLOCK


def split(x):
    hi = x.astype(BF16)
    return hi, (x - hi.astype(F32)).astype(BF16)


def over_lanes(a, b):
    return lax.dot_general(a, b, (((1,), (1,)), ((), ())), preferred_element_type=F32)


def is_even():
    return lax.rem(lax.axis_index("gy"), 2) == 0


def band_matrices(kernel, heads, wide):
    ch, taps = kernel.shape
    w = kernel[...]
    hi, lo = split(w)
    wide[...] = jnp.zeros_like(wide)
    wide[pl.ds(0, ch), pl.ds(0, taps)] = hi.astype(F32)
    wide[pl.ds(ch, ch), pl.ds(0, taps)] = lo.astype(F32)
    both = wide[...].astype(BF16)
    kind, tap = columns()
    base = jnp.dot(both, own_taps(kind, tap), preferred_element_type=F32)
    rim = jnp.dot(both, rim_taps(kind, tap), preferred_element_type=F32)
    n = base.shape[1]
    kind = jnp.broadcast_to(kind[0:1], base.shape)
    main = jnp.where(kind < 3, base, 0.0)
    bands = []
    for y in range(8):
        rows = main
        if y == 0:
            rows = jnp.where(kind == 0, 0.0, rows)
        if y == 7:
            rows = jnp.where(kind == 2, 0.0, rows)
        if y != 1:
            rows = pltpu.roll(rows, (y - 1) % n, 1)
        if y == 0:
            rows = rows + jnp.where(kind == 9, base, 0.0)
        if y == 7:
            rows = rows + jnp.where(kind == 10, base, 0.0)
        bands.append(rows)
    bands.append(jnp.where((kind == 0) | (kind == 8) | (kind == 9), rim, 0.0))
    bands.append(jnp.where((kind == 7) | (kind == 10) | (kind == 11), rim, 0.0))
    full = jnp.concatenate([b[:ch] for b in bands] + [b[ch:] for b in bands], axis=0)
    w_rows = full.astype(BF16)
    kept = full.shape[0] // 2
    cols = jnp.concatenate([full[:kept], full[:kept], full[kept:]], axis=0)
    cols = jnp.concatenate([cols, jnp.zeros((512 - 3 * kept, n), F32)], axis=0)
    own_cols = []
    for q in range(3):
        own_cols += [cols[:, (3 * q + o) * BLOCK : (3 * q + o) * BLOCK + 40] for o in range(3)]
        own_cols.append(jnp.zeros((512, 8), F32))
    w_cols = jnp.concatenate(own_cols, axis=1).T.astype(BF16)
    total = jnp.sum(w * level_taps(w.shape), axis=1, keepdims=True)
    total = jnp.broadcast_to(total, (ch, 128))
    bias = jnp.concatenate([total] * 10, axis=0)

    h_hi, h_lo = split(STEP * heads[...])
    none = jnp.zeros((3, ch), F32)
    pair = jnp.concatenate([h_hi.astype(F32), none, h_lo.astype(F32), none], axis=0).astype(BF16)
    r = lax.broadcasted_iota(jnp.int32, (kept, ch), 0)
    q = lax.broadcasted_iota(jnp.int32, (kept, ch), 1)
    spread = jnp.where((r & (ch - 1)) == q, 1.0, 0.0).astype(BF16)
    picked = over_lanes(pair, spread)
    y_of = lax.broadcasted_iota(jnp.int32, (8, kept), 0)
    col = lax.broadcasted_iota(jnp.int32, (8, kept), 1)
    same = (col >= y_of * ch) & (col < (y_of + 1) * ch)
    split_heads = []
    for at in (0, 8):
        rows = [
            jnp.where(same, jnp.broadcast_to(picked[at + e : at + e + 1], (8, kept)), 0.0)
            for e in range(5)
        ]
        five = picked[at : at + 8]
        rows.append(jnp.where((col >= 8 * ch) & (col < 9 * ch), five, 0.0))
        rows.append(jnp.where(col >= 9 * ch, five, 0.0))
        rows.append(jnp.zeros((8, kept), F32))
        split_heads.append(jnp.concatenate(rows, axis=0))
    three = jnp.concatenate([split_heads[0], split_heads[1], split_heads[0]], axis=0)
    w_head = three.T.astype(BF16)
    return w_rows, w_cols, w_head, bias


def c_kernel(
    fields, twin, other, kernel, heads,
    own, parts,
    t, acc, edge, gedge, wide,
):
    state, cot, _ = views(fields)
    nx = state.shape[1]
    ch, taps = kernel.shape
    w_rows, w_cols, w_head, bias = band_matrices(kernel, heads, wide)
    rim_state, rim_cot, _ = from_rims(twin, other)

    for v in range(5):
        level = 1.0 if v in (0, 4) else 0.0
        for q, row in enumerate((-2, -1, 8, 9)):
            edge[pl.ds(5 * q + v, nx, stride=24), :] = rim_state(row, v) - level
        gedge[pl.ds(v, nx, stride=16), :] = rim_cot(-1, v)
        gedge[pl.ds(8 + v, nx, stride=16), :] = rim_cot(8, v)
    for q in range(20, 24):
        edge[pl.ds(q, nx, stride=24), :] = jnp.zeros((nx, 128), F32)
    for q in (5, 6, 7):
        gedge[pl.ds(q, nx, stride=16), :] = jnp.zeros((nx, 128), F32)
        gedge[pl.ds(8 + q, nx, stride=16), :] = jnp.zeros((nx, 128), F32)
    for x in range(nx):
        rows = [state[v, x] - (1.0 if v in (0, 4) else 0.0) for v in range(5)]
        rows.append(edge[pl.ds(x * 24, 24), :])
        mid = jnp.concatenate(rows, axis=0)
        at = (x + 1) * SLOT
        t[pl.ds(at, BLOCK), :] = pltpu.roll(mid, 1, 1).astype(BF16)
        t[pl.ds(at + BLOCK, BLOCK), :] = mid.astype(BF16)
        t[pl.ds(at + 2 * BLOCK, BLOCK), :] = pltpu.roll(mid, 127, 1).astype(BF16)
    t[pl.ds(0, SLOT), :] = t[pl.ds(nx * SLOT, SLOT), :]
    t[pl.ds((nx + 1) * SLOT, SLOT), :] = t[pl.ds(SLOT, SLOT), :]

    kept = 8 * ch
    kg = hg = dsum = None
    zeros8 = jnp.zeros((8, 128 * WIDE), F32)
    written = set()
    for x in range(0, nx, WIDE):
        s = jnp.concatenate([t[pl.ds((x + j) * SLOT, 3 * SLOT), :] for j in range(WIDE)], axis=1)
        z2 = jnp.dot(w_rows, s, preferred_element_type=F32)
        rows = z2.shape[0] // 2
        z = z2[:rows] + z2[rows:] + jnp.concatenate([bias] * WIDE, axis=1)
        hidden = jnp.tanh(z)
        g = jnp.concatenate(
            [
                jnp.concatenate(
                    [cot[v, x + j] for v in range(5)] + [gedge[pl.ds((x + j) * 16, 16), :]], axis=0
                )
                for j in range(WIDE)
            ],
            axis=1,
        )
        g_hi, g_lo = split(g)
        g_hi32, g_lo32 = g_hi.astype(F32), g_lo.astype(F32)
        g3 = jnp.concatenate(
            [g_hi32, zeros8, g_hi32, zeros8, g_lo32, zeros8], axis=0
        ).astype(BF16)
        d = (1.0 - hidden * hidden) * jnp.dot(w_head, g3, preferred_element_type=F32)
        d_hi, d_lo = split(d)
        zeros = jnp.zeros((512 - 3 * rows, 128 * WIDE), BF16)
        back = jnp.dot(
            w_cols,
            jnp.concatenate([d_hi, d_lo, d_hi, zeros], axis=0),
            preferred_element_type=F32,
        )
        k2 = over_lanes(jnp.concatenate([d_hi[:kept], d_lo[:kept]], axis=0), s)
        k2 = k2[:kept] + k2[kept:]
        kg = k2 if kg is None else kg + k2
        hid2 = jnp.concatenate(split(hidden[:kept]), axis=0)
        g2 = jnp.concatenate([g_hi32[:40], g_lo32[:40]], axis=0).astype(BF16)
        h2 = over_lanes(hid2, g2)
        hg = h2 if hg is None else hg + h2
        for j in range(WIDE):
            level = d[:kept, 128 * j : 128 * (j + 1)]
            dsum = level if dsum is None else dsum + level
        for m in range(WIDE + 2):
            total = None
            for j in range(WIDE):
                if 0 <= m - j < 3:
                    q = m - j
                    piece = back[q * 128 : q * 128 + 120, 128 * j : 128 * (j + 1)]
                    total = piece if total is None else total + piece
            here = (x + m - 1) % nx
            if here in written:
                total = total + acc[pl.ds(here * 120, 120), :]
            written.add(here)
            acc[pl.ds(here * 120, 120), :] = total
    for x in range(nx):
        at = x * 120
        total = (
            acc[pl.ds(at + 40, 40), :]
            + pltpu.roll(acc[pl.ds(at, 40), :], 127, 1)
            + pltpu.roll(acc[pl.ds(at + 80, 40), :], 1, 1)
        )
        for v in range(5):
            own[v, x] = total[8 * v : 8 * v + 8]

    sums = jnp.sum(dsum, axis=1, keepdims=True)
    y_row = lax.broadcasted_iota(jnp.int32, (kept, 40), 0)
    y_col = lax.broadcasted_iota(jnp.int32, (kept, 40), 1) & 7
    same_y = (y_row >= y_col * ch) & (y_row < (y_col + 1) * ch)
    h_all = (hg[:kept, :40] + hg[kept:, :40]) + (hg[:kept, 40:80] + hg[kept:, 40:80])
    h_all = jnp.where(same_y, h_all, 0.0)
    level_sum = jnp.zeros((ch, 1), F32)
    head_sum = jnp.zeros((ch, 40), F32)
    n = kg.shape[1]
    columns_at, tap = columns()
    kind = jnp.broadcast_to(columns_at[0:1], (ch, n))
    total = jnp.zeros((ch, n), F32)
    for y in range(8):
        rows = kg[y * ch : (y + 1) * ch]
        moved = rows if y == 1 else pltpu.roll(rows, (1 - y) % n, 1)
        keep = kind < 3
        if y == 0:
            keep = (kind == 1) | (kind == 2)
            total = total + jnp.where(kind == 9, rows, 0.0)
        if y == 7:
            keep = kind < 2
            total = total + jnp.where(kind == 10, rows, 0.0)
        total = total + jnp.where(keep, moved, 0.0)
        level_sum = level_sum + sums[y * ch : (y + 1) * ch]
        head_sum = head_sum + h_all[y * ch : (y + 1) * ch]
    grads = over_lanes(jnp.concatenate(split(total), axis=0), own_taps(columns_at, tap))
    n_pick = grads.shape[1]
    parts[...] = jnp.zeros_like(parts)
    parts[:, pl.ds(0, n_pick)] = grads[:ch] + grads[ch:]
    parts[:, pl.ds(0, taps)] = parts[:, pl.ds(0, taps)] + level_sum * level_taps((ch, taps))
    e_row = lax.broadcasted_iota(jnp.int32, (40, 128), 0) >> 3
    e_col = lax.broadcasted_iota(jnp.int32, (40, 128), 1) - 16
    to_col = jnp.where(e_row == e_col, 1.0, 0.0).astype(BF16)
    head_out = jnp.dot(
        jnp.concatenate(split(head_sum * STEP), axis=0), to_col, preferred_element_type=F32
    )
    parts[:, pl.ds(128, 128)] = parts[:, pl.ds(128, 128)] + (head_out[:ch] + head_out[ch:])


def columns():
    lane = lax.broadcasted_iota(jnp.int32, (8, 9 * BLOCK), 1)
    o = lane >> 6
    r = lane & (BLOCK - 1)
    q = r - 40
    which = sum((q >= 5 * i).astype(jnp.int32) for i in (1, 2, 3, 4))
    main = r < 40
    kind = jnp.where(main, r & 7, 8 + which)
    v = jnp.where(main, r >> 3, q - 5 * which)
    return kind, o * 5 + v


def taps_of(columns_at):
    n = columns_at.shape[1]
    row = lax.broadcasted_iota(jnp.int32, (144, n), 0)
    return jnp.where(row == jnp.broadcast_to(columns_at[0:1], (144, n)), 1.0, 0.0).astype(BF16)


def own_taps(kind, tap):
    at = jnp.where(kind < 3, tap + 45 * kind, 1000)
    at = jnp.where(kind == 9, tap, at)
    return taps_of(jnp.where(kind == 10, tap + 90, at))


def rim_taps(kind, tap):
    first = (kind == 8) | (kind == 7)
    middle = (kind == 9) | (kind == 10)
    last = (kind == 0) | (kind == 11)
    at = jnp.where(first, tap, jnp.where(middle, tap + 45, 1000))
    return taps_of(jnp.where(last, tap + 90, at))


def level_taps(shape):
    t = lax.broadcasted_iota(jnp.int32, shape, 1).astype(F32)
    v = t - 5.0 * jnp.floor((t + 0.5) * 0.2)
    return jnp.where((v < 0.5) | (v > 3.5), 1.0, 0.0)


def call(kernel, outs, scratch, us, n_in, order=0):
    spec = pl.BlockSpec(memory_space=pltpu.VMEM)
    return pl.pallas_call(
        kernel,
        out_shape=outs,
        in_specs=[spec] * n_in + [pl.BlockSpec(memory_space=pl.ANY)] * order,
        scratch_shapes=scratch,
        compiler_params=pltpu.CompilerParams(vmem_limit_bytes=VMEM),
        cost_estimate=pl.CostEstimate(
            flops=0, bytes_accessed=int(us * 3.69e6), transcendentals=0
        ),
    )


def body(state, cot, flags, kernel, heads):
    _, nx, ny, nz = state.shape
    ch, taps = kernel.shape
    count = lax.axis_size("gy")
    cells = nx * ny * nz
    half = nx // 2
    shape = lambda *dims: jax.ShapeDtypeStruct(dims, F32)
    full, part = shape(5, nx, ny, nz), shape(5, half, ny, nz)
    with_twin = [(i, i ^ 1) for i in range(count)]
    with_other = [(i, (i + 1) % count if i % 2 else (i - 1) % count) for i in range(count)]
    vm = pltpu.VMEM
    lines = 5 * nx * ny

    flat = jnp.concatenate(
        [
            state.reshape(lines, nz),
            cot.reshape(lines, nz),
            flags.reshape(3 * nx * ny, nz).astype(F32),
        ]
    )
    fields = flat.reshape(13, nx, ny, nz)

    sent = shape(SENT, nx, nz)
    to_twin, to_other = call(pack_kernel, (sent, sent), [], 0.2, 1)(flat)
    twin = lax.ppermute(to_twin, "gy", with_twin)
    other = lax.ppermute(to_other, "gy", with_other)

    first = call(
        x_kernel,
        full,
        [
            vm((5, nx + 5, ny, nz), F32),
            vm((5, nx + 1, ny, nz), F32),
            vm((5, nx + 5, ny, nz), F32),
        ],
        3.3,
        1,
    )(fields)
    first, twin, other = lax.optimization_barrier((first, twin, other))
    own, parts = call(
        c_kernel,
        (full, shape(ch, 256)),
        [
            vm(((nx + 2) * SLOT, nz), BF16),
            vm((nx * 120, nz), F32),
            vm((24 * nx, nz), F32),
            vm((16 * nx, nz), F32),
            vm((2 * ch, 144), F32),
        ],
        5.0,
        5,
    )(fields, twin, other, kernel, heads)

    def exchanged(value, bit):
        return lax.ppermute(value, "gy", [(i, i ^ bit) for i in range(count)])

    bits = [1 << b for b in range(count.bit_length() - 1)]
    sums = parts
    for bit in bits[:-4]:
        sums = sums + exchanged(sums, bit)
    halos = [vm((lines, nz), F32)] * 2
    got = exchanged(sums, bits[-4])
    rim = call(e_kernel, shape(lines, nz), [], 1.1, 3, 1)(flat, twin, other, sums)
    got, rim = lax.optimization_barrier((got, rim))
    sums = sums + got
    got = exchanged(sums, bits[-3])
    first = call(z_kernel, full, [], 3.3, 2, 1)(fields, first, sums)
    got, first = lax.optimization_barrier((got, first))
    sums = sums + got
    got = exchanged(sums, bits[-2])
    y0 = call(y_kernel, part, halos, 1.6, 6, 1)(fields, twin, other, own, first, rim, sums)
    got, y0 = lax.optimization_barrier((got, y0))
    sums = sums + got
    got = exchanged(sums, bits[-1])
    flow = call(y_last_kernel, full, halos, 2.0, 7, 1)(
        fields, twin, other, own, first, rim, y0, sums
    )
    scale = float(cells * count) ** (-0.5)
    k_out, h_out = call(
        functools.partial(sum_kernel, scale), (shape(ch, taps), shape(5, ch)), [], 0.5, 2
    )(sums, got)
    return flow, k_out, h_out


def solution(mesh):
    split_y = P(None, "ens", "gy", None)
    return jax.shard_map(
        body,
        mesh=mesh,
        in_specs=(split_y, split_y, split_y, P(), P()),
        out_specs=(split_y, P("ens", None), P("ens", None)),
        check_vma=False,
    )
```

```python
import functools

import jax
import jax.numpy as jnp
from jax import lax
from jax.experimental import pallas as pl
from jax.experimental.pallas import tpu as pltpu
from jax.sharding import PartitionSpec as P

STEP = 0.3
FLOOR = 0.01
BELOW, ABOVE = 2, 3
SLABS = 2
WIDE = 4
VMEM = 48 * 1024 * 1024
F32 = jnp.float32
BF16 = jnp.bfloat16


def rcp(x):
    return pl.reciprocal(x, approx=True)


def shared_terms(v):
    p = [v[i + 1] - v[i] for i in range(5)]
    d = [p[i + 1] - p[i] for i in range(4)]
    h = [(4.0 / 3.0) * x for x in d]
    k = [h[i] * d[i] + FLOOR for i in range(4)]
    g = [x + x for x in h]
    t = [d[i + 1] - d[i] for i in range(3)]
    return p, d, k, g, t


def side_value(pa, pm, pm2, ka, kb, kc, m0, m2, td, t1, smooth, c0, c2):
    i0 = rcp(ka + pa * m0)
    i1 = rcp(kb + pa * pm)
    i2 = rcp(kc + pm * m2)
    w0 = i0 * i0
    w1 = 6.0 * (i1 * i1)
    w2 = 3.0 * (i2 * i2)
    r = rcp(w0 + w1 + w2)
    o0 = jnp.where(smooth, w0 * r, c0)
    o2 = jnp.where(smooth, w2 * r, c2)
    u = o0 * td + o2 * t1
    return (pa + pm2) - u, (i0, i1, i2, w0, w1, w2, r, o0, o2, u)


def side_pull(mu, pa, pm, m0, m2, td, t1, smooth, saved):
    i0, i1, i2, w0, w1, w2, r, o0, o2, u = saved
    mu2 = mu + mu
    rm = jnp.where(smooth, mu2, 0.0) * r
    s0 = (w0 * i0) * rm * (td - u)
    s1 = (w1 * i1) * rm * u
    s2 = (w2 * i2) * rm * (t1 - u)
    pa_bar = s0 * (m0 + pa) - s1 * pm + mu
    pm_bar = s2 * (m2 + pm) - s1 * pa + mu2
    return s0, s1, s2, pa_bar, pm_bar, o0 * mu2, o2 * mu


def hllc_pull(left, right, normal, flags, cot):
    region = flags & 3
    is_right = region >= 2
    star = ((region + 1) & 2) != 0
    n_at = 1 + normal
    tang = [1 + i for i in range(3) if i != normal]
    rl, rr_, pl_, pr_, nl, nr = left[0], right[0], left[4], right[4], left[n_at], right[n_at]

    def sound(r, p):
        inv = rcp(r)
        t = 1.4 * p * inv
        inv_c = lax.rsqrt(t)
        return inv, inv_c, t * inv_c

    inv_rl, inv_cl, cl = sound(rl, pl_)
    inv_rr, inv_cr, cr = sound(rr_, pr_)
    c = 0.5 * (cl + cr)
    r2 = rl + rr_
    inv = rcp(r2 * c)
    nm = 0.5 * (nl + nr)
    gap = (pl_ - pr_) * inv
    sm = nm + gap
    sc = jnp.where(is_right, c, -c)
    s = nm + sc
    pick = [jnp.where(is_right, right[i], left[i]) for i in range(5)]
    r, un, u1, u2, p = pick[0], pick[n_at], pick[tang[0]], pick[tang[1]], pick[4]
    a = s - un
    dl = sm - un
    si = jnp.where(star, rcp(sc - gap), 0.0)
    j = s * si
    kap = j * dl
    g0, gn, g1, g2, ge = cot[0], cot[n_at], cot[tang[0]], cot[tang[1]], cot[4]
    w = un + kap
    half_q = 0.5 * (un * un + u1 * u1 + u2 * u2)
    enthalpy = 3.5 * p + r * half_q
    b = g0 + u1 * g1 + u2 * g2 + un * gn
    m = r * b + enthalpy * ge
    n = gn + sm * ge
    rkap = r * kap
    f_kap = m + r * a * n
    f_a = rkap * n
    si2 = si * si
    s_bar = f_a - f_kap * (dl * sm * si2)
    sm_bar = f_kap * (s * a * si2) + rkap * a * ge
    wr = w * r
    k_bar = [None] * 5
    k_bar[0] = w * (b + half_q * ge) + kap * a * n
    k_bar[n_at] = m + wr * (gn + un * ge) - f_kap * j - f_a
    k_bar[tang[0]] = wr * (g1 + u1 * ge)
    k_bar[tang[1]] = wr * (g2 + u2 * ge)
    k_bar[4] = 3.5 * (w * ge) + gn
    e = sm_bar * inv
    eg = e * gap
    c_half = 0.5 * (jnp.where(is_right, s_bar, -s_bar) - eg * r2)
    n_half = 0.5 * (s_bar + sm_bar)
    r_both = -(eg * c)
    xl = c_half * inv_rl
    xr = c_half * inv_rr
    base_l = {0: r_both - 0.5 * (xl * cl), n_at: n_half, 4: 0.7 * (xl * inv_cl) + e}
    base_r = {0: r_both - 0.5 * (xr * cr), n_at: n_half, 4: 0.7 * (xr * inv_cr) - e}
    l_bar, r_bar = [], []
    for i in range(5):
        kr = jnp.where(is_right, k_bar[i], 0.0)
        kl = k_bar[i] - kr
        l_bar.append(base_l[i] + kl if i in base_l else kl)
        r_bar.append(base_r[i] + kr if i in base_r else kr)
    return l_bar, r_bar


def face_pull(cells, cot, flags, normal):
    stencil = flags >> 2
    smooth = stencil == 0
    c0 = jnp.where(stencil == 1, 1.0, 0.0)
    c2 = jnp.where(stencil == 3, 1.0, 0.0)
    left, right, kept = [], [], []
    for v in cells:
        p, d, k, g, t = shared_terms(v)
        pm2 = p[2] + p[2]
        args_l = (p[1], p[2], p[1] + d[0], p[2] - d[2], t[0] + t[0], t[1])
        args_r = (p[3], p[2], p[3] - d[3], p[2] + d[1], t[2] + t[2], t[1])
        hl, saved_l = side_value(
            p[1], p[2], pm2, k[0], k[1], k[2], *args_l[2:], smooth, c0, c2
        )
        hr, saved_r = side_value(
            p[3], p[2], pm2, k[3], k[2], k[1], *args_r[2:], smooth, c0, c2
        )
        left.append(v[2] + hl * (1.0 / 6.0))
        right.append(v[3] - hr * (1.0 / 6.0))
        kept.append((p, g, args_l, args_r, saved_l, saved_r))
    l_bar, r_bar = hllc_pull(left, right, normal, flags, cot)
    out = []
    for i in range(5):
        p, g, args_l, args_r, saved_l, saved_r = kept[i]
        a0, a1, a2, pa_l, pm_l, x0, x2 = side_pull(
            l_bar[i] * (1.0 / 6.0), *args_l, smooth, saved_l
        )
        b0, b1, b2, pa_r, pm_r, y0, y2 = side_pull(
            r_bar[i] * (-1.0 / 6.0), *args_r, smooth, saved_r
        )
        d0 = a0 * (g[0] + p[1]) + x0
        d1 = (b2 * (g[1] + p[2]) - a1 * g[1]) + (x2 - x0) + y2
        d2 = (a2 * (g[2] - p[2]) - b1 * g[2]) + (y0 - y2) - x2
        d3 = b0 * (g[3] - p[3]) - y0
        p2 = pa_l + (d0 - d1)
        p3 = pm_l + pm_r + (d1 - d2)
        p4 = pa_r + (d2 - d3)
        out.append([d0, -d0 - p2, l_bar[i] + (p2 - p3), r_bar[i] + (p3 - p4), p4 - d3, d3])
    return out


def conserved_pull(s, g):
    half_q = 0.5 * (s[1] * s[1] + s[2] * s[2] + s[3] * s[3])
    return [
        g[0] + s[1] * g[1] + s[2] * g[2] + s[3] * g[3] + half_q * g[4],
        s[0] * (g[1] + s[1] * g[4]),
        s[0] * (g[2] + s[2] * g[4]),
        s[0] * (g[3] + s[3] * g[4]),
        2.5 * g[4],
    ]


NEAR_STATE, FAR_STATE = 2, 3
NEAR_COT, FAR_COT = 1, 2
FLAG_ROWS = 3
NEAR = 5 * (NEAR_STATE + NEAR_COT)
FAR = 5 * (FAR_STATE + FAR_COT) + FLAG_ROWS


def views(fields):
    n = fields.shape[0] // 2
    return fields.at[pl.ds(0, n)], fields.at[pl.ds(n, n)]


def pack(ref, rows, first, twin, other, at):
    even = is_even()
    nx = twin.shape[1]
    count = ref.shape[0] // (8 * nx)
    for r in rows:
        for v in range(count):
            low = ref[pl.ds(v * nx * 8 + r, nx, stride=8), :].astype(F32)
            top = ref[pl.ds(v * nx * 8 + 7 - r, nx, stride=8), :].astype(F32)
            i = at + (r - first) * count + v
            twin[i] = jnp.where(even, top, low)
            other[i] = jnp.where(even, low, top)


def near_kernel(flat, twin, other):
    s, g = views(flat)
    pack(s, range(NEAR_STATE), 0, twin, other, 0)
    pack(g, range(NEAR_COT), 0, twin, other, 5 * NEAR_STATE)


def far_rows(flat, flags, twin, other):
    s, g = views(flat)
    n = flags.shape[0] // 3
    pack(s, range(NEAR_STATE, NEAR_STATE + FAR_STATE), NEAR_STATE, twin, other, 0)
    pack(g, range(NEAR_COT, NEAR_COT + FAR_COT), NEAR_COT, twin, other, 5 * FAR_STATE)
    pack(flags.at[pl.ds(n, n)], range(FLAG_ROWS), 0, twin, other, FAR - FLAG_ROWS)


def from_rims(near_twin, near_other, far_twin=None, far_other=None):
    even = is_even()

    def pick(twin, other, i, below):
        if below:
            return jnp.where(even, other[i], twin[i])
        return jnp.where(even, twin[i], other[i])

    def read(row, near, near_at, far_at, v):
        below = row < 0
        r = -1 - row if below else row - 8
        if r < near:
            return pick(near_twin, near_other, near_at + r * 5 + v, below)
        return pick(far_twin, far_other, far_at + (r - near) * 5 + v, below)

    def state(row, v):
        return read(row, NEAR_STATE, 0, 0, v)

    def cot(row, v):
        return read(row, NEAR_COT, 5 * NEAR_STATE, 5 * FAR_STATE, v)

    def flags(row):
        below = row < 0
        r = -1 - row if below else row - 8
        return pick(far_twin, far_other, FAR - FLAG_ROWS + r, below).astype(jnp.int32)

    return state, cot, flags


def x_kernel(fields, flags, before, out, pad, gpad, acc):
    state, cot = views(fields)
    nx = state.shape[1]
    for v in range(5):
        pad[v, pl.ds(2, nx)] = state[v]
        pad[v, pl.ds(0, 2)] = state[v, pl.ds(nx - 2, 2)]
        pad[v, pl.ds(nx + 2, 3)] = state[v, pl.ds(0, 3)]
        gpad[v, pl.ds(0, nx)] = cot[v]
        gpad[v, pl.ds(nx, 1)] = cot[v, pl.ds(0, 1)]
    acc[...] = jnp.zeros_like(acc)

    def step(i, carry):
        x = i * SLABS
        cells = [[pad[v, pl.ds(x + k, SLABS)] for k in range(6)] for v in range(5)]
        g = [gpad[v, pl.ds(x, SLABS)] for v in range(5)]
        face = [STEP * (gpad[v, pl.ds(x + 1, SLABS)] - g[v]) for v in range(5)]
        terms = face_pull(cells, face, flags[0, pl.ds(x, SLABS)], 0)
        own = conserved_pull([cells[v][2] for v in range(5)], g)
        for v in range(5):
            terms[v][2] = terms[v][2] + own[v]
            for s in range(SLABS + 5):
                total = None
                for k in range(6):
                    if 0 <= s - k < SLABS:
                        part = terms[v][k][s - k]
                        total = part if total is None else total + part
                acc[v, x + s] = acc[v, x + s] + total
        return carry

    lax.fori_loop(0, nx // SLABS, step, 0)
    for v in range(5):
        acc[v, pl.ds(nx, 2)] = acc[v, pl.ds(nx, 2)] + acc[v, pl.ds(0, 2)]
        acc[v, pl.ds(2, 3)] = acc[v, pl.ds(2, 3)] + acc[v, pl.ds(nx + 2, 3)]

    for v in range(5):
        out[v] = acc[v, pl.ds(2, nx)] + before[v]


def z_kernel(fields, flags, before, order, out):
    del order
    state, cot = views(fields)
    nx = state.shape[1]

    def z_step(i, carry):
        x = i * SLABS
        cells, face = [], []
        for v in range(5):
            mid = state[v, pl.ds(x, SLABS)]
            cells.append([mid if k == 0 else pltpu.roll(mid, (-k) % 128, 2) for k in range(-2, 4)])
            g = cot[v, pl.ds(x, SLABS)]
            face.append(STEP * (pltpu.roll(g, 127, 2) - g))
        terms = face_pull(cells, face, flags[2, pl.ds(x, SLABS)], 2)
        for v in range(5):
            t = before[v, pl.ds(x, SLABS)] + terms[v][2]
            for k in (-2, -1, 1, 2, 3):
                t = t + pltpu.roll(terms[v][k + 2], k % 128, 2)
            out[v, pl.ds(x, SLABS)] = t
        return carry

    lax.fori_loop(0, nx // SLABS, z_step, 0)


def e_faces(state, cot, rims, out):
    nx = out.shape[0] // 40
    rim_state, rim_cot, rim_flags = rims

    def own(ref, row, v):
        return ref[pl.ds(v * nx * 8 + row, nx, stride=8), :]

    state_rows, cot_rows = {}, {}
    for v in range(5):
        for row in (*range(-5, 3), *range(6, 13)):
            inside = 0 <= row < 8
            state_rows[row, v] = own(state, row, v) if inside else rim_state(row, v)
        for row in (-3, -2, -1, 0, 8, 9, 10):
            inside = 0 <= row < 8
            cot_rows[row, v] = own(cot, row, v) if inside else rim_cot(row, v)
    sums = {}
    for j in (-3, -2, -1, 8, 9):
        cells = [[state_rows[j + k, v] for k in range(-2, 4)] for v in range(5)]
        face = [STEP * (cot_rows[j + 1, v] - cot_rows[j, v]) for v in range(5)]
        terms = face_pull(cells, face, rim_flags(j), 1)
        for v in range(5):
            for k in range(-2, 4):
                if 0 <= j + k < 8:
                    t = terms[v][k + 2]
                    sums[j + k, v] = sums[j + k, v] + t if (j + k, v) in sums else t
    for v in range(5):
        for row in range(8):
            value = sums[row, v] if (row, v) in sums else jnp.zeros((nx, 128), F32)
            out[pl.ds(v * nx * 8 + row, nx, stride=8), :] = value


def y_kernel(fields, flat, flags, near_twin, near_other, far_twin, far_other, before, order, out, rim, halo, ghalo):
    del order
    state, cot = views(fields)
    rims = from_rims(near_twin, near_other, far_twin, far_other)
    e_faces(*views(flat), rims, rim)
    rim_state, rim_cot, _ = rims
    nx = out.shape[1]
    for v in range(5):
        base = v * nx * 8
        for r in range(ABOVE):
            halo[pl.ds(base + r, nx, stride=8), :] = rim_state(8 + r, v)
        for r in range(BELOW):
            halo[pl.ds(base + 8 - BELOW + r, nx, stride=8), :] = rim_state(r - BELOW, v)
        ghalo[pl.ds(base, nx, stride=8), :] = rim_cot(8, v)
    row = lax.broadcasted_iota(jnp.int32, (SLABS, 8, 128), 1)
    inside = {}
    for k in (-2, -1, 1, 2, 3):
        inside[k] = (row < 8 + k) if k < 0 else (row >= k)

    def step(i, carry):
        x = i * SLABS
        cells, face = [], []
        for v in range(5):
            at = pl.multiple_of((v * nx + x) * 8, 8)
            rim_rows = halo[pl.ds(at, 8 * SLABS), :].reshape(SLABS, 8, 128)
            mid = state[v, pl.ds(x, SLABS)]
            line = []
            for k in range(-2, 4):
                if k == 0:
                    line.append(mid)
                else:
                    line.append(pltpu.roll(jnp.where(inside[k], mid, rim_rows), (-k) % 8, 1))
            cells.append(line)
            g = cot[v, pl.ds(x, SLABS)]
            g_rim = ghalo[pl.ds(at, 8 * SLABS), :].reshape(SLABS, 8, 128)
            face.append(STEP * (pltpu.roll(jnp.where(inside[1], g, g_rim), 7, 1) - g))
        terms = face_pull(cells, face, flags[1, pl.ds(x, SLABS)], 1)
        for v in range(5):
            at = pl.multiple_of((v * nx + x) * 8, 8)
            total = before[v, pl.ds(x, SLABS)] + terms[v][2]
            total = total + rim[pl.ds(at, 8 * SLABS), :].reshape(SLABS, 8, 128)
            for k in (-2, -1, 1, 2, 3):
                moved = pltpu.roll(terms[v][k + 2], k % 8, 1)
                total = total + jnp.where(inside[k], moved, 0.0)
            out[v, pl.ds(x, SLABS)] = total
        return carry

    lax.fori_loop(0, nx // SLABS, step, 0)


def sum_kernel(scale, mine, theirs, k_out, h_out):
    total = (mine[...] + theirs[...]) * scale
    k_out[...] = total[:, : k_out.shape[1]]
    ch = total.shape[0]
    pick = (
        lax.broadcasted_iota(jnp.int32, (8, 128), 1)
        == lax.broadcasted_iota(jnp.int32, (8, 128), 0) + 16
    ).astype(F32)
    heads = lax.dot_general(
        pick,
        total[:, 128:],
        (((1,), (1,)), ((), ())),
        precision=lax.Precision.HIGHEST,
        preferred_element_type=F32,
    )
    h_out[...] = heads[: h_out.shape[0], :ch]


MAIN, RIM = 48, 32
COLUMNS = 9 * (MAIN + RIM)


def split(x):
    hi = x.astype(BF16)
    return hi, (x - hi.astype(F32)).astype(BF16)


def over_lanes(a, b):
    return lax.dot_general(a, b, (((1,), (1,)), ((), ())), preferred_element_type=F32)


def is_even():
    return lax.rem(lax.axis_index("gy"), 2) == 0


def prepare_kernel(fields, flat, flags, kernel, heads, twin, other, w_rows, w_cols, w_head, bias, t, wide):
    far_rows(flat, flags, twin, other)
    state, _ = views(fields)
    nx = state.shape[1]
    for x in range(nx):
        rows = [state[v, x] - (1.0 if v in (0, 4) else 0.0) for v in range(5)]
        mid = jnp.concatenate([*rows, jnp.zeros((8, 128), F32)], axis=0)
        at = (x + 1) * 3 * MAIN
        t[pl.ds(at, MAIN), :] = pltpu.roll(mid, 1, 1).astype(BF16)
        t[pl.ds(at + MAIN, MAIN), :] = mid.astype(BF16)
        t[pl.ds(at + 2 * MAIN, MAIN), :] = pltpu.roll(mid, 127, 1).astype(BF16)
    t[pl.ds(0, 3 * MAIN), :] = t[pl.ds(nx * 3 * MAIN, 3 * MAIN), :]
    t[pl.ds((nx + 1) * 3 * MAIN, 3 * MAIN), :] = t[pl.ds(3 * MAIN, 3 * MAIN), :]

    ch, taps = kernel.shape
    w = kernel[...]
    hi, lo = split(w)
    wide[...] = jnp.zeros_like(wide)
    wide[pl.ds(0, ch), pl.ds(0, taps)] = hi.astype(F32)
    wide[pl.ds(ch, ch), pl.ds(0, taps)] = lo.astype(F32)
    both = wide[...].astype(BF16)
    kind, tap = columns()
    base = jnp.dot(both, own_taps(kind, tap), preferred_element_type=F32)
    rim = jnp.dot(both, rim_taps(kind, tap), preferred_element_type=F32)
    n = base.shape[1]
    kind = jnp.broadcast_to(kind[0:1], base.shape)
    main = jnp.where(kind < 3, base, 0.0)
    bands = []
    for y in range(8):
        rows = main
        if y == 0:
            rows = jnp.where(kind == 0, 0.0, rows)
        if y == 7:
            rows = jnp.where(kind == 2, 0.0, rows)
        if y != 1:
            rows = pltpu.roll(rows, (y - 1) % n, 1)
        if y == 0:
            rows = rows + jnp.where(kind == 8, base, 0.0)
        if y == 7:
            rows = rows + jnp.where(kind == 10, base, 0.0)
        bands.append(rows)
    bands.append(jnp.where((kind == 0) | (kind == 8) | (kind == 9), rim, 0.0))
    bands.append(jnp.where((kind == 7) | (kind == 10) | (kind == 11), rim, 0.0))
    full = jnp.concatenate([b[:ch] for b in bands] + [b[ch:] for b in bands], axis=0)
    w_rows[...] = full.astype(BF16)
    kept = full.shape[0] // 2
    cols = jnp.concatenate([full[:kept], full[:kept], full[kept:]], axis=0)
    cols = jnp.concatenate([cols, jnp.zeros((512 - 3 * kept, n), F32)], axis=0)
    own_cols = []
    for q in range(3):
        own_cols += [cols[:, (3 * q + o) * MAIN : (3 * q + o) * MAIN + 40] for o in range(3)]
        own_cols.append(jnp.zeros((512, 8), F32))
    w_cols[...] = jnp.concatenate(own_cols, axis=1).T.astype(BF16)
    total = jnp.sum(w * level_taps(w.shape), axis=1, keepdims=True)
    total = jnp.broadcast_to(total, (ch, 128))
    bias[...] = jnp.concatenate([total] * 10, axis=0)

    h_hi, h_lo = split(STEP * heads[...])
    none = jnp.zeros((3, ch), F32)
    pair = jnp.concatenate([h_hi.astype(F32), none, h_lo.astype(F32), none], axis=0).astype(BF16)
    r = lax.broadcasted_iota(jnp.int32, (kept, ch), 0)
    q = lax.broadcasted_iota(jnp.int32, (kept, ch), 1)
    spread = jnp.where((r & (ch - 1)) == q, 1.0, 0.0).astype(BF16)
    picked = over_lanes(pair, spread)
    y_of = lax.broadcasted_iota(jnp.int32, (8, kept), 0)
    col = lax.broadcasted_iota(jnp.int32, (8, kept), 1)
    same = (col >= y_of * ch) & (col < (y_of + 1) * ch)
    split_heads = []
    for at in (0, 8):
        rows = [
            jnp.where(same, jnp.broadcast_to(picked[at + e : at + e + 1], (8, kept)), 0.0)
            for e in range(5)
        ]
        five = picked[at : at + 8]
        rows.append(jnp.where((col >= 8 * ch) & (col < 9 * ch), five, 0.0))
        rows.append(jnp.where(col >= 9 * ch, five, 0.0))
        rows.append(jnp.zeros((8, kept), F32))
        split_heads.append(jnp.concatenate(rows, axis=0))
    three = jnp.concatenate([split_heads[0], split_heads[1], split_heads[0]], axis=0)
    w_head[...] = three.T.astype(BF16)


def c_kernel(
    fields, near_twin, near_other, kernel, w_rows, w_cols, w_head, bias, t,
    own, parts,
    t_rim, acc, edge, gedge,
):
    _, cot = views(fields)
    nx = cot.shape[1]
    ch, taps = kernel.shape
    rim_state, rim_cot, _ = from_rims(near_twin, near_other)

    for v in range(5):
        level = 1.0 if v in (0, 4) else 0.0
        for q, row in enumerate((-1, -2, 8, 9)):
            edge[pl.ds(5 * q + v, nx, stride=RIM), :] = rim_state(row, v) - level
        gedge[pl.ds(v, nx, stride=16), :] = rim_cot(-1, v)
        gedge[pl.ds(8 + v, nx, stride=16), :] = rim_cot(8, v)
    none = jnp.zeros((nx, 128), F32)
    for q in range(20, RIM):
        edge[pl.ds(q, nx, stride=RIM), :] = none
    for q in (5, 6, 7):
        gedge[pl.ds(q, nx, stride=16), :] = none
        gedge[pl.ds(8 + q, nx, stride=16), :] = none
    for x in range(nx):
        mid = edge[pl.ds(x * RIM, RIM), :]
        at = (x + 1) * 3 * RIM
        t_rim[pl.ds(at, RIM), :] = pltpu.roll(mid, 1, 1).astype(BF16)
        t_rim[pl.ds(at + RIM, RIM), :] = mid.astype(BF16)
        t_rim[pl.ds(at + 2 * RIM, RIM), :] = pltpu.roll(mid, 127, 1).astype(BF16)
    t_rim[pl.ds(0, 3 * RIM), :] = t_rim[pl.ds(nx * 3 * RIM, 3 * RIM), :]
    t_rim[pl.ds((nx + 1) * 3 * RIM, 3 * RIM), :] = t_rim[pl.ds(3 * RIM, 3 * RIM), :]

    kept = 8 * ch
    kg = hg = dsum = None
    zeros8 = jnp.zeros((8, 128 * WIDE), F32)
    written = set()
    for x in range(0, nx, WIDE):
        s = jnp.concatenate(
            [
                jnp.concatenate(
                    [
                        t[pl.ds((x + j) * 3 * MAIN, 9 * MAIN), :],
                        t_rim[pl.ds((x + j) * 3 * RIM, 9 * RIM), :],
                    ],
                    axis=0,
                )
                for j in range(WIDE)
            ],
            axis=1,
        )
        z2 = jnp.dot(w_rows[...], s, preferred_element_type=F32)
        rows = z2.shape[0] // 2
        z = z2[:rows] + z2[rows:] + jnp.concatenate([bias[...]] * WIDE, axis=1)
        hidden = jnp.tanh(z)
        g = jnp.concatenate(
            [
                jnp.concatenate(
                    [cot[v, x + j] for v in range(5)] + [gedge[pl.ds((x + j) * 16, 16), :]], axis=0
                )
                for j in range(WIDE)
            ],
            axis=1,
        )
        g_hi, g_lo = split(g)
        g_hi32, g_lo32 = g_hi.astype(F32), g_lo.astype(F32)
        g3 = jnp.concatenate(
            [g_hi32, zeros8, g_hi32, zeros8, g_lo32, zeros8], axis=0
        ).astype(BF16)
        d = (1.0 - hidden * hidden) * jnp.dot(w_head[...], g3, preferred_element_type=F32)
        d_hi, d_lo = split(d)
        zeros = jnp.zeros((512 - 3 * rows, 128 * WIDE), BF16)
        back = jnp.dot(
            w_cols[...],
            jnp.concatenate([d_hi, d_lo, d_hi, zeros], axis=0),
            preferred_element_type=F32,
        )
        k2 = over_lanes(jnp.concatenate([d_hi[:kept], d_lo[:kept]], axis=0), s)
        k2 = k2[:kept] + k2[kept:]
        kg = k2 if kg is None else kg + k2
        hid2 = jnp.concatenate(split(hidden[:kept]), axis=0)
        g2 = jnp.concatenate([g_hi32[:40], g_lo32[:40]], axis=0).astype(BF16)
        h2 = over_lanes(hid2, g2)
        hg = h2 if hg is None else hg + h2
        for j in range(WIDE):
            level = d[:kept, 128 * j : 128 * (j + 1)]
            dsum = level if dsum is None else dsum + level
        for m in range(WIDE + 2):
            total = None
            for j in range(WIDE):
                if 0 <= m - j < 3:
                    q = m - j
                    piece = back[q * 128 : q * 128 + 120, 128 * j : 128 * (j + 1)]
                    total = piece if total is None else total + piece
            here = (x + m - 1) % nx
            if here in written:
                total = total + acc[pl.ds(here * 120, 120), :]
            written.add(here)
            acc[pl.ds(here * 120, 120), :] = total
    for x in range(nx):
        at = x * 120
        total = (
            acc[pl.ds(at + 40, 40), :]
            + pltpu.roll(acc[pl.ds(at, 40), :], 127, 1)
            + pltpu.roll(acc[pl.ds(at + 80, 40), :], 1, 1)
        )
        for v in range(5):
            own[v, x] = total[8 * v : 8 * v + 8]

    sums = jnp.sum(dsum, axis=1, keepdims=True)
    y_row = lax.broadcasted_iota(jnp.int32, (kept, 40), 0)
    y_col = lax.broadcasted_iota(jnp.int32, (kept, 40), 1) & 7
    same_y = (y_row >= y_col * ch) & (y_row < (y_col + 1) * ch)
    h_all = (hg[:kept, :40] + hg[kept:, :40]) + (hg[:kept, 40:80] + hg[kept:, 40:80])
    h_all = jnp.where(same_y, h_all, 0.0)
    level_sum = jnp.zeros((ch, 1), F32)
    head_sum = jnp.zeros((ch, 40), F32)
    n = kg.shape[1]
    columns_at, tap = columns()
    kind = jnp.broadcast_to(columns_at[0:1], (ch, n))
    total = jnp.zeros((ch, n), F32)
    for y in range(8):
        rows = kg[y * ch : (y + 1) * ch]
        moved = rows if y == 1 else pltpu.roll(rows, (1 - y) % n, 1)
        keep = kind < 3
        if y == 0:
            keep = (kind == 1) | (kind == 2)
            total = total + jnp.where(kind == 8, rows, 0.0)
        if y == 7:
            keep = kind < 2
            total = total + jnp.where(kind == 10, rows, 0.0)
        total = total + jnp.where(keep, moved, 0.0)
        level_sum = level_sum + sums[y * ch : (y + 1) * ch]
        head_sum = head_sum + h_all[y * ch : (y + 1) * ch]
    grads = over_lanes(jnp.concatenate(split(total), axis=0), own_taps(columns_at, tap))
    n_pick = grads.shape[1]
    parts[...] = jnp.zeros_like(parts)
    parts[:, pl.ds(0, n_pick)] = grads[:ch] + grads[ch:]
    parts[:, pl.ds(0, taps)] = parts[:, pl.ds(0, taps)] + level_sum * level_taps((ch, taps))
    e_row = lax.broadcasted_iota(jnp.int32, (40, 128), 0) >> 3
    e_col = lax.broadcasted_iota(jnp.int32, (40, 128), 1) - 16
    to_col = jnp.where(e_row == e_col, 1.0, 0.0).astype(BF16)
    head_out = jnp.dot(
        jnp.concatenate(split(head_sum * STEP), axis=0), to_col, preferred_element_type=F32
    )
    parts[:, pl.ds(128, 128)] = parts[:, pl.ds(128, 128)] + (head_out[:ch] + head_out[ch:])


def columns():
    lane = lax.broadcasted_iota(jnp.int32, (8, COLUMNS), 1)
    main = lane < 9 * MAIN
    past = lane - 9 * MAIN
    block = sum((lane >= MAIN * i).astype(jnp.int32) for i in range(1, 9))
    o = jnp.where(main, block, past >> 5)
    r = jnp.where(main, lane - MAIN * block, past & (RIM - 1))
    which = sum((r >= 5 * i).astype(jnp.int32) for i in (1, 2, 3, 4))
    kind = jnp.where(main, jnp.where(r < 40, r & 7, 12), 8 + which)
    v = jnp.where(main, r >> 3, r - 5 * which)
    return kind, o * 5 + v


def taps_of(columns_at):
    n = columns_at.shape[1]
    row = lax.broadcasted_iota(jnp.int32, (144, n), 0)
    return jnp.where(row == jnp.broadcast_to(columns_at[0:1], (144, n)), 1.0, 0.0).astype(BF16)


def own_taps(kind, tap):
    at = jnp.where(kind < 3, tap + 45 * kind, 1000)
    at = jnp.where(kind == 8, tap, at)
    return taps_of(jnp.where(kind == 10, tap + 90, at))


def rim_taps(kind, tap):
    first = (kind == 9) | (kind == 7)
    middle = (kind == 8) | (kind == 10)
    last = (kind == 0) | (kind == 11)
    at = jnp.where(first, tap, jnp.where(middle, tap + 45, 1000))
    return taps_of(jnp.where(last, tap + 90, at))


def level_taps(shape):
    t = lax.broadcasted_iota(jnp.int32, shape, 1).astype(F32)
    v = t - 5.0 * jnp.floor((t + 0.5) * 0.2)
    return jnp.where((v < 0.5) | (v > 3.5), 1.0, 0.0)


def call(kernel, outs, scratch, us, n_in, order=0):
    spec = pl.BlockSpec(memory_space=pltpu.VMEM)
    return pl.pallas_call(
        kernel,
        out_shape=outs,
        in_specs=[spec] * n_in + [pl.BlockSpec(memory_space=pl.ANY)] * order,
        scratch_shapes=scratch,
        compiler_params=pltpu.CompilerParams(vmem_limit_bytes=VMEM),
        cost_estimate=pl.CostEstimate(
            flops=0, bytes_accessed=int(us * 3.69e6), transcendentals=0
        ),
    )


def body(state, cot, flags, kernel, heads):
    _, nx, ny, nz = state.shape
    ch, taps = kernel.shape
    count = lax.axis_size("gy")
    cells = nx * ny * nz
    shape = lambda *dims: jax.ShapeDtypeStruct(dims, F32)
    half_shape = lambda *dims: jax.ShapeDtypeStruct(dims, BF16)
    full = shape(5, nx, ny, nz)
    with_twin = [(i, i ^ 1) for i in range(count)]
    with_other = [(i, (i + 1) % count if i % 2 else (i - 1) % count) for i in range(count)]
    vm = pltpu.VMEM
    lines = 5 * nx * ny

    flat = jnp.concatenate([state.reshape(lines, nz), cot.reshape(lines, nz)])
    fields = flat.reshape(10, nx, ny, nz)
    near, far = shape(NEAR, nx, nz), shape(FAR, nx, nz)
    near_twin, near_other = call(near_kernel, (near, near), [], 0.2, 1)(flat)
    near_rims = (
        lax.ppermute(near_twin, "gy", with_twin),
        lax.ppermute(near_other, "gy", with_other),
    )
    far_twin, far_other, *prepared, patches = call(
        prepare_kernel,
        (
            far,
            far,
            half_shape(20 * ch, COLUMNS),
            half_shape(384, 512),
            half_shape(10 * ch, 192),
            shape(10 * ch, 128),
            half_shape((nx + 2) * 3 * MAIN, nz),
        ),
        [vm((2 * ch, 144), F32)],
        1.5,
        5,
    )(fields, flat, flags.reshape(3 * nx * ny, nz), kernel, heads)
    far_rims = (
        lax.ppermute(far_twin, "gy", with_twin),
        lax.ppermute(far_other, "gy", with_other),
    )
    near_rims, patches = lax.optimization_barrier((near_rims, patches))
    own, parts = call(
        c_kernel,
        (full, shape(ch, 256)),
        [
            vm(((nx + 2) * 3 * RIM, nz), BF16),
            vm((nx * 120, nz), F32),
            vm((RIM * nx, nz), F32),
            vm((16 * nx, nz), F32),
        ],
        3.5,
        9,
    )(fields, *near_rims, kernel, *prepared, patches)

    def exchanged(value, bit):
        return lax.ppermute(value, "gy", [(i, i ^ bit) for i in range(count)])

    bits = [1 << b for b in range(count.bit_length() - 1)]
    sums = parts
    for bit in bits[:-3]:
        sums = sums + exchanged(sums, bit)
    got = exchanged(sums, bits[-3])
    total = call(z_kernel, full, [], 3.5, 3, 1)(fields, flags, own, sums)
    got, total = lax.optimization_barrier((got, total))
    sums = sums + got
    got = exchanged(sums, bits[-2])
    total = call(
        x_kernel,
        full,
        [
            vm((5, nx + 5, ny, nz), F32),
            vm((5, nx + 1, ny, nz), F32),
            vm((5, nx + 5, ny, nz), F32),
        ],
        2.8,
        3,
    )(fields, flags, total)
    got, total = lax.optimization_barrier((got, total))
    sums = sums + got
    got = exchanged(sums, bits[-1])
    flow = call(y_kernel, full, [vm((lines, nz), F32)] * 3, 4.5, 8, 1)(
        fields, flat, flags, *near_rims, *far_rims, total, sums
    )
    got, flow = lax.optimization_barrier((got, flow))
    scale = float(cells * count) ** (-0.5)
    k_out, h_out = call(
        functools.partial(sum_kernel, scale), (shape(ch, taps), shape(5, ch)), [], 0.5, 2
    )(sums, got)
    return flow, k_out, h_out


def solution(mesh):
    split_y = P(None, "ens", "gy", None)
    return jax.shard_map(
        body,
        mesh=mesh,
        in_specs=(split_y, split_y, split_y, P(), P()),
        out_specs=(split_y, P("ens", None), P("ens", None)),
        check_vma=False,
    )
```

```python
import functools

import jax
import jax.numpy as jnp
from jax import lax
from jax.experimental import pallas as pl
from jax.experimental.pallas import tpu as pltpu
from jax.sharding import PartitionSpec as P

STEP = 0.3
FLOOR = 0.01
BELOW, ABOVE = 2, 3
SLABS = 2
WIDE = 4
VMEM = 48 * 1024 * 1024
F32 = jnp.float32
BF16 = jnp.bfloat16


def rcp(x):
    return pl.reciprocal(x, approx=True)


def shared_terms(v):
    p = [v[i + 1] - v[i] for i in range(5)]
    d = [p[i + 1] - p[i] for i in range(4)]
    h = [(4.0 / 3.0) * x for x in d]
    k = [h[i] * d[i] + FLOOR for i in range(4)]
    g = [x + x for x in h]
    t = [d[i + 1] - d[i] for i in range(3)]
    return p, d, k, g, t


def side_value(pa, pm, pm2, ka, kb, kc, m0, m2, td, t1, smooth, c0, c2):
    i0 = rcp(ka + pa * m0)
    i1 = rcp(kb + pa * pm)
    i2 = rcp(kc + pm * m2)
    w0 = i0 * i0
    w1 = 6.0 * (i1 * i1)
    w2 = 3.0 * (i2 * i2)
    r = rcp(w0 + w1 + w2)
    o0 = jnp.where(smooth, w0 * r, c0)
    o2 = jnp.where(smooth, w2 * r, c2)
    u = o0 * td + o2 * t1
    return (pa + pm2) - u, (i0, i1, i2, w0, w1, w2, r, o0, o2, u)


def side_pull(mu, pa, pm, m0, m2, td, t1, smooth, saved):
    i0, i1, i2, w0, w1, w2, r, o0, o2, u = saved
    mu2 = mu + mu
    rm = jnp.where(smooth, mu2, 0.0) * r
    s0 = (w0 * i0) * rm * (td - u)
    s1 = (w1 * i1) * rm * u
    s2 = (w2 * i2) * rm * (t1 - u)
    pa_bar = s0 * (m0 + pa) - s1 * pm + mu
    pm_bar = s2 * (m2 + pm) - s1 * pa + mu2
    return s0, s1, s2, pa_bar, pm_bar, o0 * mu2, o2 * mu


def hllc_pull(left, right, normal, flags, cot):
    region = flags & 3
    is_right = region >= 2
    star = ((region + 1) & 2) != 0
    n_at = 1 + normal
    tang = [1 + i for i in range(3) if i != normal]
    rl, rr_, pl_, pr_, nl, nr = left[0], right[0], left[4], right[4], left[n_at], right[n_at]

    def sound(r, p):
        inv = rcp(r)
        t = 1.4 * p * inv
        inv_c = lax.rsqrt(t)
        return inv, inv_c, t * inv_c

    inv_rl, inv_cl, cl = sound(rl, pl_)
    inv_rr, inv_cr, cr = sound(rr_, pr_)
    c = 0.5 * (cl + cr)
    r2 = rl + rr_
    inv = rcp(r2 * c)
    nm = 0.5 * (nl + nr)
    gap = (pl_ - pr_) * inv
    sm = nm + gap
    sc = jnp.where(is_right, c, -c)
    s = nm + sc
    pick = [jnp.where(is_right, right[i], left[i]) for i in range(5)]
    r, un, u1, u2, p = pick[0], pick[n_at], pick[tang[0]], pick[tang[1]], pick[4]
    a = s - un
    dl = sm - un
    si = jnp.where(star, rcp(sc - gap), 0.0)
    j = s * si
    kap = j * dl
    g0, gn, g1, g2, ge = cot[0], cot[n_at], cot[tang[0]], cot[tang[1]], cot[4]
    w = un + kap
    half_q = 0.5 * (un * un + u1 * u1 + u2 * u2)
    enthalpy = 3.5 * p + r * half_q
    b = g0 + u1 * g1 + u2 * g2 + un * gn
    m = r * b + enthalpy * ge
    n = gn + sm * ge
    rkap = r * kap
    f_kap = m + r * a * n
    f_a = rkap * n
    si2 = si * si
    s_bar = f_a - f_kap * (dl * sm * si2)
    sm_bar = f_kap * (s * a * si2) + rkap * a * ge
    wr = w * r
    k_bar = [None] * 5
    k_bar[0] = w * (b + half_q * ge) + kap * a * n
    k_bar[n_at] = m + wr * (gn + un * ge) - f_kap * j - f_a
    k_bar[tang[0]] = wr * (g1 + u1 * ge)
    k_bar[tang[1]] = wr * (g2 + u2 * ge)
    k_bar[4] = 3.5 * (w * ge) + gn
    e = sm_bar * inv
    eg = e * gap
    c_half = 0.5 * (jnp.where(is_right, s_bar, -s_bar) - eg * r2)
    n_half = 0.5 * (s_bar + sm_bar)
    r_both = -(eg * c)
    xl = c_half * inv_rl
    xr = c_half * inv_rr
    base_l = {0: r_both - 0.5 * (xl * cl), n_at: n_half, 4: 0.7 * (xl * inv_cl) + e}
    base_r = {0: r_both - 0.5 * (xr * cr), n_at: n_half, 4: 0.7 * (xr * inv_cr) - e}
    l_bar, r_bar = [], []
    for i in range(5):
        kr = jnp.where(is_right, k_bar[i], 0.0)
        kl = k_bar[i] - kr
        l_bar.append(base_l[i] + kl if i in base_l else kl)
        r_bar.append(base_r[i] + kr if i in base_r else kr)
    return l_bar, r_bar


def face_pull(cells, cot, flags, normal):
    stencil = flags >> 2
    smooth = stencil == 0
    c0 = jnp.where(stencil == 1, 1.0, 0.0)
    c2 = jnp.where(stencil == 3, 1.0, 0.0)
    left, right, kept = [], [], []
    for v in cells:
        p, d, k, g, t = shared_terms(v)
        pm2 = p[2] + p[2]
        args_l = (p[1], p[2], p[1] + d[0], p[2] - d[2], t[0] + t[0], t[1])
        args_r = (p[3], p[2], p[3] - d[3], p[2] + d[1], t[2] + t[2], t[1])
        hl, saved_l = side_value(
            p[1], p[2], pm2, k[0], k[1], k[2], *args_l[2:], smooth, c0, c2
        )
        hr, saved_r = side_value(
            p[3], p[2], pm2, k[3], k[2], k[1], *args_r[2:], smooth, c0, c2
        )
        left.append(v[2] + hl * (1.0 / 6.0))
        right.append(v[3] - hr * (1.0 / 6.0))
        kept.append((p, g, args_l, args_r, saved_l, saved_r))
    l_bar, r_bar = hllc_pull(left, right, normal, flags, cot)
    out = []
    for i in range(5):
        p, g, args_l, args_r, saved_l, saved_r = kept[i]
        a0, a1, a2, pa_l, pm_l, x0, x2 = side_pull(
            l_bar[i] * (1.0 / 6.0), *args_l, smooth, saved_l
        )
        b0, b1, b2, pa_r, pm_r, y0, y2 = side_pull(
            r_bar[i] * (-1.0 / 6.0), *args_r, smooth, saved_r
        )
        d0 = a0 * (g[0] + p[1]) + x0
        d1 = (b2 * (g[1] + p[2]) - a1 * g[1]) + (x2 - x0) + y2
        d2 = (a2 * (g[2] - p[2]) - b1 * g[2]) + (y0 - y2) - x2
        d3 = b0 * (g[3] - p[3]) - y0
        p2 = pa_l + (d0 - d1)
        p3 = pm_l + pm_r + (d1 - d2)
        p4 = pa_r + (d2 - d3)
        out.append([d0, -d0 - p2, l_bar[i] + (p2 - p3), r_bar[i] + (p3 - p4), p4 - d3, d3])
    return out


def conserved_pull(s, g):
    half_q = 0.5 * (s[1] * s[1] + s[2] * s[2] + s[3] * s[3])
    return [
        g[0] + s[1] * g[1] + s[2] * g[2] + s[3] * g[3] + half_q * g[4],
        s[0] * (g[1] + s[1] * g[4]),
        s[0] * (g[2] + s[2] * g[4]),
        s[0] * (g[3] + s[3] * g[4]),
        2.5 * g[4],
    ]


NEAR_STATE, FAR_STATE = 2, 3
NEAR_COT, FAR_COT = 1, 2
FLAG_ROWS = 3
NEAR = 5 * (NEAR_STATE + NEAR_COT)
FAR = 5 * (FAR_STATE + FAR_COT) + FLAG_ROWS


def views(fields):
    n = fields.shape[0] // 2
    return fields.at[pl.ds(0, n)], fields.at[pl.ds(n, n)]


def pack(ref, rows, first, twin, other, at):
    even = is_even()
    nx = twin.shape[1]
    count = ref.shape[0] // (8 * nx)
    for r in rows:
        for v in range(count):
            low = ref[pl.ds(v * nx * 8 + r, nx, stride=8), :].astype(F32)
            top = ref[pl.ds(v * nx * 8 + 7 - r, nx, stride=8), :].astype(F32)
            i = at + (r - first) * count + v
            twin[i] = jnp.where(even, top, low)
            other[i] = jnp.where(even, low, top)


def near_kernel(flat, twin, other):
    s, g = views(flat)
    pack(s, range(NEAR_STATE), 0, twin, other, 0)
    pack(g, range(NEAR_COT), 0, twin, other, 5 * NEAR_STATE)


def far_kernel(flat, flags, order, order2, twin, other):
    del order, order2
    s, g = views(flat)
    n = flags.shape[0] // 3
    pack(s, range(NEAR_STATE, NEAR_STATE + FAR_STATE), NEAR_STATE, twin, other, 0)
    pack(g, range(NEAR_COT, NEAR_COT + FAR_COT), NEAR_COT, twin, other, 5 * FAR_STATE)
    pack(flags.at[pl.ds(n, n)], range(FLAG_ROWS), 0, twin, other, FAR - FLAG_ROWS)


def from_rims(near_twin, near_other, far_twin=None, far_other=None):
    even = is_even()

    def pick(twin, other, i, below):
        if below:
            return jnp.where(even, other[i], twin[i])
        return jnp.where(even, twin[i], other[i])

    def read(row, near, near_at, far_at, v):
        below = row < 0
        r = -1 - row if below else row - 8
        if r < near:
            return pick(near_twin, near_other, near_at + r * 5 + v, below)
        return pick(far_twin, far_other, far_at + (r - near) * 5 + v, below)

    def state(row, v):
        return read(row, NEAR_STATE, 0, 0, v)

    def cot(row, v):
        return read(row, NEAR_COT, 5 * NEAR_STATE, 5 * FAR_STATE, v)

    def flags(row):
        below = row < 0
        r = -1 - row if below else row - 8
        return pick(far_twin, far_other, FAR - FLAG_ROWS + r, below).astype(jnp.int32)

    return state, cot, flags


def x_kernel(fields, flags, before, order, out, pad, gpad, acc):
    del order
    state, cot = views(fields)
    nx = state.shape[1]
    for v in range(5):
        pad[v, pl.ds(2, nx)] = state[v]
        pad[v, pl.ds(0, 2)] = state[v, pl.ds(nx - 2, 2)]
        pad[v, pl.ds(nx + 2, 3)] = state[v, pl.ds(0, 3)]
        gpad[v, pl.ds(0, nx)] = cot[v]
        gpad[v, pl.ds(nx, 1)] = cot[v, pl.ds(0, 1)]
    acc[...] = jnp.zeros_like(acc)

    def step(i, carry):
        x = i * SLABS
        cells = [[pad[v, pl.ds(x + k, SLABS)] for k in range(6)] for v in range(5)]
        g = [gpad[v, pl.ds(x, SLABS)] for v in range(5)]
        face = [STEP * (gpad[v, pl.ds(x + 1, SLABS)] - g[v]) for v in range(5)]
        terms = face_pull(cells, face, flags[0, pl.ds(x, SLABS)], 0)
        own = conserved_pull([cells[v][2] for v in range(5)], g)
        for v in range(5):
            terms[v][2] = terms[v][2] + own[v]
            for s in range(SLABS + 5):
                total = None
                for k in range(6):
                    if 0 <= s - k < SLABS:
                        part = terms[v][k][s - k]
                        total = part if total is None else total + part
                acc[v, x + s] = acc[v, x + s] + total
        return carry

    lax.fori_loop(0, nx // SLABS, step, 0)
    for v in range(5):
        acc[v, pl.ds(nx, 2)] = acc[v, pl.ds(nx, 2)] + acc[v, pl.ds(0, 2)]
        acc[v, pl.ds(2, 3)] = acc[v, pl.ds(2, 3)] + acc[v, pl.ds(nx + 2, 3)]

    for v in range(5):
        out[v] = acc[v, pl.ds(2, nx)] + before[v]


def z_kernel(half, fields, flags, before, order, out):
    del order
    state, cot = views(fields)
    nx = state.shape[1] // 2
    for v in range(5):
        out[v, pl.ds((1 - half) * nx, nx)] = before[v, pl.ds((1 - half) * nx, nx)]

    def z_step(i, carry):
        x = half * nx + i * SLABS
        cells, face = [], []
        for v in range(5):
            mid = state[v, pl.ds(x, SLABS)]
            cells.append([mid if k == 0 else pltpu.roll(mid, (-k) % 128, 2) for k in range(-2, 4)])
            g = cot[v, pl.ds(x, SLABS)]
            face.append(STEP * (pltpu.roll(g, 127, 2) - g))
        terms = face_pull(cells, face, flags[2, pl.ds(x, SLABS)], 2)
        for v in range(5):
            t = before[v, pl.ds(x, SLABS)] + terms[v][2]
            for k in (-2, -1, 1, 2, 3):
                t = t + pltpu.roll(terms[v][k + 2], k % 128, 2)
            out[v, pl.ds(x, SLABS)] = t
        return carry

    lax.fori_loop(0, nx // SLABS, z_step, 0)


def e_faces(state, cot, rims, out):
    nx = out.shape[0] // 40
    rim_state, rim_cot, rim_flags = rims

    def own(ref, row, v):
        return ref[pl.ds(v * nx * 8 + row, nx, stride=8), :]

    state_rows, cot_rows = {}, {}
    for v in range(5):
        for row in (*range(-5, 3), *range(6, 13)):
            inside = 0 <= row < 8
            state_rows[row, v] = own(state, row, v) if inside else rim_state(row, v)
        for row in (-3, -2, -1, 0, 8, 9, 10):
            inside = 0 <= row < 8
            cot_rows[row, v] = own(cot, row, v) if inside else rim_cot(row, v)
    sums = {}
    for j in (-3, -2, -1, 8, 9):
        cells = [[state_rows[j + k, v] for k in range(-2, 4)] for v in range(5)]
        face = [STEP * (cot_rows[j + 1, v] - cot_rows[j, v]) for v in range(5)]
        terms = face_pull(cells, face, rim_flags(j), 1)
        for v in range(5):
            for k in range(-2, 4):
                if 0 <= j + k < 8:
                    t = terms[v][k + 2]
                    sums[j + k, v] = sums[j + k, v] + t if (j + k, v) in sums else t
    for v in range(5):
        for row in range(8):
            value = sums[row, v] if (row, v) in sums else jnp.zeros((nx, 128), F32)
            out[pl.ds(v * nx * 8 + row, nx, stride=8), :] = value


def y_kernel(fields, flat, flags, near_twin, near_other, far_twin, far_other, before, order, out, rim, halo, ghalo):
    del order
    state, cot = views(fields)
    rims = from_rims(near_twin, near_other, far_twin, far_other)
    e_faces(*views(flat), rims, rim)
    rim_state, rim_cot, _ = rims
    nx = out.shape[1]
    for v in range(5):
        base = v * nx * 8
        for r in range(ABOVE):
            halo[pl.ds(base + r, nx, stride=8), :] = rim_state(8 + r, v)
        for r in range(BELOW):
            halo[pl.ds(base + 8 - BELOW + r, nx, stride=8), :] = rim_state(r - BELOW, v)
        ghalo[pl.ds(base, nx, stride=8), :] = rim_cot(8, v)
    row = lax.broadcasted_iota(jnp.int32, (SLABS, 8, 128), 1)
    inside = {}
    for k in (-2, -1, 1, 2, 3):
        inside[k] = (row < 8 + k) if k < 0 else (row >= k)

    def step(i, carry):
        x = i * SLABS
        cells, face = [], []
        for v in range(5):
            at = pl.multiple_of((v * nx + x) * 8, 8)
            rim_rows = halo[pl.ds(at, 8 * SLABS), :].reshape(SLABS, 8, 128)
            mid = state[v, pl.ds(x, SLABS)]
            line = []
            for k in range(-2, 4):
                if k == 0:
                    line.append(mid)
                else:
                    line.append(pltpu.roll(jnp.where(inside[k], mid, rim_rows), (-k) % 8, 1))
            cells.append(line)
            g = cot[v, pl.ds(x, SLABS)]
            g_rim = ghalo[pl.ds(at, 8 * SLABS), :].reshape(SLABS, 8, 128)
            face.append(STEP * (pltpu.roll(jnp.where(inside[1], g, g_rim), 7, 1) - g))
        terms = face_pull(cells, face, flags[1, pl.ds(x, SLABS)], 1)
        for v in range(5):
            at = pl.multiple_of((v * nx + x) * 8, 8)
            total = before[v, pl.ds(x, SLABS)] + terms[v][2]
            total = total + rim[pl.ds(at, 8 * SLABS), :].reshape(SLABS, 8, 128)
            for k in (-2, -1, 1, 2, 3):
                moved = pltpu.roll(terms[v][k + 2], k % 8, 1)
                total = total + jnp.where(inside[k], moved, 0.0)
            out[v, pl.ds(x, SLABS)] = total
        return carry

    lax.fori_loop(0, nx // SLABS, step, 0)


def sum_kernel(scale, mine, theirs, k_out, h_out):
    total = (mine[...] + theirs[...]) * scale
    k_out[...] = total[:, : k_out.shape[1]]
    ch = total.shape[0]
    pick = (
        lax.broadcasted_iota(jnp.int32, (8, 128), 1)
        == lax.broadcasted_iota(jnp.int32, (8, 128), 0) + 16
    ).astype(F32)
    heads = lax.dot_general(
        pick,
        total[:, 128:],
        (((1,), (1,)), ((), ())),
        precision=lax.Precision.HIGHEST,
        preferred_element_type=F32,
    )
    h_out[...] = heads[: h_out.shape[0], :ch]


MAIN, RIM = 48, 32
COLUMNS = 9 * (MAIN + RIM)


def split(x):
    hi = x.astype(BF16)
    return hi, (x - hi.astype(F32)).astype(BF16)


def over_lanes(a, b):
    return lax.dot_general(a, b, (((1,), (1,)), ((), ())), preferred_element_type=F32)


def is_even():
    return lax.rem(lax.axis_index("gy"), 2) == 0


def prepare_kernel(fields, kernel, heads, order, order2, w_rows, w_cols, w_head, bias, t, wide):
    del order, order2
    state, _ = views(fields)
    nx = state.shape[1]
    for x in range(nx):
        rows = [state[v, x] - (1.0 if v in (0, 4) else 0.0) for v in range(5)]
        mid = jnp.concatenate([*rows, jnp.zeros((8, 128), F32)], axis=0)
        at = (x + 1) * 3 * MAIN
        t[pl.ds(at, MAIN), :] = pltpu.roll(mid, 1, 1).astype(BF16)
        t[pl.ds(at + MAIN, MAIN), :] = mid.astype(BF16)
        t[pl.ds(at + 2 * MAIN, MAIN), :] = pltpu.roll(mid, 127, 1).astype(BF16)
    t[pl.ds(0, 3 * MAIN), :] = t[pl.ds(nx * 3 * MAIN, 3 * MAIN), :]
    t[pl.ds((nx + 1) * 3 * MAIN, 3 * MAIN), :] = t[pl.ds(3 * MAIN, 3 * MAIN), :]

    ch, taps = kernel.shape
    w = kernel[...]
    hi, lo = split(w)
    wide[...] = jnp.zeros_like(wide)
    wide[pl.ds(0, ch), pl.ds(0, taps)] = hi.astype(F32)
    wide[pl.ds(ch, ch), pl.ds(0, taps)] = lo.astype(F32)
    both = wide[...].astype(BF16)
    kind, tap = columns()
    base = jnp.dot(both, own_taps(kind, tap), preferred_element_type=F32)
    rim = jnp.dot(both, rim_taps(kind, tap), preferred_element_type=F32)
    n = base.shape[1]
    kind = jnp.broadcast_to(kind[0:1], base.shape)
    main = jnp.where(kind < 3, base, 0.0)
    bands = []
    for y in range(8):
        rows = main
        if y == 0:
            rows = jnp.where(kind == 0, 0.0, rows)
        if y == 7:
            rows = jnp.where(kind == 2, 0.0, rows)
        if y != 1:
            rows = pltpu.roll(rows, (y - 1) % n, 1)
        if y == 0:
            rows = rows + jnp.where(kind == 8, base, 0.0)
        if y == 7:
            rows = rows + jnp.where(kind == 10, base, 0.0)
        bands.append(rows)
    bands.append(jnp.where((kind == 0) | (kind == 8) | (kind == 9), rim, 0.0))
    bands.append(jnp.where((kind == 7) | (kind == 10) | (kind == 11), rim, 0.0))
    full = jnp.concatenate([b[:ch] for b in bands] + [b[ch:] for b in bands], axis=0)
    w_rows[...] = full.astype(BF16)
    kept = full.shape[0] // 2
    cols = jnp.concatenate([full[:kept], full[:kept], full[kept:]], axis=0)
    cols = jnp.concatenate([cols, jnp.zeros((512 - 3 * kept, n), F32)], axis=0)
    own_cols = []
    for q in range(3):
        own_cols += [cols[:, (3 * q + o) * MAIN : (3 * q + o) * MAIN + 40] for o in range(3)]
        own_cols.append(jnp.zeros((512, 8), F32))
    w_cols[...] = jnp.concatenate(own_cols, axis=1).T.astype(BF16)
    total = jnp.sum(w * level_taps(w.shape), axis=1, keepdims=True)
    total = jnp.broadcast_to(total, (ch, 128))
    bias[...] = jnp.concatenate([total] * 10, axis=0)

    h_hi, h_lo = split(STEP * heads[...])
    none = jnp.zeros((3, ch), F32)
    pair = jnp.concatenate([h_hi.astype(F32), none, h_lo.astype(F32), none], axis=0).astype(BF16)
    r = lax.broadcasted_iota(jnp.int32, (kept, ch), 0)
    q = lax.broadcasted_iota(jnp.int32, (kept, ch), 1)
    spread = jnp.where((r & (ch - 1)) == q, 1.0, 0.0).astype(BF16)
    picked = over_lanes(pair, spread)
    y_of = lax.broadcasted_iota(jnp.int32, (8, kept), 0)
    col = lax.broadcasted_iota(jnp.int32, (8, kept), 1)
    same = (col >= y_of * ch) & (col < (y_of + 1) * ch)
    split_heads = []
    for at in (0, 8):
        rows = [
            jnp.where(same, jnp.broadcast_to(picked[at + e : at + e + 1], (8, kept)), 0.0)
            for e in range(5)
        ]
        five = picked[at : at + 8]
        rows.append(jnp.where((col >= 8 * ch) & (col < 9 * ch), five, 0.0))
        rows.append(jnp.where(col >= 9 * ch, five, 0.0))
        rows.append(jnp.zeros((8, kept), F32))
        split_heads.append(jnp.concatenate(rows, axis=0))
    three = jnp.concatenate([split_heads[0], split_heads[1], split_heads[0]], axis=0)
    w_head[...] = three.T.astype(BF16)


def c_kernel(
    fields, near_twin, near_other, kernel, w_rows, w_cols, w_head, bias, t,
    own, parts,
    t_rim, acc, edge, gedge,
):
    _, cot = views(fields)
    nx = cot.shape[1]
    ch, taps = kernel.shape
    rim_state, rim_cot, _ = from_rims(near_twin, near_other)

    for v in range(5):
        level = 1.0 if v in (0, 4) else 0.0
        for q, row in enumerate((-1, -2, 8, 9)):
            edge[pl.ds(5 * q + v, nx, stride=RIM), :] = rim_state(row, v) - level
        gedge[pl.ds(v, nx, stride=16), :] = rim_cot(-1, v)
        gedge[pl.ds(8 + v, nx, stride=16), :] = rim_cot(8, v)
    none = jnp.zeros((nx, 128), F32)
    for q in range(20, RIM):
        edge[pl.ds(q, nx, stride=RIM), :] = none
    for q in (5, 6, 7):
        gedge[pl.ds(q, nx, stride=16), :] = none
        gedge[pl.ds(8 + q, nx, stride=16), :] = none
    for x in range(nx):
        mid = edge[pl.ds(x * RIM, RIM), :]
        at = (x + 1) * 3 * RIM
        t_rim[pl.ds(at, RIM), :] = pltpu.roll(mid, 1, 1).astype(BF16)
        t_rim[pl.ds(at + RIM, RIM), :] = mid.astype(BF16)
        t_rim[pl.ds(at + 2 * RIM, RIM), :] = pltpu.roll(mid, 127, 1).astype(BF16)
    t_rim[pl.ds(0, 3 * RIM), :] = t_rim[pl.ds(nx * 3 * RIM, 3 * RIM), :]
    t_rim[pl.ds((nx + 1) * 3 * RIM, 3 * RIM), :] = t_rim[pl.ds(3 * RIM, 3 * RIM), :]

    kept = 8 * ch
    kg = hg = dsum = None
    zeros8 = jnp.zeros((8, 128 * WIDE), F32)
    written = set()
    for x in range(0, nx, WIDE):
        s = jnp.concatenate(
            [
                jnp.concatenate(
                    [
                        t[pl.ds((x + j) * 3 * MAIN, 9 * MAIN), :],
                        t_rim[pl.ds((x + j) * 3 * RIM, 9 * RIM), :],
                    ],
                    axis=0,
                )
                for j in range(WIDE)
            ],
            axis=1,
        )
        z2 = jnp.dot(w_rows[...], s, preferred_element_type=F32)
        rows = z2.shape[0] // 2
        z = z2[:rows] + z2[rows:] + jnp.concatenate([bias[...]] * WIDE, axis=1)
        hidden = jnp.tanh(z)
        g = jnp.concatenate(
            [
                jnp.concatenate(
                    [cot[v, x + j] for v in range(5)] + [gedge[pl.ds((x + j) * 16, 16), :]], axis=0
                )
                for j in range(WIDE)
            ],
            axis=1,
        )
        g_hi, g_lo = split(g)
        g_hi32, g_lo32 = g_hi.astype(F32), g_lo.astype(F32)
        g3 = jnp.concatenate(
            [g_hi32, zeros8, g_hi32, zeros8, g_lo32, zeros8], axis=0
        ).astype(BF16)
        d = (1.0 - hidden * hidden) * jnp.dot(w_head[...], g3, preferred_element_type=F32)
        d_hi, d_lo = split(d)
        zeros = jnp.zeros((512 - 3 * rows, 128 * WIDE), BF16)
        back = jnp.dot(
            w_cols[...],
            jnp.concatenate([d_hi, d_lo, d_hi, zeros], axis=0),
            preferred_element_type=F32,
        )
        k2 = over_lanes(s, jnp.concatenate([d_hi[:kept], d_lo[:kept]], axis=0))
        k2 = k2[:, :kept] + k2[:, kept:]
        kg = k2 if kg is None else kg + k2
        hid2 = jnp.concatenate(split(hidden[:kept]), axis=0)
        g2 = jnp.concatenate([g_hi32[:40], g_lo32[:40]], axis=0).astype(BF16)
        h2 = over_lanes(g2, hid2)
        hg = h2 if hg is None else hg + h2
        for j in range(WIDE):
            level = d[:kept, 128 * j : 128 * (j + 1)]
            dsum = level if dsum is None else dsum + level
        for m in range(WIDE + 2):
            total = None
            for j in range(WIDE):
                if 0 <= m - j < 3:
                    q = m - j
                    piece = back[q * 128 : q * 128 + 120, 128 * j : 128 * (j + 1)]
                    total = piece if total is None else total + piece
            here = (x + m - 1) % nx
            if here in written:
                total = total + acc[pl.ds(here * 120, 120), :]
            written.add(here)
            acc[pl.ds(here * 120, 120), :] = total
    for x in range(nx):
        at = x * 120
        total = (
            acc[pl.ds(at + 40, 40), :]
            + pltpu.roll(acc[pl.ds(at, 40), :], 127, 1)
            + pltpu.roll(acc[pl.ds(at + 80, 40), :], 1, 1)
        )
        for v in range(5):
            own[v, x] = total[8 * v : 8 * v + 8]

    sums = jnp.sum(dsum, axis=1, keepdims=True)
    kg = kg.T
    hg = (hg[:40, :kept] + hg[40:, :kept]) + (hg[:40, kept:] + hg[40:, kept:])
    y_row = lax.broadcasted_iota(jnp.int32, (40, kept), 0) & 7
    y_col = lax.broadcasted_iota(jnp.int32, (40, kept), 1)
    same_y = (y_col >= y_row * ch) & (y_col < (y_row + 1) * ch)
    hg = jnp.where(same_y, hg, 0.0)
    by_eq = jnp.concatenate(
        [jnp.sum(hg[8 * e : 8 * e + 8], axis=0, keepdims=True) for e in range(5)]
        + [jnp.zeros((123, kept), F32)],
        axis=0,
    ).T
    level_sum = jnp.zeros((ch, 1), F32)
    head_sum = jnp.zeros((ch, 128), F32)
    n = kg.shape[1]
    columns_at, tap = columns()
    kind = jnp.broadcast_to(columns_at[0:1], (ch, n))
    total = jnp.zeros((ch, n), F32)
    for y in range(8):
        rows = kg[y * ch : (y + 1) * ch]
        moved = rows if y == 1 else pltpu.roll(rows, (1 - y) % n, 1)
        keep = kind < 3
        if y == 0:
            keep = (kind == 1) | (kind == 2)
            total = total + jnp.where(kind == 8, rows, 0.0)
        if y == 7:
            keep = kind < 2
            total = total + jnp.where(kind == 10, rows, 0.0)
        total = total + jnp.where(keep, moved, 0.0)
        level_sum = level_sum + sums[y * ch : (y + 1) * ch]
        head_sum = head_sum + by_eq[y * ch : (y + 1) * ch]
    grads = over_lanes(jnp.concatenate(split(total), axis=0), own_taps(columns_at, tap))
    n_pick = grads.shape[1]
    parts[...] = jnp.zeros_like(parts)
    parts[:, pl.ds(0, n_pick)] = grads[:ch] + grads[ch:]
    parts[:, pl.ds(0, taps)] = parts[:, pl.ds(0, taps)] + level_sum * level_taps((ch, taps))
    parts[:, pl.ds(128, 128)] = parts[:, pl.ds(128, 128)] + pltpu.roll(head_sum * STEP, 16, 1)


def columns():
    lane = lax.broadcasted_iota(jnp.int32, (8, COLUMNS), 1)
    main = lane < 9 * MAIN
    past = lane - 9 * MAIN
    block = sum((lane >= MAIN * i).astype(jnp.int32) for i in range(1, 9))
    o = jnp.where(main, block, past >> 5)
    r = jnp.where(main, lane - MAIN * block, past & (RIM - 1))
    which = sum((r >= 5 * i).astype(jnp.int32) for i in (1, 2, 3, 4))
    kind = jnp.where(main, jnp.where(r < 40, r & 7, 12), 8 + which)
    v = jnp.where(main, r >> 3, r - 5 * which)
    return kind, o * 5 + v


def taps_of(columns_at):
    n = columns_at.shape[1]
    row = lax.broadcasted_iota(jnp.int32, (144, n), 0)
    return jnp.where(row == jnp.broadcast_to(columns_at[0:1], (144, n)), 1.0, 0.0).astype(BF16)


def own_taps(kind, tap):
    at = jnp.where(kind < 3, tap + 45 * kind, 1000)
    at = jnp.where(kind == 8, tap, at)
    return taps_of(jnp.where(kind == 10, tap + 90, at))


def rim_taps(kind, tap):
    first = (kind == 9) | (kind == 7)
    middle = (kind == 8) | (kind == 10)
    last = (kind == 0) | (kind == 11)
    at = jnp.where(first, tap, jnp.where(middle, tap + 45, 1000))
    return taps_of(jnp.where(last, tap + 90, at))


def level_taps(shape):
    t = lax.broadcasted_iota(jnp.int32, shape, 1).astype(F32)
    v = t - 5.0 * jnp.floor((t + 0.5) * 0.2)
    return jnp.where((v < 0.5) | (v > 3.5), 1.0, 0.0)


def call(kernel, outs, scratch, us, n_in, order=0):
    spec = pl.BlockSpec(memory_space=pltpu.VMEM)
    return pl.pallas_call(
        kernel,
        out_shape=outs,
        in_specs=[spec] * n_in + [pl.BlockSpec(memory_space=pl.ANY)] * order,
        scratch_shapes=scratch,
        compiler_params=pltpu.CompilerParams(vmem_limit_bytes=VMEM),
        cost_estimate=pl.CostEstimate(
            flops=int(us * 1.15e9), bytes_accessed=int(us * 3.69e6), transcendentals=0
        ),
    )


def body(state, cot, flags, kernel, heads):
    _, nx, ny, nz = state.shape
    ch, taps = kernel.shape
    count = lax.axis_size("gy")
    cells = nx * ny * nz
    shape = lambda *dims: jax.ShapeDtypeStruct(dims, F32)
    half_shape = lambda *dims: jax.ShapeDtypeStruct(dims, BF16)
    full = shape(5, nx, ny, nz)
    with_twin = [(i, i ^ 1) for i in range(count)]
    with_other = [(i, (i + 1) % count if i % 2 else (i - 1) % count) for i in range(count)]
    vm = pltpu.VMEM
    lines = 5 * nx * ny

    flat = jnp.concatenate([state.reshape(lines, nz), cot.reshape(lines, nz)])
    fields = flat.reshape(10, nx, ny, nz)
    near, far = shape(NEAR, nx, nz), shape(FAR, nx, nz)
    near_twin, near_other = call(near_kernel, (near, near), [], 0.2, 1)(flat)
    near_rims = (
        lax.ppermute(near_twin, "gy", with_twin),
        lax.ppermute(near_other, "gy", with_other),
    )
    far_twin, far_other = call(far_kernel, (far, far), [], 0.2, 2, 2)(
        flat, flags.reshape(3 * nx * ny, nz), near_twin, near_other
    )
    *prepared, patches = call(
        prepare_kernel,
        (
            half_shape(20 * ch, COLUMNS),
            half_shape(384, 512),
            half_shape(10 * ch, 192),
            shape(10 * ch, 128),
            half_shape((nx + 2) * 3 * MAIN, nz),
        ),
        [vm((2 * ch, 144), F32)],
        1.5,
        3,
        2,
    )(fields, kernel, heads, near_twin, near_other)
    far_rims = (
        lax.ppermute(far_twin, "gy", with_twin),
        lax.ppermute(far_other, "gy", with_other),
    )
    near_rims, patches = lax.optimization_barrier((near_rims, patches))
    own, parts = call(
        c_kernel,
        (full, shape(ch, 256)),
        [
            vm(((nx + 2) * 3 * RIM, nz), BF16),
            vm((nx * 120, nz), F32),
            vm((RIM * nx, nz), F32),
            vm((16 * nx, nz), F32),
        ],
        3.5,
        9,
    )(fields, *near_rims, kernel, *prepared, patches)

    def exchanged(value, bit):
        return lax.ppermute(value, "gy", [(i, i ^ bit) for i in range(count)])

    bits = [1 << b for b in range(count.bit_length() - 1)]
    sums = parts
    for bit in bits[:-4]:
        sums = sums + exchanged(sums, bit)
    z_half = lambda half, before, order: call(
        functools.partial(z_kernel, half), full, [], 1.9, 3, 1
    )(fields, flags, before, order)
    got = exchanged(sums, bits[-4])
    total = z_half(0, own, sums)
    got, total = lax.optimization_barrier((got, total))
    sums = sums + got
    got = exchanged(sums, bits[-3])
    total = call(
        x_kernel,
        full,
        [
            vm((5, nx + 5, ny, nz), F32),
            vm((5, nx + 1, ny, nz), F32),
            vm((5, nx + 5, ny, nz), F32),
        ],
        2.8,
        3,
        1,
    )(fields, flags, total, sums)
    got, total = lax.optimization_barrier((got, total))
    sums = sums + got
    got = exchanged(sums, bits[-2])
    total = z_half(1, total, sums)
    got, total = lax.optimization_barrier((got, total))
    sums = sums + got
    got = exchanged(sums, bits[-1])
    flow = call(y_kernel, full, [vm((lines, nz), F32)] * 3, 4.5, 8, 1)(
        fields, flat, flags, *near_rims, *far_rims, total, sums
    )
    got, flow = lax.optimization_barrier((got, flow))
    scale = float(cells * count) ** (-0.5)
    k_out, h_out = call(
        functools.partial(sum_kernel, scale), (shape(ch, taps), shape(5, ch)), [], 0.5, 2
    )(sums, got)
    return flow, k_out, h_out


def solution(mesh):
    split_y = P(None, "ens", "gy", None)
    return jax.shard_map(
        body,
        mesh=mesh,
        in_specs=(split_y, split_y, split_y, P(), P()),
        out_specs=(split_y, P("ens", None), P("ens", None)),
        check_vma=False,
    )
```

```python
import functools

import jax
import jax.numpy as jnp
from jax import lax
from jax.experimental import pallas as pl
from jax.experimental.pallas import tpu as pltpu
from jax.sharding import PartitionSpec as P

STEP = 0.3
FLOOR = 0.01
BELOW, ABOVE = 2, 3
SLABS = 2
WIDE = 4
VMEM = 48 * 1024 * 1024
F32 = jnp.float32
BF16 = jnp.bfloat16


def rcp(x):
    return pl.reciprocal(x, approx=True)


def shared_terms(v):
    p = [v[i + 1] - v[i] for i in range(5)]
    d = [p[i + 1] - p[i] for i in range(4)]
    h = [(4.0 / 3.0) * x for x in d]
    k = [h[i] * d[i] + FLOOR for i in range(4)]
    g = [x + x for x in h]
    t = [d[i + 1] - d[i] for i in range(3)]
    return p, d, k, g, t


def side_value(pa, pm, pm2, ka, kb, kc, m0, m2, td, t1, smooth, c0, c2):
    i0 = rcp(ka + pa * m0)
    i1 = rcp(kb + pa * pm)
    i2 = rcp(kc + pm * m2)
    w0 = i0 * i0
    w1 = 6.0 * (i1 * i1)
    w2 = 3.0 * (i2 * i2)
    r = rcp(w0 + w1 + w2)
    o0 = jnp.where(smooth, w0 * r, c0)
    o2 = jnp.where(smooth, w2 * r, c2)
    u = o0 * td + o2 * t1
    return (pa + pm2) - u, (i0, i1, i2, w0, w1, w2, r, o0, o2, u)


def side_pull(mu, pa, pm, m0, m2, td, t1, smooth, saved):
    i0, i1, i2, w0, w1, w2, r, o0, o2, u = saved
    mu2 = mu + mu
    rm = jnp.where(smooth, mu2, 0.0) * r
    s0 = (w0 * i0) * rm * (td - u)
    s1 = (w1 * i1) * rm * u
    s2 = (w2 * i2) * rm * (t1 - u)
    pa_bar = s0 * (m0 + pa) - s1 * pm + mu
    pm_bar = s2 * (m2 + pm) - s1 * pa + mu2
    return s0, s1, s2, pa_bar, pm_bar, o0 * mu2, o2 * mu


def hllc_pull(left, right, normal, flags, cot):
    region = flags & 3
    is_right = region >= 2
    star = ((region + 1) & 2) != 0
    n_at = 1 + normal
    tang = [1 + i for i in range(3) if i != normal]
    rl, rr_, pl_, pr_, nl, nr = left[0], right[0], left[4], right[4], left[n_at], right[n_at]

    def sound(r, p):
        inv = rcp(r)
        t = 1.4 * p * inv
        inv_c = lax.rsqrt(t)
        return inv, inv_c, t * inv_c

    inv_rl, inv_cl, cl = sound(rl, pl_)
    inv_rr, inv_cr, cr = sound(rr_, pr_)
    c = 0.5 * (cl + cr)
    r2 = rl + rr_
    inv = rcp(r2 * c)
    nm = 0.5 * (nl + nr)
    gap = (pl_ - pr_) * inv
    sm = nm + gap
    sc = jnp.where(is_right, c, -c)
    s = nm + sc
    pick = [jnp.where(is_right, right[i], left[i]) for i in range(5)]
    r, un, u1, u2, p = pick[0], pick[n_at], pick[tang[0]], pick[tang[1]], pick[4]
    a = s - un
    dl = sm - un
    si = jnp.where(star, rcp(sc - gap), 0.0)
    j = s * si
    kap = j * dl
    g0, gn, g1, g2, ge = cot[0], cot[n_at], cot[tang[0]], cot[tang[1]], cot[4]
    w = un + kap
    half_q = 0.5 * (un * un + u1 * u1 + u2 * u2)
    enthalpy = 3.5 * p + r * half_q
    b = g0 + u1 * g1 + u2 * g2 + un * gn
    m = r * b + enthalpy * ge
    n = gn + sm * ge
    rkap = r * kap
    f_kap = m + r * a * n
    f_a = rkap * n
    si2 = si * si
    s_bar = f_a - f_kap * (dl * sm * si2)
    sm_bar = f_kap * (s * a * si2) + rkap * a * ge
    wr = w * r
    k_bar = [None] * 5
    k_bar[0] = w * (b + half_q * ge) + kap * a * n
    k_bar[n_at] = m + wr * (gn + un * ge) - f_kap * j - f_a
    k_bar[tang[0]] = wr * (g1 + u1 * ge)
    k_bar[tang[1]] = wr * (g2 + u2 * ge)
    k_bar[4] = 3.5 * (w * ge) + gn
    e = sm_bar * inv
    eg = e * gap
    c_half = 0.5 * (jnp.where(is_right, s_bar, -s_bar) - eg * r2)
    n_half = 0.5 * (s_bar + sm_bar)
    r_both = -(eg * c)
    xl = c_half * inv_rl
    xr = c_half * inv_rr
    base_l = {0: r_both - 0.5 * (xl * cl), n_at: n_half, 4: 0.7 * (xl * inv_cl) + e}
    base_r = {0: r_both - 0.5 * (xr * cr), n_at: n_half, 4: 0.7 * (xr * inv_cr) - e}
    l_bar, r_bar = [], []
    for i in range(5):
        kr = jnp.where(is_right, k_bar[i], 0.0)
        kl = k_bar[i] - kr
        l_bar.append(base_l[i] + kl if i in base_l else kl)
        r_bar.append(base_r[i] + kr if i in base_r else kr)
    return l_bar, r_bar


def face_pull(cells, cot, flags, normal):
    stencil = flags >> 2
    smooth = stencil == 0
    c0 = jnp.where(stencil == 1, 1.0, 0.0)
    c2 = jnp.where(stencil == 3, 1.0, 0.0)
    left, right, kept = [], [], []
    for v in cells:
        p, d, k, g, t = shared_terms(v)
        pm2 = p[2] + p[2]
        args_l = (p[1], p[2], p[1] + d[0], p[2] - d[2], t[0] + t[0], t[1])
        args_r = (p[3], p[2], p[3] - d[3], p[2] + d[1], t[2] + t[2], t[1])
        hl, saved_l = side_value(
            p[1], p[2], pm2, k[0], k[1], k[2], *args_l[2:], smooth, c0, c2
        )
        hr, saved_r = side_value(
            p[3], p[2], pm2, k[3], k[2], k[1], *args_r[2:], smooth, c0, c2
        )
        left.append(v[2] + hl * (1.0 / 6.0))
        right.append(v[3] - hr * (1.0 / 6.0))
        kept.append((p, g, args_l, args_r, saved_l, saved_r))
    l_bar, r_bar = hllc_pull(left, right, normal, flags, cot)
    out = []
    for i in range(5):
        p, g, args_l, args_r, saved_l, saved_r = kept[i]
        a0, a1, a2, pa_l, pm_l, x0, x2 = side_pull(
            l_bar[i] * (1.0 / 6.0), *args_l, smooth, saved_l
        )
        b0, b1, b2, pa_r, pm_r, y0, y2 = side_pull(
            r_bar[i] * (-1.0 / 6.0), *args_r, smooth, saved_r
        )
        d0 = a0 * (g[0] + p[1]) + x0
        d1 = (b2 * (g[1] + p[2]) - a1 * g[1]) + (x2 - x0) + y2
        d2 = (a2 * (g[2] - p[2]) - b1 * g[2]) + (y0 - y2) - x2
        d3 = b0 * (g[3] - p[3]) - y0
        p2 = pa_l + (d0 - d1)
        p3 = pm_l + pm_r + (d1 - d2)
        p4 = pa_r + (d2 - d3)
        out.append([d0, -d0 - p2, l_bar[i] + (p2 - p3), r_bar[i] + (p3 - p4), p4 - d3, d3])
    return out


def conserved_pull(s, g):
    half_q = 0.5 * (s[1] * s[1] + s[2] * s[2] + s[3] * s[3])
    return [
        g[0] + s[1] * g[1] + s[2] * g[2] + s[3] * g[3] + half_q * g[4],
        s[0] * (g[1] + s[1] * g[4]),
        s[0] * (g[2] + s[2] * g[4]),
        s[0] * (g[3] + s[3] * g[4]),
        2.5 * g[4],
    ]


NEAR_STATE, FAR_STATE = 2, 3
NEAR_COT, FAR_COT = 1, 2
FLAG_ROWS = 3
NEAR = 5 * (NEAR_STATE + NEAR_COT)
FAR = 5 * (FAR_STATE + FAR_COT) + FLAG_ROWS


def views(fields):
    n = fields.shape[0] // 2
    return fields.at[pl.ds(0, n)], fields.at[pl.ds(n, n)]


def pack(ref, rows, first, twin, other, at):
    even = is_even()
    nx = twin.shape[1]
    count = ref.shape[0] // (8 * nx)
    for r in rows:
        for v in range(count):
            low = ref[pl.ds(v * nx * 8 + r, nx, stride=8), :].astype(F32)
            top = ref[pl.ds(v * nx * 8 + 7 - r, nx, stride=8), :].astype(F32)
            i = at + (r - first) * count + v
            twin[i] = jnp.where(even, top, low)
            other[i] = jnp.where(even, low, top)


def near_kernel(flat, twin, other):
    s, g = views(flat)
    pack(s, range(NEAR_STATE), 0, twin, other, 0)
    pack(g, range(NEAR_COT), 0, twin, other, 5 * NEAR_STATE)


def far_kernel(flat, flags, order, twin, other):
    del order
    s, g = views(flat)
    n = flags.shape[0] // 3
    pack(s, range(NEAR_STATE, NEAR_STATE + FAR_STATE), NEAR_STATE, twin, other, 0)
    pack(g, range(NEAR_COT, NEAR_COT + FAR_COT), NEAR_COT, twin, other, 5 * FAR_STATE)
    pack(flags.at[pl.ds(n, n)], range(FLAG_ROWS), 0, twin, other, FAR - FLAG_ROWS)


def from_rims(near_twin, near_other, far_twin=None, far_other=None):
    even = is_even()

    def pick(twin, other, i, below):
        if below:
            return jnp.where(even, other[i], twin[i])
        return jnp.where(even, twin[i], other[i])

    def read(row, near, near_at, far_at, v):
        below = row < 0
        r = -1 - row if below else row - 8
        if r < near:
            return pick(near_twin, near_other, near_at + r * 5 + v, below)
        return pick(far_twin, far_other, far_at + (r - near) * 5 + v, below)

    def state(row, v):
        return read(row, NEAR_STATE, 0, 0, v)

    def cot(row, v):
        return read(row, NEAR_COT, 5 * NEAR_STATE, 5 * FAR_STATE, v)

    def flags(row):
        below = row < 0
        r = -1 - row if below else row - 8
        return pick(far_twin, far_other, FAR - FLAG_ROWS + r, below).astype(jnp.int32)

    return state, cot, flags


def x_kernel(fields, flags, order, order2, out, pad, gpad, acc):
    del order, order2
    state, cot = views(fields)
    nx = state.shape[1]
    for v in range(5):
        pad[v, pl.ds(2, nx)] = state[v]
        pad[v, pl.ds(0, 2)] = state[v, pl.ds(nx - 2, 2)]
        pad[v, pl.ds(nx + 2, 3)] = state[v, pl.ds(0, 3)]
        gpad[v, pl.ds(0, nx)] = cot[v]
        gpad[v, pl.ds(nx, 1)] = cot[v, pl.ds(0, 1)]
    acc[...] = jnp.zeros_like(acc)

    def step(i, carry):
        x = i * SLABS
        cells = [[pad[v, pl.ds(x + k, SLABS)] for k in range(6)] for v in range(5)]
        g = [gpad[v, pl.ds(x, SLABS)] for v in range(5)]
        face = [STEP * (gpad[v, pl.ds(x + 1, SLABS)] - g[v]) for v in range(5)]
        terms = face_pull(cells, face, flags[0, pl.ds(x, SLABS)], 0)
        own = conserved_pull([cells[v][2] for v in range(5)], g)
        for v in range(5):
            terms[v][2] = terms[v][2] + own[v]
            for s in range(SLABS + 5):
                total = None
                for k in range(6):
                    if 0 <= s - k < SLABS:
                        part = terms[v][k][s - k]
                        total = part if total is None else total + part
                acc[v, x + s] = acc[v, x + s] + total
        return carry

    lax.fori_loop(0, nx // SLABS, step, 0)
    for v in range(5):
        acc[v, pl.ds(nx, 2)] = acc[v, pl.ds(nx, 2)] + acc[v, pl.ds(0, 2)]
        acc[v, pl.ds(2, 3)] = acc[v, pl.ds(2, 3)] + acc[v, pl.ds(nx + 2, 3)]

    for v in range(5):
        out[v] = acc[v, pl.ds(2, nx)]


def z_kernel(half, fields, flags, before, more, order, out):
    del order
    state, cot = views(fields)
    nx = state.shape[1] // 2
    for v in range(5):
        kept = pl.ds((1 - half) * nx, nx)
        out[v, kept] = before[v, kept]

    def z_step(i, carry):
        x = half * nx + i * SLABS
        cells, face = [], []
        for v in range(5):
            mid = state[v, pl.ds(x, SLABS)]
            cells.append([mid if k == 0 else pltpu.roll(mid, (-k) % 128, 2) for k in range(-2, 4)])
            g = cot[v, pl.ds(x, SLABS)]
            face.append(STEP * (pltpu.roll(g, 127, 2) - g))
        terms = face_pull(cells, face, flags[2, pl.ds(x, SLABS)], 2)
        for v in range(5):
            t = before[v, pl.ds(x, SLABS)] + more[v, pl.ds(x, SLABS)] + terms[v][2]
            for k in (-2, -1, 1, 2, 3):
                t = t + pltpu.roll(terms[v][k + 2], k % 128, 2)
            out[v, pl.ds(x, SLABS)] = t
        return carry

    lax.fori_loop(0, nx // SLABS, z_step, 0)


def e_faces(state, cot, rims, out):
    nx = out.shape[0] // 40
    rim_state, rim_cot, rim_flags = rims

    def own(ref, row, v):
        return ref[pl.ds(v * nx * 8 + row, nx, stride=8), :]

    state_rows, cot_rows = {}, {}
    for v in range(5):
        for row in (*range(-5, 3), *range(6, 13)):
            inside = 0 <= row < 8
            state_rows[row, v] = own(state, row, v) if inside else rim_state(row, v)
        for row in (-3, -2, -1, 0, 8, 9, 10):
            inside = 0 <= row < 8
            cot_rows[row, v] = own(cot, row, v) if inside else rim_cot(row, v)
    sums = {}
    for j in (-3, -2, -1, 8, 9):
        cells = [[state_rows[j + k, v] for k in range(-2, 4)] for v in range(5)]
        face = [STEP * (cot_rows[j + 1, v] - cot_rows[j, v]) for v in range(5)]
        terms = face_pull(cells, face, rim_flags(j), 1)
        for v in range(5):
            for k in range(-2, 4):
                if 0 <= j + k < 8:
                    t = terms[v][k + 2]
                    sums[j + k, v] = sums[j + k, v] + t if (j + k, v) in sums else t
    for v in range(5):
        for row in range(8):
            value = sums[row, v] if (row, v) in sums else jnp.zeros((nx, 128), F32)
            out[pl.ds(v * nx * 8 + row, nx, stride=8), :] = value


def y_kernel(fields, flat, flags, near_twin, near_other, far_twin, far_other, before, order, out, rim, halo, ghalo):
    del order
    state, cot = views(fields)
    rims = from_rims(near_twin, near_other, far_twin, far_other)
    e_faces(*views(flat), rims, rim)
    rim_state, rim_cot, _ = rims
    nx = out.shape[1]
    for v in range(5):
        base = v * nx * 8
        for r in range(ABOVE):
            halo[pl.ds(base + r, nx, stride=8), :] = rim_state(8 + r, v)
        for r in range(BELOW):
            halo[pl.ds(base + 8 - BELOW + r, nx, stride=8), :] = rim_state(r - BELOW, v)
        ghalo[pl.ds(base, nx, stride=8), :] = rim_cot(8, v)
    row = lax.broadcasted_iota(jnp.int32, (SLABS, 8, 128), 1)
    inside = {}
    for k in (-2, -1, 1, 2, 3):
        inside[k] = (row < 8 + k) if k < 0 else (row >= k)

    def step(i, carry):
        x = i * SLABS
        cells, face = [], []
        for v in range(5):
            at = pl.multiple_of((v * nx + x) * 8, 8)
            rim_rows = halo[pl.ds(at, 8 * SLABS), :].reshape(SLABS, 8, 128)
            mid = state[v, pl.ds(x, SLABS)]
            line = []
            for k in range(-2, 4):
                if k == 0:
                    line.append(mid)
                else:
                    line.append(pltpu.roll(jnp.where(inside[k], mid, rim_rows), (-k) % 8, 1))
            cells.append(line)
            g = cot[v, pl.ds(x, SLABS)]
            g_rim = ghalo[pl.ds(at, 8 * SLABS), :].reshape(SLABS, 8, 128)
            face.append(STEP * (pltpu.roll(jnp.where(inside[1], g, g_rim), 7, 1) - g))
        terms = face_pull(cells, face, flags[1, pl.ds(x, SLABS)], 1)
        for v in range(5):
            at = pl.multiple_of((v * nx + x) * 8, 8)
            total = before[v, pl.ds(x, SLABS)] + terms[v][2]
            total = total + rim[pl.ds(at, 8 * SLABS), :].reshape(SLABS, 8, 128)
            for k in (-2, -1, 1, 2, 3):
                moved = pltpu.roll(terms[v][k + 2], k % 8, 1)
                total = total + jnp.where(inside[k], moved, 0.0)
            out[v, pl.ds(x, SLABS)] = total
        return carry

    lax.fori_loop(0, nx // SLABS, step, 0)


def sum_kernel(scale, mine, theirs, k_out, h_out):
    total = (mine[...] + theirs[...]) * scale
    k_out[...] = total[:, : k_out.shape[1]]
    ch = total.shape[0]
    pick = (
        lax.broadcasted_iota(jnp.int32, (8, 128), 1)
        == lax.broadcasted_iota(jnp.int32, (8, 128), 0) + 16
    ).astype(F32)
    heads = lax.dot_general(
        pick,
        total[:, 128:],
        (((1,), (1,)), ((), ())),
        precision=lax.Precision.HIGHEST,
        preferred_element_type=F32,
    )
    h_out[...] = heads[: h_out.shape[0], :ch]


MAIN, RIM = 48, 32
COLUMNS = 9 * (MAIN + RIM)


def split(x):
    hi = x.astype(BF16)
    return hi, (x - hi.astype(F32)).astype(BF16)


def over_lanes(a, b):
    return lax.dot_general(a, b, (((1,), (1,)), ((), ())), preferred_element_type=F32)


def is_even():
    return lax.rem(lax.axis_index("gy"), 2) == 0


def prepare_kernel(fields, kernel, heads, order, order2, w_rows, w_cols, w_head, bias, t, wide):
    del order, order2
    state, _ = views(fields)
    nx = state.shape[1]
    for x in range(nx):
        rows = [state[v, x] - (1.0 if v in (0, 4) else 0.0) for v in range(5)]
        mid = jnp.concatenate([*rows, jnp.zeros((8, 128), F32)], axis=0)
        at = (x + 1) * 3 * MAIN
        t[pl.ds(at, MAIN), :] = pltpu.roll(mid, 1, 1).astype(BF16)
        t[pl.ds(at + MAIN, MAIN), :] = mid.astype(BF16)
        t[pl.ds(at + 2 * MAIN, MAIN), :] = pltpu.roll(mid, 127, 1).astype(BF16)
    t[pl.ds(0, 3 * MAIN), :] = t[pl.ds(nx * 3 * MAIN, 3 * MAIN), :]
    t[pl.ds((nx + 1) * 3 * MAIN, 3 * MAIN), :] = t[pl.ds(3 * MAIN, 3 * MAIN), :]

    ch, taps = kernel.shape
    w = kernel[...]
    hi, lo = split(w)
    wide[...] = jnp.zeros_like(wide)
    wide[pl.ds(0, ch), pl.ds(0, taps)] = hi.astype(F32)
    wide[pl.ds(ch, ch), pl.ds(0, taps)] = lo.astype(F32)
    both = wide[...].astype(BF16)
    kind, tap = columns()
    base = jnp.dot(both, own_taps(kind, tap), preferred_element_type=F32)
    rim = jnp.dot(both, rim_taps(kind, tap), preferred_element_type=F32)
    n = base.shape[1]
    kind = jnp.broadcast_to(kind[0:1], base.shape)
    main = jnp.where(kind < 3, base, 0.0)
    bands = []
    for y in range(8):
        rows = main
        if y == 0:
            rows = jnp.where(kind == 0, 0.0, rows)
        if y == 7:
            rows = jnp.where(kind == 2, 0.0, rows)
        if y != 1:
            rows = pltpu.roll(rows, (y - 1) % n, 1)
        if y == 0:
            rows = rows + jnp.where(kind == 8, base, 0.0)
        if y == 7:
            rows = rows + jnp.where(kind == 10, base, 0.0)
        bands.append(rows)
    bands.append(jnp.where((kind == 0) | (kind == 8) | (kind == 9), rim, 0.0))
    bands.append(jnp.where((kind == 7) | (kind == 10) | (kind == 11), rim, 0.0))
    full = jnp.concatenate([b[:ch] for b in bands] + [b[ch:] for b in bands], axis=0)
    w_rows[...] = full.astype(BF16)
    kept = full.shape[0] // 2
    cols = jnp.concatenate([full[:kept], full[:kept], full[kept:]], axis=0)
    cols = jnp.concatenate([cols, jnp.zeros((512 - 3 * kept, n), F32)], axis=0)
    own_cols = []
    for q in range(3):
        own_cols += [cols[:, (3 * q + o) * MAIN : (3 * q + o) * MAIN + 40] for o in range(3)]
        own_cols.append(jnp.zeros((512, 8), F32))
    w_cols[...] = jnp.concatenate(own_cols, axis=1).T.astype(BF16)
    total = jnp.sum(w * level_taps(w.shape), axis=1, keepdims=True)
    total = jnp.broadcast_to(total, (ch, 128))
    bias[...] = jnp.concatenate([total] * 10, axis=0)

    h_hi, h_lo = split(STEP * heads[...])
    none = jnp.zeros((3, ch), F32)
    pair = jnp.concatenate([h_hi.astype(F32), none, h_lo.astype(F32), none], axis=0).astype(BF16)
    r = lax.broadcasted_iota(jnp.int32, (kept, ch), 0)
    q = lax.broadcasted_iota(jnp.int32, (kept, ch), 1)
    spread = jnp.where((r & (ch - 1)) == q, 1.0, 0.0).astype(BF16)
    picked = over_lanes(pair, spread)
    y_of = lax.broadcasted_iota(jnp.int32, (8, kept), 0)
    col = lax.broadcasted_iota(jnp.int32, (8, kept), 1)
    same = (col >= y_of * ch) & (col < (y_of + 1) * ch)
    split_heads = []
    for at in (0, 8):
        rows = [
            jnp.where(same, jnp.broadcast_to(picked[at + e : at + e + 1], (8, kept)), 0.0)
            for e in range(5)
        ]
        five = picked[at : at + 8]
        rows.append(jnp.where((col >= 8 * ch) & (col < 9 * ch), five, 0.0))
        rows.append(jnp.where(col >= 9 * ch, five, 0.0))
        rows.append(jnp.zeros((8, kept), F32))
        split_heads.append(jnp.concatenate(rows, axis=0))
    three = jnp.concatenate([split_heads[0], split_heads[1], split_heads[0]], axis=0)
    w_head[...] = three.T.astype(BF16)


def c_kernel(
    fields, near_twin, near_other, kernel, w_rows, w_cols, w_head, bias, t,
    own, parts,
    t_rim, acc, edge, gedge,
):
    _, cot = views(fields)
    nx = cot.shape[1]
    ch, taps = kernel.shape
    rim_state, rim_cot, _ = from_rims(near_twin, near_other)

    for v in range(5):
        level = 1.0 if v in (0, 4) else 0.0
        for q, row in enumerate((-1, -2, 8, 9)):
            edge[pl.ds(5 * q + v, nx, stride=RIM), :] = rim_state(row, v) - level
        gedge[pl.ds(v, nx, stride=16), :] = rim_cot(-1, v)
        gedge[pl.ds(8 + v, nx, stride=16), :] = rim_cot(8, v)
    none = jnp.zeros((nx, 128), F32)
    for q in range(20, RIM):
        edge[pl.ds(q, nx, stride=RIM), :] = none
    for q in (5, 6, 7):
        gedge[pl.ds(q, nx, stride=16), :] = none
        gedge[pl.ds(8 + q, nx, stride=16), :] = none
    for x in range(nx):
        mid = edge[pl.ds(x * RIM, RIM), :]
        at = (x + 1) * 3 * RIM
        t_rim[pl.ds(at, RIM), :] = pltpu.roll(mid, 1, 1).astype(BF16)
        t_rim[pl.ds(at + RIM, RIM), :] = mid.astype(BF16)
        t_rim[pl.ds(at + 2 * RIM, RIM), :] = pltpu.roll(mid, 127, 1).astype(BF16)
    t_rim[pl.ds(0, 3 * RIM), :] = t_rim[pl.ds(nx * 3 * RIM, 3 * RIM), :]
    t_rim[pl.ds((nx + 1) * 3 * RIM, 3 * RIM), :] = t_rim[pl.ds(3 * RIM, 3 * RIM), :]

    kept = 8 * ch
    kg = hg = dsum = None
    zeros8 = jnp.zeros((8, 128 * WIDE), F32)
    written = set()
    for x in range(0, nx, WIDE):
        s = jnp.concatenate(
            [
                jnp.concatenate(
                    [
                        t[pl.ds((x + j) * 3 * MAIN, 9 * MAIN), :],
                        t_rim[pl.ds((x + j) * 3 * RIM, 9 * RIM), :],
                    ],
                    axis=0,
                )
                for j in range(WIDE)
            ],
            axis=1,
        )
        z2 = jnp.dot(w_rows[...], s, preferred_element_type=F32)
        rows = z2.shape[0] // 2
        z = z2[:rows] + z2[rows:] + jnp.concatenate([bias[...]] * WIDE, axis=1)
        hidden = jnp.tanh(z)
        g = jnp.concatenate(
            [
                jnp.concatenate(
                    [cot[v, x + j] for v in range(5)] + [gedge[pl.ds((x + j) * 16, 16), :]], axis=0
                )
                for j in range(WIDE)
            ],
            axis=1,
        )
        g_hi, g_lo = split(g)
        g_hi32, g_lo32 = g_hi.astype(F32), g_lo.astype(F32)
        g3 = jnp.concatenate(
            [g_hi32, zeros8, g_hi32, zeros8, g_lo32, zeros8], axis=0
        ).astype(BF16)
        d = (1.0 - hidden * hidden) * jnp.dot(w_head[...], g3, preferred_element_type=F32)
        d_hi, d_lo = split(d)
        zeros = jnp.zeros((512 - 3 * rows, 128 * WIDE), BF16)
        back = jnp.dot(
            w_cols[...],
            jnp.concatenate([d_hi, d_lo, d_hi, zeros], axis=0),
            preferred_element_type=F32,
        )
        k2 = over_lanes(s, jnp.concatenate([d_hi[:kept], d_lo[:kept]], axis=0))
        k2 = k2[:, :kept] + k2[:, kept:]
        kg = k2 if kg is None else kg + k2
        hid2 = jnp.concatenate(split(hidden[:kept]), axis=0)
        g2 = jnp.concatenate([g_hi32[:40], g_lo32[:40]], axis=0).astype(BF16)
        h2 = over_lanes(g2, hid2)
        hg = h2 if hg is None else hg + h2
        for j in range(WIDE):
            level = d[:kept, 128 * j : 128 * (j + 1)]
            dsum = level if dsum is None else dsum + level
        for m in range(WIDE + 2):
            total = None
            for j in range(WIDE):
                if 0 <= m - j < 3:
                    q = m - j
                    piece = back[q * 128 : q * 128 + 120, 128 * j : 128 * (j + 1)]
                    total = piece if total is None else total + piece
            here = (x + m - 1) % nx
            if here in written:
                total = total + acc[pl.ds(here * 120, 120), :]
            written.add(here)
            acc[pl.ds(here * 120, 120), :] = total
    for x in range(nx):
        at = x * 120
        total = (
            acc[pl.ds(at + 40, 40), :]
            + pltpu.roll(acc[pl.ds(at, 40), :], 127, 1)
            + pltpu.roll(acc[pl.ds(at + 80, 40), :], 1, 1)
        )
        for v in range(5):
            own[v, x] = total[8 * v : 8 * v + 8]

    sums = jnp.sum(dsum, axis=1, keepdims=True)
    kg = kg.T
    hg = (hg[:40, :kept] + hg[40:, :kept]) + (hg[:40, kept:] + hg[40:, kept:])
    y_row = lax.broadcasted_iota(jnp.int32, (40, kept), 0) & 7
    y_col = lax.broadcasted_iota(jnp.int32, (40, kept), 1)
    same_y = (y_col >= y_row * ch) & (y_col < (y_row + 1) * ch)
    hg = jnp.where(same_y, hg, 0.0)
    by_eq = jnp.concatenate(
        [jnp.sum(hg[8 * e : 8 * e + 8], axis=0, keepdims=True) for e in range(5)]
        + [jnp.zeros((123, kept), F32)],
        axis=0,
    ).T
    level_sum = jnp.zeros((ch, 1), F32)
    head_sum = jnp.zeros((ch, 128), F32)
    n = kg.shape[1]
    columns_at, tap = columns()
    kind = jnp.broadcast_to(columns_at[0:1], (ch, n))
    total = jnp.zeros((ch, n), F32)
    for y in range(8):
        rows = kg[y * ch : (y + 1) * ch]
        moved = rows if y == 1 else pltpu.roll(rows, (1 - y) % n, 1)
        keep = kind < 3
        if y == 0:
            keep = (kind == 1) | (kind == 2)
            total = total + jnp.where(kind == 8, rows, 0.0)
        if y == 7:
            keep = kind < 2
            total = total + jnp.where(kind == 10, rows, 0.0)
        total = total + jnp.where(keep, moved, 0.0)
        level_sum = level_sum + sums[y * ch : (y + 1) * ch]
        head_sum = head_sum + by_eq[y * ch : (y + 1) * ch]
    grads = over_lanes(jnp.concatenate(split(total), axis=0), own_taps(columns_at, tap))
    n_pick = grads.shape[1]
    parts[...] = jnp.zeros_like(parts)
    parts[:, pl.ds(0, n_pick)] = grads[:ch] + grads[ch:]
    parts[:, pl.ds(0, taps)] = parts[:, pl.ds(0, taps)] + level_sum * level_taps((ch, taps))
    parts[:, pl.ds(128, 128)] = parts[:, pl.ds(128, 128)] + pltpu.roll(head_sum * STEP, 16, 1)


def columns():
    lane = lax.broadcasted_iota(jnp.int32, (8, COLUMNS), 1)
    main = lane < 9 * MAIN
    past = lane - 9 * MAIN
    block = sum((lane >= MAIN * i).astype(jnp.int32) for i in range(1, 9))
    o = jnp.where(main, block, past >> 5)
    r = jnp.where(main, lane - MAIN * block, past & (RIM - 1))
    which = sum((r >= 5 * i).astype(jnp.int32) for i in (1, 2, 3, 4))
    kind = jnp.where(main, jnp.where(r < 40, r & 7, 12), 8 + which)
    v = jnp.where(main, r >> 3, r - 5 * which)
    return kind, o * 5 + v


def taps_of(columns_at):
    n = columns_at.shape[1]
    row = lax.broadcasted_iota(jnp.int32, (144, n), 0)
    return jnp.where(row == jnp.broadcast_to(columns_at[0:1], (144, n)), 1.0, 0.0).astype(BF16)


def own_taps(kind, tap):
    at = jnp.where(kind < 3, tap + 45 * kind, 1000)
    at = jnp.where(kind == 8, tap, at)
    return taps_of(jnp.where(kind == 10, tap + 90, at))


def rim_taps(kind, tap):
    first = (kind == 9) | (kind == 7)
    middle = (kind == 8) | (kind == 10)
    last = (kind == 0) | (kind == 11)
    at = jnp.where(first, tap, jnp.where(middle, tap + 45, 1000))
    return taps_of(jnp.where(last, tap + 90, at))


def level_taps(shape):
    t = lax.broadcasted_iota(jnp.int32, shape, 1).astype(F32)
    v = t - 5.0 * jnp.floor((t + 0.5) * 0.2)
    return jnp.where((v < 0.5) | (v > 3.5), 1.0, 0.0)


def call(kernel, outs, scratch, us, n_in, order=0):
    spec = pl.BlockSpec(memory_space=pltpu.VMEM)
    return pl.pallas_call(
        kernel,
        out_shape=outs,
        in_specs=[spec] * n_in + [pl.BlockSpec(memory_space=pl.ANY)] * order,
        scratch_shapes=scratch,
        compiler_params=pltpu.CompilerParams(vmem_limit_bytes=VMEM),
        cost_estimate=pl.CostEstimate(
            flops=int(us * 1.15e9), bytes_accessed=int(us * 3.69e6), transcendentals=0
        ),
    )


def body(state, cot, flags, kernel, heads):
    _, nx, ny, nz = state.shape
    ch, taps = kernel.shape
    count = lax.axis_size("gy")
    cells = nx * ny * nz
    shape = lambda *dims: jax.ShapeDtypeStruct(dims, F32)
    half_shape = lambda *dims: jax.ShapeDtypeStruct(dims, BF16)
    full = shape(5, nx, ny, nz)
    with_twin = [(i, i ^ 1) for i in range(count)]
    with_other = [(i, (i + 1) % count if i % 2 else (i - 1) % count) for i in range(count)]
    vm = pltpu.VMEM
    lines = 5 * nx * ny

    flat = jnp.concatenate([state.reshape(lines, nz), cot.reshape(lines, nz)])
    fields = flat.reshape(10, nx, ny, nz)
    near, far = shape(NEAR, nx, nz), shape(FAR, nx, nz)
    near_twin, near_other = call(near_kernel, (near, near), [], 0.2, 1)(flat)
    near_rims = (
        lax.ppermute(near_twin, "gy", with_twin),
        lax.ppermute(near_other, "gy", with_other),
    )
    *prepared, patches = call(
        prepare_kernel,
        (
            half_shape(20 * ch, COLUMNS),
            half_shape(384, 512),
            half_shape(10 * ch, 192),
            shape(10 * ch, 128),
            half_shape((nx + 2) * 3 * MAIN, nz),
        ),
        [vm((2 * ch, 144), F32)],
        1.5,
        3,
        2,
    )(fields, kernel, heads, near_twin, near_other)
    first = call(
        x_kernel,
        full,
        [
            vm((5, nx + 5, ny, nz), F32),
            vm((5, nx + 1, ny, nz), F32),
            vm((5, nx + 5, ny, nz), F32),
        ],
        2.8,
        2,
        2,
    )(fields, flags, near_twin, near_other)
    near_rims, patches, first = lax.optimization_barrier((near_rims, patches, first))
    own, parts = call(
        c_kernel,
        (full, shape(ch, 256)),
        [
            vm(((nx + 2) * 3 * RIM, nz), BF16),
            vm((nx * 120, nz), F32),
            vm((RIM * nx, nz), F32),
            vm((16 * nx, nz), F32),
        ],
        3.5,
        9,
    )(fields, *near_rims, kernel, *prepared, patches)

    def exchanged(value, bit):
        return lax.ppermute(value, "gy", [(i, i ^ bit) for i in range(count)])

    bits = [1 << b for b in range(count.bit_length() - 1)]
    sums = parts
    for bit in bits[:-4]:
        sums = sums + exchanged(sums, bit)
    z_half = lambda half, before, order: call(
        functools.partial(z_kernel, half), full, [], 1.9, 4, 1
    )(fields, flags, before, first, order)
    got = exchanged(sums, bits[-4])
    far_twin, far_other = call(far_kernel, (far, far), [], 0.2, 2, 1)(
        flat, flags.reshape(3 * nx * ny, nz), parts
    )
    far_rims = (
        lax.ppermute(far_twin, "gy", with_twin),
        lax.ppermute(far_other, "gy", with_other),
    )
    sums = sums + got
    got = exchanged(sums, bits[-3])
    total = z_half(0, own, sums)
    got, total = lax.optimization_barrier((got, total))
    sums = sums + got
    got = exchanged(sums, bits[-2])
    total = z_half(1, total, sums)
    got, total = lax.optimization_barrier((got, total))
    sums = sums + got
    got = exchanged(sums, bits[-1])
    flow = call(y_kernel, full, [vm((lines, nz), F32)] * 3, 4.5, 8, 1)(
        fields, flat, flags, *near_rims, *far_rims, total, sums
    )
    got, flow = lax.optimization_barrier((got, flow))
    scale = float(cells * count) ** (-0.5)
    k_out, h_out = call(
        functools.partial(sum_kernel, scale), (shape(ch, taps), shape(5, ch)), [], 0.5, 2
    )(sums, got)
    return flow, k_out, h_out


def solution(mesh):
    split_y = P(None, "ens", "gy", None)
    return jax.shard_map(
        body,
        mesh=mesh,
        in_specs=(split_y, split_y, split_y, P(), P()),
        out_specs=(split_y, P("ens", None), P("ens", None)),
        check_vma=False,
    )
```

```python
import functools

import jax
import jax.numpy as jnp
from jax import lax
from jax.experimental import pallas as pl
from jax.experimental.pallas import tpu as pltpu
from jax.sharding import PartitionSpec as P

STEP = 0.3
FLOOR = 0.01
BELOW, ABOVE = 2, 3
SLABS = 2
WIDE = 4
VMEM = 48 * 1024 * 1024
F32 = jnp.float32
BF16 = jnp.bfloat16


def rcp(x):
    return pl.reciprocal(x, approx=True)


def shared_terms(v):
    p = [v[i + 1] - v[i] for i in range(5)]
    d = [p[i + 1] - p[i] for i in range(4)]
    h = [(4.0 / 3.0) * x for x in d]
    k = [h[i] * d[i] + FLOOR for i in range(4)]
    g = [x + x for x in h]
    t = [d[i + 1] - d[i] for i in range(3)]
    return p, d, k, g, t


def side_value(pa, pm, pm2, ka, kb, kc, m0, m2, td, t1, smooth, c0, c2):
    i0 = rcp(ka + pa * m0)
    i1 = rcp(kb + pa * pm)
    i2 = rcp(kc + pm * m2)
    w0 = i0 * i0
    w1 = 6.0 * (i1 * i1)
    w2 = 3.0 * (i2 * i2)
    r = rcp(w0 + w1 + w2)
    o0 = jnp.where(smooth, w0 * r, c0)
    o2 = jnp.where(smooth, w2 * r, c2)
    u = o0 * td + o2 * t1
    return (pa + pm2) - u, (i0, i1, i2, w0, w1, w2, r, o0, o2, u)


def side_pull(mu, pa, pm, m0, m2, td, t1, smooth, saved):
    i0, i1, i2, w0, w1, w2, r, o0, o2, u = saved
    mu2 = mu + mu
    rm = jnp.where(smooth, mu2, 0.0) * r
    s0 = (w0 * i0) * rm * (td - u)
    s1 = (w1 * i1) * rm * u
    s2 = (w2 * i2) * rm * (t1 - u)
    pa_bar = s0 * (m0 + pa) - s1 * pm + mu
    pm_bar = s2 * (m2 + pm) - s1 * pa + mu2
    return s0, s1, s2, pa_bar, pm_bar, o0 * mu2, o2 * mu


def hllc_pull(left, right, normal, flags, cot):
    region = flags & 3
    is_right = region >= 2
    star = ((region + 1) & 2) != 0
    n_at = 1 + normal
    tang = [1 + i for i in range(3) if i != normal]
    rl, rr_, pl_, pr_, nl, nr = left[0], right[0], left[4], right[4], left[n_at], right[n_at]

    def sound(r, p):
        inv = rcp(r)
        t = 1.4 * p * inv
        inv_c = lax.rsqrt(t)
        return inv, inv_c, t * inv_c

    inv_rl, inv_cl, cl = sound(rl, pl_)
    inv_rr, inv_cr, cr = sound(rr_, pr_)
    c = 0.5 * (cl + cr)
    r2 = rl + rr_
    inv = rcp(r2 * c)
    nm = 0.5 * (nl + nr)
    gap = (pl_ - pr_) * inv
    sm = nm + gap
    sc = jnp.where(is_right, c, -c)
    s = nm + sc
    pick = [jnp.where(is_right, right[i], left[i]) for i in range(5)]
    r, un, u1, u2, p = pick[0], pick[n_at], pick[tang[0]], pick[tang[1]], pick[4]
    a = s - un
    dl = sm - un
    si = jnp.where(star, rcp(sc - gap), 0.0)
    j = s * si
    kap = j * dl
    g0, gn, g1, g2, ge = cot[0], cot[n_at], cot[tang[0]], cot[tang[1]], cot[4]
    w = un + kap
    half_q = 0.5 * (un * un + u1 * u1 + u2 * u2)
    enthalpy = 3.5 * p + r * half_q
    b = g0 + u1 * g1 + u2 * g2 + un * gn
    m = r * b + enthalpy * ge
    n = gn + sm * ge
    rkap = r * kap
    f_kap = m + r * a * n
    f_a = rkap * n
    si2 = si * si
    s_bar = f_a - f_kap * (dl * sm * si2)
    sm_bar = f_kap * (s * a * si2) + rkap * a * ge
    wr = w * r
    k_bar = [None] * 5
    k_bar[0] = w * (b + half_q * ge) + kap * a * n
    k_bar[n_at] = m + wr * (gn + un * ge) - f_kap * j - f_a
    k_bar[tang[0]] = wr * (g1 + u1 * ge)
    k_bar[tang[1]] = wr * (g2 + u2 * ge)
    k_bar[4] = 3.5 * (w * ge) + gn
    e = sm_bar * inv
    eg = e * gap
    c_half = 0.5 * (jnp.where(is_right, s_bar, -s_bar) - eg * r2)
    n_half = 0.5 * (s_bar + sm_bar)
    r_both = -(eg * c)
    xl = c_half * inv_rl
    xr = c_half * inv_rr
    base_l = {0: r_both - 0.5 * (xl * cl), n_at: n_half, 4: 0.7 * (xl * inv_cl) + e}
    base_r = {0: r_both - 0.5 * (xr * cr), n_at: n_half, 4: 0.7 * (xr * inv_cr) - e}
    l_bar, r_bar = [], []
    for i in range(5):
        kr = jnp.where(is_right, k_bar[i], 0.0)
        kl = k_bar[i] - kr
        l_bar.append(base_l[i] + kl if i in base_l else kl)
        r_bar.append(base_r[i] + kr if i in base_r else kr)
    return l_bar, r_bar


def face_pull(cells, cot, flags, normal):
    stencil = flags >> 2
    smooth = stencil == 0
    c0 = jnp.where(stencil == 1, 1.0, 0.0)
    c2 = jnp.where(stencil == 3, 1.0, 0.0)
    left, right, kept = [], [], []
    for v in cells:
        p, d, k, g, t = shared_terms(v)
        pm2 = p[2] + p[2]
        args_l = (p[1], p[2], p[1] + d[0], p[2] - d[2], t[0] + t[0], t[1])
        args_r = (p[3], p[2], p[3] - d[3], p[2] + d[1], t[2] + t[2], t[1])
        hl, saved_l = side_value(
            p[1], p[2], pm2, k[0], k[1], k[2], *args_l[2:], smooth, c0, c2
        )
        hr, saved_r = side_value(
            p[3], p[2], pm2, k[3], k[2], k[1], *args_r[2:], smooth, c0, c2
        )
        left.append(v[2] + hl * (1.0 / 6.0))
        right.append(v[3] - hr * (1.0 / 6.0))
        kept.append((p, g, args_l, args_r, saved_l, saved_r))
    l_bar, r_bar = hllc_pull(left, right, normal, flags, cot)
    out = []
    for i in range(5):
        p, g, args_l, args_r, saved_l, saved_r = kept[i]
        a0, a1, a2, pa_l, pm_l, x0, x2 = side_pull(
            l_bar[i] * (1.0 / 6.0), *args_l, smooth, saved_l
        )
        b0, b1, b2, pa_r, pm_r, y0, y2 = side_pull(
            r_bar[i] * (-1.0 / 6.0), *args_r, smooth, saved_r
        )
        d0 = a0 * (g[0] + p[1]) + x0
        d1 = (b2 * (g[1] + p[2]) - a1 * g[1]) + (x2 - x0) + y2
        d2 = (a2 * (g[2] - p[2]) - b1 * g[2]) + (y0 - y2) - x2
        d3 = b0 * (g[3] - p[3]) - y0
        p2 = pa_l + (d0 - d1)
        p3 = pm_l + pm_r + (d1 - d2)
        p4 = pa_r + (d2 - d3)
        out.append([d0, -d0 - p2, l_bar[i] + (p2 - p3), r_bar[i] + (p3 - p4), p4 - d3, d3])
    return out


def conserved_pull(s, g):
    half_q = 0.5 * (s[1] * s[1] + s[2] * s[2] + s[3] * s[3])
    return [
        g[0] + s[1] * g[1] + s[2] * g[2] + s[3] * g[3] + half_q * g[4],
        s[0] * (g[1] + s[1] * g[4]),
        s[0] * (g[2] + s[2] * g[4]),
        s[0] * (g[3] + s[3] * g[4]),
        2.5 * g[4],
    ]


NEAR_STATE, FAR_STATE = 2, 3
NEAR_COT, FAR_COT = 1, 2
FLAG_ROWS = 3
NEAR = 5 * (NEAR_STATE + NEAR_COT)
FAR = 5 * (FAR_STATE + FAR_COT) + FLAG_ROWS


def views(fields):
    n = fields.shape[0] // 2
    return fields.at[pl.ds(0, n)], fields.at[pl.ds(n, n)]


def pack(ref, rows, first, twin, other, at):
    even = is_even()
    nx = twin.shape[1]
    count = ref.shape[0] // (8 * nx)
    for r in rows:
        for v in range(count):
            low = ref[pl.ds(v * nx * 8 + r, nx, stride=8), :].astype(F32)
            top = ref[pl.ds(v * nx * 8 + 7 - r, nx, stride=8), :].astype(F32)
            i = at + (r - first) * count + v
            twin[i] = jnp.where(even, top, low)
            other[i] = jnp.where(even, low, top)


def near_kernel(flat, twin, other):
    s, g = views(flat)
    pack(s, range(NEAR_STATE), 0, twin, other, 0)
    pack(g, range(NEAR_COT), 0, twin, other, 5 * NEAR_STATE)


def far_kernel(flat, flags, order, twin, other):
    del order
    s, g = views(flat)
    n = flags.shape[0] // 3
    pack(s, range(NEAR_STATE, NEAR_STATE + FAR_STATE), NEAR_STATE, twin, other, 0)
    pack(g, range(NEAR_COT, NEAR_COT + FAR_COT), NEAR_COT, twin, other, 5 * FAR_STATE)
    pack(flags.at[pl.ds(n, n)], range(FLAG_ROWS), 0, twin, other, FAR - FLAG_ROWS)


def from_rims(near_twin, near_other, far_twin=None, far_other=None):
    even = is_even()

    def pick(twin, other, i, below):
        if below:
            return jnp.where(even, other[i], twin[i])
        return jnp.where(even, twin[i], other[i])

    def read(row, near, near_at, far_at, v):
        below = row < 0
        r = -1 - row if below else row - 8
        if r < near:
            return pick(near_twin, near_other, near_at + r * 5 + v, below)
        return pick(far_twin, far_other, far_at + (r - near) * 5 + v, below)

    def state(row, v):
        return read(row, NEAR_STATE, 0, 0, v)

    def cot(row, v):
        return read(row, NEAR_COT, 5 * NEAR_STATE, 5 * FAR_STATE, v)

    def flags(row):
        below = row < 0
        r = -1 - row if below else row - 8
        return pick(far_twin, far_other, FAR - FLAG_ROWS + r, below).astype(jnp.int32)

    return state, cot, flags


def x_kernel(fields, flags, order, order2, out, pad, gpad, acc):
    del order, order2
    state, cot = views(fields)
    nx = state.shape[1]
    for v in range(5):
        pad[v, pl.ds(2, nx)] = state[v]
        pad[v, pl.ds(0, 2)] = state[v, pl.ds(nx - 2, 2)]
        pad[v, pl.ds(nx + 2, 3)] = state[v, pl.ds(0, 3)]
        gpad[v, pl.ds(0, nx)] = cot[v]
        gpad[v, pl.ds(nx, 1)] = cot[v, pl.ds(0, 1)]
    acc[...] = jnp.zeros_like(acc)

    def step(i, carry):
        x = i * SLABS
        cells = [[pad[v, pl.ds(x + k, SLABS)] for k in range(6)] for v in range(5)]
        g = [gpad[v, pl.ds(x, SLABS)] for v in range(5)]
        face = [STEP * (gpad[v, pl.ds(x + 1, SLABS)] - g[v]) for v in range(5)]
        terms = face_pull(cells, face, flags[0, pl.ds(x, SLABS)], 0)
        own = conserved_pull([cells[v][2] for v in range(5)], g)
        for v in range(5):
            terms[v][2] = terms[v][2] + own[v]
            for s in range(SLABS + 5):
                total = None
                for k in range(6):
                    if 0 <= s - k < SLABS:
                        part = terms[v][k][s - k]
                        total = part if total is None else total + part
                acc[v, x + s] = acc[v, x + s] + total
        return carry

    lax.fori_loop(0, nx // SLABS, step, 0)
    for v in range(5):
        acc[v, pl.ds(nx, 2)] = acc[v, pl.ds(nx, 2)] + acc[v, pl.ds(0, 2)]
        acc[v, pl.ds(2, 3)] = acc[v, pl.ds(2, 3)] + acc[v, pl.ds(nx + 2, 3)]

    for v in range(5):
        out[v] = acc[v, pl.ds(2, nx)]


def z_kernel(half, fields, flags, before, more, order, out):
    del order
    state, cot = views(fields)
    nx = state.shape[1] // 2
    for v in range(5):
        kept = pl.ds((1 - half) * nx, nx)
        out[v, kept] = before[v, kept]

    def z_step(i, carry):
        x = half * nx + i * SLABS
        cells, face = [], []
        for v in range(5):
            mid = state[v, pl.ds(x, SLABS)]
            cells.append([mid if k == 0 else pltpu.roll(mid, (-k) % 128, 2) for k in range(-2, 4)])
            g = cot[v, pl.ds(x, SLABS)]
            face.append(STEP * (pltpu.roll(g, 127, 2) - g))
        terms = face_pull(cells, face, flags[2, pl.ds(x, SLABS)], 2)
        for v in range(5):
            t = before[v, pl.ds(x, SLABS)] + more[v, pl.ds(x, SLABS)] + terms[v][2]
            for k in (-2, -1, 1, 2, 3):
                t = t + pltpu.roll(terms[v][k + 2], k % 128, 2)
            out[v, pl.ds(x, SLABS)] = t
        return carry

    lax.fori_loop(0, nx // SLABS, z_step, 0)


def e_kernel(flat, near_twin, near_other, far_twin, far_other, order, out):
    del order
    state, cot = views(flat)
    nx = out.shape[0] // 40
    rim_state, rim_cot, rim_flags = from_rims(near_twin, near_other, far_twin, far_other)

    def own(ref, row, v):
        return ref[pl.ds(v * nx * 8 + row, nx, stride=8), :]

    state_rows, cot_rows = {}, {}
    for v in range(5):
        for row in (*range(-5, 3), *range(6, 13)):
            inside = 0 <= row < 8
            state_rows[row, v] = own(state, row, v) if inside else rim_state(row, v)
        for row in (-3, -2, -1, 0, 8, 9, 10):
            inside = 0 <= row < 8
            cot_rows[row, v] = own(cot, row, v) if inside else rim_cot(row, v)
    sums = {}
    for j in (-3, -2, -1, 8, 9):
        cells = [[state_rows[j + k, v] for k in range(-2, 4)] for v in range(5)]
        face = [STEP * (cot_rows[j + 1, v] - cot_rows[j, v]) for v in range(5)]
        terms = face_pull(cells, face, rim_flags(j), 1)
        for v in range(5):
            for k in range(-2, 4):
                if 0 <= j + k < 8:
                    t = terms[v][k + 2]
                    sums[j + k, v] = sums[j + k, v] + t if (j + k, v) in sums else t
    for v in range(5):
        for row in range(8):
            value = sums[row, v] if (row, v) in sums else jnp.zeros((nx, 128), F32)
            out[pl.ds(v * nx * 8 + row, nx, stride=8), :] = value


def y_kernel(fields, flags, near_twin, near_other, far_twin, far_other, before, rim, order, out, halo, ghalo):
    del order
    state, cot = views(fields)
    rims = from_rims(near_twin, near_other, far_twin, far_other)
    rim_state, rim_cot, _ = rims
    nx = out.shape[1]
    for v in range(5):
        base = v * nx * 8
        for r in range(ABOVE):
            halo[pl.ds(base + r, nx, stride=8), :] = rim_state(8 + r, v)
        for r in range(BELOW):
            halo[pl.ds(base + 8 - BELOW + r, nx, stride=8), :] = rim_state(r - BELOW, v)
        ghalo[pl.ds(base, nx, stride=8), :] = rim_cot(8, v)
    row = lax.broadcasted_iota(jnp.int32, (SLABS, 8, 128), 1)
    inside = {}
    for k in (-2, -1, 1, 2, 3):
        inside[k] = (row < 8 + k) if k < 0 else (row >= k)

    def step(i, carry):
        x = i * SLABS
        cells, face = [], []
        for v in range(5):
            at = pl.multiple_of((v * nx + x) * 8, 8)
            rim_rows = halo[pl.ds(at, 8 * SLABS), :].reshape(SLABS, 8, 128)
            mid = state[v, pl.ds(x, SLABS)]
            line = []
            for k in range(-2, 4):
                if k == 0:
                    line.append(mid)
                else:
                    line.append(pltpu.roll(jnp.where(inside[k], mid, rim_rows), (-k) % 8, 1))
            cells.append(line)
            g = cot[v, pl.ds(x, SLABS)]
            g_rim = ghalo[pl.ds(at, 8 * SLABS), :].reshape(SLABS, 8, 128)
            face.append(STEP * (pltpu.roll(jnp.where(inside[1], g, g_rim), 7, 1) - g))
        terms = face_pull(cells, face, flags[1, pl.ds(x, SLABS)], 1)
        for v in range(5):
            at = pl.multiple_of((v * nx + x) * 8, 8)
            total = before[v, pl.ds(x, SLABS)] + terms[v][2]
            total = total + rim[pl.ds(at, 8 * SLABS), :].reshape(SLABS, 8, 128)
            for k in (-2, -1, 1, 2, 3):
                moved = pltpu.roll(terms[v][k + 2], k % 8, 1)
                total = total + jnp.where(inside[k], moved, 0.0)
            out[v, pl.ds(x, SLABS)] = total
        return carry

    lax.fori_loop(0, nx // SLABS, step, 0)


def sum_kernel(scale, mine, theirs, k_out, h_out):
    total = (mine[...] + theirs[...]) * scale
    k_out[...] = total[:, : k_out.shape[1]]
    ch = total.shape[0]
    pick = (
        lax.broadcasted_iota(jnp.int32, (8, 128), 1)
        == lax.broadcasted_iota(jnp.int32, (8, 128), 0) + 16
    ).astype(F32)
    heads = lax.dot_general(
        pick,
        total[:, 128:],
        (((1,), (1,)), ((), ())),
        precision=lax.Precision.HIGHEST,
        preferred_element_type=F32,
    )
    h_out[...] = heads[: h_out.shape[0], :ch]


MAIN, RIM = 48, 32
COLUMNS = 9 * (MAIN + RIM)


def split(x):
    hi = x.astype(BF16)
    return hi, (x - hi.astype(F32)).astype(BF16)


def over_lanes(a, b):
    return lax.dot_general(a, b, (((1,), (1,)), ((), ())), preferred_element_type=F32)


def is_even():
    return lax.rem(lax.axis_index("gy"), 2) == 0


def prepare_kernel(fields, kernel, heads, order, order2, w_rows, w_cols, w_head, bias, t, wide):
    del order, order2
    state, _ = views(fields)
    nx = state.shape[1]
    for x in range(nx):
        rows = [state[v, x] - (1.0 if v in (0, 4) else 0.0) for v in range(5)]
        mid = jnp.concatenate([*rows, jnp.zeros((8, 128), F32)], axis=0)
        at = (x + 1) * 3 * MAIN
        t[pl.ds(at, MAIN), :] = pltpu.roll(mid, 1, 1).astype(BF16)
        t[pl.ds(at + MAIN, MAIN), :] = mid.astype(BF16)
        t[pl.ds(at + 2 * MAIN, MAIN), :] = pltpu.roll(mid, 127, 1).astype(BF16)
    t[pl.ds(0, 3 * MAIN), :] = t[pl.ds(nx * 3 * MAIN, 3 * MAIN), :]
    t[pl.ds((nx + 1) * 3 * MAIN, 3 * MAIN), :] = t[pl.ds(3 * MAIN, 3 * MAIN), :]

    ch, taps = kernel.shape
    w = kernel[...]
    hi, lo = split(w)
    wide[...] = jnp.zeros_like(wide)
    wide[pl.ds(0, ch), pl.ds(0, taps)] = hi.astype(F32)
    wide[pl.ds(ch, ch), pl.ds(0, taps)] = lo.astype(F32)
    both = wide[...].astype(BF16)
    kind, tap = columns()
    base = jnp.dot(both, own_taps(kind, tap), preferred_element_type=F32)
    rim = jnp.dot(both, rim_taps(kind, tap), preferred_element_type=F32)
    n = base.shape[1]
    kind = jnp.broadcast_to(kind[0:1], base.shape)
    main = jnp.where(kind < 3, base, 0.0)
    bands = []
    for y in range(8):
        rows = main
        if y == 0:
            rows = jnp.where(kind == 0, 0.0, rows)
        if y == 7:
            rows = jnp.where(kind == 2, 0.0, rows)
        if y != 1:
            rows = pltpu.roll(rows, (y - 1) % n, 1)
        if y == 0:
            rows = rows + jnp.where(kind == 8, base, 0.0)
        if y == 7:
            rows = rows + jnp.where(kind == 10, base, 0.0)
        bands.append(rows)
    bands.append(jnp.where((kind == 0) | (kind == 8) | (kind == 9), rim, 0.0))
    bands.append(jnp.where((kind == 7) | (kind == 10) | (kind == 11), rim, 0.0))
    full = jnp.concatenate([b[:ch] for b in bands] + [b[ch:] for b in bands], axis=0)
    w_rows[...] = full.astype(BF16)
    kept = full.shape[0] // 2
    cols = jnp.concatenate([full[:kept], full[:kept], full[kept:]], axis=0)
    cols = jnp.concatenate([cols, jnp.zeros((512 - 3 * kept, n), F32)], axis=0)
    own_cols = []
    for q in range(3):
        own_cols += [cols[:, (3 * q + o) * MAIN : (3 * q + o) * MAIN + 40] for o in range(3)]
        own_cols.append(jnp.zeros((512, 8), F32))
    w_cols[...] = jnp.concatenate(own_cols, axis=1).T.astype(BF16)
    total = jnp.sum(w * level_taps(w.shape), axis=1, keepdims=True)
    total = jnp.broadcast_to(total, (ch, 128))
    bias[...] = jnp.concatenate([total] * 10, axis=0)

    h_hi, h_lo = split(STEP * heads[...])
    none = jnp.zeros((3, ch), F32)
    pair = jnp.concatenate([h_hi.astype(F32), none, h_lo.astype(F32), none], axis=0).astype(BF16)
    r = lax.broadcasted_iota(jnp.int32, (kept, ch), 0)
    q = lax.broadcasted_iota(jnp.int32, (kept, ch), 1)
    spread = jnp.where((r & (ch - 1)) == q, 1.0, 0.0).astype(BF16)
    picked = over_lanes(pair, spread)
    y_of = lax.broadcasted_iota(jnp.int32, (8, kept), 0)
    col = lax.broadcasted_iota(jnp.int32, (8, kept), 1)
    same = (col >= y_of * ch) & (col < (y_of + 1) * ch)
    split_heads = []
    for at in (0, 8):
        rows = [
            jnp.where(same, jnp.broadcast_to(picked[at + e : at + e + 1], (8, kept)), 0.0)
            for e in range(5)
        ]
        five = picked[at : at + 8]
        rows.append(jnp.where((col >= 8 * ch) & (col < 9 * ch), five, 0.0))
        rows.append(jnp.where(col >= 9 * ch, five, 0.0))
        rows.append(jnp.zeros((8, kept), F32))
        split_heads.append(jnp.concatenate(rows, axis=0))
    three = jnp.concatenate([split_heads[0], split_heads[1], split_heads[0]], axis=0)
    w_head[...] = three.T.astype(BF16)


def c_kernel(
    fields, near_twin, near_other, kernel, w_rows, w_cols, w_head, bias, t,
    own, parts,
    t_rim, acc, edge, gedge,
):
    _, cot = views(fields)
    nx = cot.shape[1]
    ch, taps = kernel.shape
    rim_state, rim_cot, _ = from_rims(near_twin, near_other)

    for v in range(5):
        level = 1.0 if v in (0, 4) else 0.0
        for q, row in enumerate((-1, -2, 8, 9)):
            edge[pl.ds(5 * q + v, nx, stride=RIM), :] = rim_state(row, v) - level
        gedge[pl.ds(v, nx, stride=16), :] = rim_cot(-1, v)
        gedge[pl.ds(8 + v, nx, stride=16), :] = rim_cot(8, v)
    none = jnp.zeros((nx, 128), F32)
    for q in range(20, RIM):
        edge[pl.ds(q, nx, stride=RIM), :] = none
    for q in (5, 6, 7):
        gedge[pl.ds(q, nx, stride=16), :] = none
        gedge[pl.ds(8 + q, nx, stride=16), :] = none
    for x in range(nx):
        mid = edge[pl.ds(x * RIM, RIM), :]
        at = (x + 1) * 3 * RIM
        t_rim[pl.ds(at, RIM), :] = pltpu.roll(mid, 1, 1).astype(BF16)
        t_rim[pl.ds(at + RIM, RIM), :] = mid.astype(BF16)
        t_rim[pl.ds(at + 2 * RIM, RIM), :] = pltpu.roll(mid, 127, 1).astype(BF16)
    t_rim[pl.ds(0, 3 * RIM), :] = t_rim[pl.ds(nx * 3 * RIM, 3 * RIM), :]
    t_rim[pl.ds((nx + 1) * 3 * RIM, 3 * RIM), :] = t_rim[pl.ds(3 * RIM, 3 * RIM), :]

    kept = 8 * ch
    kg = hg = dsum = None
    zeros8 = jnp.zeros((8, 128 * WIDE), F32)
    written = set()
    for x in range(0, nx, WIDE):
        s = jnp.concatenate(
            [
                jnp.concatenate(
                    [
                        t[pl.ds((x + j) * 3 * MAIN, 9 * MAIN), :],
                        t_rim[pl.ds((x + j) * 3 * RIM, 9 * RIM), :],
                    ],
                    axis=0,
                )
                for j in range(WIDE)
            ],
            axis=1,
        )
        z2 = jnp.dot(w_rows[...], s, preferred_element_type=F32)
        rows = z2.shape[0] // 2
        z = z2[:rows] + z2[rows:] + jnp.concatenate([bias[...]] * WIDE, axis=1)
        hidden = jnp.tanh(z)
        g = jnp.concatenate(
            [
                jnp.concatenate(
                    [cot[v, x + j] for v in range(5)] + [gedge[pl.ds((x + j) * 16, 16), :]], axis=0
                )
                for j in range(WIDE)
            ],
            axis=1,
        )
        g_hi, g_lo = split(g)
        g_hi32, g_lo32 = g_hi.astype(F32), g_lo.astype(F32)
        g3 = jnp.concatenate(
            [g_hi32, zeros8, g_hi32, zeros8, g_lo32, zeros8], axis=0
        ).astype(BF16)
        d = (1.0 - hidden * hidden) * jnp.dot(w_head[...], g3, preferred_element_type=F32)
        d_hi, d_lo = split(d)
        zeros = jnp.zeros((512 - 3 * rows, 128 * WIDE), BF16)
        back = jnp.dot(
            w_cols[...],
            jnp.concatenate([d_hi, d_lo, d_hi, zeros], axis=0),
            preferred_element_type=F32,
        )
        k2 = over_lanes(s, jnp.concatenate([d_hi[:kept], d_lo[:kept]], axis=0))
        k2 = k2[:, :kept] + k2[:, kept:]
        kg = k2 if kg is None else kg + k2
        hid2 = jnp.concatenate(split(hidden[:kept]), axis=0)
        g2 = jnp.concatenate([g_hi32[:40], g_lo32[:40]], axis=0).astype(BF16)
        h2 = over_lanes(g2, hid2)
        hg = h2 if hg is None else hg + h2
        for j in range(WIDE):
            level = d[:kept, 128 * j : 128 * (j + 1)]
            dsum = level if dsum is None else dsum + level
        for m in range(WIDE + 2):
            total = None
            for j in range(WIDE):
                if 0 <= m - j < 3:
                    q = m - j
                    piece = back[q * 128 : q * 128 + 120, 128 * j : 128 * (j + 1)]
                    total = piece if total is None else total + piece
            here = (x + m - 1) % nx
            if here in written:
                total = total + acc[pl.ds(here * 120, 120), :]
            written.add(here)
            acc[pl.ds(here * 120, 120), :] = total
    for x in range(nx):
        at = x * 120
        total = (
            acc[pl.ds(at + 40, 40), :]
            + pltpu.roll(acc[pl.ds(at, 40), :], 127, 1)
            + pltpu.roll(acc[pl.ds(at + 80, 40), :], 1, 1)
        )
        for v in range(5):
            own[v, x] = total[8 * v : 8 * v + 8]

    sums = jnp.sum(dsum, axis=1, keepdims=True)
    kg = kg.T
    hg = (hg[:40, :kept] + hg[40:, :kept]) + (hg[:40, kept:] + hg[40:, kept:])
    y_row = lax.broadcasted_iota(jnp.int32, (40, kept), 0) & 7
    y_col = lax.broadcasted_iota(jnp.int32, (40, kept), 1)
    same_y = (y_col >= y_row * ch) & (y_col < (y_row + 1) * ch)
    hg = jnp.where(same_y, hg, 0.0)
    by_eq = jnp.concatenate(
        [jnp.sum(hg[8 * e : 8 * e + 8], axis=0, keepdims=True) for e in range(5)]
        + [jnp.zeros((123, kept), F32)],
        axis=0,
    ).T
    level_sum = jnp.zeros((ch, 1), F32)
    head_sum = jnp.zeros((ch, 128), F32)
    n = kg.shape[1]
    columns_at, tap = columns()
    kind = jnp.broadcast_to(columns_at[0:1], (ch, n))
    total = jnp.zeros((ch, n), F32)
    for y in range(8):
        rows = kg[y * ch : (y + 1) * ch]
        moved = rows if y == 1 else pltpu.roll(rows, (1 - y) % n, 1)
        keep = kind < 3
        if y == 0:
            keep = (kind == 1) | (kind == 2)
            total = total + jnp.where(kind == 8, rows, 0.0)
        if y == 7:
            keep = kind < 2
            total = total + jnp.where(kind == 10, rows, 0.0)
        total = total + jnp.where(keep, moved, 0.0)
        level_sum = level_sum + sums[y * ch : (y + 1) * ch]
        head_sum = head_sum + by_eq[y * ch : (y + 1) * ch]
    grads = over_lanes(jnp.concatenate(split(total), axis=0), own_taps(columns_at, tap))
    n_pick = grads.shape[1]
    parts[...] = jnp.zeros_like(parts)
    parts[:, pl.ds(0, n_pick)] = grads[:ch] + grads[ch:]
    parts[:, pl.ds(0, taps)] = parts[:, pl.ds(0, taps)] + level_sum * level_taps((ch, taps))
    parts[:, pl.ds(128, 128)] = parts[:, pl.ds(128, 128)] + pltpu.roll(head_sum * STEP, 16, 1)


def columns():
    lane = lax.broadcasted_iota(jnp.int32, (8, COLUMNS), 1)
    main = lane < 9 * MAIN
    past = lane - 9 * MAIN
    block = sum((lane >= MAIN * i).astype(jnp.int32) for i in range(1, 9))
    o = jnp.where(main, block, past >> 5)
    r = jnp.where(main, lane - MAIN * block, past & (RIM - 1))
    which = sum((r >= 5 * i).astype(jnp.int32) for i in (1, 2, 3, 4))
    kind = jnp.where(main, jnp.where(r < 40, r & 7, 12), 8 + which)
    v = jnp.where(main, r >> 3, r - 5 * which)
    return kind, o * 5 + v


def taps_of(columns_at):
    n = columns_at.shape[1]
    row = lax.broadcasted_iota(jnp.int32, (144, n), 0)
    return jnp.where(row == jnp.broadcast_to(columns_at[0:1], (144, n)), 1.0, 0.0).astype(BF16)


def own_taps(kind, tap):
    at = jnp.where(kind < 3, tap + 45 * kind, 1000)
    at = jnp.where(kind == 8, tap, at)
    return taps_of(jnp.where(kind == 10, tap + 90, at))


def rim_taps(kind, tap):
    first = (kind == 9) | (kind == 7)
    middle = (kind == 8) | (kind == 10)
    last = (kind == 0) | (kind == 11)
    at = jnp.where(first, tap, jnp.where(middle, tap + 45, 1000))
    return taps_of(jnp.where(last, tap + 90, at))


def level_taps(shape):
    t = lax.broadcasted_iota(jnp.int32, shape, 1).astype(F32)
    v = t - 5.0 * jnp.floor((t + 0.5) * 0.2)
    return jnp.where((v < 0.5) | (v > 3.5), 1.0, 0.0)


def call(kernel, outs, scratch, us, n_in, order=0):
    spec = pl.BlockSpec(memory_space=pltpu.VMEM)
    return pl.pallas_call(
        kernel,
        out_shape=outs,
        in_specs=[spec] * n_in + [pl.BlockSpec(memory_space=pl.ANY)] * order,
        scratch_shapes=scratch,
        compiler_params=pltpu.CompilerParams(vmem_limit_bytes=VMEM),
        cost_estimate=pl.CostEstimate(
            flops=int(us * 1.15e9), bytes_accessed=int(us * 3.69e6), transcendentals=0
        ),
    )


def body(state, cot, flags, kernel, heads):
    _, nx, ny, nz = state.shape
    ch, taps = kernel.shape
    count = lax.axis_size("gy")
    cells = nx * ny * nz
    shape = lambda *dims: jax.ShapeDtypeStruct(dims, F32)
    half_shape = lambda *dims: jax.ShapeDtypeStruct(dims, BF16)
    full = shape(5, nx, ny, nz)
    with_twin = [(i, i ^ 1) for i in range(count)]
    with_other = [(i, (i + 1) % count if i % 2 else (i - 1) % count) for i in range(count)]
    vm = pltpu.VMEM
    lines = 5 * nx * ny

    flat = jnp.concatenate([state.reshape(lines, nz), cot.reshape(lines, nz)])
    fields = flat.reshape(10, nx, ny, nz)
    near, far = shape(NEAR, nx, nz), shape(FAR, nx, nz)
    near_twin, near_other = call(near_kernel, (near, near), [], 0.2, 1)(flat)
    near_rims = (
        lax.ppermute(near_twin, "gy", with_twin),
        lax.ppermute(near_other, "gy", with_other),
    )
    first = call(
        x_kernel,
        full,
        [
            vm((5, nx + 5, ny, nz), F32),
            vm((5, nx + 1, ny, nz), F32),
            vm((5, nx + 5, ny, nz), F32),
        ],
        2.8,
        2,
        2,
    )(fields, flags, near_twin, near_other)
    far_twin, far_other = call(far_kernel, (far, far), [], 0.2, 2, 1)(
        flat, flags.reshape(3 * nx * ny, nz), first
    )
    far_rims = (
        lax.ppermute(far_twin, "gy", with_twin),
        lax.ppermute(far_other, "gy", with_other),
    )
    *prepared, patches = call(
        prepare_kernel,
        (
            half_shape(20 * ch, COLUMNS),
            half_shape(384, 512),
            half_shape(10 * ch, 192),
            shape(10 * ch, 128),
            half_shape((nx + 2) * 3 * MAIN, nz),
        ),
        [vm((2 * ch, 144), F32)],
        1.5,
        3,
        2,
    )(fields, kernel, heads, far_twin, far_other)
    near_rims, patches, first = lax.optimization_barrier((near_rims, patches, first))
    own, parts = call(
        c_kernel,
        (full, shape(ch, 256)),
        [
            vm(((nx + 2) * 3 * RIM, nz), BF16),
            vm((nx * 120, nz), F32),
            vm((RIM * nx, nz), F32),
            vm((16 * nx, nz), F32),
        ],
        3.5,
        9,
    )(fields, *near_rims, kernel, *prepared, patches)

    def exchanged(value, bit):
        return lax.ppermute(value, "gy", [(i, i ^ bit) for i in range(count)])

    bits = [1 << b for b in range(count.bit_length() - 1)]
    sums = parts
    for bit in bits[:-4]:
        sums = sums + exchanged(sums, bit)
    z_half = lambda half, before, order: call(
        functools.partial(z_kernel, half), full, [], 1.9, 4, 1
    )(fields, flags, before, first, order)
    got = exchanged(sums, bits[-4])
    total = z_half(0, own, sums)
    got, total = lax.optimization_barrier((got, total))
    sums = sums + got
    got = exchanged(sums, bits[-3])
    total = z_half(1, total, sums)
    got, total = lax.optimization_barrier((got, total))
    sums = sums + got
    got = exchanged(sums, bits[-2])
    rim = call(e_kernel, shape(lines, nz), [], 1.1, 5, 1)(flat, *near_rims, *far_rims, sums)
    got, rim = lax.optimization_barrier((got, rim))
    sums = sums + got
    got = exchanged(sums, bits[-1])
    flow = call(y_kernel, full, [vm((lines, nz), F32)] * 2, 3.7, 8, 1)(
        fields, flags, *near_rims, *far_rims, total, rim, sums
    )
    got, flow = lax.optimization_barrier((got, flow))
    scale = float(cells * count) ** (-0.5)
    k_out, h_out = call(
        functools.partial(sum_kernel, scale), (shape(ch, taps), shape(5, ch)), [], 0.5, 2
    )(sums, got)
    return flow, k_out, h_out


def solution(mesh):
    split_y = P(None, "ens", "gy", None)
    return jax.shard_map(
        body,
        mesh=mesh,
        in_specs=(split_y, split_y, split_y, P(), P()),
        out_specs=(split_y, P("ens", None), P("ens", None)),
        check_vma=False,
    )
```

```python
import functools

import jax
import jax.numpy as jnp
from jax import lax
from jax.experimental import pallas as pl
from jax.experimental.pallas import tpu as pltpu
from jax.sharding import PartitionSpec as P

STEP = 0.3
FLOOR = 0.01
BELOW, ABOVE = 2, 3
SLABS = 2
WIDE = 4
VMEM = 48 * 1024 * 1024
F32 = jnp.float32
BF16 = jnp.bfloat16


def rcp(x):
    return pl.reciprocal(x, approx=True)


def shared_terms(v):
    p = [v[i + 1] - v[i] for i in range(5)]
    d = [p[i + 1] - p[i] for i in range(4)]
    h = [(4.0 / 3.0) * x for x in d]
    k = [h[i] * d[i] + FLOOR for i in range(4)]
    g = [x + x for x in h]
    t = [d[i + 1] - d[i] for i in range(3)]
    return p, d, k, g, t


def side_value(pa, pm, pm2, ka, kb, kc, m0, m2, td, t1, smooth, c0, c2):
    i0 = rcp(ka + pa * m0)
    i1 = rcp(kb + pa * pm)
    i2 = rcp(kc + pm * m2)
    w0 = i0 * i0
    w1 = 6.0 * (i1 * i1)
    w2 = 3.0 * (i2 * i2)
    r = rcp(w0 + w1 + w2)
    o0 = jnp.where(smooth, w0 * r, c0)
    o2 = jnp.where(smooth, w2 * r, c2)
    u = o0 * td + o2 * t1
    b0 = w0 * i0 * (td - u)
    b1 = w1 * i1 * u
    b2 = w2 * i2 * (t1 - u)
    return (pa + pm2) - u, (b0, b1, b2, r, o0, o2)


def side_pull(mu, pa, pm, m0, m2, smooth, saved):
    b0, b1, b2, r, o0, o2 = saved
    mu2 = mu + mu
    rm = jnp.where(smooth, mu2, 0.0) * r
    s0, s1, s2 = b0 * rm, b1 * rm, b2 * rm
    pa_bar = s0 * (m0 + pa) - s1 * pm + mu
    pm_bar = s2 * (m2 + pm) - s1 * pa + mu2
    return s0, s1, s2, pa_bar, pm_bar, o0 * mu2, o2 * mu


def hllc_pull(left, right, normal, flags, cot):
    region = flags & 3
    is_right = region >= 2
    star = ((region + 1) & 2) != 0
    n_at = 1 + normal
    tang = [1 + i for i in range(3) if i != normal]
    rl, rr_, pl_, pr_, nl, nr = left[0], right[0], left[4], right[4], left[n_at], right[n_at]

    def sound(r, p):
        inv = rcp(r)
        t = 1.4 * p * inv
        inv_c = lax.rsqrt(t)
        return inv, inv_c, t * inv_c

    inv_rl, inv_cl, cl = sound(rl, pl_)
    inv_rr, inv_cr, cr = sound(rr_, pr_)
    c = 0.5 * (cl + cr)
    r2 = rl + rr_
    inv = rcp(r2 * c)
    nm = 0.5 * (nl + nr)
    gap = (pl_ - pr_) * inv
    sm = nm + gap
    sc = jnp.where(is_right, c, -c)
    s = nm + sc
    pick = [jnp.where(is_right, right[i], left[i]) for i in range(5)]
    r, un, u1, u2, p = pick[0], pick[n_at], pick[tang[0]], pick[tang[1]], pick[4]
    a = s - un
    dl = sm - un
    si = jnp.where(star, rcp(sc - gap), 0.0)
    j = s * si
    kap = j * dl
    g0, gn, g1, g2, ge = cot[0], cot[n_at], cot[tang[0]], cot[tang[1]], cot[4]
    w = un + kap
    half_q = 0.5 * (un * un + u1 * u1 + u2 * u2)
    enthalpy = 3.5 * p + r * half_q
    b = g0 + u1 * g1 + u2 * g2 + un * gn
    m = r * b + enthalpy * ge
    n = gn + sm * ge
    rkap = r * kap
    f_kap = m + r * a * n
    f_a = rkap * n
    si2 = si * si
    s_bar = f_a - f_kap * (dl * sm * si2)
    sm_bar = f_kap * (s * a * si2) + rkap * a * ge
    wr = w * r
    k_bar = [None] * 5
    k_bar[0] = w * (b + half_q * ge) + kap * a * n
    k_bar[n_at] = m + wr * (gn + un * ge) - f_kap * j - f_a
    k_bar[tang[0]] = wr * (g1 + u1 * ge)
    k_bar[tang[1]] = wr * (g2 + u2 * ge)
    k_bar[4] = 3.5 * (w * ge) + gn
    e = sm_bar * inv
    eg = e * gap
    c_half = 0.5 * (jnp.where(is_right, s_bar, -s_bar) - eg * r2)
    n_half = 0.5 * (s_bar + sm_bar)
    r_both = -(eg * c)
    xl = c_half * inv_rl
    xr = c_half * inv_rr
    base_l = {0: r_both - 0.5 * (xl * cl), n_at: n_half, 4: 0.7 * (xl * inv_cl) + e}
    base_r = {0: r_both - 0.5 * (xr * cr), n_at: n_half, 4: 0.7 * (xr * inv_cr) - e}
    l_bar, r_bar = [], []
    for i in range(5):
        kr = jnp.where(is_right, k_bar[i], 0.0)
        kl = k_bar[i] - kr
        l_bar.append(base_l[i] + kl if i in base_l else kl)
        r_bar.append(base_r[i] + kr if i in base_r else kr)
    return l_bar, r_bar


def face_pull(cells, cot, flags, normal):
    stencil = flags >> 2
    smooth = stencil == 0
    c0 = jnp.where(stencil == 1, 1.0, 0.0)
    c2 = jnp.where(stencil == 3, 1.0, 0.0)
    left, right, kept = [], [], []
    for v in cells:
        p, d, k, g, t = shared_terms(v)
        pm2 = p[2] + p[2]
        args_l = (p[1], p[2], p[1] + d[0], p[2] - d[2], t[0] + t[0], t[1])
        args_r = (p[3], p[2], p[3] - d[3], p[2] + d[1], t[2] + t[2], t[1])
        hl, saved_l = side_value(
            p[1], p[2], pm2, k[0], k[1], k[2], *args_l[2:], smooth, c0, c2
        )
        hr, saved_r = side_value(
            p[3], p[2], pm2, k[3], k[2], k[1], *args_r[2:], smooth, c0, c2
        )
        left.append(v[2] + hl * (1.0 / 6.0))
        right.append(v[3] - hr * (1.0 / 6.0))
        kept.append((p, g, args_l[:4], args_r[:4], saved_l, saved_r))
    l_bar, r_bar = hllc_pull(left, right, normal, flags, cot)
    out = []
    for i in range(5):
        p, g, args_l, args_r, saved_l, saved_r = kept[i]
        a0, a1, a2, pa_l, pm_l, x0, x2 = side_pull(
            l_bar[i] * (1.0 / 6.0), *args_l, smooth, saved_l
        )
        b0, b1, b2, pa_r, pm_r, y0, y2 = side_pull(
            r_bar[i] * (-1.0 / 6.0), *args_r, smooth, saved_r
        )
        d0 = a0 * (g[0] + p[1]) + x0
        d1 = (b2 * (g[1] + p[2]) - a1 * g[1]) + (x2 - x0) + y2
        d2 = (a2 * (g[2] - p[2]) - b1 * g[2]) + (y0 - y2) - x2
        d3 = b0 * (g[3] - p[3]) - y0
        p2 = pa_l + (d0 - d1)
        p3 = pm_l + pm_r + (d1 - d2)
        p4 = pa_r + (d2 - d3)
        out.append([d0, -d0 - p2, l_bar[i] + (p2 - p3), r_bar[i] + (p3 - p4), p4 - d3, d3])
    return out


def conserved_pull(s, g):
    half_q = 0.5 * (s[1] * s[1] + s[2] * s[2] + s[3] * s[3])
    return [
        g[0] + s[1] * g[1] + s[2] * g[2] + s[3] * g[3] + half_q * g[4],
        s[0] * (g[1] + s[1] * g[4]),
        s[0] * (g[2] + s[2] * g[4]),
        s[0] * (g[3] + s[3] * g[4]),
        2.5 * g[4],
    ]


NEAR_STATE, FAR_STATE = 2, 3
NEAR_COT, FAR_COT = 1, 2
FLAG_ROWS = 3
NEAR = 5 * (NEAR_STATE + NEAR_COT)
FAR = 5 * (FAR_STATE + FAR_COT) + FLAG_ROWS


def views(fields):
    n = fields.shape[0] // 2
    return fields.at[pl.ds(0, n)], fields.at[pl.ds(n, n)]


def pack(ref, rows, first, twin, other, at):
    even = is_even()
    nx = twin.shape[1]
    count = ref.shape[0] // (8 * nx)
    for r in rows:
        for v in range(count):
            low = ref[pl.ds(v * nx * 8 + r, nx, stride=8), :].astype(F32)
            top = ref[pl.ds(v * nx * 8 + 7 - r, nx, stride=8), :].astype(F32)
            i = at + (r - first) * count + v
            twin[i] = jnp.where(even, top, low)
            other[i] = jnp.where(even, low, top)


def near_kernel(flat, twin, other):
    s, g = views(flat)
    pack(s, range(NEAR_STATE), 0, twin, other, 0)
    pack(g, range(NEAR_COT), 0, twin, other, 5 * NEAR_STATE)


def far_kernel(flat, flags, order, twin, other):
    del order
    s, g = views(flat)
    n = flags.shape[0] // 3
    pack(s, range(NEAR_STATE, NEAR_STATE + FAR_STATE), NEAR_STATE, twin, other, 0)
    pack(g, range(NEAR_COT, NEAR_COT + FAR_COT), NEAR_COT, twin, other, 5 * FAR_STATE)
    pack(flags.at[pl.ds(n, n)], range(FLAG_ROWS), 0, twin, other, FAR - FLAG_ROWS)


def from_rims(near_twin, near_other, far_twin=None, far_other=None):
    even = is_even()

    def pick(twin, other, i, below):
        if below:
            return jnp.where(even, other[i], twin[i])
        return jnp.where(even, twin[i], other[i])

    def read(row, near, near_at, far_at, v):
        below = row < 0
        r = -1 - row if below else row - 8
        if r < near:
            return pick(near_twin, near_other, near_at + r * 5 + v, below)
        return pick(far_twin, far_other, far_at + (r - near) * 5 + v, below)

    def state(row, v):
        return read(row, NEAR_STATE, 0, 0, v)

    def cot(row, v):
        return read(row, NEAR_COT, 5 * NEAR_STATE, 5 * FAR_STATE, v)

    def flags(row):
        below = row < 0
        r = -1 - row if below else row - 8
        return pick(far_twin, far_other, FAR - FLAG_ROWS + r, below).astype(jnp.int32)

    return state, cot, flags


def x_kernel(fields, flags, order, order2, out, pad, gpad, acc):
    del order, order2
    state, cot = views(fields)
    nx = state.shape[1]
    for v in range(5):
        pad[v, pl.ds(2, nx)] = state[v]
        pad[v, pl.ds(0, 2)] = state[v, pl.ds(nx - 2, 2)]
        pad[v, pl.ds(nx + 2, 3)] = state[v, pl.ds(0, 3)]
        gpad[v, pl.ds(0, nx)] = cot[v]
        gpad[v, pl.ds(nx, 1)] = cot[v, pl.ds(0, 1)]
    acc[...] = jnp.zeros_like(acc)

    def step(i, carry):
        x = i * SLABS
        cells = [[pad[v, pl.ds(x + k, SLABS)] for k in range(6)] for v in range(5)]
        g = [gpad[v, pl.ds(x, SLABS)] for v in range(5)]
        face = [STEP * (gpad[v, pl.ds(x + 1, SLABS)] - g[v]) for v in range(5)]
        terms = face_pull(cells, face, flags[0, pl.ds(x, SLABS)], 0)
        own = conserved_pull([cells[v][2] for v in range(5)], g)
        for v in range(5):
            terms[v][2] = terms[v][2] + own[v]
            for s in range(SLABS + 5):
                total = None
                for k in range(6):
                    if 0 <= s - k < SLABS:
                        part = terms[v][k][s - k]
                        total = part if total is None else total + part
                acc[v, x + s] = acc[v, x + s] + total
        return carry

    lax.fori_loop(0, nx // SLABS, step, 0)
    for v in range(5):
        acc[v, pl.ds(nx, 2)] = acc[v, pl.ds(nx, 2)] + acc[v, pl.ds(0, 2)]
        acc[v, pl.ds(2, 3)] = acc[v, pl.ds(2, 3)] + acc[v, pl.ds(nx + 2, 3)]

    for v in range(5):
        out[v] = acc[v, pl.ds(2, nx)]


def z_kernel(half, fields, flags, before, more, order, out):
    del order
    state, cot = views(fields)
    nx = state.shape[1] // 2
    for v in range(5):
        kept = pl.ds((1 - half) * nx, nx)
        out[v, kept] = before[v, kept]

    def z_step(i, carry):
        x = half * nx + i * SLABS
        cells, face = [], []
        for v in range(5):
            mid = state[v, pl.ds(x, SLABS)]
            cells.append([mid if k == 0 else pltpu.roll(mid, (-k) % 128, 2) for k in range(-2, 4)])
            g = cot[v, pl.ds(x, SLABS)]
            face.append(STEP * (pltpu.roll(g, 127, 2) - g))
        terms = face_pull(cells, face, flags[2, pl.ds(x, SLABS)], 2)
        for v in range(5):
            t = before[v, pl.ds(x, SLABS)] + more[v, pl.ds(x, SLABS)] + terms[v][2]
            for k in (-2, -1, 1, 2, 3):
                t = t + pltpu.roll(terms[v][k + 2], k % 128, 2)
            out[v, pl.ds(x, SLABS)] = t
        return carry

    lax.fori_loop(0, nx // SLABS, z_step, 0)


def e_kernel(flat, near_twin, near_other, far_twin, far_other, order, out):
    del order
    state, cot = views(flat)
    nx = out.shape[0] // 40
    rim_state, rim_cot, rim_flags = from_rims(near_twin, near_other, far_twin, far_other)

    def own(ref, row, v):
        return ref[pl.ds(v * nx * 8 + row, nx, stride=8), :]

    state_rows, cot_rows = {}, {}
    for v in range(5):
        for row in (*range(-5, 3), *range(6, 13)):
            inside = 0 <= row < 8
            state_rows[row, v] = own(state, row, v) if inside else rim_state(row, v)
        for row in (-3, -2, -1, 0, 8, 9, 10):
            inside = 0 <= row < 8
            cot_rows[row, v] = own(cot, row, v) if inside else rim_cot(row, v)
    sums = {}
    for j in (-3, -2, -1, 8, 9):
        cells = [[state_rows[j + k, v] for k in range(-2, 4)] for v in range(5)]
        face = [STEP * (cot_rows[j + 1, v] - cot_rows[j, v]) for v in range(5)]
        terms = face_pull(cells, face, rim_flags(j), 1)
        for v in range(5):
            for k in range(-2, 4):
                if 0 <= j + k < 8:
                    t = terms[v][k + 2]
                    sums[j + k, v] = sums[j + k, v] + t if (j + k, v) in sums else t
    for v in range(5):
        for row in range(8):
            value = sums[row, v] if (row, v) in sums else jnp.zeros((nx, 128), F32)
            out[pl.ds(v * nx * 8 + row, nx, stride=8), :] = value


def y_kernel(fields, flags, near_twin, near_other, far_twin, far_other, before, rim, order, out, halo, ghalo):
    del order
    state, cot = views(fields)
    rims = from_rims(near_twin, near_other, far_twin, far_other)
    rim_state, rim_cot, _ = rims
    nx = out.shape[1]
    for v in range(5):
        base = v * nx * 8
        for r in range(ABOVE):
            halo[pl.ds(base + r, nx, stride=8), :] = rim_state(8 + r, v)
        for r in range(BELOW):
            halo[pl.ds(base + 8 - BELOW + r, nx, stride=8), :] = rim_state(r - BELOW, v)
        ghalo[pl.ds(base, nx, stride=8), :] = rim_cot(8, v)
    row = lax.broadcasted_iota(jnp.int32, (SLABS, 8, 128), 1)
    inside = {}
    for k in (-2, -1, 1, 2, 3):
        inside[k] = (row < 8 + k) if k < 0 else (row >= k)

    def step(i, carry):
        x = i * SLABS
        cells, face = [], []
        for v in range(5):
            at = pl.multiple_of((v * nx + x) * 8, 8)
            rim_rows = halo[pl.ds(at, 8 * SLABS), :].reshape(SLABS, 8, 128)
            mid = state[v, pl.ds(x, SLABS)]
            line = []
            for k in range(-2, 4):
                if k == 0:
                    line.append(mid)
                else:
                    line.append(pltpu.roll(jnp.where(inside[k], mid, rim_rows), (-k) % 8, 1))
            cells.append(line)
            g = cot[v, pl.ds(x, SLABS)]
            g_rim = ghalo[pl.ds(at, 8 * SLABS), :].reshape(SLABS, 8, 128)
            face.append(STEP * (pltpu.roll(jnp.where(inside[1], g, g_rim), 7, 1) - g))
        terms = face_pull(cells, face, flags[1, pl.ds(x, SLABS)], 1)
        for v in range(5):
            at = pl.multiple_of((v * nx + x) * 8, 8)
            total = before[v, pl.ds(x, SLABS)] + terms[v][2]
            total = total + rim[pl.ds(at, 8 * SLABS), :].reshape(SLABS, 8, 128)
            for k in (-2, -1, 1, 2, 3):
                moved = pltpu.roll(terms[v][k + 2], k % 8, 1)
                total = total + jnp.where(inside[k], moved, 0.0)
            out[v, pl.ds(x, SLABS)] = total
        return carry

    lax.fori_loop(0, nx // SLABS, step, 0)


def sum_kernel(scale, mine, theirs, k_out, h_out):
    total = (mine[...] + theirs[...]) * scale
    k_out[...] = total[:, : k_out.shape[1]]
    ch = total.shape[0]
    pick = (
        lax.broadcasted_iota(jnp.int32, (8, 128), 1)
        == lax.broadcasted_iota(jnp.int32, (8, 128), 0) + 16
    ).astype(F32)
    heads = lax.dot_general(
        pick,
        total[:, 128:],
        (((1,), (1,)), ((), ())),
        precision=lax.Precision.HIGHEST,
        preferred_element_type=F32,
    )
    h_out[...] = heads[: h_out.shape[0], :ch]


MAIN, RIM = 48, 16
OWN_COLUMNS = 9 * (MAIN + RIM)
COLUMNS = OWN_COLUMNS + 9 * RIM


def split(x):
    hi = x.astype(BF16)
    return hi, (x - hi.astype(F32)).astype(BF16)


def over_lanes(a, b):
    return lax.dot_general(a, b, (((1,), (1,)), ((), ())), preferred_element_type=F32)


def is_even():
    return lax.rem(lax.axis_index("gy"), 2) == 0


def put_patches(high, low, x, rows):
    n = rows.shape[0]
    hi, lo = split(rows)
    hi32, lo32 = hi.astype(F32), lo.astype(F32)
    for q, turn in enumerate((1, 0, 127)):
        at = pl.ds((x + 1) * 3 * n + q * n, n)
        high[at, :] = pltpu.roll(hi32, turn, 1).astype(BF16) if turn else hi
        low[at, :] = pltpu.roll(lo32, turn, 1).astype(BF16) if turn else lo


def wrap_patches(high, low, nx, rows):
    n = 3 * rows
    for ref in (high, low):
        ref[pl.ds(0, n), :] = ref[pl.ds(nx * n, n), :]
        ref[pl.ds((nx + 1) * n, n), :] = ref[pl.ds(n, n), :]


def prepare_kernel(fields, kernel, heads, order, order2, w_rows, w_cols, w_head, bias, t, t_low, wide):
    del order, order2
    state, _ = views(fields)
    nx = state.shape[1]
    for x in range(nx):
        rows = [state[v, x] - (1.0 if v in (0, 4) else 0.0) for v in range(5)]
        mid = jnp.concatenate([*rows, jnp.zeros((8, 128), F32)], axis=0)
        put_patches(t, t_low, x, mid)
    wrap_patches(t, t_low, nx, MAIN)

    ch, taps = kernel.shape
    w = kernel[...]
    hi, lo = split(w)
    wide[...] = jnp.zeros_like(wide)
    wide[pl.ds(0, ch), pl.ds(0, taps)] = hi.astype(F32)
    wide[pl.ds(ch, ch), pl.ds(0, taps)] = lo.astype(F32)
    both = wide[...].astype(BF16)
    kind, tap = columns(COLUMNS)
    base = jnp.dot(both, own_taps(kind, tap), preferred_element_type=F32)
    rim = jnp.dot(both, rim_taps(kind, tap), preferred_element_type=F32)
    n = base.shape[1]
    kind = jnp.broadcast_to(kind[0:1], base.shape)
    main = jnp.where(kind < 3, base, 0.0)
    bands = []
    for y in range(8):
        rows = main
        if y == 0:
            rows = jnp.where(kind == 0, 0.0, rows)
        if y == 7:
            rows = jnp.where(kind == 2, 0.0, rows)
        if y != 1:
            rows = pltpu.roll(rows, (y - 1) % n, 1)
        if y == 0:
            rows = rows + jnp.where(kind == 8, base, 0.0)
        if y == 7:
            rows = rows + jnp.where(kind == 10, base, 0.0)
        bands.append(rows)
    bands.append(jnp.where((kind == 0) | (kind == 8) | (kind == 9), rim, 0.0))
    bands.append(jnp.where((kind == 7) | (kind == 10) | (kind == 11), rim, 0.0))
    full = jnp.concatenate([b[:ch] for b in bands] + [b[ch:] for b in bands], axis=0)
    w_rows[...] = full.astype(BF16)
    kept = full.shape[0] // 2
    cols = jnp.concatenate([full[:kept], full[:kept], full[kept:]], axis=0)
    cols = jnp.concatenate([cols, jnp.zeros((512 - 3 * kept, n), F32)], axis=0)
    own_cols = []
    for q in range(3):
        own_cols += [cols[:, (3 * q + o) * MAIN : (3 * q + o) * MAIN + 40] for o in range(3)]
        own_cols.append(jnp.zeros((512, 8), F32))
    w_cols[...] = jnp.concatenate(own_cols, axis=1).T.astype(BF16)
    total = jnp.sum(w * level_taps(w.shape), axis=1, keepdims=True)
    total = jnp.broadcast_to(total, (ch, 128))
    bias[...] = jnp.concatenate([total] * 10, axis=0)

    h_hi, h_lo = split(STEP * heads[...])
    none = jnp.zeros((3, ch), F32)
    pair = jnp.concatenate([h_hi.astype(F32), none, h_lo.astype(F32), none], axis=0).astype(BF16)
    r = lax.broadcasted_iota(jnp.int32, (kept, ch), 0)
    q = lax.broadcasted_iota(jnp.int32, (kept, ch), 1)
    spread = jnp.where((r & (ch - 1)) == q, 1.0, 0.0).astype(BF16)
    picked = over_lanes(pair, spread)
    y_of = lax.broadcasted_iota(jnp.int32, (8, kept), 0)
    col = lax.broadcasted_iota(jnp.int32, (8, kept), 1)
    same = (col >= y_of * ch) & (col < (y_of + 1) * ch)
    split_heads = []
    for at in (0, 8):
        rows = [
            jnp.where(same, jnp.broadcast_to(picked[at + e : at + e + 1], (8, kept)), 0.0)
            for e in range(5)
        ]
        five = picked[at : at + 8]
        rows.append(jnp.where((col >= 8 * ch) & (col < 9 * ch), five, 0.0))
        rows.append(jnp.where(col >= 9 * ch, five, 0.0))
        rows.append(jnp.zeros((8, kept), F32))
        split_heads.append(jnp.concatenate(rows, axis=0))
    three = jnp.concatenate([split_heads[0], split_heads[1], split_heads[0]], axis=0)
    w_head[...] = three.T.astype(BF16)


def c_kernel(
    fields, near_twin, near_other, kernel, w_rows, w_cols, w_head, bias, t, t_low,
    own, parts,
    rim, rim_low, outer, outer_low, acc, edge, gedge,
):
    _, cot = views(fields)
    nx = cot.shape[1]
    ch, taps = kernel.shape
    rim_state, rim_cot, _ = from_rims(near_twin, near_other)

    for v in range(5):
        level = 1.0 if v in (0, 4) else 0.0
        for q, row in enumerate((-1, 8, -2, 9)):
            at = q // 2 * RIM + 5 * (q % 2) + v
            edge[pl.ds(at, nx, stride=2 * RIM), :] = rim_state(row, v) - level
        gedge[pl.ds(v, nx, stride=16), :] = rim_cot(-1, v)
        gedge[pl.ds(8 + v, nx, stride=16), :] = rim_cot(8, v)
    none = jnp.zeros((nx, 128), F32)
    for q in range(10, RIM):
        edge[pl.ds(q, nx, stride=2 * RIM), :] = none
        edge[pl.ds(RIM + q, nx, stride=2 * RIM), :] = none
    for q in (5, 6, 7):
        gedge[pl.ds(q, nx, stride=16), :] = none
        gedge[pl.ds(8 + q, nx, stride=16), :] = none
    for x in range(nx):
        put_patches(rim, rim_low, x, edge[pl.ds(2 * x * RIM, RIM), :])
        put_patches(outer, outer_low, x, edge[pl.ds((2 * x + 1) * RIM, RIM), :])
    wrap_patches(rim, rim_low, nx, RIM)
    wrap_patches(outer, outer_low, nx, RIM)

    def gathered(x, *blocks):
        columns = []
        for j in range(WIDE):
            rows = [ref[pl.ds((x + j) * 3 * n, 9 * n), :] for ref, n in blocks]
            columns.append(jnp.concatenate(rows, axis=0) if len(rows) > 1 else rows[0])
        return jnp.concatenate(columns, axis=1)

    kept = 8 * ch
    kg = hg = dsum = None
    zeros8 = jnp.zeros((8, 128 * WIDE), F32)
    written = set()
    for x in range(0, nx, WIDE):
        s_hi = gathered(x, (t, MAIN), (rim, RIM))
        s_lo = gathered(x, (t_low, MAIN), (rim_low, RIM))
        far_hi, far_lo = gathered(x, (outer, RIM)), gathered(x, (outer_low, RIM))
        z2 = jnp.dot(
            w_rows[...], jnp.concatenate([s_hi, far_hi], axis=0), preferred_element_type=F32
        )
        rows = z2.shape[0] // 2
        z3 = jnp.dot(
            w_rows[pl.ds(0, rows), :],
            jnp.concatenate([s_lo, far_lo], axis=0),
            preferred_element_type=F32,
        )
        z = z2[:rows] + (z2[rows:] + z3) + jnp.concatenate([bias[...]] * WIDE, axis=1)
        hidden = jnp.tanh(z)
        g = jnp.concatenate(
            [
                jnp.concatenate(
                    [cot[v, x + j] for v in range(5)] + [gedge[pl.ds((x + j) * 16, 16), :]], axis=0
                )
                for j in range(WIDE)
            ],
            axis=1,
        )
        g_hi, g_lo = split(g)
        g_hi32, g_lo32 = g_hi.astype(F32), g_lo.astype(F32)
        g3 = jnp.concatenate(
            [g_hi32, zeros8, g_hi32, zeros8, g_lo32, zeros8], axis=0
        ).astype(BF16)
        d = (1.0 - hidden * hidden) * jnp.dot(w_head[...], g3, preferred_element_type=F32)
        d_hi, d_lo = split(d)
        zeros = jnp.zeros((512 - 3 * rows, 128 * WIDE), BF16)
        back = jnp.dot(
            w_cols[...],
            jnp.concatenate([d_hi, d_lo, d_hi, zeros], axis=0),
            preferred_element_type=F32,
        )
        k2 = over_lanes(
            jnp.concatenate([s_hi, s_lo], axis=0),
            jnp.concatenate([d_hi[:kept], d_lo[:kept]], axis=0),
        )
        k2 = k2[:OWN_COLUMNS, :kept] + (k2[:OWN_COLUMNS, kept:] + k2[OWN_COLUMNS:, :kept])
        kg = k2 if kg is None else kg + k2
        hid2 = jnp.concatenate(split(hidden[:kept]), axis=0)
        g2 = jnp.concatenate([g_hi32[:40], g_lo32[:40]], axis=0).astype(BF16)
        h2 = over_lanes(g2, hid2)
        hg = h2 if hg is None else hg + h2
        for j in range(WIDE):
            level = d[:kept, 128 * j : 128 * (j + 1)]
            dsum = level if dsum is None else dsum + level
        for m in range(WIDE + 2):
            total = None
            for j in range(WIDE):
                if 0 <= m - j < 3:
                    q = m - j
                    piece = back[q * 128 : q * 128 + 120, 128 * j : 128 * (j + 1)]
                    total = piece if total is None else total + piece
            here = (x + m - 1) % nx
            if here in written:
                total = total + acc[pl.ds(here * 120, 120), :]
            written.add(here)
            acc[pl.ds(here * 120, 120), :] = total
    for x in range(nx):
        at = x * 120
        total = (
            acc[pl.ds(at + 40, 40), :]
            + pltpu.roll(acc[pl.ds(at, 40), :], 127, 1)
            + pltpu.roll(acc[pl.ds(at + 80, 40), :], 1, 1)
        )
        for v in range(5):
            own[v, x] = total[8 * v : 8 * v + 8]

    sums = jnp.sum(dsum, axis=1, keepdims=True)
    kg = kg.T
    hg = (hg[:40, :kept] + hg[40:, :kept]) + (hg[:40, kept:] + hg[40:, kept:])
    y_row = lax.broadcasted_iota(jnp.int32, (40, kept), 0) & 7
    y_col = lax.broadcasted_iota(jnp.int32, (40, kept), 1)
    same_y = (y_col >= y_row * ch) & (y_col < (y_row + 1) * ch)
    hg = jnp.where(same_y, hg, 0.0)
    by_eq = jnp.concatenate(
        [jnp.sum(hg[8 * e : 8 * e + 8], axis=0, keepdims=True) for e in range(5)]
        + [jnp.zeros((123, kept), F32)],
        axis=0,
    ).T
    level_sum = jnp.zeros((ch, 1), F32)
    head_sum = jnp.zeros((ch, 128), F32)
    n = kg.shape[1]
    columns_at, tap = columns(n)
    kind = jnp.broadcast_to(columns_at[0:1], (ch, n))
    total = jnp.zeros((ch, n), F32)
    for y in range(8):
        rows = kg[y * ch : (y + 1) * ch]
        moved = rows if y == 1 else pltpu.roll(rows, (1 - y) % n, 1)
        keep = kind < 3
        if y == 0:
            keep = (kind == 1) | (kind == 2)
            total = total + jnp.where(kind == 8, rows, 0.0)
        if y == 7:
            keep = kind < 2
            total = total + jnp.where(kind == 10, rows, 0.0)
        total = total + jnp.where(keep, moved, 0.0)
        level_sum = level_sum + sums[y * ch : (y + 1) * ch]
        head_sum = head_sum + by_eq[y * ch : (y + 1) * ch]
    grads = over_lanes(jnp.concatenate(split(total), axis=0), own_taps(columns_at, tap))
    n_pick = grads.shape[1]
    parts[...] = jnp.zeros_like(parts)
    parts[:, pl.ds(0, n_pick)] = grads[:ch] + grads[ch:]
    parts[:, pl.ds(0, taps)] = parts[:, pl.ds(0, taps)] + level_sum * level_taps((ch, taps))
    parts[:, pl.ds(128, 128)] = parts[:, pl.ds(128, 128)] + pltpu.roll(head_sum * STEP, 16, 1)


def columns(n):
    lane = lax.broadcasted_iota(jnp.int32, (8, n), 1)
    main = lane < 9 * MAIN
    far = lane >= OWN_COLUMNS
    past = lane - jnp.where(far, OWN_COLUMNS, 9 * MAIN)
    block = sum((lane >= MAIN * i).astype(jnp.int32) for i in range(1, 9))
    o = jnp.where(main, block, past >> 4)
    r = jnp.where(main, lane - MAIN * block, past & (RIM - 1))
    second = (r >= 5).astype(jnp.int32)
    rim = jnp.where(r < 10, 8 + 2 * second + far.astype(jnp.int32), 12)
    kind = jnp.where(main, jnp.where(r < 40, r & 7, 12), rim)
    v = jnp.where(main, r >> 3, r - 5 * second)
    return kind, o * 5 + v


def taps_of(columns_at):
    n = columns_at.shape[1]
    row = lax.broadcasted_iota(jnp.int32, (144, n), 0)
    return jnp.where(row == jnp.broadcast_to(columns_at[0:1], (144, n)), 1.0, 0.0).astype(BF16)


def own_taps(kind, tap):
    at = jnp.where(kind < 3, tap + 45 * kind, 1000)
    at = jnp.where(kind == 8, tap, at)
    return taps_of(jnp.where(kind == 10, tap + 90, at))


def rim_taps(kind, tap):
    first = (kind == 9) | (kind == 7)
    middle = (kind == 8) | (kind == 10)
    last = (kind == 0) | (kind == 11)
    at = jnp.where(first, tap, jnp.where(middle, tap + 45, 1000))
    return taps_of(jnp.where(last, tap + 90, at))


def level_taps(shape):
    t = lax.broadcasted_iota(jnp.int32, shape, 1).astype(F32)
    v = t - 5.0 * jnp.floor((t + 0.5) * 0.2)
    return jnp.where((v < 0.5) | (v > 3.5), 1.0, 0.0)


def call(kernel, outs, scratch, us, n_in, order=0):
    spec = pl.BlockSpec(memory_space=pltpu.VMEM)
    return pl.pallas_call(
        kernel,
        out_shape=outs,
        in_specs=[spec] * n_in + [pl.BlockSpec(memory_space=pl.ANY)] * order,
        scratch_shapes=scratch,
        compiler_params=pltpu.CompilerParams(vmem_limit_bytes=VMEM),
        cost_estimate=pl.CostEstimate(
            flops=int(us * 1.15e9), bytes_accessed=int(us * 3.69e6), transcendentals=0
        ),
    )


def body(state, cot, flags, kernel, heads):
    _, nx, ny, nz = state.shape
    ch, taps = kernel.shape
    count = lax.axis_size("gy")
    cells = nx * ny * nz
    shape = lambda *dims: jax.ShapeDtypeStruct(dims, F32)
    half_shape = lambda *dims: jax.ShapeDtypeStruct(dims, BF16)
    full = shape(5, nx, ny, nz)
    with_twin = [(i, i ^ 1) for i in range(count)]
    with_other = [(i, (i + 1) % count if i % 2 else (i - 1) % count) for i in range(count)]
    vm = pltpu.VMEM
    lines = 5 * nx * ny

    flat = jnp.concatenate([state.reshape(lines, nz), cot.reshape(lines, nz)])
    fields = flat.reshape(10, nx, ny, nz)
    near, far = shape(NEAR, nx, nz), shape(FAR, nx, nz)
    near_twin, near_other = call(near_kernel, (near, near), [], 0.2, 1)(flat)
    near_rims = (
        lax.ppermute(near_twin, "gy", with_twin),
        lax.ppermute(near_other, "gy", with_other),
    )
    first = call(
        x_kernel,
        full,
        [
            vm((5, nx + 5, ny, nz), F32),
            vm((5, nx + 1, ny, nz), F32),
            vm((5, nx + 5, ny, nz), F32),
        ],
        2.8,
        2,
        2,
    )(fields, flags, near_twin, near_other)
    far_twin, far_other = call(far_kernel, (far, far), [], 0.2, 2, 1)(
        flat, flags.reshape(3 * nx * ny, nz), first
    )
    far_rims = (
        lax.ppermute(far_twin, "gy", with_twin),
        lax.ppermute(far_other, "gy", with_other),
    )
    *prepared, patches, patches_low = call(
        prepare_kernel,
        (
            half_shape(20 * ch, COLUMNS),
            half_shape(384, 512),
            half_shape(10 * ch, 192),
            shape(10 * ch, 128),
            half_shape((nx + 2) * 3 * MAIN, nz),
            half_shape((nx + 2) * 3 * MAIN, nz),
        ),
        [vm((2 * ch, 144), F32)],
        1.5,
        3,
        2,
    )(fields, kernel, heads, far_twin, far_other)
    near_rims, patches, first = lax.optimization_barrier((near_rims, patches, first))
    own, parts = call(
        c_kernel,
        (full, shape(ch, 256)),
        [
            *[vm(((nx + 2) * 3 * RIM, nz), BF16)] * 4,
            vm((nx * 120, nz), F32),
            vm((2 * RIM * nx, nz), F32),
            vm((16 * nx, nz), F32),
        ],
        5.5,
        10,
    )(fields, *near_rims, kernel, *prepared, patches, patches_low)

    def exchanged(value, bit):
        return lax.ppermute(value, "gy", [(i, i ^ bit) for i in range(count)])

    bits = [1 << b for b in range(count.bit_length() - 1)]
    sums = parts
    for bit in bits[:-4]:
        sums = sums + exchanged(sums, bit)
    z_half = lambda half, before, order: call(
        functools.partial(z_kernel, half), full, [], 1.9, 4, 1
    )(fields, flags, before, first, order)
    got = exchanged(sums, bits[-4])
    total = z_half(0, own, sums)
    got, total = lax.optimization_barrier((got, total))
    sums = sums + got
    got = exchanged(sums, bits[-3])
    total = z_half(1, total, sums)
    got, total = lax.optimization_barrier((got, total))
    sums = sums + got
    got = exchanged(sums, bits[-2])
    rim = call(e_kernel, shape(lines, nz), [], 1.1, 5, 1)(flat, *near_rims, *far_rims, sums)
    got, rim = lax.optimization_barrier((got, rim))
    sums = sums + got
    got = exchanged(sums, bits[-1])
    flow = call(y_kernel, full, [vm((lines, nz), F32)] * 2, 3.7, 8, 1)(
        fields, flags, *near_rims, *far_rims, total, rim, sums
    )
    got, flow = lax.optimization_barrier((got, flow))
    scale = float(cells * count) ** (-0.5)
    k_out, h_out = call(
        functools.partial(sum_kernel, scale), (shape(ch, taps), shape(5, ch)), [], 0.5, 2
    )(sums, got)
    return flow, k_out, h_out


def solution(mesh):
    split_y = P(None, "ens", "gy", None)
    return jax.shard_map(
        body,
        mesh=mesh,
        in_specs=(split_y, split_y, split_y, P(), P()),
        out_specs=(split_y, P("ens", None), P("ens", None)),
        check_vma=False,
    )
```

```python
import functools

import jax
import jax.numpy as jnp
from jax import lax
from jax.experimental import pallas as pl
from jax.experimental.pallas import tpu as pltpu
from jax.sharding import PartitionSpec as P

STEP = 0.3
FLOOR = 0.01
BELOW, ABOVE = 2, 3
SLABS = 2
WIDE = 4
VMEM = 48 * 1024 * 1024
F32 = jnp.float32
BF16 = jnp.bfloat16


def rcp(x):
    return pl.reciprocal(x, approx=True)


def shared_terms(v):
    p = [v[i + 1] - v[i] for i in range(5)]
    d = [p[i + 1] - p[i] for i in range(4)]
    h = [(4.0 / 3.0) * x for x in d]
    k = [h[i] * d[i] + FLOOR for i in range(4)]
    g = [x + x for x in h]
    t = [d[i + 1] - d[i] for i in range(3)]
    return p, d, k, g, t


def side_value(pa, pm, pm2, ka, kb, kc, m0, m2, td, t1, smooth, c0, c2):
    i0 = rcp(ka + pa * m0)
    i1 = rcp(kb + pa * pm)
    i2 = rcp(kc + pm * m2)
    w0 = i0 * i0
    w1 = 6.0 * (i1 * i1)
    w2 = 3.0 * (i2 * i2)
    r = rcp(w0 + w1 + w2)
    o0 = jnp.where(smooth, w0 * r, c0)
    o2 = jnp.where(smooth, w2 * r, c2)
    u = o0 * td + o2 * t1
    b0 = w0 * i0 * (td - u)
    b1 = w1 * i1 * u
    b2 = w2 * i2 * (t1 - u)
    return (pa + pm2) - u, (b0, b1, b2, r, o0, o2)


def side_pull(mu, pa, pm, m0, m2, smooth, saved):
    b0, b1, b2, r, o0, o2 = saved
    mu2 = mu + mu
    rm = jnp.where(smooth, mu2, 0.0) * r
    s0, s1, s2 = b0 * rm, b1 * rm, b2 * rm
    pa_bar = s0 * (m0 + pa) - s1 * pm + mu
    pm_bar = s2 * (m2 + pm) - s1 * pa + mu2
    return s0, s1, s2, pa_bar, pm_bar, o0 * mu2, o2 * mu


def hllc_pull(left, right, normal, flags, cot):
    region = flags & 3
    is_right = region >= 2
    star = ((region + 1) & 2) != 0
    n_at = 1 + normal
    tang = [1 + i for i in range(3) if i != normal]
    rl, rr_, pl_, pr_, nl, nr = left[0], right[0], left[4], right[4], left[n_at], right[n_at]

    def sound(r, p):
        inv = rcp(r)
        t = 1.4 * p * inv
        inv_c = lax.rsqrt(t)
        return inv, inv_c, t * inv_c

    inv_rl, inv_cl, cl = sound(rl, pl_)
    inv_rr, inv_cr, cr = sound(rr_, pr_)
    c = 0.5 * (cl + cr)
    r2 = rl + rr_
    inv = rcp(r2 * c)
    nm = 0.5 * (nl + nr)
    gap = (pl_ - pr_) * inv
    sm = nm + gap
    sc = jnp.where(is_right, c, -c)
    s = nm + sc
    pick = [jnp.where(is_right, right[i], left[i]) for i in range(5)]
    r, un, u1, u2, p = pick[0], pick[n_at], pick[tang[0]], pick[tang[1]], pick[4]
    a = s - un
    dl = sm - un
    si = jnp.where(star, rcp(sc - gap), 0.0)
    j = s * si
    kap = j * dl
    g0, gn, g1, g2, ge = cot[0], cot[n_at], cot[tang[0]], cot[tang[1]], cot[4]
    w = un + kap
    half_q = 0.5 * (un * un + u1 * u1 + u2 * u2)
    enthalpy = 3.5 * p + r * half_q
    b = g0 + u1 * g1 + u2 * g2 + un * gn
    m = r * b + enthalpy * ge
    n = gn + sm * ge
    rkap = r * kap
    f_kap = m + r * a * n
    f_a = rkap * n
    si2 = si * si
    s_bar = f_a - f_kap * (dl * sm * si2)
    sm_bar = f_kap * (s * a * si2) + rkap * a * ge
    wr = w * r
    k_bar = [None] * 5
    k_bar[0] = w * (b + half_q * ge) + kap * a * n
    k_bar[n_at] = m + wr * (gn + un * ge) - f_kap * j - f_a
    k_bar[tang[0]] = wr * (g1 + u1 * ge)
    k_bar[tang[1]] = wr * (g2 + u2 * ge)
    k_bar[4] = 3.5 * (w * ge) + gn
    e = sm_bar * inv
    eg = e * gap
    c_half = 0.5 * (jnp.where(is_right, s_bar, -s_bar) - eg * r2)
    n_half = 0.5 * (s_bar + sm_bar)
    r_both = -(eg * c)
    xl = c_half * inv_rl
    xr = c_half * inv_rr
    base_l = {0: r_both - 0.5 * (xl * cl), n_at: n_half, 4: 0.7 * (xl * inv_cl) + e}
    base_r = {0: r_both - 0.5 * (xr * cr), n_at: n_half, 4: 0.7 * (xr * inv_cr) - e}
    l_bar, r_bar = [], []
    for i in range(5):
        kr = jnp.where(is_right, k_bar[i], 0.0)
        kl = k_bar[i] - kr
        l_bar.append(base_l[i] + kl if i in base_l else kl)
        r_bar.append(base_r[i] + kr if i in base_r else kr)
    return l_bar, r_bar


def face_pull(cells, cot, flags, normal):
    stencil = flags >> 2
    smooth = stencil == 0
    c0 = jnp.where(stencil == 1, 1.0, 0.0)
    c2 = jnp.where(stencil == 3, 1.0, 0.0)
    left, right, kept = [], [], []
    for v in cells:
        p, d, k, g, t = shared_terms(v)
        pm2 = p[2] + p[2]
        args_l = (p[1], p[2], p[1] + d[0], p[2] - d[2], t[0] + t[0], t[1])
        args_r = (p[3], p[2], p[3] - d[3], p[2] + d[1], t[2] + t[2], t[1])
        hl, saved_l = side_value(
            p[1], p[2], pm2, k[0], k[1], k[2], *args_l[2:], smooth, c0, c2
        )
        hr, saved_r = side_value(
            p[3], p[2], pm2, k[3], k[2], k[1], *args_r[2:], smooth, c0, c2
        )
        left.append(v[2] + hl * (1.0 / 6.0))
        right.append(v[3] - hr * (1.0 / 6.0))
        kept.append((p, g, args_l[:4], args_r[:4], saved_l, saved_r))
    l_bar, r_bar = hllc_pull(left, right, normal, flags, cot)
    out = []
    for i in range(5):
        p, g, args_l, args_r, saved_l, saved_r = kept[i]
        a0, a1, a2, pa_l, pm_l, x0, x2 = side_pull(
            l_bar[i] * (1.0 / 6.0), *args_l, smooth, saved_l
        )
        b0, b1, b2, pa_r, pm_r, y0, y2 = side_pull(
            r_bar[i] * (-1.0 / 6.0), *args_r, smooth, saved_r
        )
        d0 = a0 * (g[0] + p[1]) + x0
        d1 = (b2 * (g[1] + p[2]) - a1 * g[1]) + (x2 - x0) + y2
        d2 = (a2 * (g[2] - p[2]) - b1 * g[2]) + (y0 - y2) - x2
        d3 = b0 * (g[3] - p[3]) - y0
        p2 = pa_l + (d0 - d1)
        p3 = pm_l + pm_r + (d1 - d2)
        p4 = pa_r + (d2 - d3)
        out.append([d0, -d0 - p2, l_bar[i] + (p2 - p3), r_bar[i] + (p3 - p4), p4 - d3, d3])
    return out


def conserved_pull(s, g):
    half_q = 0.5 * (s[1] * s[1] + s[2] * s[2] + s[3] * s[3])
    return [
        g[0] + s[1] * g[1] + s[2] * g[2] + s[3] * g[3] + half_q * g[4],
        s[0] * (g[1] + s[1] * g[4]),
        s[0] * (g[2] + s[2] * g[4]),
        s[0] * (g[3] + s[3] * g[4]),
        2.5 * g[4],
    ]


NEAR_STATE, FAR_STATE = 2, 3
NEAR_COT, FAR_COT = 1, 2
FLAG_ROWS = 3
NEAR = 5 * (NEAR_STATE + NEAR_COT)
FAR = 5 * (FAR_STATE + FAR_COT) + FLAG_ROWS


def views(fields):
    n = fields.shape[0] // 2
    return fields.at[pl.ds(0, n)], fields.at[pl.ds(n, n)]


def pack(ref, rows, first, twin, other, at):
    even = is_even()
    nx = twin.shape[1]
    count = ref.shape[0] // (8 * nx)
    for r in rows:
        for v in range(count):
            low = ref[pl.ds(v * nx * 8 + r, nx, stride=8), :].astype(F32)
            top = ref[pl.ds(v * nx * 8 + 7 - r, nx, stride=8), :].astype(F32)
            i = at + (r - first) * count + v
            twin[i] = jnp.where(even, top, low)
            other[i] = jnp.where(even, low, top)


def near_kernel(flat, twin, other):
    s, g = views(flat)
    pack(s, range(NEAR_STATE), 0, twin, other, 0)
    pack(g, range(NEAR_COT), 0, twin, other, 5 * NEAR_STATE)


def far_kernel(flat, flags, order, twin, other):
    del order
    s, g = views(flat)
    n = flags.shape[0] // 3
    pack(s, range(NEAR_STATE, NEAR_STATE + FAR_STATE), NEAR_STATE, twin, other, 0)
    pack(g, range(NEAR_COT, NEAR_COT + FAR_COT), NEAR_COT, twin, other, 5 * FAR_STATE)
    pack(flags.at[pl.ds(n, n)], range(FLAG_ROWS), 0, twin, other, FAR - FLAG_ROWS)


def from_rims(near_twin, near_other, far_twin=None, far_other=None):
    even = is_even()

    def pick(twin, other, i, below):
        if below:
            return jnp.where(even, other[i], twin[i])
        return jnp.where(even, twin[i], other[i])

    def read(row, near, near_at, far_at, v):
        below = row < 0
        r = -1 - row if below else row - 8
        if r < near:
            return pick(near_twin, near_other, near_at + r * 5 + v, below)
        return pick(far_twin, far_other, far_at + (r - near) * 5 + v, below)

    def state(row, v):
        return read(row, NEAR_STATE, 0, 0, v)

    def cot(row, v):
        return read(row, NEAR_COT, 5 * NEAR_STATE, 5 * FAR_STATE, v)

    def flags(row):
        below = row < 0
        r = -1 - row if below else row - 8
        return pick(far_twin, far_other, FAR - FLAG_ROWS + r, below).astype(jnp.int32)

    return state, cot, flags


def x_kernel(fields, flags, order, order2, out, pad, gpad, acc):
    del order, order2
    state, cot = views(fields)
    nx = state.shape[1]
    for v in range(5):
        pad[v, pl.ds(2, nx)] = state[v]
        pad[v, pl.ds(0, 2)] = state[v, pl.ds(nx - 2, 2)]
        pad[v, pl.ds(nx + 2, 3)] = state[v, pl.ds(0, 3)]
        gpad[v, pl.ds(0, nx)] = cot[v]
        gpad[v, pl.ds(nx, 1)] = cot[v, pl.ds(0, 1)]
    acc[...] = jnp.zeros_like(acc)

    def step(i, carry):
        x = i * SLABS
        cells = [[pad[v, pl.ds(x + k, SLABS)] for k in range(6)] for v in range(5)]
        g = [gpad[v, pl.ds(x, SLABS)] for v in range(5)]
        face = [STEP * (gpad[v, pl.ds(x + 1, SLABS)] - g[v]) for v in range(5)]
        terms = face_pull(cells, face, flags[0, pl.ds(x, SLABS)], 0)
        own = conserved_pull([cells[v][2] for v in range(5)], g)
        for v in range(5):
            terms[v][2] = terms[v][2] + own[v]
            for s in range(SLABS + 5):
                total = None
                for k in range(6):
                    if 0 <= s - k < SLABS:
                        part = terms[v][k][s - k]
                        total = part if total is None else total + part
                acc[v, x + s] = acc[v, x + s] + total
        return carry

    lax.fori_loop(0, nx // SLABS, step, 0)
    for v in range(5):
        acc[v, pl.ds(nx, 2)] = acc[v, pl.ds(nx, 2)] + acc[v, pl.ds(0, 2)]
        acc[v, pl.ds(2, 3)] = acc[v, pl.ds(2, 3)] + acc[v, pl.ds(nx + 2, 3)]

    for v in range(5):
        out[v] = acc[v, pl.ds(2, nx)]


def z_faces(state, cot, flags, x):
    cells, face = [], []
    for v in range(5):
        mid = state[v, pl.ds(x, SLABS)]
        cells.append([mid if k == 0 else pltpu.roll(mid, (-k) % 128, 2) for k in range(-2, 4)])
        g = cot[v, pl.ds(x, SLABS)]
        face.append(STEP * (pltpu.roll(g, 127, 2) - g))
    terms = face_pull(cells, face, flags[2, pl.ds(x, SLABS)], 2)
    total = []
    for v in range(5):
        t = terms[v][2]
        for k in (-2, -1, 1, 2, 3):
            t = t + pltpu.roll(terms[v][k + 2], k % 128, 2)
        total.append(t)
    return total


def e_kernel(flat, near_twin, near_other, far_twin, far_other, order, out):
    del order
    state, cot = views(flat)
    nx = out.shape[0] // 40
    rim_state, rim_cot, rim_flags = from_rims(near_twin, near_other, far_twin, far_other)

    def own(ref, row, v):
        return ref[pl.ds(v * nx * 8 + row, nx, stride=8), :]

    state_rows, cot_rows = {}, {}
    for v in range(5):
        for row in (*range(-5, 3), *range(6, 13)):
            inside = 0 <= row < 8
            state_rows[row, v] = own(state, row, v) if inside else rim_state(row, v)
        for row in (-3, -2, -1, 0, 8, 9, 10):
            inside = 0 <= row < 8
            cot_rows[row, v] = own(cot, row, v) if inside else rim_cot(row, v)
    sums = {}
    for j in (-3, -2, -1, 8, 9):
        cells = [[state_rows[j + k, v] for k in range(-2, 4)] for v in range(5)]
        face = [STEP * (cot_rows[j + 1, v] - cot_rows[j, v]) for v in range(5)]
        terms = face_pull(cells, face, rim_flags(j), 1)
        for v in range(5):
            for k in range(-2, 4):
                if 0 <= j + k < 8:
                    t = terms[v][k + 2]
                    sums[j + k, v] = sums[j + k, v] + t if (j + k, v) in sums else t
    for v in range(5):
        for row in range(8):
            value = sums[row, v] if (row, v) in sums else jnp.zeros((nx, 128), F32)
            out[pl.ds(v * nx * 8 + row, nx, stride=8), :] = value


def y_kernel(half, fields, flags, near_twin, near_other, far_twin, far_other, before, rim, order, out, halo, ghalo):
    del order
    state, cot = views(fields)
    rims = from_rims(near_twin, near_other, far_twin, far_other)
    rim_state, rim_cot, _ = rims
    nx = out.shape[1]
    part = nx // 2
    for v in range(5):
        kept = pl.ds((1 - half) * part, part)
        out[v, kept] = before[v, kept]
    for v in range(5):
        base = v * nx * 8
        for r in range(ABOVE):
            halo[pl.ds(base + r, nx, stride=8), :] = rim_state(8 + r, v)
        for r in range(BELOW):
            halo[pl.ds(base + 8 - BELOW + r, nx, stride=8), :] = rim_state(r - BELOW, v)
        ghalo[pl.ds(base, nx, stride=8), :] = rim_cot(8, v)
    row = lax.broadcasted_iota(jnp.int32, (SLABS, 8, 128), 1)
    inside = {}
    for k in (-2, -1, 1, 2, 3):
        inside[k] = (row < 8 + k) if k < 0 else (row >= k)

    def step(i, carry):
        x = half * part + i * SLABS
        cells, face = [], []
        for v in range(5):
            at = pl.multiple_of((v * nx + x) * 8, 8)
            rim_rows = halo[pl.ds(at, 8 * SLABS), :].reshape(SLABS, 8, 128)
            mid = state[v, pl.ds(x, SLABS)]
            line = []
            for k in range(-2, 4):
                if k == 0:
                    line.append(mid)
                else:
                    line.append(pltpu.roll(jnp.where(inside[k], mid, rim_rows), (-k) % 8, 1))
            cells.append(line)
            g = cot[v, pl.ds(x, SLABS)]
            g_rim = ghalo[pl.ds(at, 8 * SLABS), :].reshape(SLABS, 8, 128)
            face.append(STEP * (pltpu.roll(jnp.where(inside[1], g, g_rim), 7, 1) - g))
        terms = face_pull(cells, face, flags[1, pl.ds(x, SLABS)], 1)
        for v in range(5):
            at = pl.multiple_of((v * nx + x) * 8, 8)
            total = before[v, pl.ds(x, SLABS)] + terms[v][2]
            total = total + rim[pl.ds(at, 8 * SLABS), :].reshape(SLABS, 8, 128)
            for k in (-2, -1, 1, 2, 3):
                moved = pltpu.roll(terms[v][k + 2], k % 8, 1)
                total = total + jnp.where(inside[k], moved, 0.0)
            out[v, pl.ds(x, SLABS)] = total
        return carry

    lax.fori_loop(0, part // SLABS, step, 0)


def sum_kernel(scale, mine, theirs, k_out, h_out):
    total = (mine[...] + theirs[...]) * scale
    k_out[...] = total[:, : k_out.shape[1]]
    ch = total.shape[0]
    pick = (
        lax.broadcasted_iota(jnp.int32, (8, 128), 1)
        == lax.broadcasted_iota(jnp.int32, (8, 128), 0) + 16
    ).astype(F32)
    heads = lax.dot_general(
        pick,
        total[:, 128:],
        (((1,), (1,)), ((), ())),
        precision=lax.Precision.HIGHEST,
        preferred_element_type=F32,
    )
    h_out[...] = heads[: h_out.shape[0], :ch]


MAIN, RIM = 48, 16
OWN_COLUMNS = 9 * (MAIN + RIM)
COLUMNS = OWN_COLUMNS + 9 * RIM


def split(x):
    hi = x.astype(BF16)
    return hi, (x - hi.astype(F32)).astype(BF16)


def over_lanes(a, b):
    return lax.dot_general(a, b, (((1,), (1,)), ((), ())), preferred_element_type=F32)


def is_even():
    return lax.rem(lax.axis_index("gy"), 2) == 0


def put_patches(high, low, x, rows):
    n = rows.shape[0]
    hi, lo = split(rows)
    hi32, lo32 = hi.astype(F32), lo.astype(F32)
    for q, turn in enumerate((1, 0, 127)):
        at = pl.ds((x + 1) * 3 * n + q * n, n)
        high[at, :] = pltpu.roll(hi32, turn, 1).astype(BF16) if turn else hi
        low[at, :] = pltpu.roll(lo32, turn, 1).astype(BF16) if turn else lo


def wrap_patches(high, low, nx, rows):
    n = 3 * rows
    for ref in (high, low):
        ref[pl.ds(0, n), :] = ref[pl.ds(nx * n, n), :]
        ref[pl.ds((nx + 1) * n, n), :] = ref[pl.ds(n, n), :]


def prepare_kernel(fields, kernel, heads, order, order2, w_rows, w_cols, w_head, bias, t, t_low, wide):
    del order, order2
    state, _ = views(fields)
    nx = state.shape[1]
    for x in range(nx):
        rows = [state[v, x] - (1.0 if v in (0, 4) else 0.0) for v in range(5)]
        mid = jnp.concatenate([*rows, jnp.zeros((8, 128), F32)], axis=0)
        put_patches(t, t_low, x, mid)
    wrap_patches(t, t_low, nx, MAIN)

    ch, taps = kernel.shape
    w = kernel[...]
    hi, lo = split(w)
    wide[...] = jnp.zeros_like(wide)
    wide[pl.ds(0, ch), pl.ds(0, taps)] = hi.astype(F32)
    wide[pl.ds(ch, ch), pl.ds(0, taps)] = lo.astype(F32)
    both = wide[...].astype(BF16)
    kind, tap = columns(COLUMNS)
    base = jnp.dot(both, own_taps(kind, tap), preferred_element_type=F32)
    rim = jnp.dot(both, rim_taps(kind, tap), preferred_element_type=F32)
    n = base.shape[1]
    kind = jnp.broadcast_to(kind[0:1], base.shape)
    main = jnp.where(kind < 3, base, 0.0)
    bands = []
    for y in range(8):
        rows = main
        if y == 0:
            rows = jnp.where(kind == 0, 0.0, rows)
        if y == 7:
            rows = jnp.where(kind == 2, 0.0, rows)
        if y != 1:
            rows = pltpu.roll(rows, (y - 1) % n, 1)
        if y == 0:
            rows = rows + jnp.where(kind == 8, base, 0.0)
        if y == 7:
            rows = rows + jnp.where(kind == 10, base, 0.0)
        bands.append(rows)
    bands.append(jnp.where((kind == 0) | (kind == 8) | (kind == 9), rim, 0.0))
    bands.append(jnp.where((kind == 7) | (kind == 10) | (kind == 11), rim, 0.0))
    full = jnp.concatenate([b[:ch] for b in bands] + [b[ch:] for b in bands], axis=0)
    w_rows[...] = full.astype(BF16)
    kept = full.shape[0] // 2
    cols = jnp.concatenate([full[:kept], full[:kept], full[kept:]], axis=0)
    cols = jnp.concatenate([cols, jnp.zeros((512 - 3 * kept, n), F32)], axis=0)
    own_cols = []
    for q in range(3):
        own_cols += [cols[:, (3 * q + o) * MAIN : (3 * q + o) * MAIN + 40] for o in range(3)]
        own_cols.append(jnp.zeros((512, 8), F32))
    w_cols[...] = jnp.concatenate(own_cols, axis=1).T.astype(BF16)
    total = jnp.sum(w * level_taps(w.shape), axis=1, keepdims=True)
    total = jnp.broadcast_to(total, (ch, 128))
    bias[...] = jnp.concatenate([total] * 10, axis=0)

    h_hi, h_lo = split(STEP * heads[...])
    none = jnp.zeros((3, ch), F32)
    pair = jnp.concatenate([h_hi.astype(F32), none, h_lo.astype(F32), none], axis=0).astype(BF16)
    r = lax.broadcasted_iota(jnp.int32, (kept, ch), 0)
    q = lax.broadcasted_iota(jnp.int32, (kept, ch), 1)
    spread = jnp.where((r & (ch - 1)) == q, 1.0, 0.0).astype(BF16)
    picked = over_lanes(pair, spread)
    y_of = lax.broadcasted_iota(jnp.int32, (8, kept), 0)
    col = lax.broadcasted_iota(jnp.int32, (8, kept), 1)
    same = (col >= y_of * ch) & (col < (y_of + 1) * ch)
    split_heads = []
    for at in (0, 8):
        rows = [
            jnp.where(same, jnp.broadcast_to(picked[at + e : at + e + 1], (8, kept)), 0.0)
            for e in range(5)
        ]
        five = picked[at : at + 8]
        rows.append(jnp.where((col >= 8 * ch) & (col < 9 * ch), five, 0.0))
        rows.append(jnp.where(col >= 9 * ch, five, 0.0))
        rows.append(jnp.zeros((8, kept), F32))
        split_heads.append(jnp.concatenate(rows, axis=0))
    three = jnp.concatenate([split_heads[0], split_heads[1], split_heads[0]], axis=0)
    w_head[...] = three.T.astype(BF16)


def c_kernel(
    fields, flags, near_twin, near_other, kernel, w_rows, w_cols, w_head, bias, t, t_low, before,
    own, parts,
    rim, rim_low, outer, outer_low, acc, edge, gedge,
):
    state, cot = views(fields)
    nx = cot.shape[1]
    ch, taps = kernel.shape
    rim_state, rim_cot, _ = from_rims(near_twin, near_other)

    for v in range(5):
        level = 1.0 if v in (0, 4) else 0.0
        for q, row in enumerate((-1, 8, -2, 9)):
            at = q // 2 * RIM + 5 * (q % 2) + v
            edge[pl.ds(at, nx, stride=2 * RIM), :] = rim_state(row, v) - level
        gedge[pl.ds(v, nx, stride=16), :] = rim_cot(-1, v)
        gedge[pl.ds(8 + v, nx, stride=16), :] = rim_cot(8, v)
    none = jnp.zeros((nx, 128), F32)
    for q in range(10, RIM):
        edge[pl.ds(q, nx, stride=2 * RIM), :] = none
        edge[pl.ds(RIM + q, nx, stride=2 * RIM), :] = none
    for q in (5, 6, 7):
        gedge[pl.ds(q, nx, stride=16), :] = none
        gedge[pl.ds(8 + q, nx, stride=16), :] = none
    for x in range(nx):
        put_patches(rim, rim_low, x, edge[pl.ds(2 * x * RIM, RIM), :])
        put_patches(outer, outer_low, x, edge[pl.ds((2 * x + 1) * RIM, RIM), :])
    wrap_patches(rim, rim_low, nx, RIM)
    wrap_patches(outer, outer_low, nx, RIM)

    def gathered(x, *blocks):
        columns = []
        for j in range(WIDE):
            rows = [ref[pl.ds((x + j) * 3 * n, 9 * n), :] for ref, n in blocks]
            columns.append(jnp.concatenate(rows, axis=0) if len(rows) > 1 else rows[0])
        return jnp.concatenate(columns, axis=1)

    kept = 8 * ch
    kg = hg = dsum = None
    zeros8 = jnp.zeros((8, 128 * WIDE), F32)
    written = set()
    for x in range(0, nx, WIDE):
        s_hi = gathered(x, (t, MAIN), (rim, RIM))
        s_lo = gathered(x, (t_low, MAIN), (rim_low, RIM))
        far_hi, far_lo = gathered(x, (outer, RIM)), gathered(x, (outer_low, RIM))
        z2 = jnp.dot(
            w_rows[...], jnp.concatenate([s_hi, far_hi], axis=0), preferred_element_type=F32
        )
        rows = z2.shape[0] // 2
        z3 = jnp.dot(
            w_rows[pl.ds(0, rows), :],
            jnp.concatenate([s_lo, far_lo], axis=0),
            preferred_element_type=F32,
        )
        for here in range(x, x + WIDE, SLABS):
            faces = z_faces(state, cot, flags, here)
            for v in range(5):
                own[v, pl.ds(here, SLABS)] = before[v, pl.ds(here, SLABS)] + faces[v]
        z = z2[:rows] + (z2[rows:] + z3) + jnp.concatenate([bias[...]] * WIDE, axis=1)
        hidden = jnp.tanh(z)
        g = jnp.concatenate(
            [
                jnp.concatenate(
                    [cot[v, x + j] for v in range(5)] + [gedge[pl.ds((x + j) * 16, 16), :]], axis=0
                )
                for j in range(WIDE)
            ],
            axis=1,
        )
        g_hi, g_lo = split(g)
        g_hi32, g_lo32 = g_hi.astype(F32), g_lo.astype(F32)
        g3 = jnp.concatenate(
            [g_hi32, zeros8, g_hi32, zeros8, g_lo32, zeros8], axis=0
        ).astype(BF16)
        d = (1.0 - hidden * hidden) * jnp.dot(w_head[...], g3, preferred_element_type=F32)
        d_hi, d_lo = split(d)
        zeros = jnp.zeros((512 - 3 * rows, 128 * WIDE), BF16)
        back = jnp.dot(
            w_cols[...],
            jnp.concatenate([d_hi, d_lo, d_hi, zeros], axis=0),
            preferred_element_type=F32,
        )
        k2 = over_lanes(
            jnp.concatenate([s_hi, s_lo], axis=0),
            jnp.concatenate([d_hi[:kept], d_lo[:kept]], axis=0),
        )
        k2 = k2[:OWN_COLUMNS, :kept] + (k2[:OWN_COLUMNS, kept:] + k2[OWN_COLUMNS:, :kept])
        kg = k2 if kg is None else kg + k2
        hid2 = jnp.concatenate(split(hidden[:kept]), axis=0)
        g2 = jnp.concatenate([g_hi32[:40], g_lo32[:40]], axis=0).astype(BF16)
        h2 = over_lanes(g2, hid2)
        hg = h2 if hg is None else hg + h2
        for j in range(WIDE):
            level = d[:kept, 128 * j : 128 * (j + 1)]
            dsum = level if dsum is None else dsum + level
        for m in range(WIDE + 2):
            total = None
            for j in range(WIDE):
                if 0 <= m - j < 3:
                    q = m - j
                    piece = back[q * 128 : q * 128 + 120, 128 * j : 128 * (j + 1)]
                    total = piece if total is None else total + piece
            here = (x + m - 1) % nx
            if here in written:
                total = total + acc[pl.ds(here * 120, 120), :]
            written.add(here)
            acc[pl.ds(here * 120, 120), :] = total
    for x in range(nx):
        at = x * 120
        total = (
            acc[pl.ds(at + 40, 40), :]
            + pltpu.roll(acc[pl.ds(at, 40), :], 127, 1)
            + pltpu.roll(acc[pl.ds(at + 80, 40), :], 1, 1)
        )
        for v in range(5):
            own[v, x] = own[v, x] + total[8 * v : 8 * v + 8]

    sums = jnp.sum(dsum, axis=1, keepdims=True)
    kg = kg.T
    hg = (hg[:40, :kept] + hg[40:, :kept]) + (hg[:40, kept:] + hg[40:, kept:])
    y_row = lax.broadcasted_iota(jnp.int32, (40, kept), 0) & 7
    y_col = lax.broadcasted_iota(jnp.int32, (40, kept), 1)
    same_y = (y_col >= y_row * ch) & (y_col < (y_row + 1) * ch)
    hg = jnp.where(same_y, hg, 0.0)
    by_eq = jnp.concatenate(
        [jnp.sum(hg[8 * e : 8 * e + 8], axis=0, keepdims=True) for e in range(5)]
        + [jnp.zeros((123, kept), F32)],
        axis=0,
    ).T
    level_sum = jnp.zeros((ch, 1), F32)
    head_sum = jnp.zeros((ch, 128), F32)
    n = kg.shape[1]
    columns_at, tap = columns(n)
    kind = jnp.broadcast_to(columns_at[0:1], (ch, n))
    total = jnp.zeros((ch, n), F32)
    for y in range(8):
        rows = kg[y * ch : (y + 1) * ch]
        moved = rows if y == 1 else pltpu.roll(rows, (1 - y) % n, 1)
        keep = kind < 3
        if y == 0:
            keep = (kind == 1) | (kind == 2)
            total = total + jnp.where(kind == 8, rows, 0.0)
        if y == 7:
            keep = kind < 2
            total = total + jnp.where(kind == 10, rows, 0.0)
        total = total + jnp.where(keep, moved, 0.0)
        level_sum = level_sum + sums[y * ch : (y + 1) * ch]
        head_sum = head_sum + by_eq[y * ch : (y + 1) * ch]
    grads = over_lanes(jnp.concatenate(split(total), axis=0), own_taps(columns_at, tap))
    n_pick = grads.shape[1]
    parts[...] = jnp.zeros_like(parts)
    parts[:, pl.ds(0, n_pick)] = grads[:ch] + grads[ch:]
    parts[:, pl.ds(0, taps)] = parts[:, pl.ds(0, taps)] + level_sum * level_taps((ch, taps))
    parts[:, pl.ds(128, 128)] = parts[:, pl.ds(128, 128)] + pltpu.roll(head_sum * STEP, 16, 1)


def columns(n):
    lane = lax.broadcasted_iota(jnp.int32, (8, n), 1)
    main = lane < 9 * MAIN
    far = lane >= OWN_COLUMNS
    past = lane - jnp.where(far, OWN_COLUMNS, 9 * MAIN)
    block = sum((lane >= MAIN * i).astype(jnp.int32) for i in range(1, 9))
    o = jnp.where(main, block, past >> 4)
    r = jnp.where(main, lane - MAIN * block, past & (RIM - 1))
    second = (r >= 5).astype(jnp.int32)
    rim = jnp.where(r < 10, 8 + 2 * second + far.astype(jnp.int32), 12)
    kind = jnp.where(main, jnp.where(r < 40, r & 7, 12), rim)
    v = jnp.where(main, r >> 3, r - 5 * second)
    return kind, o * 5 + v


def taps_of(columns_at):
    n = columns_at.shape[1]
    row = lax.broadcasted_iota(jnp.int32, (144, n), 0)
    return jnp.where(row == jnp.broadcast_to(columns_at[0:1], (144, n)), 1.0, 0.0).astype(BF16)


def own_taps(kind, tap):
    at = jnp.where(kind < 3, tap + 45 * kind, 1000)
    at = jnp.where(kind == 8, tap, at)
    return taps_of(jnp.where(kind == 10, tap + 90, at))


def rim_taps(kind, tap):
    first = (kind == 9) | (kind == 7)
    middle = (kind == 8) | (kind == 10)
    last = (kind == 0) | (kind == 11)
    at = jnp.where(first, tap, jnp.where(middle, tap + 45, 1000))
    return taps_of(jnp.where(last, tap + 90, at))


def level_taps(shape):
    t = lax.broadcasted_iota(jnp.int32, shape, 1).astype(F32)
    v = t - 5.0 * jnp.floor((t + 0.5) * 0.2)
    return jnp.where((v < 0.5) | (v > 3.5), 1.0, 0.0)


def call(kernel, outs, scratch, us, n_in, order=0):
    spec = pl.BlockSpec(memory_space=pltpu.VMEM)
    return pl.pallas_call(
        kernel,
        out_shape=outs,
        in_specs=[spec] * n_in + [pl.BlockSpec(memory_space=pl.ANY)] * order,
        scratch_shapes=scratch,
        compiler_params=pltpu.CompilerParams(vmem_limit_bytes=VMEM),
        cost_estimate=pl.CostEstimate(
            flops=int(us * 1.15e9), bytes_accessed=int(us * 3.69e6), transcendentals=0
        ),
    )


def body(state, cot, flags, kernel, heads):
    _, nx, ny, nz = state.shape
    ch, taps = kernel.shape
    count = lax.axis_size("gy")
    cells = nx * ny * nz
    shape = lambda *dims: jax.ShapeDtypeStruct(dims, F32)
    half_shape = lambda *dims: jax.ShapeDtypeStruct(dims, BF16)
    full = shape(5, nx, ny, nz)
    with_twin = [(i, i ^ 1) for i in range(count)]
    with_other = [(i, (i + 1) % count if i % 2 else (i - 1) % count) for i in range(count)]
    vm = pltpu.VMEM
    lines = 5 * nx * ny

    flat = jnp.concatenate([state.reshape(lines, nz), cot.reshape(lines, nz)])
    fields = flat.reshape(10, nx, ny, nz)
    near, far = shape(NEAR, nx, nz), shape(FAR, nx, nz)
    near_twin, near_other = call(near_kernel, (near, near), [], 0.2, 1)(flat)
    near_rims = (
        lax.ppermute(near_twin, "gy", with_twin),
        lax.ppermute(near_other, "gy", with_other),
    )
    first = call(
        x_kernel,
        full,
        [
            vm((5, nx + 5, ny, nz), F32),
            vm((5, nx + 1, ny, nz), F32),
            vm((5, nx + 5, ny, nz), F32),
        ],
        2.8,
        2,
        2,
    )(fields, flags, near_twin, near_other)
    far_twin, far_other = call(far_kernel, (far, far), [], 0.2, 2, 1)(
        flat, flags.reshape(3 * nx * ny, nz), first
    )
    far_rims = (
        lax.ppermute(far_twin, "gy", with_twin),
        lax.ppermute(far_other, "gy", with_other),
    )
    *prepared, patches, patches_low = call(
        prepare_kernel,
        (
            half_shape(20 * ch, COLUMNS),
            half_shape(384, 512),
            half_shape(10 * ch, 192),
            shape(10 * ch, 128),
            half_shape((nx + 2) * 3 * MAIN, nz),
            half_shape((nx + 2) * 3 * MAIN, nz),
        ),
        [vm((2 * ch, 144), F32)],
        1.5,
        3,
        2,
    )(fields, kernel, heads, far_twin, far_other)
    near_rims, patches, first = lax.optimization_barrier((near_rims, patches, first))
    own, parts = call(
        c_kernel,
        (full, shape(ch, 256)),
        [
            *[vm(((nx + 2) * 3 * RIM, nz), BF16)] * 4,
            vm((nx * 120, nz), F32),
            vm((2 * RIM * nx, nz), F32),
            vm((16 * nx, nz), F32),
        ],
        8.0,
        12,
    )(fields, flags, *near_rims, kernel, *prepared, patches, patches_low, first)

    def exchanged(value, bit):
        return lax.ppermute(value, "gy", [(i, i ^ bit) for i in range(count)])

    bits = [1 << b for b in range(count.bit_length() - 1)]
    sums = parts
    for bit in bits[:-4]:
        sums = sums + exchanged(sums, bit)
    y_half = lambda half, before, order: call(
        functools.partial(y_kernel, half), full, [vm((lines, nz), F32)] * 2, 1.9, 8, 1
    )(fields, flags, *near_rims, *far_rims, before, rim, order)
    sums = sums + exchanged(sums, bits[-4])
    got = exchanged(sums, bits[-3])
    rim = call(e_kernel, shape(lines, nz), [], 1.1, 5, 1)(flat, *near_rims, *far_rims, sums)
    got, rim = lax.optimization_barrier((got, rim))
    sums = sums + got
    got = exchanged(sums, bits[-2])
    total = y_half(0, own, sums)
    got, total = lax.optimization_barrier((got, total))
    sums = sums + got
    got = exchanged(sums, bits[-1])
    flow = y_half(1, total, sums)
    got, flow = lax.optimization_barrier((got, flow))
    scale = float(cells * count) ** (-0.5)
    k_out, h_out = call(
        functools.partial(sum_kernel, scale), (shape(ch, taps), shape(5, ch)), [], 0.5, 2
    )(sums, got)
    return flow, k_out, h_out


def solution(mesh):
    split_y = P(None, "ens", "gy", None)
    return jax.shard_map(
        body,
        mesh=mesh,
        in_specs=(split_y, split_y, split_y, P(), P()),
        out_specs=(split_y, P("ens", None), P("ens", None)),
        check_vma=False,
    )
```

```python
import functools

import jax
import jax.numpy as jnp
from jax import lax
from jax.experimental import pallas as pl
from jax.experimental.pallas import tpu as pltpu
from jax.sharding import PartitionSpec as P

STEP = 0.3
FLOOR = 0.01
BELOW, ABOVE = 2, 3
SLABS = 2
WIDE = 4
VMEM = 48 * 1024 * 1024
F32 = jnp.float32
BF16 = jnp.bfloat16


def rcp(x):
    return pl.reciprocal(x, approx=True)


def shared_terms(v):
    p = [v[i + 1] - v[i] for i in range(5)]
    d = [p[i + 1] - p[i] for i in range(4)]
    h = [(4.0 / 3.0) * x for x in d]
    k = [h[i] * d[i] + FLOOR for i in range(4)]
    g = [x + x for x in h]
    t = [d[i + 1] - d[i] for i in range(3)]
    return p, d, k, g, t


def side_value(pa, pm, pm2, ka, kb, kc, m0, m2, td, t1, smooth, c0, c2):
    i0 = rcp(ka + pa * m0)
    i1 = rcp(kb + pa * pm)
    i2 = rcp(kc + pm * m2)
    w0 = i0 * i0
    w1 = 6.0 * (i1 * i1)
    w2 = 3.0 * (i2 * i2)
    r = rcp(w0 + w1 + w2)
    o0 = jnp.where(smooth, w0 * r, c0)
    o2 = jnp.where(smooth, w2 * r, c2)
    u = o0 * td + o2 * t1
    b0 = w0 * i0 * (td - u)
    b1 = w1 * i1 * u
    b2 = w2 * i2 * (t1 - u)
    return (pa + pm2) - u, (b0, b1, b2, r, o0, o2)


def side_pull(mu, pa, pm, m0, m2, smooth, saved):
    b0, b1, b2, r, o0, o2 = saved
    mu2 = mu + mu
    rm = jnp.where(smooth, mu2, 0.0) * r
    s0, s1, s2 = b0 * rm, b1 * rm, b2 * rm
    pa_bar = s0 * (m0 + pa) - s1 * pm + mu
    pm_bar = s2 * (m2 + pm) - s1 * pa + mu2
    return s0, s1, s2, pa_bar, pm_bar, o0 * mu2, o2 * mu


def hllc_pull(left, right, normal, flags, cot):
    region = flags & 3
    is_right = region >= 2
    star = ((region + 1) & 2) != 0
    n_at = 1 + normal
    tang = [1 + i for i in range(3) if i != normal]
    rl, rr_, pl_, pr_, nl, nr = left[0], right[0], left[4], right[4], left[n_at], right[n_at]

    def sound(r, p):
        inv = rcp(r)
        t = 1.4 * p * inv
        inv_c = lax.rsqrt(t)
        return inv, inv_c, t * inv_c

    inv_rl, inv_cl, cl = sound(rl, pl_)
    inv_rr, inv_cr, cr = sound(rr_, pr_)
    c = 0.5 * (cl + cr)
    r2 = rl + rr_
    inv = rcp(r2 * c)
    nm = 0.5 * (nl + nr)
    gap = (pl_ - pr_) * inv
    sm = nm + gap
    sc = jnp.where(is_right, c, -c)
    s = nm + sc
    pick = [jnp.where(is_right, right[i], left[i]) for i in range(5)]
    r, un, u1, u2, p = pick[0], pick[n_at], pick[tang[0]], pick[tang[1]], pick[4]
    a = s - un
    dl = sm - un
    si = jnp.where(star, rcp(sc - gap), 0.0)
    j = s * si
    kap = j * dl
    g0, gn, g1, g2, ge = cot[0], cot[n_at], cot[tang[0]], cot[tang[1]], cot[4]
    w = un + kap
    half_q = 0.5 * (un * un + u1 * u1 + u2 * u2)
    enthalpy = 3.5 * p + r * half_q
    b = g0 + u1 * g1 + u2 * g2 + un * gn
    m = r * b + enthalpy * ge
    n = gn + sm * ge
    rkap = r * kap
    f_kap = m + r * a * n
    f_a = rkap * n
    si2 = si * si
    s_bar = f_a - f_kap * (dl * sm * si2)
    sm_bar = f_kap * (s * a * si2) + rkap * a * ge
    wr = w * r
    k_bar = [None] * 5
    k_bar[0] = w * (b + half_q * ge) + kap * a * n
    k_bar[n_at] = m + wr * (gn + un * ge) - f_kap * j - f_a
    k_bar[tang[0]] = wr * (g1 + u1 * ge)
    k_bar[tang[1]] = wr * (g2 + u2 * ge)
    k_bar[4] = 3.5 * (w * ge) + gn
    e = sm_bar * inv
    eg = e * gap
    c_half = 0.5 * (jnp.where(is_right, s_bar, -s_bar) - eg * r2)
    n_half = 0.5 * (s_bar + sm_bar)
    r_both = -(eg * c)
    xl = c_half * inv_rl
    xr = c_half * inv_rr
    base_l = {0: r_both - 0.5 * (xl * cl), n_at: n_half, 4: 0.7 * (xl * inv_cl) + e}
    base_r = {0: r_both - 0.5 * (xr * cr), n_at: n_half, 4: 0.7 * (xr * inv_cr) - e}
    l_bar, r_bar = [], []
    for i in range(5):
        kr = jnp.where(is_right, k_bar[i], 0.0)
        kl = k_bar[i] - kr
        l_bar.append(base_l[i] + kl if i in base_l else kl)
        r_bar.append(base_r[i] + kr if i in base_r else kr)
    return l_bar, r_bar


def face_pull(cells, cot, flags, normal):
    stencil = flags >> 2
    smooth = stencil == 0
    c0 = jnp.where(stencil == 1, 1.0, 0.0)
    c2 = jnp.where(stencil == 3, 1.0, 0.0)
    left, right, kept = [], [], []
    for v in cells:
        p, d, k, g, t = shared_terms(v)
        pm2 = p[2] + p[2]
        args_l = (p[1], p[2], p[1] + d[0], p[2] - d[2], t[0] + t[0], t[1])
        args_r = (p[3], p[2], p[3] - d[3], p[2] + d[1], t[2] + t[2], t[1])
        hl, saved_l = side_value(
            p[1], p[2], pm2, k[0], k[1], k[2], *args_l[2:], smooth, c0, c2
        )
        hr, saved_r = side_value(
            p[3], p[2], pm2, k[3], k[2], k[1], *args_r[2:], smooth, c0, c2
        )
        left.append(v[2] + hl * (1.0 / 6.0))
        right.append(v[3] - hr * (1.0 / 6.0))
        kept.append((p, g, args_l[:4], args_r[:4], saved_l, saved_r))
    l_bar, r_bar = hllc_pull(left, right, normal, flags, cot)
    out = []
    for i in range(5):
        p, g, args_l, args_r, saved_l, saved_r = kept[i]
        a0, a1, a2, pa_l, pm_l, x0, x2 = side_pull(
            l_bar[i] * (1.0 / 6.0), *args_l, smooth, saved_l
        )
        b0, b1, b2, pa_r, pm_r, y0, y2 = side_pull(
            r_bar[i] * (-1.0 / 6.0), *args_r, smooth, saved_r
        )
        d0 = a0 * (g[0] + p[1]) + x0
        d1 = (b2 * (g[1] + p[2]) - a1 * g[1]) + (x2 - x0) + y2
        d2 = (a2 * (g[2] - p[2]) - b1 * g[2]) + (y0 - y2) - x2
        d3 = b0 * (g[3] - p[3]) - y0
        p2 = pa_l + (d0 - d1)
        p3 = pm_l + pm_r + (d1 - d2)
        p4 = pa_r + (d2 - d3)
        out.append([d0, -d0 - p2, l_bar[i] + (p2 - p3), r_bar[i] + (p3 - p4), p4 - d3, d3])
    return out


def conserved_pull(s, g):
    half_q = 0.5 * (s[1] * s[1] + s[2] * s[2] + s[3] * s[3])
    return [
        g[0] + s[1] * g[1] + s[2] * g[2] + s[3] * g[3] + half_q * g[4],
        s[0] * (g[1] + s[1] * g[4]),
        s[0] * (g[2] + s[2] * g[4]),
        s[0] * (g[3] + s[3] * g[4]),
        2.5 * g[4],
    ]


NEAR_STATE, FAR_STATE = 2, 3
NEAR_COT, FAR_COT = 1, 2
FLAG_ROWS = 3
NEAR = 5 * (NEAR_STATE + NEAR_COT)
FAR = 5 * (FAR_STATE + FAR_COT) + FLAG_ROWS


def views(fields):
    n = fields.shape[0] // 2
    return fields.at[pl.ds(0, n)], fields.at[pl.ds(n, n)]


def pack(ref, rows, first, twin, other, at):
    even = is_even()
    nx = twin.shape[1]
    count = ref.shape[0] // (8 * nx)
    for r in rows:
        for v in range(count):
            low = ref[pl.ds(v * nx * 8 + r, nx, stride=8), :].astype(F32)
            top = ref[pl.ds(v * nx * 8 + 7 - r, nx, stride=8), :].astype(F32)
            i = at + (r - first) * count + v
            twin[i] = jnp.where(even, top, low)
            other[i] = jnp.where(even, low, top)


def near_kernel(flat, twin, other):
    s, g = views(flat)
    pack(s, range(NEAR_STATE), 0, twin, other, 0)
    pack(g, range(NEAR_COT), 0, twin, other, 5 * NEAR_STATE)


def far_kernel(flat, flags, order, twin, other):
    del order
    s, g = views(flat)
    n = flags.shape[0] // 3
    pack(s, range(NEAR_STATE, NEAR_STATE + FAR_STATE), NEAR_STATE, twin, other, 0)
    pack(g, range(NEAR_COT, NEAR_COT + FAR_COT), NEAR_COT, twin, other, 5 * FAR_STATE)
    pack(flags.at[pl.ds(n, n)], range(FLAG_ROWS), 0, twin, other, FAR - FLAG_ROWS)


def from_rims(near_twin, near_other, far_twin=None, far_other=None):
    even = is_even()

    def pick(twin, other, i, below):
        if below:
            return jnp.where(even, other[i], twin[i])
        return jnp.where(even, twin[i], other[i])

    def read(row, near, near_at, far_at, v):
        below = row < 0
        r = -1 - row if below else row - 8
        if r < near:
            return pick(near_twin, near_other, near_at + r * 5 + v, below)
        return pick(far_twin, far_other, far_at + (r - near) * 5 + v, below)

    def state(row, v):
        return read(row, NEAR_STATE, 0, 0, v)

    def cot(row, v):
        return read(row, NEAR_COT, 5 * NEAR_STATE, 5 * FAR_STATE, v)

    def flags(row):
        below = row < 0
        r = -1 - row if below else row - 8
        return pick(far_twin, far_other, FAR - FLAG_ROWS + r, below).astype(jnp.int32)

    return state, cot, flags


def x_kernel(fields, flags, before, order, out, pad, gpad, acc):
    del order
    state, cot = views(fields)
    nx = state.shape[1]
    for v in range(5):
        pad[v, pl.ds(2, nx)] = state[v]
        pad[v, pl.ds(0, 2)] = state[v, pl.ds(nx - 2, 2)]
        pad[v, pl.ds(nx + 2, 3)] = state[v, pl.ds(0, 3)]
        gpad[v, pl.ds(0, nx)] = cot[v]
        gpad[v, pl.ds(nx, 1)] = cot[v, pl.ds(0, 1)]
    acc[...] = jnp.zeros_like(acc)

    def step(i, carry):
        x = i * SLABS
        cells = [[pad[v, pl.ds(x + k, SLABS)] for k in range(6)] for v in range(5)]
        g = [gpad[v, pl.ds(x, SLABS)] for v in range(5)]
        face = [STEP * (gpad[v, pl.ds(x + 1, SLABS)] - g[v]) for v in range(5)]
        terms = face_pull(cells, face, flags[0, pl.ds(x, SLABS)], 0)
        own = conserved_pull([cells[v][2] for v in range(5)], g)
        for v in range(5):
            terms[v][2] = terms[v][2] + own[v]
            for s in range(SLABS + 5):
                total = None
                for k in range(6):
                    if 0 <= s - k < SLABS:
                        part = terms[v][k][s - k]
                        total = part if total is None else total + part
                acc[v, x + s] = acc[v, x + s] + total
        return carry

    lax.fori_loop(0, nx // SLABS, step, 0)
    for v in range(5):
        acc[v, pl.ds(nx, 2)] = acc[v, pl.ds(nx, 2)] + acc[v, pl.ds(0, 2)]
        acc[v, pl.ds(2, 3)] = acc[v, pl.ds(2, 3)] + acc[v, pl.ds(nx + 2, 3)]

    for v in range(5):
        out[v] = acc[v, pl.ds(2, nx)] + before[v]


def z_faces(state, cot, flags, x):
    cells, face = [], []
    for v in range(5):
        mid = state[v, pl.ds(x, SLABS)]
        cells.append([mid if k == 0 else pltpu.roll(mid, (-k) % 128, 2) for k in range(-2, 4)])
        g = cot[v, pl.ds(x, SLABS)]
        face.append(STEP * (pltpu.roll(g, 127, 2) - g))
    terms = face_pull(cells, face, flags[2, pl.ds(x, SLABS)], 2)
    total = []
    for v in range(5):
        t = terms[v][2]
        for k in (-2, -1, 1, 2, 3):
            t = t + pltpu.roll(terms[v][k + 2], k % 128, 2)
        total.append(t)
    return total


def e_kernel(flat, near_twin, near_other, far_twin, far_other, order, out):
    del order
    state, cot = views(flat)
    nx = out.shape[0] // 40
    rim_state, rim_cot, rim_flags = from_rims(near_twin, near_other, far_twin, far_other)

    def own(ref, row, v):
        return ref[pl.ds(v * nx * 8 + row, nx, stride=8), :]

    state_rows, cot_rows = {}, {}
    for v in range(5):
        for row in (*range(-5, 3), *range(6, 13)):
            inside = 0 <= row < 8
            state_rows[row, v] = own(state, row, v) if inside else rim_state(row, v)
        for row in (-3, -2, -1, 0, 8, 9, 10):
            inside = 0 <= row < 8
            cot_rows[row, v] = own(cot, row, v) if inside else rim_cot(row, v)
    sums = {}
    for j in (-3, -2, -1, 8, 9):
        cells = [[state_rows[j + k, v] for k in range(-2, 4)] for v in range(5)]
        face = [STEP * (cot_rows[j + 1, v] - cot_rows[j, v]) for v in range(5)]
        terms = face_pull(cells, face, rim_flags(j), 1)
        for v in range(5):
            for k in range(-2, 4):
                if 0 <= j + k < 8:
                    t = terms[v][k + 2]
                    sums[j + k, v] = sums[j + k, v] + t if (j + k, v) in sums else t
    for v in range(5):
        for row in range(8):
            value = sums[row, v] if (row, v) in sums else jnp.zeros((nx, 128), F32)
            out[pl.ds(v * nx * 8 + row, nx, stride=8), :] = value


def yz_kernel(half, fields, flags, near_twin, near_other, far_twin, far_other, before, rim, order, out, halo, ghalo):
    del order
    state, cot = views(fields)
    rims = from_rims(near_twin, near_other, far_twin, far_other)
    rim_state, rim_cot, _ = rims
    nx = out.shape[1]
    part = nx // 2
    for v in range(5):
        kept = pl.ds((1 - half) * part, part)
        out[v, kept] = before[v, kept]
    for v in range(5):
        base = v * nx * 8
        for r in range(ABOVE):
            halo[pl.ds(base + r, nx, stride=8), :] = rim_state(8 + r, v)
        for r in range(BELOW):
            halo[pl.ds(base + 8 - BELOW + r, nx, stride=8), :] = rim_state(r - BELOW, v)
        ghalo[pl.ds(base, nx, stride=8), :] = rim_cot(8, v)
    row = lax.broadcasted_iota(jnp.int32, (SLABS, 8, 128), 1)
    inside = {}
    for k in (-2, -1, 1, 2, 3):
        inside[k] = (row < 8 + k) if k < 0 else (row >= k)

    def step(i, carry):
        x = half * part + i * SLABS
        cells, face = [], []
        for v in range(5):
            at = pl.multiple_of((v * nx + x) * 8, 8)
            rim_rows = halo[pl.ds(at, 8 * SLABS), :].reshape(SLABS, 8, 128)
            mid = state[v, pl.ds(x, SLABS)]
            line = []
            for k in range(-2, 4):
                if k == 0:
                    line.append(mid)
                else:
                    line.append(pltpu.roll(jnp.where(inside[k], mid, rim_rows), (-k) % 8, 1))
            cells.append(line)
            g = cot[v, pl.ds(x, SLABS)]
            g_rim = ghalo[pl.ds(at, 8 * SLABS), :].reshape(SLABS, 8, 128)
            face.append(STEP * (pltpu.roll(jnp.where(inside[1], g, g_rim), 7, 1) - g))
        terms = face_pull(cells, face, flags[1, pl.ds(x, SLABS)], 1)
        along_z = z_faces(state, cot, flags, x)
        for v in range(5):
            at = pl.multiple_of((v * nx + x) * 8, 8)
            total = before[v, pl.ds(x, SLABS)] + along_z[v] + terms[v][2]
            total = total + rim[pl.ds(at, 8 * SLABS), :].reshape(SLABS, 8, 128)
            for k in (-2, -1, 1, 2, 3):
                moved = pltpu.roll(terms[v][k + 2], k % 8, 1)
                total = total + jnp.where(inside[k], moved, 0.0)
            out[v, pl.ds(x, SLABS)] = total
        return carry

    lax.fori_loop(0, part // SLABS, step, 0)


def sum_kernel(scale, mine, theirs, k_out, h_out):
    total = (mine[...] + theirs[...]) * scale
    k_out[...] = total[:, : k_out.shape[1]]
    ch = total.shape[0]
    pick = (
        lax.broadcasted_iota(jnp.int32, (8, 128), 1)
        == lax.broadcasted_iota(jnp.int32, (8, 128), 0) + 16
    ).astype(F32)
    heads = lax.dot_general(
        pick,
        total[:, 128:],
        (((1,), (1,)), ((), ())),
        precision=lax.Precision.HIGHEST,
        preferred_element_type=F32,
    )
    h_out[...] = heads[: h_out.shape[0], :ch]


MAIN, RIM = 48, 16
OWN_COLUMNS = 9 * (MAIN + RIM)
COLUMNS = OWN_COLUMNS + 9 * RIM


def split(x):
    hi = x.astype(BF16)
    return hi, (x - hi.astype(F32)).astype(BF16)


def over_lanes(a, b):
    return lax.dot_general(a, b, (((1,), (1,)), ((), ())), preferred_element_type=F32)


def is_even():
    return lax.rem(lax.axis_index("gy"), 2) == 0


def put_patches(high, low, x, rows):
    n = rows.shape[0]
    hi, lo = split(rows)
    hi32, lo32 = hi.astype(F32), lo.astype(F32)
    for q, turn in enumerate((1, 0, 127)):
        at = pl.ds((x + 1) * 3 * n + q * n, n)
        high[at, :] = pltpu.roll(hi32, turn, 1).astype(BF16) if turn else hi
        low[at, :] = pltpu.roll(lo32, turn, 1).astype(BF16) if turn else lo


def wrap_patches(high, low, nx, rows):
    n = 3 * rows
    for ref in (high, low):
        ref[pl.ds(0, n), :] = ref[pl.ds(nx * n, n), :]
        ref[pl.ds((nx + 1) * n, n), :] = ref[pl.ds(n, n), :]


def prepare_kernel(fields, kernel, heads, order, order2, w_rows, w_cols, w_head, bias, t, t_low, wide):
    del order, order2
    state, _ = views(fields)
    nx = state.shape[1]
    for x in range(nx):
        rows = [state[v, x] - (1.0 if v in (0, 4) else 0.0) for v in range(5)]
        mid = jnp.concatenate([*rows, jnp.zeros((8, 128), F32)], axis=0)
        put_patches(t, t_low, x, mid)
    wrap_patches(t, t_low, nx, MAIN)

    ch, taps = kernel.shape
    w = kernel[...]
    hi, lo = split(w)
    wide[...] = jnp.zeros_like(wide)
    wide[pl.ds(0, ch), pl.ds(0, taps)] = hi.astype(F32)
    wide[pl.ds(ch, ch), pl.ds(0, taps)] = lo.astype(F32)
    both = wide[...].astype(BF16)
    kind, tap = columns(COLUMNS)
    base = jnp.dot(both, own_taps(kind, tap), preferred_element_type=F32)
    rim = jnp.dot(both, rim_taps(kind, tap), preferred_element_type=F32)
    n = base.shape[1]
    kind = jnp.broadcast_to(kind[0:1], base.shape)
    main = jnp.where(kind < 3, base, 0.0)
    bands = []
    for y in range(8):
        rows = main
        if y == 0:
            rows = jnp.where(kind == 0, 0.0, rows)
        if y == 7:
            rows = jnp.where(kind == 2, 0.0, rows)
        if y != 1:
            rows = pltpu.roll(rows, (y - 1) % n, 1)
        if y == 0:
            rows = rows + jnp.where(kind == 8, base, 0.0)
        if y == 7:
            rows = rows + jnp.where(kind == 10, base, 0.0)
        bands.append(rows)
    bands.append(jnp.where((kind == 0) | (kind == 8) | (kind == 9), rim, 0.0))
    bands.append(jnp.where((kind == 7) | (kind == 10) | (kind == 11), rim, 0.0))
    full = jnp.concatenate([b[:ch] for b in bands] + [b[ch:] for b in bands], axis=0)
    w_rows[...] = full.astype(BF16)
    kept = full.shape[0] // 2
    cols = jnp.concatenate([full[:kept], full[:kept], full[kept:]], axis=0)
    cols = jnp.concatenate([cols, jnp.zeros((512 - 3 * kept, n), F32)], axis=0)
    own_cols = []
    for q in range(3):
        own_cols += [cols[:, (3 * q + o) * MAIN : (3 * q + o) * MAIN + 40] for o in range(3)]
        own_cols.append(jnp.zeros((512, 8), F32))
    w_cols[...] = jnp.concatenate(own_cols, axis=1).T.astype(BF16)
    total = jnp.sum(w * level_taps(w.shape), axis=1, keepdims=True)
    total = jnp.broadcast_to(total, (ch, 128))
    bias[...] = jnp.concatenate([total] * 10, axis=0)

    h_hi, h_lo = split(STEP * heads[...])
    none = jnp.zeros((3, ch), F32)
    pair = jnp.concatenate([h_hi.astype(F32), none, h_lo.astype(F32), none], axis=0).astype(BF16)
    r = lax.broadcasted_iota(jnp.int32, (kept, ch), 0)
    q = lax.broadcasted_iota(jnp.int32, (kept, ch), 1)
    spread = jnp.where((r & (ch - 1)) == q, 1.0, 0.0).astype(BF16)
    picked = over_lanes(pair, spread)
    y_of = lax.broadcasted_iota(jnp.int32, (8, kept), 0)
    col = lax.broadcasted_iota(jnp.int32, (8, kept), 1)
    same = (col >= y_of * ch) & (col < (y_of + 1) * ch)
    split_heads = []
    for at in (0, 8):
        rows = [
            jnp.where(same, jnp.broadcast_to(picked[at + e : at + e + 1], (8, kept)), 0.0)
            for e in range(5)
        ]
        five = picked[at : at + 8]
        rows.append(jnp.where((col >= 8 * ch) & (col < 9 * ch), five, 0.0))
        rows.append(jnp.where(col >= 9 * ch, five, 0.0))
        rows.append(jnp.zeros((8, kept), F32))
        split_heads.append(jnp.concatenate(rows, axis=0))
    three = jnp.concatenate([split_heads[0], split_heads[1], split_heads[0]], axis=0)
    w_head[...] = three.T.astype(BF16)


def c_kernel(
    fields, near_twin, near_other, kernel, w_rows, w_cols, w_head, bias, t, t_low,
    own, parts,
    rim, rim_low, outer, outer_low, acc, edge, gedge,
):
    _, cot = views(fields)
    nx = cot.shape[1]
    ch, taps = kernel.shape
    rim_state, rim_cot, _ = from_rims(near_twin, near_other)

    for v in range(5):
        level = 1.0 if v in (0, 4) else 0.0
        for q, row in enumerate((-1, 8, -2, 9)):
            at = q // 2 * RIM + 5 * (q % 2) + v
            edge[pl.ds(at, nx, stride=2 * RIM), :] = rim_state(row, v) - level
        gedge[pl.ds(v, nx, stride=16), :] = rim_cot(-1, v)
        gedge[pl.ds(8 + v, nx, stride=16), :] = rim_cot(8, v)
    none = jnp.zeros((nx, 128), F32)
    for q in range(10, RIM):
        edge[pl.ds(q, nx, stride=2 * RIM), :] = none
        edge[pl.ds(RIM + q, nx, stride=2 * RIM), :] = none
    for q in (5, 6, 7):
        gedge[pl.ds(q, nx, stride=16), :] = none
        gedge[pl.ds(8 + q, nx, stride=16), :] = none
    for x in range(nx):
        put_patches(rim, rim_low, x, edge[pl.ds(2 * x * RIM, RIM), :])
        put_patches(outer, outer_low, x, edge[pl.ds((2 * x + 1) * RIM, RIM), :])
    wrap_patches(rim, rim_low, nx, RIM)
    wrap_patches(outer, outer_low, nx, RIM)

    def gathered(x, *blocks):
        columns = []
        for j in range(WIDE):
            rows = [ref[pl.ds((x + j) * 3 * n, 9 * n), :] for ref, n in blocks]
            columns.append(jnp.concatenate(rows, axis=0) if len(rows) > 1 else rows[0])
        return jnp.concatenate(columns, axis=1)

    kept = 8 * ch
    kg = hg = dsum = None
    zeros8 = jnp.zeros((8, 128 * WIDE), F32)
    written = set()
    for x in range(0, nx, WIDE):
        s_hi = gathered(x, (t, MAIN), (rim, RIM))
        s_lo = gathered(x, (t_low, MAIN), (rim_low, RIM))
        far_hi, far_lo = gathered(x, (outer, RIM)), gathered(x, (outer_low, RIM))
        z2 = jnp.dot(
            w_rows[...], jnp.concatenate([s_hi, far_hi], axis=0), preferred_element_type=F32
        )
        rows = z2.shape[0] // 2
        z3 = jnp.dot(
            w_rows[pl.ds(0, rows), :],
            jnp.concatenate([s_lo, far_lo], axis=0),
            preferred_element_type=F32,
        )
        z = z2[:rows] + (z2[rows:] + z3) + jnp.concatenate([bias[...]] * WIDE, axis=1)
        hidden = jnp.tanh(z)
        g = jnp.concatenate(
            [
                jnp.concatenate(
                    [cot[v, x + j] for v in range(5)] + [gedge[pl.ds((x + j) * 16, 16), :]], axis=0
                )
                for j in range(WIDE)
            ],
            axis=1,
        )
        g_hi, g_lo = split(g)
        g_hi32, g_lo32 = g_hi.astype(F32), g_lo.astype(F32)
        g3 = jnp.concatenate(
            [g_hi32, zeros8, g_hi32, zeros8, g_lo32, zeros8], axis=0
        ).astype(BF16)
        d = (1.0 - hidden * hidden) * jnp.dot(w_head[...], g3, preferred_element_type=F32)
        d_hi, d_lo = split(d)
        zeros = jnp.zeros((512 - 3 * rows, 128 * WIDE), BF16)
        back = jnp.dot(
            w_cols[...],
            jnp.concatenate([d_hi, d_lo, d_hi, zeros], axis=0),
            preferred_element_type=F32,
        )
        k2 = over_lanes(
            jnp.concatenate([s_hi, s_lo], axis=0),
            jnp.concatenate([d_hi[:kept], d_lo[:kept]], axis=0),
        )
        k2 = k2[:OWN_COLUMNS, :kept] + (k2[:OWN_COLUMNS, kept:] + k2[OWN_COLUMNS:, :kept])
        kg = k2 if kg is None else kg + k2
        hid2 = jnp.concatenate(split(hidden[:kept]), axis=0)
        g2 = jnp.concatenate([g_hi32[:40], g_lo32[:40]], axis=0).astype(BF16)
        h2 = over_lanes(g2, hid2)
        hg = h2 if hg is None else hg + h2
        for j in range(WIDE):
            level = d[:kept, 128 * j : 128 * (j + 1)]
            dsum = level if dsum is None else dsum + level
        for m in range(WIDE + 2):
            total = None
            for j in range(WIDE):
                if 0 <= m - j < 3:
                    q = m - j
                    piece = back[q * 128 : q * 128 + 120, 128 * j : 128 * (j + 1)]
                    total = piece if total is None else total + piece
            here = (x + m - 1) % nx
            if here in written:
                total = total + acc[pl.ds(here * 120, 120), :]
            written.add(here)
            acc[pl.ds(here * 120, 120), :] = total
    for x in range(nx):
        at = x * 120
        total = (
            acc[pl.ds(at + 40, 40), :]
            + pltpu.roll(acc[pl.ds(at, 40), :], 127, 1)
            + pltpu.roll(acc[pl.ds(at + 80, 40), :], 1, 1)
        )
        for v in range(5):
            own[v, x] = total[8 * v : 8 * v + 8]

    sums = jnp.sum(dsum, axis=1, keepdims=True)
    kg = kg.T
    hg = (hg[:40, :kept] + hg[40:, :kept]) + (hg[:40, kept:] + hg[40:, kept:])
    y_row = lax.broadcasted_iota(jnp.int32, (40, kept), 0) & 7
    y_col = lax.broadcasted_iota(jnp.int32, (40, kept), 1)
    same_y = (y_col >= y_row * ch) & (y_col < (y_row + 1) * ch)
    hg = jnp.where(same_y, hg, 0.0)
    by_eq = jnp.concatenate(
        [jnp.sum(hg[8 * e : 8 * e + 8], axis=0, keepdims=True) for e in range(5)]
        + [jnp.zeros((123, kept), F32)],
        axis=0,
    ).T
    level_sum = jnp.zeros((ch, 1), F32)
    head_sum = jnp.zeros((ch, 128), F32)
    n = kg.shape[1]
    columns_at, tap = columns(n)
    kind = jnp.broadcast_to(columns_at[0:1], (ch, n))
    total = jnp.zeros((ch, n), F32)
    for y in range(8):
        rows = kg[y * ch : (y + 1) * ch]
        moved = rows if y == 1 else pltpu.roll(rows, (1 - y) % n, 1)
        keep = kind < 3
        if y == 0:
            keep = (kind == 1) | (kind == 2)
            total = total + jnp.where(kind == 8, rows, 0.0)
        if y == 7:
            keep = kind < 2
            total = total + jnp.where(kind == 10, rows, 0.0)
        total = total + jnp.where(keep, moved, 0.0)
        level_sum = level_sum + sums[y * ch : (y + 1) * ch]
        head_sum = head_sum + by_eq[y * ch : (y + 1) * ch]
    grads = over_lanes(jnp.concatenate(split(total), axis=0), own_taps(columns_at, tap))
    n_pick = grads.shape[1]
    parts[...] = jnp.zeros_like(parts)
    parts[:, pl.ds(0, n_pick)] = grads[:ch] + grads[ch:]
    parts[:, pl.ds(0, taps)] = parts[:, pl.ds(0, taps)] + level_sum * level_taps((ch, taps))
    parts[:, pl.ds(128, 128)] = parts[:, pl.ds(128, 128)] + pltpu.roll(head_sum * STEP, 16, 1)


def columns(n):
    lane = lax.broadcasted_iota(jnp.int32, (8, n), 1)
    main = lane < 9 * MAIN
    far = lane >= OWN_COLUMNS
    past = lane - jnp.where(far, OWN_COLUMNS, 9 * MAIN)
    block = sum((lane >= MAIN * i).astype(jnp.int32) for i in range(1, 9))
    o = jnp.where(main, block, past >> 4)
    r = jnp.where(main, lane - MAIN * block, past & (RIM - 1))
    second = (r >= 5).astype(jnp.int32)
    rim = jnp.where(r < 10, 8 + 2 * second + far.astype(jnp.int32), 12)
    kind = jnp.where(main, jnp.where(r < 40, r & 7, 12), rim)
    v = jnp.where(main, r >> 3, r - 5 * second)
    return kind, o * 5 + v


def taps_of(columns_at):
    n = columns_at.shape[1]
    row = lax.broadcasted_iota(jnp.int32, (144, n), 0)
    return jnp.where(row == jnp.broadcast_to(columns_at[0:1], (144, n)), 1.0, 0.0).astype(BF16)


def own_taps(kind, tap):
    at = jnp.where(kind < 3, tap + 45 * kind, 1000)
    at = jnp.where(kind == 8, tap, at)
    return taps_of(jnp.where(kind == 10, tap + 90, at))


def rim_taps(kind, tap):
    first = (kind == 9) | (kind == 7)
    middle = (kind == 8) | (kind == 10)
    last = (kind == 0) | (kind == 11)
    at = jnp.where(first, tap, jnp.where(middle, tap + 45, 1000))
    return taps_of(jnp.where(last, tap + 90, at))


def level_taps(shape):
    t = lax.broadcasted_iota(jnp.int32, shape, 1).astype(F32)
    v = t - 5.0 * jnp.floor((t + 0.5) * 0.2)
    return jnp.where((v < 0.5) | (v > 3.5), 1.0, 0.0)


def call(kernel, outs, scratch, us, n_in, order=0):
    spec = pl.BlockSpec(memory_space=pltpu.VMEM)
    return pl.pallas_call(
        kernel,
        out_shape=outs,
        in_specs=[spec] * n_in + [pl.BlockSpec(memory_space=pl.ANY)] * order,
        scratch_shapes=scratch,
        compiler_params=pltpu.CompilerParams(vmem_limit_bytes=VMEM),
        cost_estimate=pl.CostEstimate(
            flops=int(us * 1.15e9), bytes_accessed=int(us * 3.69e6), transcendentals=0
        ),
    )


def body(state, cot, flags, kernel, heads):
    _, nx, ny, nz = state.shape
    ch, taps = kernel.shape
    count = lax.axis_size("gy")
    cells = nx * ny * nz
    shape = lambda *dims: jax.ShapeDtypeStruct(dims, F32)
    half_shape = lambda *dims: jax.ShapeDtypeStruct(dims, BF16)
    full = shape(5, nx, ny, nz)
    with_twin = [(i, i ^ 1) for i in range(count)]
    with_other = [(i, (i + 1) % count if i % 2 else (i - 1) % count) for i in range(count)]
    vm = pltpu.VMEM
    lines = 5 * nx * ny

    flat = jnp.concatenate([state.reshape(lines, nz), cot.reshape(lines, nz)])
    fields = flat.reshape(10, nx, ny, nz)
    near, far = shape(NEAR, nx, nz), shape(FAR, nx, nz)
    near_twin, near_other = call(near_kernel, (near, near), [], 0.2, 1)(flat)
    near_rims = (
        lax.ppermute(near_twin, "gy", with_twin),
        lax.ppermute(near_other, "gy", with_other),
    )
    *prepared, patches, patches_low = call(
        prepare_kernel,
        (
            half_shape(20 * ch, COLUMNS),
            half_shape(384, 512),
            half_shape(10 * ch, 192),
            shape(10 * ch, 128),
            half_shape((nx + 2) * 3 * MAIN, nz),
            half_shape((nx + 2) * 3 * MAIN, nz),
        ),
        [vm((2 * ch, 144), F32)],
        1.5,
        3,
        2,
    )(fields, kernel, heads, near_twin, near_other)
    far_twin, far_other = call(far_kernel, (far, far), [], 0.2, 2, 1)(
        flat, flags.reshape(3 * nx * ny, nz), patches
    )
    far_rims = (
        lax.ppermute(far_twin, "gy", with_twin),
        lax.ppermute(far_other, "gy", with_other),
    )
    near_rims, patches = lax.optimization_barrier((near_rims, patches))
    own, parts = call(
        c_kernel,
        (full, shape(ch, 256)),
        [
            *[vm(((nx + 2) * 3 * RIM, nz), BF16)] * 4,
            vm((nx * 120, nz), F32),
            vm((2 * RIM * nx, nz), F32),
            vm((16 * nx, nz), F32),
        ],
        6.0,
        10,
    )(fields, *near_rims, kernel, *prepared, patches, patches_low)

    def exchanged(value, bit):
        return lax.ppermute(value, "gy", [(i, i ^ bit) for i in range(count)])

    bits = [1 << b for b in range(count.bit_length() - 1)]
    sums = parts
    for bit in bits[:-4]:
        sums = sums + exchanged(sums, bit)
    yz_half = lambda half, before, order: call(
        functools.partial(yz_kernel, half), full, [vm((lines, nz), F32)] * 2, 3.3, 8, 1
    )(fields, flags, *near_rims, *far_rims, before, rim, order)
    got = exchanged(sums, bits[-4])
    rim = call(e_kernel, shape(lines, nz), [], 1.1, 5, 1)(flat, *near_rims, *far_rims, sums)
    got, rim = lax.optimization_barrier((got, rim))
    sums = sums + got
    got = exchanged(sums, bits[-3])
    total = call(
        x_kernel,
        full,
        [
            vm((5, nx + 5, ny, nz), F32),
            vm((5, nx + 1, ny, nz), F32),
            vm((5, nx + 5, ny, nz), F32),
        ],
        2.8,
        3,
        1,
    )(fields, flags, own, sums)
    got, total = lax.optimization_barrier((got, total))
    sums = sums + got
    got = exchanged(sums, bits[-2])
    total = yz_half(0, total, sums)
    got, total = lax.optimization_barrier((got, total))
    sums = sums + got
    got = exchanged(sums, bits[-1])
    flow = yz_half(1, total, sums)
    got, flow = lax.optimization_barrier((got, flow))
    scale = float(cells * count) ** (-0.5)
    k_out, h_out = call(
        functools.partial(sum_kernel, scale), (shape(ch, taps), shape(5, ch)), [], 0.5, 2
    )(sums, got)
    return flow, k_out, h_out


def solution(mesh):
    split_y = P(None, "ens", "gy", None)
    return jax.shard_map(
        body,
        mesh=mesh,
        in_specs=(split_y, split_y, split_y, P(), P()),
        out_specs=(split_y, P("ens", None), P("ens", None)),
        check_vma=False,
    )
```

```python
import functools

import jax
import jax.numpy as jnp
from jax import lax
from jax.experimental import pallas as pl
from jax.experimental.pallas import tpu as pltpu
from jax.sharding import PartitionSpec as P

STEP = 0.3
FLOOR = 0.01
BELOW, ABOVE = 2, 3
SLABS = 4
WIDE = 4
VMEM = 48 * 1024 * 1024
F32 = jnp.float32
BF16 = jnp.bfloat16


def rcp(x):
    return pl.reciprocal(x, approx=True)


def shared_terms(v):
    p = [v[i + 1] - v[i] for i in range(5)]
    d = [p[i + 1] - p[i] for i in range(4)]
    h = [(4.0 / 3.0) * x for x in d]
    k = [h[i] * d[i] + FLOOR for i in range(4)]
    g = [x + x for x in h]
    t = [d[i + 1] - d[i] for i in range(3)]
    return p, d, k, g, t


def side_value(pa, pm, pm2, ka, kb, kc, m0, m2, td, t1, smooth, c0, c2):
    i0 = rcp(ka + pa * m0)
    i1 = rcp(kb + pa * pm)
    i2 = rcp(kc + pm * m2)
    w0 = i0 * i0
    w1 = 6.0 * (i1 * i1)
    w2 = 3.0 * (i2 * i2)
    r = rcp(w0 + w1 + w2)
    o0 = jnp.where(smooth, w0 * r, c0)
    o2 = jnp.where(smooth, w2 * r, c2)
    u = o0 * td + o2 * t1
    b0 = w0 * i0 * (td - u)
    b1 = w1 * i1 * u
    b2 = w2 * i2 * (t1 - u)
    return (pa + pm2) - u, (b0, b1, b2, r, o0, o2)


def side_pull(mu, pa, pm, m0, m2, smooth, saved):
    b0, b1, b2, r, o0, o2 = saved
    mu2 = mu + mu
    rm = jnp.where(smooth, mu2, 0.0) * r
    s0, s1, s2 = b0 * rm, b1 * rm, b2 * rm
    pa_bar = s0 * (m0 + pa) - s1 * pm + mu
    pm_bar = s2 * (m2 + pm) - s1 * pa + mu2
    return s0, s1, s2, pa_bar, pm_bar, o0 * mu2, o2 * mu


def hllc_pull(left, right, normal, flags, cot):
    region = flags & 3
    is_right = region >= 2
    star = ((region + 1) & 2) != 0
    n_at = 1 + normal
    tang = [1 + i for i in range(3) if i != normal]
    rl, rr_, pl_, pr_, nl, nr = left[0], right[0], left[4], right[4], left[n_at], right[n_at]

    def sound(r, p):
        inv = rcp(r)
        t = 1.4 * p * inv
        inv_c = lax.rsqrt(t)
        return inv, inv_c, t * inv_c

    inv_rl, inv_cl, cl = sound(rl, pl_)
    inv_rr, inv_cr, cr = sound(rr_, pr_)
    c = 0.5 * (cl + cr)
    r2 = rl + rr_
    inv = rcp(r2 * c)
    nm = 0.5 * (nl + nr)
    gap = (pl_ - pr_) * inv
    sm = nm + gap
    sc = jnp.where(is_right, c, -c)
    s = nm + sc
    pick = [jnp.where(is_right, right[i], left[i]) for i in range(5)]
    r, un, u1, u2, p = pick[0], pick[n_at], pick[tang[0]], pick[tang[1]], pick[4]
    a = s - un
    dl = sm - un
    si = jnp.where(star, rcp(sc - gap), 0.0)
    j = s * si
    kap = j * dl
    g0, gn, g1, g2, ge = cot[0], cot[n_at], cot[tang[0]], cot[tang[1]], cot[4]
    w = un + kap
    half_q = 0.5 * (un * un + u1 * u1 + u2 * u2)
    enthalpy = 3.5 * p + r * half_q
    b = g0 + u1 * g1 + u2 * g2 + un * gn
    m = r * b + enthalpy * ge
    n = gn + sm * ge
    rkap = r * kap
    f_kap = m + r * a * n
    f_a = rkap * n
    si2 = si * si
    s_bar = f_a - f_kap * (dl * sm * si2)
    sm_bar = f_kap * (s * a * si2) + rkap * a * ge
    wr = w * r
    k_bar = [None] * 5
    k_bar[0] = w * (b + half_q * ge) + kap * a * n
    k_bar[n_at] = m + wr * (gn + un * ge) - f_kap * j - f_a
    k_bar[tang[0]] = wr * (g1 + u1 * ge)
    k_bar[tang[1]] = wr * (g2 + u2 * ge)
    k_bar[4] = 3.5 * (w * ge) + gn
    e = sm_bar * inv
    eg = e * gap
    c_half = 0.5 * (jnp.where(is_right, s_bar, -s_bar) - eg * r2)
    n_half = 0.5 * (s_bar + sm_bar)
    r_both = -(eg * c)
    xl = c_half * inv_rl
    xr = c_half * inv_rr
    base_l = {0: r_both - 0.5 * (xl * cl), n_at: n_half, 4: 0.7 * (xl * inv_cl) + e}
    base_r = {0: r_both - 0.5 * (xr * cr), n_at: n_half, 4: 0.7 * (xr * inv_cr) - e}
    l_bar, r_bar = [], []
    for i in range(5):
        kr = jnp.where(is_right, k_bar[i], 0.0)
        kl = k_bar[i] - kr
        l_bar.append(base_l[i] + kl if i in base_l else kl)
        r_bar.append(base_r[i] + kr if i in base_r else kr)
    return l_bar, r_bar


def face_pull(cells, cot, flags, normal):
    stencil = flags >> 2
    smooth = stencil == 0
    c0 = jnp.where(stencil == 1, 1.0, 0.0)
    c2 = jnp.where(stencil == 3, 1.0, 0.0)
    left, right, kept = [], [], []
    for v in cells:
        p, d, k, g, t = shared_terms(v)
        pm2 = p[2] + p[2]
        args_l = (p[1], p[2], p[1] + d[0], p[2] - d[2], t[0] + t[0], t[1])
        args_r = (p[3], p[2], p[3] - d[3], p[2] + d[1], t[2] + t[2], t[1])
        hl, saved_l = side_value(
            p[1], p[2], pm2, k[0], k[1], k[2], *args_l[2:], smooth, c0, c2
        )
        hr, saved_r = side_value(
            p[3], p[2], pm2, k[3], k[2], k[1], *args_r[2:], smooth, c0, c2
        )
        left.append(v[2] + hl * (1.0 / 6.0))
        right.append(v[3] - hr * (1.0 / 6.0))
        kept.append((p, g, args_l[:4], args_r[:4], saved_l, saved_r))
    l_bar, r_bar = hllc_pull(left, right, normal, flags, cot)
    out = []
    for i in range(5):
        p, g, args_l, args_r, saved_l, saved_r = kept[i]
        a0, a1, a2, pa_l, pm_l, x0, x2 = side_pull(
            l_bar[i] * (1.0 / 6.0), *args_l, smooth, saved_l
        )
        b0, b1, b2, pa_r, pm_r, y0, y2 = side_pull(
            r_bar[i] * (-1.0 / 6.0), *args_r, smooth, saved_r
        )
        d0 = a0 * (g[0] + p[1]) + x0
        d1 = (b2 * (g[1] + p[2]) - a1 * g[1]) + (x2 - x0) + y2
        d2 = (a2 * (g[2] - p[2]) - b1 * g[2]) + (y0 - y2) - x2
        d3 = b0 * (g[3] - p[3]) - y0
        p2 = pa_l + (d0 - d1)
        p3 = pm_l + pm_r + (d1 - d2)
        p4 = pa_r + (d2 - d3)
        out.append([d0, -d0 - p2, l_bar[i] + (p2 - p3), r_bar[i] + (p3 - p4), p4 - d3, d3])
    return out


def conserved_pull(s, g):
    half_q = 0.5 * (s[1] * s[1] + s[2] * s[2] + s[3] * s[3])
    return [
        g[0] + s[1] * g[1] + s[2] * g[2] + s[3] * g[3] + half_q * g[4],
        s[0] * (g[1] + s[1] * g[4]),
        s[0] * (g[2] + s[2] * g[4]),
        s[0] * (g[3] + s[3] * g[4]),
        2.5 * g[4],
    ]


NEAR_STATE, FAR_STATE = 2, 3
NEAR_COT, FAR_COT = 1, 2
FLAG_ROWS = 3
NEAR = 5 * (NEAR_STATE + NEAR_COT)
FAR = 5 * (FAR_STATE + FAR_COT) + FLAG_ROWS


def views(fields):
    n = fields.shape[0] // 2
    return fields.at[pl.ds(0, n)], fields.at[pl.ds(n, n)]


def pack(ref, rows, first, twin, other, at):
    even = is_even()
    nx = twin.shape[1]
    count = ref.shape[0] // (8 * nx)
    for r in rows:
        for v in range(count):
            low = ref[pl.ds(v * nx * 8 + r, nx, stride=8), :].astype(F32)
            top = ref[pl.ds(v * nx * 8 + 7 - r, nx, stride=8), :].astype(F32)
            i = at + (r - first) * count + v
            twin[i] = jnp.where(even, top, low)
            other[i] = jnp.where(even, low, top)


def near_kernel(flat, twin, other):
    s, g = views(flat)
    pack(s, range(NEAR_STATE), 0, twin, other, 0)
    pack(g, range(NEAR_COT), 0, twin, other, 5 * NEAR_STATE)


def far_kernel(flat, flags, order, twin, other):
    del order
    s, g = views(flat)
    n = flags.shape[0] // 3
    pack(s, range(NEAR_STATE, NEAR_STATE + FAR_STATE), NEAR_STATE, twin, other, 0)
    pack(g, range(NEAR_COT, NEAR_COT + FAR_COT), NEAR_COT, twin, other, 5 * FAR_STATE)
    pack(flags.at[pl.ds(n, n)], range(FLAG_ROWS), 0, twin, other, FAR - FLAG_ROWS)


def from_rims(near_twin, near_other, far_twin=None, far_other=None):
    even = is_even()

    def pick(twin, other, i, below):
        if below:
            return jnp.where(even, other[i], twin[i])
        return jnp.where(even, twin[i], other[i])

    def read(row, near, near_at, far_at, v):
        below = row < 0
        r = -1 - row if below else row - 8
        if r < near:
            return pick(near_twin, near_other, near_at + r * 5 + v, below)
        return pick(far_twin, far_other, far_at + (r - near) * 5 + v, below)

    def state(row, v):
        return read(row, NEAR_STATE, 0, 0, v)

    def cot(row, v):
        return read(row, NEAR_COT, 5 * NEAR_STATE, 5 * FAR_STATE, v)

    def flags(row):
        below = row < 0
        r = -1 - row if below else row - 8
        return pick(far_twin, far_other, FAR - FLAG_ROWS + r, below).astype(jnp.int32)

    return state, cot, flags


def x_kernel(fields, flags, before, order, out, pad, gpad, acc):
    del order
    state, cot = views(fields)
    nx = state.shape[1]
    for v in range(5):
        pad[v, pl.ds(2, nx)] = state[v]
        pad[v, pl.ds(0, 2)] = state[v, pl.ds(nx - 2, 2)]
        pad[v, pl.ds(nx + 2, 3)] = state[v, pl.ds(0, 3)]
        gpad[v, pl.ds(0, nx)] = cot[v]
        gpad[v, pl.ds(nx, 1)] = cot[v, pl.ds(0, 1)]
    acc[...] = jnp.zeros_like(acc)

    def step(i, carry):
        x = i * SLABS
        cells = [[pad[v, pl.ds(x + k, SLABS)] for k in range(6)] for v in range(5)]
        g = [gpad[v, pl.ds(x, SLABS)] for v in range(5)]
        face = [STEP * (gpad[v, pl.ds(x + 1, SLABS)] - g[v]) for v in range(5)]
        terms = face_pull(cells, face, flags[0, pl.ds(x, SLABS)], 0)
        own = conserved_pull([cells[v][2] for v in range(5)], g)
        for v in range(5):
            terms[v][2] = terms[v][2] + own[v]
            for s in range(SLABS + 5):
                total = None
                for k in range(6):
                    if 0 <= s - k < SLABS:
                        part = terms[v][k][s - k]
                        total = part if total is None else total + part
                acc[v, x + s] = acc[v, x + s] + total
        return carry

    lax.fori_loop(0, nx // SLABS, step, 0)
    for v in range(5):
        acc[v, pl.ds(nx, 2)] = acc[v, pl.ds(nx, 2)] + acc[v, pl.ds(0, 2)]
        acc[v, pl.ds(2, 3)] = acc[v, pl.ds(2, 3)] + acc[v, pl.ds(nx + 2, 3)]

    for v in range(5):
        out[v] = acc[v, pl.ds(2, nx)] + before[v]


def z_faces(state, cot, flags, x):
    cells, face = [], []
    for v in range(5):
        mid = state[v, pl.ds(x, SLABS)]
        cells.append([mid if k == 0 else pltpu.roll(mid, (-k) % 128, 2) for k in range(-2, 4)])
        g = cot[v, pl.ds(x, SLABS)]
        face.append(STEP * (pltpu.roll(g, 127, 2) - g))
    terms = face_pull(cells, face, flags[2, pl.ds(x, SLABS)], 2)
    total = []
    for v in range(5):
        t = terms[v][2]
        for k in (-2, -1, 1, 2, 3):
            t = t + pltpu.roll(terms[v][k + 2], k % 128, 2)
        total.append(t)
    return total


def e_kernel(flat, near_twin, near_other, far_twin, far_other, order, out):
    del order
    state, cot = views(flat)
    nx = out.shape[0] // 40
    rim_state, rim_cot, rim_flags = from_rims(near_twin, near_other, far_twin, far_other)

    def own(ref, row, v):
        return ref[pl.ds(v * nx * 8 + row, nx, stride=8), :]

    state_rows, cot_rows = {}, {}
    for v in range(5):
        for row in (*range(-5, 3), *range(6, 13)):
            inside = 0 <= row < 8
            state_rows[row, v] = own(state, row, v) if inside else rim_state(row, v)
        for row in (-3, -2, -1, 0, 8, 9, 10):
            inside = 0 <= row < 8
            cot_rows[row, v] = own(cot, row, v) if inside else rim_cot(row, v)
    sums = {}
    for j in (-3, -2, -1, 8, 9):
        cells = [[state_rows[j + k, v] for k in range(-2, 4)] for v in range(5)]
        face = [STEP * (cot_rows[j + 1, v] - cot_rows[j, v]) for v in range(5)]
        terms = face_pull(cells, face, rim_flags(j), 1)
        for v in range(5):
            for k in range(-2, 4):
                if 0 <= j + k < 8:
                    t = terms[v][k + 2]
                    sums[j + k, v] = sums[j + k, v] + t if (j + k, v) in sums else t
    for v in range(5):
        for row in range(8):
            value = sums[row, v] if (row, v) in sums else jnp.zeros((nx, 128), F32)
            out[pl.ds(v * nx * 8 + row, nx, stride=8), :] = value


def yz_kernel(half, fields, flags, near_twin, near_other, far_twin, far_other, before, rim, order, out, halo, ghalo):
    del order
    state, cot = views(fields)
    rims = from_rims(near_twin, near_other, far_twin, far_other)
    rim_state, rim_cot, _ = rims
    nx = out.shape[1]
    part = nx // 2
    for v in range(5):
        kept = pl.ds((1 - half) * part, part)
        out[v, kept] = before[v, kept]
    for v in range(5):
        base = v * nx * 8
        for r in range(ABOVE):
            halo[pl.ds(base + r, nx, stride=8), :] = rim_state(8 + r, v)
        for r in range(BELOW):
            halo[pl.ds(base + 8 - BELOW + r, nx, stride=8), :] = rim_state(r - BELOW, v)
        ghalo[pl.ds(base, nx, stride=8), :] = rim_cot(8, v)
    row = lax.broadcasted_iota(jnp.int32, (SLABS, 8, 128), 1)
    inside = {}
    for k in (-2, -1, 1, 2, 3):
        inside[k] = (row < 8 + k) if k < 0 else (row >= k)

    def step(i, carry):
        x = half * part + i * SLABS
        cells, face = [], []
        for v in range(5):
            at = pl.multiple_of((v * nx + x) * 8, 8)
            rim_rows = halo[pl.ds(at, 8 * SLABS), :].reshape(SLABS, 8, 128)
            mid = state[v, pl.ds(x, SLABS)]
            line = []
            for k in range(-2, 4):
                if k == 0:
                    line.append(mid)
                else:
                    line.append(pltpu.roll(jnp.where(inside[k], mid, rim_rows), (-k) % 8, 1))
            cells.append(line)
            g = cot[v, pl.ds(x, SLABS)]
            g_rim = ghalo[pl.ds(at, 8 * SLABS), :].reshape(SLABS, 8, 128)
            face.append(STEP * (pltpu.roll(jnp.where(inside[1], g, g_rim), 7, 1) - g))
        terms = face_pull(cells, face, flags[1, pl.ds(x, SLABS)], 1)
        along_z = z_faces(state, cot, flags, x)
        for v in range(5):
            at = pl.multiple_of((v * nx + x) * 8, 8)
            total = before[v, pl.ds(x, SLABS)] + along_z[v] + terms[v][2]
            total = total + rim[pl.ds(at, 8 * SLABS), :].reshape(SLABS, 8, 128)
            for k in (-2, -1, 1, 2, 3):
                moved = pltpu.roll(terms[v][k + 2], k % 8, 1)
                total = total + jnp.where(inside[k], moved, 0.0)
            out[v, pl.ds(x, SLABS)] = total
        return carry

    lax.fori_loop(0, part // SLABS, step, 0)


def sum_kernel(scale, mine, theirs, k_out, h_out):
    total = (mine[...] + theirs[...]) * scale
    k_out[...] = total[:, : k_out.shape[1]]
    ch = total.shape[0]
    pick = (
        lax.broadcasted_iota(jnp.int32, (8, 128), 1)
        == lax.broadcasted_iota(jnp.int32, (8, 128), 0) + 16
    ).astype(F32)
    heads = lax.dot_general(
        pick,
        total[:, 128:],
        (((1,), (1,)), ((), ())),
        precision=lax.Precision.HIGHEST,
        preferred_element_type=F32,
    )
    h_out[...] = heads[: h_out.shape[0], :ch]


MAIN, RIM = 48, 16
OWN_COLUMNS = 9 * (MAIN + RIM)
COLUMNS = OWN_COLUMNS + 9 * RIM


def split(x):
    hi = x.astype(BF16)
    return hi, (x - hi.astype(F32)).astype(BF16)


def over_lanes(a, b):
    return lax.dot_general(a, b, (((1,), (1,)), ((), ())), preferred_element_type=F32)


def is_even():
    return lax.rem(lax.axis_index("gy"), 2) == 0


def put_patches(high, low, x, rows):
    n = rows.shape[0]
    hi, lo = split(rows)
    hi32, lo32 = hi.astype(F32), lo.astype(F32)
    for q, turn in enumerate((1, 0, 127)):
        at = pl.ds((x + 1) * 3 * n + q * n, n)
        high[at, :] = pltpu.roll(hi32, turn, 1).astype(BF16) if turn else hi
        low[at, :] = pltpu.roll(lo32, turn, 1).astype(BF16) if turn else lo


def wrap_patches(high, low, nx, rows):
    n = 3 * rows
    for ref in (high, low):
        ref[pl.ds(0, n), :] = ref[pl.ds(nx * n, n), :]
        ref[pl.ds((nx + 1) * n, n), :] = ref[pl.ds(n, n), :]


def prepare_kernel(fields, kernel, heads, order, order2, w_rows, w_cols, w_head, bias, t, t_low, wide):
    del order, order2
    state, _ = views(fields)
    nx = state.shape[1]
    for x in range(nx):
        rows = [state[v, x] - (1.0 if v in (0, 4) else 0.0) for v in range(5)]
        mid = jnp.concatenate([*rows, jnp.zeros((8, 128), F32)], axis=0)
        put_patches(t, t_low, x, mid)
    wrap_patches(t, t_low, nx, MAIN)

    ch, taps = kernel.shape
    w = kernel[...]
    hi, lo = split(w)
    wide[...] = jnp.zeros_like(wide)
    wide[pl.ds(0, ch), pl.ds(0, taps)] = hi.astype(F32)
    wide[pl.ds(ch, ch), pl.ds(0, taps)] = lo.astype(F32)
    both = wide[...].astype(BF16)
    kind, tap = columns(COLUMNS)
    base = jnp.dot(both, own_taps(kind, tap), preferred_element_type=F32)
    rim = jnp.dot(both, rim_taps(kind, tap), preferred_element_type=F32)
    n = base.shape[1]
    kind = jnp.broadcast_to(kind[0:1], base.shape)
    main = jnp.where(kind < 3, base, 0.0)
    bands = []
    for y in range(8):
        rows = main
        if y == 0:
            rows = jnp.where(kind == 0, 0.0, rows)
        if y == 7:
            rows = jnp.where(kind == 2, 0.0, rows)
        if y != 1:
            rows = pltpu.roll(rows, (y - 1) % n, 1)
        if y == 0:
            rows = rows + jnp.where(kind == 8, base, 0.0)
        if y == 7:
            rows = rows + jnp.where(kind == 10, base, 0.0)
        bands.append(rows)
    bands.append(jnp.where((kind == 0) | (kind == 8) | (kind == 9), rim, 0.0))
    bands.append(jnp.where((kind == 7) | (kind == 10) | (kind == 11), rim, 0.0))
    full = jnp.concatenate([b[:ch] for b in bands] + [b[ch:] for b in bands], axis=0)
    w_rows[...] = full.astype(BF16)
    kept = full.shape[0] // 2
    cols = jnp.concatenate([full[:kept], full[:kept], full[kept:]], axis=0)
    cols = jnp.concatenate([cols, jnp.zeros((512 - 3 * kept, n), F32)], axis=0)
    own_cols = []
    for q in range(3):
        own_cols += [cols[:, (3 * q + o) * MAIN : (3 * q + o) * MAIN + 40] for o in range(3)]
        own_cols.append(jnp.zeros((512, 8), F32))
    w_cols[...] = jnp.concatenate(own_cols, axis=1).T.astype(BF16)
    total = jnp.sum(w * level_taps(w.shape), axis=1, keepdims=True)
    total = jnp.broadcast_to(total, (ch, 128))
    bias[...] = jnp.concatenate([total] * 10, axis=0)

    h_hi, h_lo = split(STEP * heads[...])
    none = jnp.zeros((3, ch), F32)
    pair = jnp.concatenate([h_hi.astype(F32), none, h_lo.astype(F32), none], axis=0).astype(BF16)
    r = lax.broadcasted_iota(jnp.int32, (kept, ch), 0)
    q = lax.broadcasted_iota(jnp.int32, (kept, ch), 1)
    spread = jnp.where((r & (ch - 1)) == q, 1.0, 0.0).astype(BF16)
    picked = over_lanes(pair, spread)
    y_of = lax.broadcasted_iota(jnp.int32, (8, kept), 0)
    col = lax.broadcasted_iota(jnp.int32, (8, kept), 1)
    same = (col >= y_of * ch) & (col < (y_of + 1) * ch)
    split_heads = []
    for at in (0, 8):
        rows = [
            jnp.where(same, jnp.broadcast_to(picked[at + e : at + e + 1], (8, kept)), 0.0)
            for e in range(5)
        ]
        five = picked[at : at + 8]
        rows.append(jnp.where((col >= 8 * ch) & (col < 9 * ch), five, 0.0))
        rows.append(jnp.where(col >= 9 * ch, five, 0.0))
        rows.append(jnp.zeros((8, kept), F32))
        split_heads.append(jnp.concatenate(rows, axis=0))
    three = jnp.concatenate([split_heads[0], split_heads[1], split_heads[0]], axis=0)
    w_head[...] = three.T.astype(BF16)


def c_kernel(
    fields, near_twin, near_other, kernel, w_rows, w_cols, w_head, bias, t, t_low,
    own, parts,
    rim, rim_low, outer, outer_low, acc, edge, gedge,
):
    _, cot = views(fields)
    nx = cot.shape[1]
    ch, taps = kernel.shape
    rim_state, rim_cot, _ = from_rims(near_twin, near_other)

    for v in range(5):
        level = 1.0 if v in (0, 4) else 0.0
        for q, row in enumerate((-1, 8, -2, 9)):
            at = q // 2 * RIM + 5 * (q % 2) + v
            edge[pl.ds(at, nx, stride=2 * RIM), :] = rim_state(row, v) - level
        gedge[pl.ds(v, nx, stride=16), :] = rim_cot(-1, v)
        gedge[pl.ds(8 + v, nx, stride=16), :] = rim_cot(8, v)
    none = jnp.zeros((nx, 128), F32)
    for q in range(10, RIM):
        edge[pl.ds(q, nx, stride=2 * RIM), :] = none
        edge[pl.ds(RIM + q, nx, stride=2 * RIM), :] = none
    for q in (5, 6, 7):
        gedge[pl.ds(q, nx, stride=16), :] = none
        gedge[pl.ds(8 + q, nx, stride=16), :] = none
    for x in range(nx):
        put_patches(rim, rim_low, x, edge[pl.ds(2 * x * RIM, RIM), :])
        put_patches(outer, outer_low, x, edge[pl.ds((2 * x + 1) * RIM, RIM), :])
    wrap_patches(rim, rim_low, nx, RIM)
    wrap_patches(outer, outer_low, nx, RIM)

    def gathered(x, *blocks):
        columns = []
        for j in range(WIDE):
            rows = [ref[pl.ds((x + j) * 3 * n, 9 * n), :] for ref, n in blocks]
            columns.append(jnp.concatenate(rows, axis=0) if len(rows) > 1 else rows[0])
        return jnp.concatenate(columns, axis=1)

    kept = 8 * ch
    kg = hg = dsum = None
    zeros8 = jnp.zeros((8, 128 * WIDE), F32)
    written = set()
    for x in range(0, nx, WIDE):
        s_hi = gathered(x, (t, MAIN), (rim, RIM))
        s_lo = gathered(x, (t_low, MAIN), (rim_low, RIM))
        far_hi, far_lo = gathered(x, (outer, RIM)), gathered(x, (outer_low, RIM))
        z2 = jnp.dot(
            w_rows[...], jnp.concatenate([s_hi, far_hi], axis=0), preferred_element_type=F32
        )
        rows = z2.shape[0] // 2
        z3 = jnp.dot(
            w_rows[pl.ds(0, rows), :],
            jnp.concatenate([s_lo, far_lo], axis=0),
            preferred_element_type=F32,
        )
        z = z2[:rows] + (z2[rows:] + z3) + jnp.concatenate([bias[...]] * WIDE, axis=1)
        hidden = jnp.tanh(z)
        g = jnp.concatenate(
            [
                jnp.concatenate(
                    [cot[v, x + j] for v in range(5)] + [gedge[pl.ds((x + j) * 16, 16), :]], axis=0
                )
                for j in range(WIDE)
            ],
            axis=1,
        )
        g_hi, g_lo = split(g)
        g_hi32, g_lo32 = g_hi.astype(F32), g_lo.astype(F32)
        g3 = jnp.concatenate(
            [g_hi32, zeros8, g_hi32, zeros8, g_lo32, zeros8], axis=0
        ).astype(BF16)
        d = (1.0 - hidden * hidden) * jnp.dot(w_head[...], g3, preferred_element_type=F32)
        d_hi, d_lo = split(d)
        zeros = jnp.zeros((512 - 3 * rows, 128 * WIDE), BF16)
        back = jnp.dot(
            w_cols[...],
            jnp.concatenate([d_hi, d_lo, d_hi, zeros], axis=0),
            preferred_element_type=F32,
        )
        k2 = over_lanes(
            jnp.concatenate([s_hi, s_lo], axis=0),
            jnp.concatenate([d_hi[:kept], d_lo[:kept]], axis=0),
        )
        k2 = k2[:OWN_COLUMNS, :kept] + (k2[:OWN_COLUMNS, kept:] + k2[OWN_COLUMNS:, :kept])
        kg = k2 if kg is None else kg + k2
        hid2 = jnp.concatenate(split(hidden[:kept]), axis=0)
        g2 = jnp.concatenate([g_hi32[:40], g_lo32[:40]], axis=0).astype(BF16)
        h2 = over_lanes(g2, hid2)
        hg = h2 if hg is None else hg + h2
        for j in range(WIDE):
            level = d[:kept, 128 * j : 128 * (j + 1)]
            dsum = level if dsum is None else dsum + level
        for m in range(WIDE + 2):
            total = None
            for j in range(WIDE):
                if 0 <= m - j < 3:
                    q = m - j
                    piece = back[q * 128 : q * 128 + 120, 128 * j : 128 * (j + 1)]
                    total = piece if total is None else total + piece
            here = (x + m - 1) % nx
            if here in written:
                total = total + acc[pl.ds(here * 120, 120), :]
            written.add(here)
            acc[pl.ds(here * 120, 120), :] = total
    for x in range(nx):
        at = x * 120
        total = (
            acc[pl.ds(at + 40, 40), :]
            + pltpu.roll(acc[pl.ds(at, 40), :], 127, 1)
            + pltpu.roll(acc[pl.ds(at + 80, 40), :], 1, 1)
        )
        for v in range(5):
            own[v, x] = total[8 * v : 8 * v + 8]

    sums = jnp.sum(dsum, axis=1, keepdims=True)
    kg = kg.T
    hg = (hg[:40, :kept] + hg[40:, :kept]) + (hg[:40, kept:] + hg[40:, kept:])
    y_row = lax.broadcasted_iota(jnp.int32, (40, kept), 0) & 7
    y_col = lax.broadcasted_iota(jnp.int32, (40, kept), 1)
    same_y = (y_col >= y_row * ch) & (y_col < (y_row + 1) * ch)
    hg = jnp.where(same_y, hg, 0.0)
    by_eq = jnp.concatenate(
        [jnp.sum(hg[8 * e : 8 * e + 8], axis=0, keepdims=True) for e in range(5)]
        + [jnp.zeros((123, kept), F32)],
        axis=0,
    ).T
    level_sum = jnp.zeros((ch, 1), F32)
    head_sum = jnp.zeros((ch, 128), F32)
    n = kg.shape[1]
    columns_at, tap = columns(n)
    kind = jnp.broadcast_to(columns_at[0:1], (ch, n))
    total = jnp.zeros((ch, n), F32)
    for y in range(8):
        rows = kg[y * ch : (y + 1) * ch]
        moved = rows if y == 1 else pltpu.roll(rows, (1 - y) % n, 1)
        keep = kind < 3
        if y == 0:
            keep = (kind == 1) | (kind == 2)
            total = total + jnp.where(kind == 8, rows, 0.0)
        if y == 7:
            keep = kind < 2
            total = total + jnp.where(kind == 10, rows, 0.0)
        total = total + jnp.where(keep, moved, 0.0)
        level_sum = level_sum + sums[y * ch : (y + 1) * ch]
        head_sum = head_sum + by_eq[y * ch : (y + 1) * ch]
    grads = over_lanes(jnp.concatenate(split(total), axis=0), own_taps(columns_at, tap))
    n_pick = grads.shape[1]
    parts[...] = jnp.zeros_like(parts)
    parts[:, pl.ds(0, n_pick)] = grads[:ch] + grads[ch:]
    parts[:, pl.ds(0, taps)] = parts[:, pl.ds(0, taps)] + level_sum * level_taps((ch, taps))
    parts[:, pl.ds(128, 128)] = parts[:, pl.ds(128, 128)] + pltpu.roll(head_sum * STEP, 16, 1)


def columns(n):
    lane = lax.broadcasted_iota(jnp.int32, (8, n), 1)
    main = lane < 9 * MAIN
    far = lane >= OWN_COLUMNS
    past = lane - jnp.where(far, OWN_COLUMNS, 9 * MAIN)
    block = sum((lane >= MAIN * i).astype(jnp.int32) for i in range(1, 9))
    o = jnp.where(main, block, past >> 4)
    r = jnp.where(main, lane - MAIN * block, past & (RIM - 1))
    second = (r >= 5).astype(jnp.int32)
    rim = jnp.where(r < 10, 8 + 2 * second + far.astype(jnp.int32), 12)
    kind = jnp.where(main, jnp.where(r < 40, r & 7, 12), rim)
    v = jnp.where(main, r >> 3, r - 5 * second)
    return kind, o * 5 + v


def taps_of(columns_at):
    n = columns_at.shape[1]
    row = lax.broadcasted_iota(jnp.int32, (144, n), 0)
    return jnp.where(row == jnp.broadcast_to(columns_at[0:1], (144, n)), 1.0, 0.0).astype(BF16)


def own_taps(kind, tap):
    at = jnp.where(kind < 3, tap + 45 * kind, 1000)
    at = jnp.where(kind == 8, tap, at)
    return taps_of(jnp.where(kind == 10, tap + 90, at))


def rim_taps(kind, tap):
    first = (kind == 9) | (kind == 7)
    middle = (kind == 8) | (kind == 10)
    last = (kind == 0) | (kind == 11)
    at = jnp.where(first, tap, jnp.where(middle, tap + 45, 1000))
    return taps_of(jnp.where(last, tap + 90, at))


def level_taps(shape):
    t = lax.broadcasted_iota(jnp.int32, shape, 1).astype(F32)
    v = t - 5.0 * jnp.floor((t + 0.5) * 0.2)
    return jnp.where((v < 0.5) | (v > 3.5), 1.0, 0.0)


def call(kernel, outs, scratch, us, n_in, order=0):
    spec = pl.BlockSpec(memory_space=pltpu.VMEM)
    return pl.pallas_call(
        kernel,
        out_shape=outs,
        in_specs=[spec] * n_in + [pl.BlockSpec(memory_space=pl.ANY)] * order,
        scratch_shapes=scratch,
        compiler_params=pltpu.CompilerParams(vmem_limit_bytes=VMEM),
        cost_estimate=pl.CostEstimate(
            flops=int(us * 1.15e9), bytes_accessed=int(us * 3.69e6), transcendentals=0
        ),
    )


def body(state, cot, flags, kernel, heads):
    _, nx, ny, nz = state.shape
    ch, taps = kernel.shape
    count = lax.axis_size("gy")
    cells = nx * ny * nz
    shape = lambda *dims: jax.ShapeDtypeStruct(dims, F32)
    half_shape = lambda *dims: jax.ShapeDtypeStruct(dims, BF16)
    full = shape(5, nx, ny, nz)
    with_twin = [(i, i ^ 1) for i in range(count)]
    with_other = [(i, (i + 1) % count if i % 2 else (i - 1) % count) for i in range(count)]
    vm = pltpu.VMEM
    lines = 5 * nx * ny

    flat = jnp.concatenate([state.reshape(lines, nz), cot.reshape(lines, nz)])
    fields = flat.reshape(10, nx, ny, nz)
    near, far = shape(NEAR, nx, nz), shape(FAR, nx, nz)
    near_twin, near_other = call(near_kernel, (near, near), [], 0.2, 1)(flat)
    near_rims = (
        lax.ppermute(near_twin, "gy", with_twin),
        lax.ppermute(near_other, "gy", with_other),
    )
    *prepared, patches, patches_low = call(
        prepare_kernel,
        (
            half_shape(20 * ch, COLUMNS),
            half_shape(384, 512),
            half_shape(10 * ch, 192),
            shape(10 * ch, 128),
            half_shape((nx + 2) * 3 * MAIN, nz),
            half_shape((nx + 2) * 3 * MAIN, nz),
        ),
        [vm((2 * ch, 144), F32)],
        1.5,
        3,
        2,
    )(fields, kernel, heads, near_twin, near_other)
    far_twin, far_other = call(far_kernel, (far, far), [], 0.2, 2, 1)(
        flat, flags.reshape(3 * nx * ny, nz), patches
    )
    far_rims = (
        lax.ppermute(far_twin, "gy", with_twin),
        lax.ppermute(far_other, "gy", with_other),
    )
    near_rims, patches = lax.optimization_barrier((near_rims, patches))
    own, parts = call(
        c_kernel,
        (full, shape(ch, 256)),
        [
            *[vm(((nx + 2) * 3 * RIM, nz), BF16)] * 4,
            vm((nx * 120, nz), F32),
            vm((2 * RIM * nx, nz), F32),
            vm((16 * nx, nz), F32),
        ],
        6.0,
        10,
    )(fields, *near_rims, kernel, *prepared, patches, patches_low)

    def exchanged(value, bit):
        return lax.ppermute(value, "gy", [(i, i ^ bit) for i in range(count)])

    bits = [1 << b for b in range(count.bit_length() - 1)]
    sums = parts
    for bit in bits[:-4]:
        sums = sums + exchanged(sums, bit)
    yz_half = lambda half, before, order: call(
        functools.partial(yz_kernel, half), full, [vm((lines, nz), F32)] * 2, 3.3, 8, 1
    )(fields, flags, *near_rims, *far_rims, before, rim, order)
    got = exchanged(sums, bits[-4])
    rim = call(e_kernel, shape(lines, nz), [], 1.1, 5, 1)(flat, *near_rims, *far_rims, sums)
    got, rim = lax.optimization_barrier((got, rim))
    sums = sums + got
    got = exchanged(sums, bits[-3])
    total = call(
        x_kernel,
        full,
        [
            vm((5, nx + 5, ny, nz), F32),
            vm((5, nx + 1, ny, nz), F32),
            vm((5, nx + 5, ny, nz), F32),
        ],
        2.8,
        3,
        1,
    )(fields, flags, own, sums)
    got, total = lax.optimization_barrier((got, total))
    sums = sums + got
    got = exchanged(sums, bits[-2])
    total = yz_half(0, total, sums)
    got, total = lax.optimization_barrier((got, total))
    sums = sums + got
    got = exchanged(sums, bits[-1])
    flow = yz_half(1, total, sums)
    got, flow = lax.optimization_barrier((got, flow))
    scale = float(cells * count) ** (-0.5)
    k_out, h_out = call(
        functools.partial(sum_kernel, scale), (shape(ch, taps), shape(5, ch)), [], 0.5, 2
    )(sums, got)
    return flow, k_out, h_out


def solution(mesh):
    split_y = P(None, "ens", "gy", None)
    return jax.shard_map(
        body,
        mesh=mesh,
        in_specs=(split_y, split_y, split_y, P(), P()),
        out_specs=(split_y, P("ens", None), P("ens", None)),
        check_vma=False,
    )
```

```python
import functools

import jax
import jax.numpy as jnp
from jax import lax
from jax.experimental import pallas as pl
from jax.experimental.pallas import tpu as pltpu
from jax.sharding import PartitionSpec as P

STEP = 0.3
FLOOR = 0.01
BELOW, ABOVE = 2, 3
SLABS = 2
WIDE = 4
VMEM = 48 * 1024 * 1024
F32 = jnp.float32
BF16 = jnp.bfloat16


def rcp(x):
    return pl.reciprocal(x, approx=True)


def shared_terms(v):
    p = [v[i + 1] - v[i] for i in range(5)]
    d = [p[i + 1] - p[i] for i in range(4)]
    h = [(4.0 / 3.0) * x for x in d]
    k = [h[i] * d[i] + FLOOR for i in range(4)]
    g = [x + x for x in h]
    t = [d[i + 1] - d[i] for i in range(3)]
    return p, d, k, g, t


def side_value(pa, pm, pm2, ka, kb, kc, m0, m2, td, t1, smooth, c0, c2):
    i0 = rcp(ka + pa * m0)
    i1 = rcp(kb + pa * pm)
    i2 = rcp(kc + pm * m2)
    w0 = i0 * i0
    w1 = 6.0 * (i1 * i1)
    w2 = 3.0 * (i2 * i2)
    r = rcp(w0 + w1 + w2)
    o0 = jnp.where(smooth, w0 * r, c0)
    o2 = jnp.where(smooth, w2 * r, c2)
    u = o0 * td + o2 * t1
    b0 = w0 * i0 * (td - u)
    b1 = w1 * i1 * u
    b2 = w2 * i2 * (t1 - u)
    return (pa + pm2) - u, (b0, b1, b2, r, o0, o2)


def side_pull(mu, pa, pm, m0, m2, smooth, saved):
    b0, b1, b2, r, o0, o2 = saved
    mu2 = mu + mu
    rm = jnp.where(smooth, mu2, 0.0) * r
    s0, s1, s2 = b0 * rm, b1 * rm, b2 * rm
    pa_bar = s0 * (m0 + pa) - s1 * pm + mu
    pm_bar = s2 * (m2 + pm) - s1 * pa + mu2
    return s0, s1, s2, pa_bar, pm_bar, o0 * mu2, o2 * mu


def hllc_pull(left, right, normal, flags, cot):
    region = flags & 3
    is_right = region >= 2
    star = ((region + 1) & 2) != 0
    n_at = 1 + normal
    tang = [1 + i for i in range(3) if i != normal]
    rl, rr_, pl_, pr_, nl, nr = left[0], right[0], left[4], right[4], left[n_at], right[n_at]

    def sound(r, p):
        inv = rcp(r)
        t = 1.4 * p * inv
        inv_c = lax.rsqrt(t)
        return inv, inv_c, t * inv_c

    inv_rl, inv_cl, cl = sound(rl, pl_)
    inv_rr, inv_cr, cr = sound(rr_, pr_)
    c = 0.5 * (cl + cr)
    r2 = rl + rr_
    inv = rcp(r2 * c)
    nm = 0.5 * (nl + nr)
    gap = (pl_ - pr_) * inv
    sm = nm + gap
    sc = jnp.where(is_right, c, -c)
    s = nm + sc
    pick = [jnp.where(is_right, right[i], left[i]) for i in range(5)]
    r, un, u1, u2, p = pick[0], pick[n_at], pick[tang[0]], pick[tang[1]], pick[4]
    a = s - un
    dl = sm - un
    si = jnp.where(star, rcp(sc - gap), 0.0)
    j = s * si
    kap = j * dl
    g0, gn, g1, g2, ge = cot[0], cot[n_at], cot[tang[0]], cot[tang[1]], cot[4]
    w = un + kap
    half_q = 0.5 * (un * un + u1 * u1 + u2 * u2)
    enthalpy = 3.5 * p + r * half_q
    b = g0 + u1 * g1 + u2 * g2 + un * gn
    m = r * b + enthalpy * ge
    n = gn + sm * ge
    rkap = r * kap
    f_kap = m + r * a * n
    f_a = rkap * n
    si2 = si * si
    s_bar = f_a - f_kap * (dl * sm * si2)
    sm_bar = f_kap * (s * a * si2) + rkap * a * ge
    wr = w * r
    k_bar = [None] * 5
    k_bar[0] = w * (b + half_q * ge) + kap * a * n
    k_bar[n_at] = m + wr * (gn + un * ge) - f_kap * j - f_a
    k_bar[tang[0]] = wr * (g1 + u1 * ge)
    k_bar[tang[1]] = wr * (g2 + u2 * ge)
    k_bar[4] = 3.5 * (w * ge) + gn
    e = sm_bar * inv
    eg = e * gap
    c_half = 0.5 * (jnp.where(is_right, s_bar, -s_bar) - eg * r2)
    n_half = 0.5 * (s_bar + sm_bar)
    r_both = -(eg * c)
    xl = c_half * inv_rl
    xr = c_half * inv_rr
    base_l = {0: r_both - 0.5 * (xl * cl), n_at: n_half, 4: 0.7 * (xl * inv_cl) + e}
    base_r = {0: r_both - 0.5 * (xr * cr), n_at: n_half, 4: 0.7 * (xr * inv_cr) - e}
    l_bar, r_bar = [], []
    for i in range(5):
        kr = jnp.where(is_right, k_bar[i], 0.0)
        kl = k_bar[i] - kr
        l_bar.append(base_l[i] + kl if i in base_l else kl)
        r_bar.append(base_r[i] + kr if i in base_r else kr)
    return l_bar, r_bar


def face_pull(cells, cot, flags, normal):
    stencil = flags >> 2
    smooth = stencil == 0
    c0 = jnp.where(stencil == 1, 1.0, 0.0)
    c2 = jnp.where(stencil == 3, 1.0, 0.0)
    left, right, kept = [], [], []
    for v in cells:
        p, d, k, g, t = shared_terms(v)
        pm2 = p[2] + p[2]
        args_l = (p[1], p[2], p[1] + d[0], p[2] - d[2], t[0] + t[0], t[1])
        args_r = (p[3], p[2], p[3] - d[3], p[2] + d[1], t[2] + t[2], t[1])
        hl, saved_l = side_value(
            p[1], p[2], pm2, k[0], k[1], k[2], *args_l[2:], smooth, c0, c2
        )
        hr, saved_r = side_value(
            p[3], p[2], pm2, k[3], k[2], k[1], *args_r[2:], smooth, c0, c2
        )
        left.append(v[2] + hl * (1.0 / 6.0))
        right.append(v[3] - hr * (1.0 / 6.0))
        kept.append((p, g, args_l[:4], args_r[:4], saved_l, saved_r))
    l_bar, r_bar = hllc_pull(left, right, normal, flags, cot)
    out = []
    for i in range(5):
        p, g, args_l, args_r, saved_l, saved_r = kept[i]
        a0, a1, a2, pa_l, pm_l, x0, x2 = side_pull(
            l_bar[i] * (1.0 / 6.0), *args_l, smooth, saved_l
        )
        b0, b1, b2, pa_r, pm_r, y0, y2 = side_pull(
            r_bar[i] * (-1.0 / 6.0), *args_r, smooth, saved_r
        )
        d0 = a0 * (g[0] + p[1]) + x0
        d1 = (b2 * (g[1] + p[2]) - a1 * g[1]) + (x2 - x0) + y2
        d2 = (a2 * (g[2] - p[2]) - b1 * g[2]) + (y0 - y2) - x2
        d3 = b0 * (g[3] - p[3]) - y0
        p2 = pa_l + (d0 - d1)
        p3 = pm_l + pm_r + (d1 - d2)
        p4 = pa_r + (d2 - d3)
        out.append([d0, -d0 - p2, l_bar[i] + (p2 - p3), r_bar[i] + (p3 - p4), p4 - d3, d3])
    return out


def conserved_pull(s, g):
    half_q = 0.5 * (s[1] * s[1] + s[2] * s[2] + s[3] * s[3])
    return [
        g[0] + s[1] * g[1] + s[2] * g[2] + s[3] * g[3] + half_q * g[4],
        s[0] * (g[1] + s[1] * g[4]),
        s[0] * (g[2] + s[2] * g[4]),
        s[0] * (g[3] + s[3] * g[4]),
        2.5 * g[4],
    ]


NEAR_STATE, FAR_STATE = 2, 3
NEAR_COT, FAR_COT = 1, 2
FLAG_ROWS = 3
NEAR = 5 * (NEAR_STATE + NEAR_COT)
FAR = 5 * (FAR_STATE + FAR_COT) + FLAG_ROWS


def views(fields):
    n = fields.shape[0] // 2
    return fields.at[pl.ds(0, n)], fields.at[pl.ds(n, n)]


def pack(ref, rows, first, twin, other, at):
    even = is_even()
    nx = twin.shape[1]
    count = ref.shape[0] // (8 * nx)
    for r in rows:
        for v in range(count):
            low = ref[pl.ds(v * nx * 8 + r, nx, stride=8), :].astype(F32)
            top = ref[pl.ds(v * nx * 8 + 7 - r, nx, stride=8), :].astype(F32)
            i = at + (r - first) * count + v
            twin[i] = jnp.where(even, top, low)
            other[i] = jnp.where(even, low, top)


def near_kernel(flat, order, twin, other):
    del order
    s, g = views(flat)
    pack(s, range(NEAR_STATE), 0, twin, other, 0)
    pack(g, range(NEAR_COT), 0, twin, other, 5 * NEAR_STATE)


def far_kernel(flat, flags, order, twin, other):
    del order
    s, g = views(flat)
    n = flags.shape[0] // 3
    pack(s, range(NEAR_STATE, NEAR_STATE + FAR_STATE), NEAR_STATE, twin, other, 0)
    pack(g, range(NEAR_COT, NEAR_COT + FAR_COT), NEAR_COT, twin, other, 5 * FAR_STATE)
    pack(flags.at[pl.ds(n, n)], range(FLAG_ROWS), 0, twin, other, FAR - FLAG_ROWS)


def from_rims(near_twin, near_other, far_twin=None, far_other=None):
    even = is_even()

    def pick(twin, other, i, below):
        if below:
            return jnp.where(even, other[i], twin[i])
        return jnp.where(even, twin[i], other[i])

    def read(row, near, near_at, far_at, v):
        below = row < 0
        r = -1 - row if below else row - 8
        if r < near:
            return pick(near_twin, near_other, near_at + r * 5 + v, below)
        return pick(far_twin, far_other, far_at + (r - near) * 5 + v, below)

    def state(row, v):
        return read(row, NEAR_STATE, 0, 0, v)

    def cot(row, v):
        return read(row, NEAR_COT, 5 * NEAR_STATE, 5 * FAR_STATE, v)

    def flags(row):
        below = row < 0
        r = -1 - row if below else row - 8
        return pick(far_twin, far_other, FAR - FLAG_ROWS + r, below).astype(jnp.int32)

    return state, cot, flags


def x_faces(fields, flags, out, pad, gpad, acc):
    state, cot = views(fields)
    nx = state.shape[1]
    for v in range(5):
        pad[v, pl.ds(2, nx)] = state[v]
        pad[v, pl.ds(0, 2)] = state[v, pl.ds(nx - 2, 2)]
        pad[v, pl.ds(nx + 2, 3)] = state[v, pl.ds(0, 3)]
        gpad[v, pl.ds(0, nx)] = cot[v]
        gpad[v, pl.ds(nx, 1)] = cot[v, pl.ds(0, 1)]
    acc[...] = jnp.zeros_like(acc)

    def step(i, carry):
        x = i * SLABS
        cells = [[pad[v, pl.ds(x + k, SLABS)] for k in range(6)] for v in range(5)]
        g = [gpad[v, pl.ds(x, SLABS)] for v in range(5)]
        face = [STEP * (gpad[v, pl.ds(x + 1, SLABS)] - g[v]) for v in range(5)]
        terms = face_pull(cells, face, flags[0, pl.ds(x, SLABS)], 0)
        own = conserved_pull([cells[v][2] for v in range(5)], g)
        for v in range(5):
            terms[v][2] = terms[v][2] + own[v]
            for s in range(SLABS + 5):
                total = None
                for k in range(6):
                    if 0 <= s - k < SLABS:
                        part = terms[v][k][s - k]
                        total = part if total is None else total + part
                acc[v, x + s] = acc[v, x + s] + total
        return carry

    lax.fori_loop(0, nx // SLABS, step, 0)
    for v in range(5):
        acc[v, pl.ds(nx, 2)] = acc[v, pl.ds(nx, 2)] + acc[v, pl.ds(0, 2)]
        acc[v, pl.ds(2, 3)] = acc[v, pl.ds(2, 3)] + acc[v, pl.ds(nx + 2, 3)]

    for v in range(5):
        out[v] = acc[v, pl.ds(2, nx)]


def x_early_kernel(fields, flags, out, *scratch):
    @pl.when(lax.axis_index("gy") == 0)
    def _():
        x_faces(fields, flags, out, *scratch)


def x_late_kernel(fields, flags, early, order, out, *scratch):
    del order
    first = lax.axis_index("gy") == 0

    @pl.when(first)
    def _():
        out[...] = early[...]

    @pl.when(jnp.logical_not(first))
    def _():
        x_faces(fields, flags, out, *scratch)


def z_faces(state, cot, flags, x):
    cells, face = [], []
    for v in range(5):
        mid = state[v, pl.ds(x, SLABS)]
        cells.append([mid if k == 0 else pltpu.roll(mid, (-k) % 128, 2) for k in range(-2, 4)])
        g = cot[v, pl.ds(x, SLABS)]
        face.append(STEP * (pltpu.roll(g, 127, 2) - g))
    terms = face_pull(cells, face, flags[2, pl.ds(x, SLABS)], 2)
    total = []
    for v in range(5):
        t = terms[v][2]
        for k in (-2, -1, 1, 2, 3):
            t = t + pltpu.roll(terms[v][k + 2], k % 128, 2)
        total.append(t)
    return total


def e_kernel(flat, near_twin, near_other, far_twin, far_other, order, out):
    del order
    state, cot = views(flat)
    nx = out.shape[0] // 40
    rim_state, rim_cot, rim_flags = from_rims(near_twin, near_other, far_twin, far_other)

    def own(ref, row, v):
        return ref[pl.ds(v * nx * 8 + row, nx, stride=8), :]

    state_rows, cot_rows = {}, {}
    for v in range(5):
        for row in (*range(-5, 3), *range(6, 13)):
            inside = 0 <= row < 8
            state_rows[row, v] = own(state, row, v) if inside else rim_state(row, v)
        for row in (-3, -2, -1, 0, 8, 9, 10):
            inside = 0 <= row < 8
            cot_rows[row, v] = own(cot, row, v) if inside else rim_cot(row, v)
    sums = {}
    for j in (-3, -2, -1, 8, 9):
        cells = [[state_rows[j + k, v] for k in range(-2, 4)] for v in range(5)]
        face = [STEP * (cot_rows[j + 1, v] - cot_rows[j, v]) for v in range(5)]
        terms = face_pull(cells, face, rim_flags(j), 1)
        for v in range(5):
            for k in range(-2, 4):
                if 0 <= j + k < 8:
                    t = terms[v][k + 2]
                    sums[j + k, v] = sums[j + k, v] + t if (j + k, v) in sums else t
    for v in range(5):
        for row in range(8):
            value = sums[row, v] if (row, v) in sums else jnp.zeros((nx, 128), F32)
            out[pl.ds(v * nx * 8 + row, nx, stride=8), :] = value


def yz_kernel(lo, hi, fields, flags, near_twin, near_other, far_twin, far_other, first, before, rim, order, out, halo, ghalo):
    del order
    state, cot = views(fields)
    rims = from_rims(near_twin, near_other, far_twin, far_other)
    rim_state, rim_cot, _ = rims
    nx = out.shape[1]
    for v in range(5):
        for kept in (pl.ds(0, lo), pl.ds(hi, nx - hi)):
            if kept.size:
                out[v, kept] = before[v, kept]
    for v in range(5):
        base = v * nx * 8
        for r in range(ABOVE):
            halo[pl.ds(base + r, nx, stride=8), :] = rim_state(8 + r, v)
        for r in range(BELOW):
            halo[pl.ds(base + 8 - BELOW + r, nx, stride=8), :] = rim_state(r - BELOW, v)
        ghalo[pl.ds(base, nx, stride=8), :] = rim_cot(8, v)
    row = lax.broadcasted_iota(jnp.int32, (SLABS, 8, 128), 1)
    inside = {}
    for k in (-2, -1, 1, 2, 3):
        inside[k] = (row < 8 + k) if k < 0 else (row >= k)

    def step(i, carry):
        x = lo + i * SLABS
        cells, face = [], []
        for v in range(5):
            at = pl.multiple_of((v * nx + x) * 8, 8)
            rim_rows = halo[pl.ds(at, 8 * SLABS), :].reshape(SLABS, 8, 128)
            mid = state[v, pl.ds(x, SLABS)]
            line = []
            for k in range(-2, 4):
                if k == 0:
                    line.append(mid)
                else:
                    line.append(pltpu.roll(jnp.where(inside[k], mid, rim_rows), (-k) % 8, 1))
            cells.append(line)
            g = cot[v, pl.ds(x, SLABS)]
            g_rim = ghalo[pl.ds(at, 8 * SLABS), :].reshape(SLABS, 8, 128)
            face.append(STEP * (pltpu.roll(jnp.where(inside[1], g, g_rim), 7, 1) - g))
        terms = face_pull(cells, face, flags[1, pl.ds(x, SLABS)], 1)
        along_z = z_faces(state, cot, flags, x)
        for v in range(5):
            at = pl.multiple_of((v * nx + x) * 8, 8)
            total = before[v, pl.ds(x, SLABS)] + first[v, pl.ds(x, SLABS)]
            total = total + along_z[v] + terms[v][2]
            total = total + rim[pl.ds(at, 8 * SLABS), :].reshape(SLABS, 8, 128)
            for k in (-2, -1, 1, 2, 3):
                moved = pltpu.roll(terms[v][k + 2], k % 8, 1)
                total = total + jnp.where(inside[k], moved, 0.0)
            out[v, pl.ds(x, SLABS)] = total
        return carry

    lax.fori_loop(0, (hi - lo) // SLABS, step, 0)


def sum_kernel(scale, mine, theirs, k_out, h_out):
    total = (mine[...] + theirs[...]) * scale
    k_out[...] = total[:, : k_out.shape[1]]
    ch = total.shape[0]
    pick = (
        lax.broadcasted_iota(jnp.int32, (8, 128), 1)
        == lax.broadcasted_iota(jnp.int32, (8, 128), 0) + 16
    ).astype(F32)
    heads = lax.dot_general(
        pick,
        total[:, 128:],
        (((1,), (1,)), ((), ())),
        precision=lax.Precision.HIGHEST,
        preferred_element_type=F32,
    )
    h_out[...] = heads[: h_out.shape[0], :ch]


MAIN, RIM = 48, 16
OWN_COLUMNS = 9 * (MAIN + RIM)
COLUMNS = OWN_COLUMNS + 9 * RIM


def split(x):
    hi = x.astype(BF16)
    return hi, (x - hi.astype(F32)).astype(BF16)


def over_lanes(a, b):
    return lax.dot_general(a, b, (((1,), (1,)), ((), ())), preferred_element_type=F32)


def is_even():
    return lax.rem(lax.axis_index("gy"), 2) == 0


def put_patches(high, low, x, rows):
    n = rows.shape[0]
    hi, lo = split(rows)
    hi32, lo32 = hi.astype(F32), lo.astype(F32)
    for q, turn in enumerate((1, 0, 127)):
        at = pl.ds((x + 1) * 3 * n + q * n, n)
        high[at, :] = pltpu.roll(hi32, turn, 1).astype(BF16) if turn else hi
        low[at, :] = pltpu.roll(lo32, turn, 1).astype(BF16) if turn else lo


def wrap_patches(high, low, nx, rows):
    n = 3 * rows
    for ref in (high, low):
        ref[pl.ds(0, n), :] = ref[pl.ds(nx * n, n), :]
        ref[pl.ds((nx + 1) * n, n), :] = ref[pl.ds(n, n), :]


def prepare_kernel(fields, kernel, heads, order, order2, w_rows, w_cols, w_head, bias, t, t_low, wide):
    del order, order2
    state, _ = views(fields)
    nx = state.shape[1]
    for x in range(nx):
        rows = [state[v, x] - (1.0 if v in (0, 4) else 0.0) for v in range(5)]
        mid = jnp.concatenate([*rows, jnp.zeros((8, 128), F32)], axis=0)
        put_patches(t, t_low, x, mid)
    wrap_patches(t, t_low, nx, MAIN)

    ch, taps = kernel.shape
    w = kernel[...]
    hi, lo = split(w)
    wide[...] = jnp.zeros_like(wide)
    wide[pl.ds(0, ch), pl.ds(0, taps)] = hi.astype(F32)
    wide[pl.ds(ch, ch), pl.ds(0, taps)] = lo.astype(F32)
    both = wide[...].astype(BF16)
    kind, tap = columns(COLUMNS)
    base = jnp.dot(both, own_taps(kind, tap), preferred_element_type=F32)
    rim = jnp.dot(both, rim_taps(kind, tap), preferred_element_type=F32)
    n = base.shape[1]
    kind = jnp.broadcast_to(kind[0:1], base.shape)
    main = jnp.where(kind < 3, base, 0.0)
    bands = []
    for y in range(8):
        rows = main
        if y == 0:
            rows = jnp.where(kind == 0, 0.0, rows)
        if y == 7:
            rows = jnp.where(kind == 2, 0.0, rows)
        if y != 1:
            rows = pltpu.roll(rows, (y - 1) % n, 1)
        if y == 0:
            rows = rows + jnp.where(kind == 8, base, 0.0)
        if y == 7:
            rows = rows + jnp.where(kind == 10, base, 0.0)
        bands.append(rows)
    bands.append(jnp.where((kind == 0) | (kind == 8) | (kind == 9), rim, 0.0))
    bands.append(jnp.where((kind == 7) | (kind == 10) | (kind == 11), rim, 0.0))
    full = jnp.concatenate([b[:ch] for b in bands] + [b[ch:] for b in bands], axis=0)
    w_rows[...] = full.astype(BF16)
    kept = full.shape[0] // 2
    cols = jnp.concatenate([full[:kept], full[:kept], full[kept:]], axis=0)
    cols = jnp.concatenate([cols, jnp.zeros((512 - 3 * kept, n), F32)], axis=0)
    own_cols = []
    for q in range(3):
        own_cols += [cols[:, (3 * q + o) * MAIN : (3 * q + o) * MAIN + 40] for o in range(3)]
        own_cols.append(jnp.zeros((512, 8), F32))
    w_cols[...] = jnp.concatenate(own_cols, axis=1).T.astype(BF16)
    total = jnp.sum(w * level_taps(w.shape), axis=1, keepdims=True)
    total = jnp.broadcast_to(total, (ch, 128))
    bias[...] = jnp.concatenate([total] * 10, axis=0)

    h_hi, h_lo = split(STEP * heads[...])
    none = jnp.zeros((3, ch), F32)
    pair = jnp.concatenate([h_hi.astype(F32), none, h_lo.astype(F32), none], axis=0).astype(BF16)
    r = lax.broadcasted_iota(jnp.int32, (kept, ch), 0)
    q = lax.broadcasted_iota(jnp.int32, (kept, ch), 1)
    spread = jnp.where((r & (ch - 1)) == q, 1.0, 0.0).astype(BF16)
    picked = over_lanes(pair, spread)
    y_of = lax.broadcasted_iota(jnp.int32, (8, kept), 0)
    col = lax.broadcasted_iota(jnp.int32, (8, kept), 1)
    same = (col >= y_of * ch) & (col < (y_of + 1) * ch)
    split_heads = []
    for at in (0, 8):
        rows = [
            jnp.where(same, jnp.broadcast_to(picked[at + e : at + e + 1], (8, kept)), 0.0)
            for e in range(5)
        ]
        five = picked[at : at + 8]
        rows.append(jnp.where((col >= 8 * ch) & (col < 9 * ch), five, 0.0))
        rows.append(jnp.where(col >= 9 * ch, five, 0.0))
        rows.append(jnp.zeros((8, kept), F32))
        split_heads.append(jnp.concatenate(rows, axis=0))
    three = jnp.concatenate([split_heads[0], split_heads[1], split_heads[0]], axis=0)
    w_head[...] = three.T.astype(BF16)


def c_kernel(
    fields, near_twin, near_other, kernel, w_rows, w_cols, w_head, bias, t, t_low,
    own, parts,
    rim, rim_low, outer, outer_low, acc, edge, gedge,
):
    _, cot = views(fields)
    nx = cot.shape[1]
    ch, taps = kernel.shape
    rim_state, rim_cot, _ = from_rims(near_twin, near_other)

    for v in range(5):
        level = 1.0 if v in (0, 4) else 0.0
        for q, row in enumerate((-1, 8, -2, 9)):
            at = q // 2 * RIM + 5 * (q % 2) + v
            edge[pl.ds(at, nx, stride=2 * RIM), :] = rim_state(row, v) - level
        gedge[pl.ds(v, nx, stride=16), :] = rim_cot(-1, v)
        gedge[pl.ds(8 + v, nx, stride=16), :] = rim_cot(8, v)
    none = jnp.zeros((nx, 128), F32)
    for q in range(10, RIM):
        edge[pl.ds(q, nx, stride=2 * RIM), :] = none
        edge[pl.ds(RIM + q, nx, stride=2 * RIM), :] = none
    for q in (5, 6, 7):
        gedge[pl.ds(q, nx, stride=16), :] = none
        gedge[pl.ds(8 + q, nx, stride=16), :] = none
    for x in range(nx):
        put_patches(rim, rim_low, x, edge[pl.ds(2 * x * RIM, RIM), :])
        put_patches(outer, outer_low, x, edge[pl.ds((2 * x + 1) * RIM, RIM), :])
    wrap_patches(rim, rim_low, nx, RIM)
    wrap_patches(outer, outer_low, nx, RIM)

    def gathered(x, *blocks):
        columns = []
        for j in range(WIDE):
            rows = [ref[pl.ds((x + j) * 3 * n, 9 * n), :] for ref, n in blocks]
            columns.append(jnp.concatenate(rows, axis=0) if len(rows) > 1 else rows[0])
        return jnp.concatenate(columns, axis=1)

    kept = 8 * ch
    kg = hg = dsum = None
    zeros8 = jnp.zeros((8, 128 * WIDE), F32)
    written = set()
    for x in range(0, nx, WIDE):
        s_hi = gathered(x, (t, MAIN), (rim, RIM))
        s_lo = gathered(x, (t_low, MAIN), (rim_low, RIM))
        far_hi, far_lo = gathered(x, (outer, RIM)), gathered(x, (outer_low, RIM))
        z2 = jnp.dot(
            w_rows[...], jnp.concatenate([s_hi, far_hi], axis=0), preferred_element_type=F32
        )
        rows = z2.shape[0] // 2
        z3 = jnp.dot(
            w_rows[pl.ds(0, rows), :],
            jnp.concatenate([s_lo, far_lo], axis=0),
            preferred_element_type=F32,
        )
        z = z2[:rows] + (z2[rows:] + z3) + jnp.concatenate([bias[...]] * WIDE, axis=1)
        hidden = jnp.tanh(z)
        g = jnp.concatenate(
            [
                jnp.concatenate(
                    [cot[v, x + j] for v in range(5)] + [gedge[pl.ds((x + j) * 16, 16), :]], axis=0
                )
                for j in range(WIDE)
            ],
            axis=1,
        )
        g_hi, g_lo = split(g)
        g_hi32, g_lo32 = g_hi.astype(F32), g_lo.astype(F32)
        g3 = jnp.concatenate(
            [g_hi32, zeros8, g_hi32, zeros8, g_lo32, zeros8], axis=0
        ).astype(BF16)
        d = (1.0 - hidden * hidden) * jnp.dot(w_head[...], g3, preferred_element_type=F32)
        d_hi, d_lo = split(d)
        zeros = jnp.zeros((512 - 3 * rows, 128 * WIDE), BF16)
        back = jnp.dot(
            w_cols[...],
            jnp.concatenate([d_hi, d_lo, d_hi, zeros], axis=0),
            preferred_element_type=F32,
        )
        k2 = over_lanes(
            jnp.concatenate([s_hi, s_lo], axis=0),
            jnp.concatenate([d_hi[:kept], d_lo[:kept]], axis=0),
        )
        k2 = k2[:OWN_COLUMNS, :kept] + (k2[:OWN_COLUMNS, kept:] + k2[OWN_COLUMNS:, :kept])
        kg = k2 if kg is None else kg + k2
        hid2 = jnp.concatenate(split(hidden[:kept]), axis=0)
        g2 = jnp.concatenate([g_hi32[:40], g_lo32[:40]], axis=0).astype(BF16)
        h2 = over_lanes(g2, hid2)
        hg = h2 if hg is None else hg + h2
        for j in range(WIDE):
            level = d[:kept, 128 * j : 128 * (j + 1)]
            dsum = level if dsum is None else dsum + level
        for m in range(WIDE + 2):
            total = None
            for j in range(WIDE):
                if 0 <= m - j < 3:
                    q = m - j
                    piece = back[q * 128 : q * 128 + 120, 128 * j : 128 * (j + 1)]
                    total = piece if total is None else total + piece
            here = (x + m - 1) % nx
            if here in written:
                total = total + acc[pl.ds(here * 120, 120), :]
            written.add(here)
            acc[pl.ds(here * 120, 120), :] = total
    for x in range(nx):
        at = x * 120
        total = (
            acc[pl.ds(at + 40, 40), :]
            + pltpu.roll(acc[pl.ds(at, 40), :], 127, 1)
            + pltpu.roll(acc[pl.ds(at + 80, 40), :], 1, 1)
        )
        for v in range(5):
            own[v, x] = total[8 * v : 8 * v + 8]

    sums = jnp.sum(dsum, axis=1, keepdims=True)
    kg = kg.T
    hg = (hg[:40, :kept] + hg[40:, :kept]) + (hg[:40, kept:] + hg[40:, kept:])
    y_row = lax.broadcasted_iota(jnp.int32, (40, kept), 0) & 7
    y_col = lax.broadcasted_iota(jnp.int32, (40, kept), 1)
    same_y = (y_col >= y_row * ch) & (y_col < (y_row + 1) * ch)
    hg = jnp.where(same_y, hg, 0.0)
    by_eq = jnp.concatenate(
        [jnp.sum(hg[8 * e : 8 * e + 8], axis=0, keepdims=True) for e in range(5)]
        + [jnp.zeros((123, kept), F32)],
        axis=0,
    ).T
    level_sum = jnp.zeros((ch, 1), F32)
    head_sum = jnp.zeros((ch, 128), F32)
    n = kg.shape[1]
    columns_at, tap = columns(n)
    kind = jnp.broadcast_to(columns_at[0:1], (ch, n))
    total = jnp.zeros((ch, n), F32)
    for y in range(8):
        rows = kg[y * ch : (y + 1) * ch]
        moved = rows if y == 1 else pltpu.roll(rows, (1 - y) % n, 1)
        keep = kind < 3
        if y == 0:
            keep = (kind == 1) | (kind == 2)
            total = total + jnp.where(kind == 8, rows, 0.0)
        if y == 7:
            keep = kind < 2
            total = total + jnp.where(kind == 10, rows, 0.0)
        total = total + jnp.where(keep, moved, 0.0)
        level_sum = level_sum + sums[y * ch : (y + 1) * ch]
        head_sum = head_sum + by_eq[y * ch : (y + 1) * ch]
    grads = over_lanes(jnp.concatenate(split(total), axis=0), own_taps(columns_at, tap))
    n_pick = grads.shape[1]
    parts[...] = jnp.zeros_like(parts)
    parts[:, pl.ds(0, n_pick)] = grads[:ch] + grads[ch:]
    parts[:, pl.ds(0, taps)] = parts[:, pl.ds(0, taps)] + level_sum * level_taps((ch, taps))
    parts[:, pl.ds(128, 128)] = parts[:, pl.ds(128, 128)] + pltpu.roll(head_sum * STEP, 16, 1)


def columns(n):
    lane = lax.broadcasted_iota(jnp.int32, (8, n), 1)
    main = lane < 9 * MAIN
    far = lane >= OWN_COLUMNS
    past = lane - jnp.where(far, OWN_COLUMNS, 9 * MAIN)
    block = sum((lane >= MAIN * i).astype(jnp.int32) for i in range(1, 9))
    o = jnp.where(main, block, past >> 4)
    r = jnp.where(main, lane - MAIN * block, past & (RIM - 1))
    second = (r >= 5).astype(jnp.int32)
    rim = jnp.where(r < 10, 8 + 2 * second + far.astype(jnp.int32), 12)
    kind = jnp.where(main, jnp.where(r < 40, r & 7, 12), rim)
    v = jnp.where(main, r >> 3, r - 5 * second)
    return kind, o * 5 + v


def taps_of(columns_at):
    n = columns_at.shape[1]
    row = lax.broadcasted_iota(jnp.int32, (144, n), 0)
    return jnp.where(row == jnp.broadcast_to(columns_at[0:1], (144, n)), 1.0, 0.0).astype(BF16)


def own_taps(kind, tap):
    at = jnp.where(kind < 3, tap + 45 * kind, 1000)
    at = jnp.where(kind == 8, tap, at)
    return taps_of(jnp.where(kind == 10, tap + 90, at))


def rim_taps(kind, tap):
    first = (kind == 9) | (kind == 7)
    middle = (kind == 8) | (kind == 10)
    last = (kind == 0) | (kind == 11)
    at = jnp.where(first, tap, jnp.where(middle, tap + 45, 1000))
    return taps_of(jnp.where(last, tap + 90, at))


def level_taps(shape):
    t = lax.broadcasted_iota(jnp.int32, shape, 1).astype(F32)
    v = t - 5.0 * jnp.floor((t + 0.5) * 0.2)
    return jnp.where((v < 0.5) | (v > 3.5), 1.0, 0.0)


def call(kernel, outs, scratch, us, n_in, order=0):
    spec = pl.BlockSpec(memory_space=pltpu.VMEM)
    return pl.pallas_call(
        kernel,
        out_shape=outs,
        in_specs=[spec] * n_in + [pl.BlockSpec(memory_space=pl.ANY)] * order,
        scratch_shapes=scratch,
        compiler_params=pltpu.CompilerParams(vmem_limit_bytes=VMEM),
        cost_estimate=pl.CostEstimate(
            flops=int(us * 1.15e9), bytes_accessed=int(us * 3.69e6), transcendentals=0
        ),
    )


def body(state, cot, flags, kernel, heads):
    _, nx, ny, nz = state.shape
    ch, taps = kernel.shape
    count = lax.axis_size("gy")
    cells = nx * ny * nz
    shape = lambda *dims: jax.ShapeDtypeStruct(dims, F32)
    half_shape = lambda *dims: jax.ShapeDtypeStruct(dims, BF16)
    full = shape(5, nx, ny, nz)
    with_twin = [(i, i ^ 1) for i in range(count)]
    with_other = [(i, (i + 1) % count if i % 2 else (i - 1) % count) for i in range(count)]
    vm = pltpu.VMEM
    lines = 5 * nx * ny

    flat = jnp.concatenate([state.reshape(lines, nz), cot.reshape(lines, nz)])
    fields = flat.reshape(10, nx, ny, nz)
    near, far = shape(NEAR, nx, nz), shape(FAR, nx, nz)
    x_scratch = [
        vm((5, nx + 5, ny, nz), F32),
        vm((5, nx + 1, ny, nz), F32),
        vm((5, nx + 5, ny, nz), F32),
    ]
    early = call(x_early_kernel, full, x_scratch, 0.2, 2)(fields, flags)
    near_twin, near_other = call(near_kernel, (near, near), [], 0.2, 1, 1)(flat, early)
    near_rims = (
        lax.ppermute(near_twin, "gy", with_twin),
        lax.ppermute(near_other, "gy", with_other),
    )
    *prepared, patches, patches_low = call(
        prepare_kernel,
        (
            half_shape(20 * ch, COLUMNS),
            half_shape(384, 512),
            half_shape(10 * ch, 192),
            shape(10 * ch, 128),
            half_shape((nx + 2) * 3 * MAIN, nz),
            half_shape((nx + 2) * 3 * MAIN, nz),
        ),
        [vm((2 * ch, 144), F32)],
        1.5,
        3,
        2,
    )(fields, kernel, heads, near_twin, near_other)
    first = call(x_late_kernel, full, x_scratch, 2.8, 3, 1)(fields, flags, early, patches)
    far_twin, far_other = call(far_kernel, (far, far), [], 0.2, 2, 1)(
        flat, flags.reshape(3 * nx * ny, nz), first
    )
    far_rims = (
        lax.ppermute(far_twin, "gy", with_twin),
        lax.ppermute(far_other, "gy", with_other),
    )
    near_rims, patches, first = lax.optimization_barrier((near_rims, patches, first))
    own, parts = call(
        c_kernel,
        (full, shape(ch, 256)),
        [
            *[vm(((nx + 2) * 3 * RIM, nz), BF16)] * 4,
            vm((nx * 120, nz), F32),
            vm((2 * RIM * nx, nz), F32),
            vm((16 * nx, nz), F32),
        ],
        6.0,
        10,
    )(fields, *near_rims, kernel, *prepared, patches, patches_low)

    def exchanged(value, bit):
        return lax.ppermute(value, "gy", [(i, i ^ bit) for i in range(count)])

    bits = [1 << b for b in range(count.bit_length() - 1)]
    sums = parts
    for bit in bits[:-4]:
        sums = sums + exchanged(sums, bit)
    third = nx // 6 * 2
    yz = lambda lo, hi, before, order: call(
        functools.partial(yz_kernel, lo, hi), full, [vm((lines, nz), F32)] * 2, 2.2, 9, 1
    )(fields, flags, *near_rims, *far_rims, first, before, rim, order)
    got = exchanged(sums, bits[-4])
    rim = call(e_kernel, shape(lines, nz), [], 1.1, 5, 1)(flat, *near_rims, *far_rims, sums)
    got, rim = lax.optimization_barrier((got, rim))
    sums = sums + got
    got = exchanged(sums, bits[-3])
    total = yz(0, third, own, sums)
    got, total = lax.optimization_barrier((got, total))
    sums = sums + got
    got = exchanged(sums, bits[-2])
    total = yz(third, nx - nx // 8 * 3, total, sums)
    got, total = lax.optimization_barrier((got, total))
    sums = sums + got
    got = exchanged(sums, bits[-1])
    flow = yz(nx - nx // 8 * 3, nx, total, sums)
    got, flow = lax.optimization_barrier((got, flow))
    scale = float(cells * count) ** (-0.5)
    k_out, h_out = call(
        functools.partial(sum_kernel, scale), (shape(ch, taps), shape(5, ch)), [], 0.5, 2
    )(sums, got)
    return flow, k_out, h_out


def solution(mesh):
    split_y = P(None, "ens", "gy", None)
    return jax.shard_map(
        body,
        mesh=mesh,
        in_specs=(split_y, split_y, split_y, P(), P()),
        out_specs=(split_y, P("ens", None), P("ens", None)),
        check_vma=False,
    )
```

```python
import functools

import jax
import jax.numpy as jnp
from jax import lax
from jax.experimental import pallas as pl
from jax.experimental.pallas import tpu as pltpu
from jax.sharding import PartitionSpec as P

STEP = 0.3
FLOOR = 0.01
BELOW, ABOVE = 2, 3
SLABS = 2
WIDE = 4
VMEM = 48 * 1024 * 1024
F32 = jnp.float32
BF16 = jnp.bfloat16


def rcp(x):
    return pl.reciprocal(x, approx=True)


def shared_terms(v):
    p = [v[i + 1] - v[i] for i in range(5)]
    d = [p[i + 1] - p[i] for i in range(4)]
    h = [(4.0 / 3.0) * x for x in d]
    k = [h[i] * d[i] + FLOOR for i in range(4)]
    g = [x + x for x in h]
    t = [d[i + 1] - d[i] for i in range(3)]
    return p, d, k, g, t


def side_value(pa, pm, pm2, ka, kb, kc, m0, m2, td, t1, smooth, c0, c2):
    i0 = rcp(ka + pa * m0)
    i1 = rcp(kb + pa * pm)
    i2 = rcp(kc + pm * m2)
    w0 = i0 * i0
    w1 = 6.0 * (i1 * i1)
    w2 = 3.0 * (i2 * i2)
    r = rcp(w0 + w1 + w2)
    o0 = jnp.where(smooth, w0 * r, c0)
    o2 = jnp.where(smooth, w2 * r, c2)
    u = o0 * td + o2 * t1
    b0 = w0 * i0 * (td - u)
    b1 = w1 * i1 * u
    b2 = w2 * i2 * (t1 - u)
    return (pa + pm2) - u, (b0, b1, b2, r, o0, o2)


def side_pull(mu, pa, pm, m0, m2, smooth, saved):
    b0, b1, b2, r, o0, o2 = saved
    mu2 = mu + mu
    rm = jnp.where(smooth, mu2, 0.0) * r
    s0, s1, s2 = b0 * rm, b1 * rm, b2 * rm
    pa_bar = s0 * (m0 + pa) - s1 * pm + mu
    pm_bar = s2 * (m2 + pm) - s1 * pa + mu2
    return s0, s1, s2, pa_bar, pm_bar, o0 * mu2, o2 * mu


def hllc_pull(left, right, normal, flags, cot):
    region = flags & 3
    is_right = region >= 2
    star = ((region + 1) & 2) != 0
    n_at = 1 + normal
    tang = [1 + i for i in range(3) if i != normal]
    rl, rr_, pl_, pr_, nl, nr = left[0], right[0], left[4], right[4], left[n_at], right[n_at]

    def sound(r, p):
        inv = rcp(r)
        t = 1.4 * p * inv
        inv_c = lax.rsqrt(t)
        return inv, inv_c, t * inv_c

    inv_rl, inv_cl, cl = sound(rl, pl_)
    inv_rr, inv_cr, cr = sound(rr_, pr_)
    c = 0.5 * (cl + cr)
    r2 = rl + rr_
    inv = rcp(r2 * c)
    nm = 0.5 * (nl + nr)
    gap = (pl_ - pr_) * inv
    sm = nm + gap
    sc = jnp.where(is_right, c, -c)
    s = nm + sc
    pick = [jnp.where(is_right, right[i], left[i]) for i in range(5)]
    r, un, u1, u2, p = pick[0], pick[n_at], pick[tang[0]], pick[tang[1]], pick[4]
    a = s - un
    dl = sm - un
    si = jnp.where(star, rcp(sc - gap), 0.0)
    j = s * si
    kap = j * dl
    g0, gn, g1, g2, ge = cot[0], cot[n_at], cot[tang[0]], cot[tang[1]], cot[4]
    w = un + kap
    half_q = 0.5 * (un * un + u1 * u1 + u2 * u2)
    enthalpy = 3.5 * p + r * half_q
    b = g0 + u1 * g1 + u2 * g2 + un * gn
    m = r * b + enthalpy * ge
    n = gn + sm * ge
    rkap = r * kap
    f_kap = m + r * a * n
    f_a = rkap * n
    si2 = si * si
    s_bar = f_a - f_kap * (dl * sm * si2)
    sm_bar = f_kap * (s * a * si2) + rkap * a * ge
    wr = w * r
    k_bar = [None] * 5
    k_bar[0] = w * (b + half_q * ge) + kap * a * n
    k_bar[n_at] = m + wr * (gn + un * ge) - f_kap * j - f_a
    k_bar[tang[0]] = wr * (g1 + u1 * ge)
    k_bar[tang[1]] = wr * (g2 + u2 * ge)
    k_bar[4] = 3.5 * (w * ge) + gn
    e = sm_bar * inv
    eg = e * gap
    c_half = 0.5 * (jnp.where(is_right, s_bar, -s_bar) - eg * r2)
    n_half = 0.5 * (s_bar + sm_bar)
    r_both = -(eg * c)
    xl = c_half * inv_rl
    xr = c_half * inv_rr
    base_l = {0: r_both - 0.5 * (xl * cl), n_at: n_half, 4: 0.7 * (xl * inv_cl) + e}
    base_r = {0: r_both - 0.5 * (xr * cr), n_at: n_half, 4: 0.7 * (xr * inv_cr) - e}
    l_bar, r_bar = [], []
    for i in range(5):
        kr = jnp.where(is_right, k_bar[i], 0.0)
        kl = k_bar[i] - kr
        l_bar.append(base_l[i] + kl if i in base_l else kl)
        r_bar.append(base_r[i] + kr if i in base_r else kr)
    return l_bar, r_bar


def face_pull(cells, cot, flags, normal):
    stencil = flags >> 2
    smooth = stencil == 0
    c0 = jnp.where(stencil == 1, 1.0, 0.0)
    c2 = jnp.where(stencil == 3, 1.0, 0.0)
    left, right, kept = [], [], []
    for v in cells:
        p, d, k, g, t = shared_terms(v)
        pm2 = p[2] + p[2]
        args_l = (p[1], p[2], p[1] + d[0], p[2] - d[2], t[0] + t[0], t[1])
        args_r = (p[3], p[2], p[3] - d[3], p[2] + d[1], t[2] + t[2], t[1])
        hl, saved_l = side_value(
            p[1], p[2], pm2, k[0], k[1], k[2], *args_l[2:], smooth, c0, c2
        )
        hr, saved_r = side_value(
            p[3], p[2], pm2, k[3], k[2], k[1], *args_r[2:], smooth, c0, c2
        )
        left.append(v[2] + hl * (1.0 / 6.0))
        right.append(v[3] - hr * (1.0 / 6.0))
        kept.append((p, g, args_l[:4], args_r[:4], saved_l, saved_r))
    l_bar, r_bar = hllc_pull(left, right, normal, flags, cot)
    out = []
    for i in range(5):
        p, g, args_l, args_r, saved_l, saved_r = kept[i]
        a0, a1, a2, pa_l, pm_l, x0, x2 = side_pull(
            l_bar[i] * (1.0 / 6.0), *args_l, smooth, saved_l
        )
        b0, b1, b2, pa_r, pm_r, y0, y2 = side_pull(
            r_bar[i] * (-1.0 / 6.0), *args_r, smooth, saved_r
        )
        d0 = a0 * (g[0] + p[1]) + x0
        d1 = (b2 * (g[1] + p[2]) - a1 * g[1]) + (x2 - x0) + y2
        d2 = (a2 * (g[2] - p[2]) - b1 * g[2]) + (y0 - y2) - x2
        d3 = b0 * (g[3] - p[3]) - y0
        p2 = pa_l + (d0 - d1)
        p3 = pm_l + pm_r + (d1 - d2)
        p4 = pa_r + (d2 - d3)
        out.append([d0, -d0 - p2, l_bar[i] + (p2 - p3), r_bar[i] + (p3 - p4), p4 - d3, d3])
    return out


def conserved_pull(s, g):
    half_q = 0.5 * (s[1] * s[1] + s[2] * s[2] + s[3] * s[3])
    return [
        g[0] + s[1] * g[1] + s[2] * g[2] + s[3] * g[3] + half_q * g[4],
        s[0] * (g[1] + s[1] * g[4]),
        s[0] * (g[2] + s[2] * g[4]),
        s[0] * (g[3] + s[3] * g[4]),
        2.5 * g[4],
    ]


NEAR_STATE, FAR_STATE = 2, 3
NEAR_COT, FAR_COT = 1, 2
FLAG_ROWS = 3
NEAR = 5 * (NEAR_STATE + NEAR_COT)
FAR = 5 * (FAR_STATE + FAR_COT) + FLAG_ROWS


def views(fields):
    n = fields.shape[0] // 2
    return fields.at[pl.ds(0, n)], fields.at[pl.ds(n, n)]


def pack(ref, rows, first, twin, other, at):
    even = is_even()
    nx = twin.shape[1]
    count = ref.shape[0] // (8 * nx)
    for r in rows:
        for v in range(count):
            low = ref[pl.ds(v * nx * 8 + r, nx, stride=8), :].astype(F32)
            top = ref[pl.ds(v * nx * 8 + 7 - r, nx, stride=8), :].astype(F32)
            i = at + (r - first) * count + v
            twin[i] = jnp.where(even, top, low)
            other[i] = jnp.where(even, low, top)


def near_kernel(flat, order, twin, other):
    del order
    s, g = views(flat)
    pack(s, range(NEAR_STATE), 0, twin, other, 0)
    pack(g, range(NEAR_COT), 0, twin, other, 5 * NEAR_STATE)


def far_kernel(flat, flags, order, twin, other):
    del order
    s, g = views(flat)
    n = flags.shape[0] // 3
    pack(s, range(NEAR_STATE, NEAR_STATE + FAR_STATE), NEAR_STATE, twin, other, 0)
    pack(g, range(NEAR_COT, NEAR_COT + FAR_COT), NEAR_COT, twin, other, 5 * FAR_STATE)
    pack(flags.at[pl.ds(n, n)], range(FLAG_ROWS), 0, twin, other, FAR - FLAG_ROWS)


def from_rims(near_twin, near_other, far_twin=None, far_other=None):
    even = is_even()

    def pick(twin, other, i, below):
        if below:
            return jnp.where(even, other[i], twin[i])
        return jnp.where(even, twin[i], other[i])

    def read(row, near, near_at, far_at, v):
        below = row < 0
        r = -1 - row if below else row - 8
        if r < near:
            return pick(near_twin, near_other, near_at + r * 5 + v, below)
        return pick(far_twin, far_other, far_at + (r - near) * 5 + v, below)

    def state(row, v):
        return read(row, NEAR_STATE, 0, 0, v)

    def cot(row, v):
        return read(row, NEAR_COT, 5 * NEAR_STATE, 5 * FAR_STATE, v)

    def flags(row):
        below = row < 0
        r = -1 - row if below else row - 8
        return pick(far_twin, far_other, FAR - FLAG_ROWS + r, below).astype(jnp.int32)

    return state, cot, flags


def x_faces(fields, flags, out, pad, gpad, acc):
    state, cot = views(fields)
    nx = state.shape[1]
    for v in range(5):
        pad[v, pl.ds(2, nx)] = state[v]
        pad[v, pl.ds(0, 2)] = state[v, pl.ds(nx - 2, 2)]
        pad[v, pl.ds(nx + 2, 3)] = state[v, pl.ds(0, 3)]
        gpad[v, pl.ds(0, nx)] = cot[v]
        gpad[v, pl.ds(nx, 1)] = cot[v, pl.ds(0, 1)]
    acc[...] = jnp.zeros_like(acc)

    def step(i, carry):
        x = i * SLABS
        cells = [[pad[v, pl.ds(x + k, SLABS)] for k in range(6)] for v in range(5)]
        g = [gpad[v, pl.ds(x, SLABS)] for v in range(5)]
        face = [STEP * (gpad[v, pl.ds(x + 1, SLABS)] - g[v]) for v in range(5)]
        terms = face_pull(cells, face, flags[0, pl.ds(x, SLABS)], 0)
        own = conserved_pull([cells[v][2] for v in range(5)], g)
        for v in range(5):
            terms[v][2] = terms[v][2] + own[v]
            for s in range(SLABS + 5):
                total = None
                for k in range(6):
                    if 0 <= s - k < SLABS:
                        part = terms[v][k][s - k]
                        total = part if total is None else total + part
                acc[v, x + s] = acc[v, x + s] + total
        return carry

    lax.fori_loop(0, nx // SLABS, step, 0)
    for v in range(5):
        acc[v, pl.ds(nx, 2)] = acc[v, pl.ds(nx, 2)] + acc[v, pl.ds(0, 2)]
        acc[v, pl.ds(2, 3)] = acc[v, pl.ds(2, 3)] + acc[v, pl.ds(nx + 2, 3)]

    for v in range(5):
        out[v] = acc[v, pl.ds(2, nx)]


def x_early_kernel(fields, flags, out, *scratch):
    @pl.when(lax.axis_index("gy") == 0)
    def _():
        x_faces(fields, flags, out, *scratch)


def x_late_kernel(fields, flags, early, order, out, *scratch):
    del order
    first = lax.axis_index("gy") == 0

    @pl.when(first)
    def _():
        out[...] = early[...]

    @pl.when(jnp.logical_not(first))
    def _():
        x_faces(fields, flags, out, *scratch)


def z_faces(state, cot, flags, x):
    cells, face = [], []
    for v in range(5):
        mid = state[v, pl.ds(x, SLABS)]
        cells.append([mid if k == 0 else pltpu.roll(mid, (-k) % 128, 2) for k in range(-2, 4)])
        g = cot[v, pl.ds(x, SLABS)]
        face.append(STEP * (pltpu.roll(g, 127, 2) - g))
    terms = face_pull(cells, face, flags[2, pl.ds(x, SLABS)], 2)
    total = []
    for v in range(5):
        t = terms[v][2]
        for k in (-2, -1, 1, 2, 3):
            t = t + pltpu.roll(terms[v][k + 2], k % 128, 2)
        total.append(t)
    return total


def e_kernel(flat, near_twin, near_other, far_twin, far_other, order, out):
    del order
    state, cot = views(flat)
    nx = out.shape[0] // 40
    rim_state, rim_cot, rim_flags = from_rims(near_twin, near_other, far_twin, far_other)

    def own(ref, row, v):
        return ref[pl.ds(v * nx * 8 + row, nx, stride=8), :]

    state_rows, cot_rows = {}, {}
    for v in range(5):
        for row in (*range(-5, 3), *range(6, 13)):
            inside = 0 <= row < 8
            state_rows[row, v] = own(state, row, v) if inside else rim_state(row, v)
        for row in (-3, -2, -1, 0, 8, 9, 10):
            inside = 0 <= row < 8
            cot_rows[row, v] = own(cot, row, v) if inside else rim_cot(row, v)
    sums = {}
    for j in (-3, -2, -1, 8, 9):
        cells = [[state_rows[j + k, v] for k in range(-2, 4)] for v in range(5)]
        face = [STEP * (cot_rows[j + 1, v] - cot_rows[j, v]) for v in range(5)]
        terms = face_pull(cells, face, rim_flags(j), 1)
        for v in range(5):
            for k in range(-2, 4):
                if 0 <= j + k < 8:
                    t = terms[v][k + 2]
                    sums[j + k, v] = sums[j + k, v] + t if (j + k, v) in sums else t
    for v in range(5):
        for row in range(8):
            value = sums[row, v] if (row, v) in sums else jnp.zeros((nx, 128), F32)
            out[pl.ds(v * nx * 8 + row, nx, stride=8), :] = value


def yz_kernel(lo, hi, fields, flags, near_twin, near_other, far_twin, far_other, first, before, rim, order, out, halo, ghalo):
    del order
    state, cot = views(fields)
    rims = from_rims(near_twin, near_other, far_twin, far_other)
    rim_state, rim_cot, _ = rims
    nx = out.shape[1]
    for v in range(5):
        for kept in (pl.ds(0, lo), pl.ds(hi, nx - hi)):
            if kept.size:
                out[v, kept] = before[v, kept]
    for v in range(5):
        base = v * nx * 8
        for r in range(ABOVE):
            halo[pl.ds(base + r, nx, stride=8), :] = rim_state(8 + r, v)
        for r in range(BELOW):
            halo[pl.ds(base + 8 - BELOW + r, nx, stride=8), :] = rim_state(r - BELOW, v)
        ghalo[pl.ds(base, nx, stride=8), :] = rim_cot(8, v)
    row = lax.broadcasted_iota(jnp.int32, (SLABS, 8, 128), 1)
    inside = {}
    for k in (-2, -1, 1, 2, 3):
        inside[k] = (row < 8 + k) if k < 0 else (row >= k)

    def step(i, carry):
        x = lo + i * SLABS
        cells, face = [], []
        for v in range(5):
            at = pl.multiple_of((v * nx + x) * 8, 8)
            rim_rows = halo[pl.ds(at, 8 * SLABS), :].reshape(SLABS, 8, 128)
            mid = state[v, pl.ds(x, SLABS)]
            line = []
            for k in range(-2, 4):
                if k == 0:
                    line.append(mid)
                else:
                    line.append(pltpu.roll(jnp.where(inside[k], mid, rim_rows), (-k) % 8, 1))
            cells.append(line)
            g = cot[v, pl.ds(x, SLABS)]
            g_rim = ghalo[pl.ds(at, 8 * SLABS), :].reshape(SLABS, 8, 128)
            face.append(STEP * (pltpu.roll(jnp.where(inside[1], g, g_rim), 7, 1) - g))
        terms = face_pull(cells, face, flags[1, pl.ds(x, SLABS)], 1)
        along_z = z_faces(state, cot, flags, x)
        for v in range(5):
            at = pl.multiple_of((v * nx + x) * 8, 8)
            total = before[v, pl.ds(x, SLABS)] + first[v, pl.ds(x, SLABS)]
            total = total + along_z[v] + terms[v][2]
            total = total + rim[pl.ds(at, 8 * SLABS), :].reshape(SLABS, 8, 128)
            for k in (-2, -1, 1, 2, 3):
                moved = pltpu.roll(terms[v][k + 2], k % 8, 1)
                total = total + jnp.where(inside[k], moved, 0.0)
            out[v, pl.ds(x, SLABS)] = total
        return carry

    lax.fori_loop(0, (hi - lo) // SLABS, step, 0)


def sum_kernel(scale, mine, theirs, k_out, h_out):
    total = (mine[...] + theirs[...]) * scale
    k_out[...] = total[:, : k_out.shape[1]]
    ch = total.shape[0]
    pick = (
        lax.broadcasted_iota(jnp.int32, (8, 128), 1)
        == lax.broadcasted_iota(jnp.int32, (8, 128), 0) + 16
    ).astype(F32)
    heads = lax.dot_general(
        pick,
        total[:, 128:],
        (((1,), (1,)), ((), ())),
        precision=lax.Precision.HIGHEST,
        preferred_element_type=F32,
    )
    h_out[...] = heads[: h_out.shape[0], :ch]


MAIN, RIM = 48, 16
OWN_COLUMNS = 9 * (MAIN + RIM)
COLUMNS = OWN_COLUMNS + 9 * RIM


def split(x):
    hi = x.astype(BF16)
    return hi, (x - hi.astype(F32)).astype(BF16)


def over_lanes(a, b):
    return lax.dot_general(a, b, (((1,), (1,)), ((), ())), preferred_element_type=F32)


def is_even():
    return lax.rem(lax.axis_index("gy"), 2) == 0


def put_patches(high, low, x, rows):
    n = rows.shape[0]
    hi, lo = split(rows)
    hi32, lo32 = hi.astype(F32), lo.astype(F32)
    for q, turn in enumerate((1, 0, 127)):
        at = pl.ds((x + 1) * 3 * n + q * n, n)
        high[at, :] = pltpu.roll(hi32, turn, 1).astype(BF16) if turn else hi
        low[at, :] = pltpu.roll(lo32, turn, 1).astype(BF16) if turn else lo


def wrap_patches(high, low, nx, rows):
    n = 3 * rows
    for ref in (high, low):
        ref[pl.ds(0, n), :] = ref[pl.ds(nx * n, n), :]
        ref[pl.ds((nx + 1) * n, n), :] = ref[pl.ds(n, n), :]


def prepare_kernel(fields, kernel, heads, order, order2, w_rows, w_cols, w_head, bias, t, t_low, wide):
    del order, order2
    state, _ = views(fields)
    nx = state.shape[1]
    for x in range(nx):
        rows = [state[v, x] - (1.0 if v in (0, 4) else 0.0) for v in range(5)]
        mid = jnp.concatenate([*rows, jnp.zeros((8, 128), F32)], axis=0)
        put_patches(t, t_low, x, mid)
    wrap_patches(t, t_low, nx, MAIN)

    ch, taps = kernel.shape
    w = kernel[...]
    hi, lo = split(w)
    wide[...] = jnp.zeros_like(wide)
    wide[pl.ds(0, ch), pl.ds(0, taps)] = hi.astype(F32)
    wide[pl.ds(ch, ch), pl.ds(0, taps)] = lo.astype(F32)
    both = wide[...].astype(BF16)
    kind, tap = columns(COLUMNS)
    base = jnp.dot(both, own_taps(kind, tap), preferred_element_type=F32)
    rim = jnp.dot(both, rim_taps(kind, tap), preferred_element_type=F32)
    n = base.shape[1]
    kind = jnp.broadcast_to(kind[0:1], base.shape)
    main = jnp.where(kind < 3, base, 0.0)
    bands = []
    for y in range(8):
        rows = main
        if y == 0:
            rows = jnp.where(kind == 0, 0.0, rows)
        if y == 7:
            rows = jnp.where(kind == 2, 0.0, rows)
        if y != 1:
            rows = pltpu.roll(rows, (y - 1) % n, 1)
        if y == 0:
            rows = rows + jnp.where(kind == 8, base, 0.0)
        if y == 7:
            rows = rows + jnp.where(kind == 10, base, 0.0)
        bands.append(rows)
    bands.append(jnp.where((kind == 0) | (kind == 8) | (kind == 9), rim, 0.0))
    bands.append(jnp.where((kind == 7) | (kind == 10) | (kind == 11), rim, 0.0))
    full = jnp.concatenate([b[:ch] for b in bands] + [b[ch:] for b in bands], axis=0)
    w_rows[...] = full.astype(BF16)
    kept = full.shape[0] // 2
    cols = jnp.concatenate([full[:kept], full[:kept], full[kept:]], axis=0)
    cols = jnp.concatenate([cols, jnp.zeros((512 - 3 * kept, n), F32)], axis=0)
    own_cols = []
    for q in range(3):
        own_cols += [cols[:, (3 * q + o) * MAIN : (3 * q + o) * MAIN + 40] for o in range(3)]
        own_cols.append(jnp.zeros((512, 8), F32))
    w_cols[...] = jnp.concatenate(own_cols, axis=1).T.astype(BF16)
    total = jnp.sum(w * level_taps(w.shape), axis=1, keepdims=True)
    total = jnp.broadcast_to(total, (ch, 128))
    bias[...] = jnp.concatenate([total] * 10, axis=0)

    h_hi, h_lo = split(STEP * heads[...])
    none = jnp.zeros((3, ch), F32)
    pair = jnp.concatenate([h_hi.astype(F32), none, h_lo.astype(F32), none], axis=0).astype(BF16)
    r = lax.broadcasted_iota(jnp.int32, (kept, ch), 0)
    q = lax.broadcasted_iota(jnp.int32, (kept, ch), 1)
    spread = jnp.where((r & (ch - 1)) == q, 1.0, 0.0).astype(BF16)
    picked = over_lanes(pair, spread)
    y_of = lax.broadcasted_iota(jnp.int32, (8, kept), 0)
    col = lax.broadcasted_iota(jnp.int32, (8, kept), 1)
    same = (col >= y_of * ch) & (col < (y_of + 1) * ch)
    split_heads = []
    for at in (0, 8):
        rows = [
            jnp.where(same, jnp.broadcast_to(picked[at + e : at + e + 1], (8, kept)), 0.0)
            for e in range(5)
        ]
        five = picked[at : at + 8]
        rows.append(jnp.where((col >= 8 * ch) & (col < 9 * ch), five, 0.0))
        rows.append(jnp.where(col >= 9 * ch, five, 0.0))
        rows.append(jnp.zeros((8, kept), F32))
        split_heads.append(jnp.concatenate(rows, axis=0))
    three = jnp.concatenate([split_heads[0], split_heads[1], split_heads[0]], axis=0)
    w_head[...] = three.T.astype(BF16)


def c_kernel(
    fields, near_twin, near_other, kernel, w_rows, w_head, bias, t, t_low,
    parts, d_high, d_low,
    rim, rim_low, outer, outer_low, edge, gedge,
):
    _, cot = views(fields)
    nx = cot.shape[1]
    ch, taps = kernel.shape
    rim_state, rim_cot, _ = from_rims(near_twin, near_other)

    for v in range(5):
        level = 1.0 if v in (0, 4) else 0.0
        for q, row in enumerate((-1, 8, -2, 9)):
            at = q // 2 * RIM + 5 * (q % 2) + v
            edge[pl.ds(at, nx, stride=2 * RIM), :] = rim_state(row, v) - level
        gedge[pl.ds(v, nx, stride=16), :] = rim_cot(-1, v)
        gedge[pl.ds(8 + v, nx, stride=16), :] = rim_cot(8, v)
    none = jnp.zeros((nx, 128), F32)
    for q in range(10, RIM):
        edge[pl.ds(q, nx, stride=2 * RIM), :] = none
        edge[pl.ds(RIM + q, nx, stride=2 * RIM), :] = none
    for q in (5, 6, 7):
        gedge[pl.ds(q, nx, stride=16), :] = none
        gedge[pl.ds(8 + q, nx, stride=16), :] = none
    for x in range(nx):
        put_patches(rim, rim_low, x, edge[pl.ds(2 * x * RIM, RIM), :])
        put_patches(outer, outer_low, x, edge[pl.ds((2 * x + 1) * RIM, RIM), :])
    wrap_patches(rim, rim_low, nx, RIM)
    wrap_patches(outer, outer_low, nx, RIM)

    def gathered(x, *blocks):
        columns = []
        for j in range(WIDE):
            rows = [ref[pl.ds((x + j) * 3 * n, 9 * n), :] for ref, n in blocks]
            columns.append(jnp.concatenate(rows, axis=0) if len(rows) > 1 else rows[0])
        return jnp.concatenate(columns, axis=1)

    kept = 8 * ch
    kg = hg = dsum = None
    zeros8 = jnp.zeros((8, 128 * WIDE), F32)
    for x in range(0, nx, WIDE):
        s_hi = gathered(x, (t, MAIN), (rim, RIM))
        s_lo = gathered(x, (t_low, MAIN), (rim_low, RIM))
        far_hi, far_lo = gathered(x, (outer, RIM)), gathered(x, (outer_low, RIM))
        z2 = jnp.dot(
            w_rows[...], jnp.concatenate([s_hi, far_hi], axis=0), preferred_element_type=F32
        )
        rows = z2.shape[0] // 2
        z3 = jnp.dot(
            w_rows[pl.ds(0, rows), :],
            jnp.concatenate([s_lo, far_lo], axis=0),
            preferred_element_type=F32,
        )
        z = z2[:rows] + (z2[rows:] + z3) + jnp.concatenate([bias[...]] * WIDE, axis=1)
        hidden = jnp.tanh(z)
        g = jnp.concatenate(
            [
                jnp.concatenate(
                    [cot[v, x + j] for v in range(5)] + [gedge[pl.ds((x + j) * 16, 16), :]], axis=0
                )
                for j in range(WIDE)
            ],
            axis=1,
        )
        g_hi, g_lo = split(g)
        g_hi32, g_lo32 = g_hi.astype(F32), g_lo.astype(F32)
        g3 = jnp.concatenate(
            [g_hi32, zeros8, g_hi32, zeros8, g_lo32, zeros8], axis=0
        ).astype(BF16)
        d = (1.0 - hidden * hidden) * jnp.dot(w_head[...], g3, preferred_element_type=F32)
        d_hi, d_lo = split(d)
        d_high[:, pl.ds(128 * x, 128 * WIDE)] = d_hi
        d_low[:, pl.ds(128 * x, 128 * WIDE)] = d_lo
        k2 = over_lanes(
            jnp.concatenate([s_hi, s_lo], axis=0),
            jnp.concatenate([d_hi[:kept], d_lo[:kept]], axis=0),
        )
        k2 = k2[:OWN_COLUMNS, :kept] + (k2[:OWN_COLUMNS, kept:] + k2[OWN_COLUMNS:, :kept])
        kg = k2 if kg is None else kg + k2
        hid2 = jnp.concatenate(split(hidden[:kept]), axis=0)
        g2 = jnp.concatenate([g_hi32[:40], g_lo32[:40]], axis=0).astype(BF16)
        h2 = over_lanes(g2, hid2)
        hg = h2 if hg is None else hg + h2
        for j in range(WIDE):
            level = d[:kept, 128 * j : 128 * (j + 1)]
            dsum = level if dsum is None else dsum + level

    sums = jnp.sum(dsum, axis=1, keepdims=True)
    kg = kg.T
    hg = (hg[:40, :kept] + hg[40:, :kept]) + (hg[:40, kept:] + hg[40:, kept:])
    y_row = lax.broadcasted_iota(jnp.int32, (40, kept), 0) & 7
    y_col = lax.broadcasted_iota(jnp.int32, (40, kept), 1)
    same_y = (y_col >= y_row * ch) & (y_col < (y_row + 1) * ch)
    hg = jnp.where(same_y, hg, 0.0)
    by_eq = jnp.concatenate(
        [jnp.sum(hg[8 * e : 8 * e + 8], axis=0, keepdims=True) for e in range(5)]
        + [jnp.zeros((123, kept), F32)],
        axis=0,
    ).T
    level_sum = jnp.zeros((ch, 1), F32)
    head_sum = jnp.zeros((ch, 128), F32)
    n = kg.shape[1]
    columns_at, tap = columns(n)
    kind = jnp.broadcast_to(columns_at[0:1], (ch, n))
    total = jnp.zeros((ch, n), F32)
    for y in range(8):
        rows = kg[y * ch : (y + 1) * ch]
        moved = rows if y == 1 else pltpu.roll(rows, (1 - y) % n, 1)
        keep = kind < 3
        if y == 0:
            keep = (kind == 1) | (kind == 2)
            total = total + jnp.where(kind == 8, rows, 0.0)
        if y == 7:
            keep = kind < 2
            total = total + jnp.where(kind == 10, rows, 0.0)
        total = total + jnp.where(keep, moved, 0.0)
        level_sum = level_sum + sums[y * ch : (y + 1) * ch]
        head_sum = head_sum + by_eq[y * ch : (y + 1) * ch]
    grads = over_lanes(jnp.concatenate(split(total), axis=0), own_taps(columns_at, tap))
    n_pick = grads.shape[1]
    parts[...] = jnp.zeros_like(parts)
    parts[:, pl.ds(0, n_pick)] = grads[:ch] + grads[ch:]
    parts[:, pl.ds(0, taps)] = parts[:, pl.ds(0, taps)] + level_sum * level_taps((ch, taps))
    parts[:, pl.ds(128, 128)] = parts[:, pl.ds(128, 128)] + pltpu.roll(head_sum * STEP, 16, 1)


def c_back_kernel(w_cols, d_high, d_low, order, own, acc):
    del order
    nx = own.shape[1]
    rows = d_high.shape[0]
    written = set()
    zeros = jnp.zeros((512 - 3 * rows, 128 * WIDE), BF16)
    for x in range(0, nx, WIDE):
        d_hi = d_high[:, pl.ds(128 * x, 128 * WIDE)]
        d_lo = d_low[:, pl.ds(128 * x, 128 * WIDE)]
        back = jnp.dot(
            w_cols[...],
            jnp.concatenate([d_hi, d_lo, d_hi, zeros], axis=0),
            preferred_element_type=F32,
        )
        for m in range(WIDE + 2):
            total = None
            for j in range(WIDE):
                if 0 <= m - j < 3:
                    q = m - j
                    piece = back[q * 128 : q * 128 + 120, 128 * j : 128 * (j + 1)]
                    total = piece if total is None else total + piece
            here = (x + m - 1) % nx
            if here in written:
                total = total + acc[pl.ds(here * 120, 120), :]
            written.add(here)
            acc[pl.ds(here * 120, 120), :] = total
    for x in range(nx):
        at = x * 120
        total = (
            acc[pl.ds(at + 40, 40), :]
            + pltpu.roll(acc[pl.ds(at, 40), :], 127, 1)
            + pltpu.roll(acc[pl.ds(at + 80, 40), :], 1, 1)
        )
        for v in range(5):
            own[v, x] = total[8 * v : 8 * v + 8]


def columns(n):
    lane = lax.broadcasted_iota(jnp.int32, (8, n), 1)
    main = lane < 9 * MAIN
    far = lane >= OWN_COLUMNS
    past = lane - jnp.where(far, OWN_COLUMNS, 9 * MAIN)
    block = sum((lane >= MAIN * i).astype(jnp.int32) for i in range(1, 9))
    o = jnp.where(main, block, past >> 4)
    r = jnp.where(main, lane - MAIN * block, past & (RIM - 1))
    second = (r >= 5).astype(jnp.int32)
    rim = jnp.where(r < 10, 8 + 2 * second + far.astype(jnp.int32), 12)
    kind = jnp.where(main, jnp.where(r < 40, r & 7, 12), rim)
    v = jnp.where(main, r >> 3, r - 5 * second)
    return kind, o * 5 + v


def taps_of(columns_at):
    n = columns_at.shape[1]
    row = lax.broadcasted_iota(jnp.int32, (144, n), 0)
    return jnp.where(row == jnp.broadcast_to(columns_at[0:1], (144, n)), 1.0, 0.0).astype(BF16)


def own_taps(kind, tap):
    at = jnp.where(kind < 3, tap + 45 * kind, 1000)
    at = jnp.where(kind == 8, tap, at)
    return taps_of(jnp.where(kind == 10, tap + 90, at))


def rim_taps(kind, tap):
    first = (kind == 9) | (kind == 7)
    middle = (kind == 8) | (kind == 10)
    last = (kind == 0) | (kind == 11)
    at = jnp.where(first, tap, jnp.where(middle, tap + 45, 1000))
    return taps_of(jnp.where(last, tap + 90, at))


def level_taps(shape):
    t = lax.broadcasted_iota(jnp.int32, shape, 1).astype(F32)
    v = t - 5.0 * jnp.floor((t + 0.5) * 0.2)
    return jnp.where((v < 0.5) | (v > 3.5), 1.0, 0.0)


def call(kernel, outs, scratch, us, n_in, order=0):
    spec = pl.BlockSpec(memory_space=pltpu.VMEM)
    return pl.pallas_call(
        kernel,
        out_shape=outs,
        in_specs=[spec] * n_in + [pl.BlockSpec(memory_space=pl.ANY)] * order,
        scratch_shapes=scratch,
        compiler_params=pltpu.CompilerParams(vmem_limit_bytes=VMEM),
        cost_estimate=pl.CostEstimate(
            flops=int(us * 1.15e9), bytes_accessed=int(us * 3.69e6), transcendentals=0
        ),
    )


def body(state, cot, flags, kernel, heads):
    _, nx, ny, nz = state.shape
    ch, taps = kernel.shape
    count = lax.axis_size("gy")
    cells = nx * ny * nz
    shape = lambda *dims: jax.ShapeDtypeStruct(dims, F32)
    half_shape = lambda *dims: jax.ShapeDtypeStruct(dims, BF16)
    full = shape(5, nx, ny, nz)
    with_twin = [(i, i ^ 1) for i in range(count)]
    with_other = [(i, (i + 1) % count if i % 2 else (i - 1) % count) for i in range(count)]
    vm = pltpu.VMEM
    lines = 5 * nx * ny

    flat = jnp.concatenate([state.reshape(lines, nz), cot.reshape(lines, nz)])
    fields = flat.reshape(10, nx, ny, nz)
    near, far = shape(NEAR, nx, nz), shape(FAR, nx, nz)
    x_scratch = [
        vm((5, nx + 5, ny, nz), F32),
        vm((5, nx + 1, ny, nz), F32),
        vm((5, nx + 5, ny, nz), F32),
    ]
    early = call(x_early_kernel, full, x_scratch, 0.2, 2)(fields, flags)
    near_twin, near_other = call(near_kernel, (near, near), [], 0.2, 1, 1)(flat, early)
    near_rims = (
        lax.ppermute(near_twin, "gy", with_twin),
        lax.ppermute(near_other, "gy", with_other),
    )
    *prepared, patches, patches_low = call(
        prepare_kernel,
        (
            half_shape(20 * ch, COLUMNS),
            half_shape(384, 512),
            half_shape(10 * ch, 192),
            shape(10 * ch, 128),
            half_shape((nx + 2) * 3 * MAIN, nz),
            half_shape((nx + 2) * 3 * MAIN, nz),
        ),
        [vm((2 * ch, 144), F32)],
        1.5,
        3,
        2,
    )(fields, kernel, heads, near_twin, near_other)
    first = call(x_late_kernel, full, x_scratch, 2.8, 3, 1)(fields, flags, early, patches)
    far_twin, far_other = call(far_kernel, (far, far), [], 0.2, 2, 1)(
        flat, flags.reshape(3 * nx * ny, nz), first
    )
    far_rims = (
        lax.ppermute(far_twin, "gy", with_twin),
        lax.ppermute(far_other, "gy", with_other),
    )
    near_rims, patches, first = lax.optimization_barrier((near_rims, patches, first))
    w_rows, w_cols, w_head, bias = prepared
    parts, d_high, d_low = call(
        c_kernel,
        (
            shape(ch, 256),
            half_shape(10 * ch, nx * nz),
            half_shape(10 * ch, nx * nz),
        ),
        [
            *[vm(((nx + 2) * 3 * RIM, nz), BF16)] * 4,
            vm((2 * RIM * nx, nz), F32),
            vm((16 * nx, nz), F32),
        ],
        4.2,
        9,
    )(fields, *near_rims, kernel, w_rows, w_head, bias, patches, patches_low)

    def exchanged(value, bit):
        return lax.ppermute(value, "gy", [(i, i ^ bit) for i in range(count)])

    bits = [1 << b for b in range(count.bit_length() - 1)]
    sums = parts
    for bit in bits[:-4]:
        sums = sums + exchanged(sums, bit)
    third = nx // 6 * 2
    yz = lambda lo, hi, before, order: call(
        functools.partial(yz_kernel, lo, hi), full, [vm((lines, nz), F32)] * 2, 2.2, 9, 1
    )(fields, flags, *near_rims, *far_rims, first, before, rim, order)
    got = exchanged(sums, bits[-4])
    rim = call(e_kernel, shape(lines, nz), [], 1.1, 5, 1)(flat, *near_rims, *far_rims, sums)
    got, rim = lax.optimization_barrier((got, rim))
    sums = sums + got
    got = exchanged(sums, bits[-3])
    own = call(c_back_kernel, full, [vm((nx * 120, nz), F32)], 2.0, 3, 1)(
        w_cols, d_high, d_low, sums
    )
    total = yz(0, third, own, sums)
    got, total = lax.optimization_barrier((got, total))
    sums = sums + got
    got = exchanged(sums, bits[-2])
    total = yz(third, nx - nx // 8 * 3, total, sums)
    got, total = lax.optimization_barrier((got, total))
    sums = sums + got
    got = exchanged(sums, bits[-1])
    flow = yz(nx - nx // 8 * 3, nx, total, sums)
    got, flow = lax.optimization_barrier((got, flow))
    scale = float(cells * count) ** (-0.5)
    k_out, h_out = call(
        functools.partial(sum_kernel, scale), (shape(ch, taps), shape(5, ch)), [], 0.5, 2
    )(sums, got)
    return flow, k_out, h_out


def solution(mesh):
    split_y = P(None, "ens", "gy", None)
    return jax.shard_map(
        body,
        mesh=mesh,
        in_specs=(split_y, split_y, split_y, P(), P()),
        out_specs=(split_y, P("ens", None), P("ens", None)),
        check_vma=False,
    )
```

```python
import functools

import jax
import jax.numpy as jnp
from jax import lax
from jax.experimental import pallas as pl
from jax.experimental.pallas import tpu as pltpu
from jax.sharding import PartitionSpec as P

STEP = 0.3
FLOOR = 0.01
BELOW, ABOVE = 2, 3
SLABS = 2
WIDE = 4
VMEM = 48 * 1024 * 1024
F32 = jnp.float32
BF16 = jnp.bfloat16


def rcp(x):
    return pl.reciprocal(x, approx=True)


def shared_terms(v):
    p = [v[i + 1] - v[i] for i in range(5)]
    d = [p[i + 1] - p[i] for i in range(4)]
    h = [(4.0 / 3.0) * x for x in d]
    k = [h[i] * d[i] + FLOOR for i in range(4)]
    g = [x + x for x in h]
    t = [d[i + 1] - d[i] for i in range(3)]
    return p, d, k, g, t


def side_value(pa, pm, pm2, ka, kb, kc, m0, m2, td, t1, smooth, c0, c2):
    i0 = rcp(ka + pa * m0)
    i1 = rcp(kb + pa * pm)
    i2 = rcp(kc + pm * m2)
    w0 = i0 * i0
    w1 = 6.0 * (i1 * i1)
    w2 = 3.0 * (i2 * i2)
    r = rcp(w0 + w1 + w2)
    o0 = jnp.where(smooth, w0 * r, c0)
    o2 = jnp.where(smooth, w2 * r, c2)
    u = o0 * td + o2 * t1
    b0 = w0 * i0 * (td - u)
    b1 = w1 * i1 * u
    b2 = w2 * i2 * (t1 - u)
    return (pa + pm2) - u, (b0, b1, b2, r, o0, o2)


def side_pull(mu, pa, pm, m0, m2, smooth, saved):
    b0, b1, b2, r, o0, o2 = saved
    mu2 = mu + mu
    rm = jnp.where(smooth, mu2, 0.0) * r
    s0, s1, s2 = b0 * rm, b1 * rm, b2 * rm
    pa_bar = s0 * (m0 + pa) - s1 * pm + mu
    pm_bar = s2 * (m2 + pm) - s1 * pa + mu2
    return s0, s1, s2, pa_bar, pm_bar, o0 * mu2, o2 * mu


def hllc_pull(left, right, normal, flags, cot):
    region = flags & 3
    is_right = region >= 2
    star = ((region + 1) & 2) != 0
    n_at = 1 + normal
    tang = [1 + i for i in range(3) if i != normal]
    rl, rr_, pl_, pr_, nl, nr = left[0], right[0], left[4], right[4], left[n_at], right[n_at]

    def sound(r, p):
        inv = rcp(r)
        t = 1.4 * p * inv
        inv_c = lax.rsqrt(t)
        return inv, inv_c, t * inv_c

    inv_rl, inv_cl, cl = sound(rl, pl_)
    inv_rr, inv_cr, cr = sound(rr_, pr_)
    c = 0.5 * (cl + cr)
    r2 = rl + rr_
    inv = rcp(r2 * c)
    nm = 0.5 * (nl + nr)
    gap = (pl_ - pr_) * inv
    sm = nm + gap
    sc = jnp.where(is_right, c, -c)
    s = nm + sc
    pick = [jnp.where(is_right, right[i], left[i]) for i in range(5)]
    r, un, u1, u2, p = pick[0], pick[n_at], pick[tang[0]], pick[tang[1]], pick[4]
    a = s - un
    dl = sm - un
    si = jnp.where(star, rcp(sc - gap), 0.0)
    j = s * si
    kap = j * dl
    g0, gn, g1, g2, ge = cot[0], cot[n_at], cot[tang[0]], cot[tang[1]], cot[4]
    w = un + kap
    half_q = 0.5 * (un * un + u1 * u1 + u2 * u2)
    enthalpy = 3.5 * p + r * half_q
    b = g0 + u1 * g1 + u2 * g2 + un * gn
    m = r * b + enthalpy * ge
    n = gn + sm * ge
    rkap = r * kap
    f_kap = m + r * a * n
    f_a = rkap * n
    si2 = si * si
    s_bar = f_a - f_kap * (dl * sm * si2)
    sm_bar = f_kap * (s * a * si2) + rkap * a * ge
    wr = w * r
    k_bar = [None] * 5
    k_bar[0] = w * (b + half_q * ge) + kap * a * n
    k_bar[n_at] = m + wr * (gn + un * ge) - f_kap * j - f_a
    k_bar[tang[0]] = wr * (g1 + u1 * ge)
    k_bar[tang[1]] = wr * (g2 + u2 * ge)
    k_bar[4] = 3.5 * (w * ge) + gn
    e = sm_bar * inv
    eg = e * gap
    c_half = 0.5 * (jnp.where(is_right, s_bar, -s_bar) - eg * r2)
    n_half = 0.5 * (s_bar + sm_bar)
    r_both = -(eg * c)
    xl = c_half * inv_rl
    xr = c_half * inv_rr
    base_l = {0: r_both - 0.5 * (xl * cl), n_at: n_half, 4: 0.7 * (xl * inv_cl) + e}
    base_r = {0: r_both - 0.5 * (xr * cr), n_at: n_half, 4: 0.7 * (xr * inv_cr) - e}
    l_bar, r_bar = [], []
    for i in range(5):
        kr = jnp.where(is_right, k_bar[i], 0.0)
        kl = k_bar[i] - kr
        l_bar.append(base_l[i] + kl if i in base_l else kl)
        r_bar.append(base_r[i] + kr if i in base_r else kr)
    return l_bar, r_bar


def face_pull(cells, cot, flags, normal):
    stencil = flags >> 2
    smooth = stencil == 0
    c0 = jnp.where(stencil == 1, 1.0, 0.0)
    c2 = jnp.where(stencil == 3, 1.0, 0.0)
    left, right, kept = [], [], []
    for v in cells:
        p, d, k, g, t = shared_terms(v)
        pm2 = p[2] + p[2]
        args_l = (p[1], p[2], p[1] + d[0], p[2] - d[2], t[0] + t[0], t[1])
        args_r = (p[3], p[2], p[3] - d[3], p[2] + d[1], t[2] + t[2], t[1])
        hl, saved_l = side_value(
            p[1], p[2], pm2, k[0], k[1], k[2], *args_l[2:], smooth, c0, c2
        )
        hr, saved_r = side_value(
            p[3], p[2], pm2, k[3], k[2], k[1], *args_r[2:], smooth, c0, c2
        )
        left.append(v[2] + hl * (1.0 / 6.0))
        right.append(v[3] - hr * (1.0 / 6.0))
        kept.append((p, g, args_l[:4], args_r[:4], saved_l, saved_r))
    l_bar, r_bar = hllc_pull(left, right, normal, flags, cot)
    out = []
    for i in range(5):
        p, g, args_l, args_r, saved_l, saved_r = kept[i]
        a0, a1, a2, pa_l, pm_l, x0, x2 = side_pull(
            l_bar[i] * (1.0 / 6.0), *args_l, smooth, saved_l
        )
        b0, b1, b2, pa_r, pm_r, y0, y2 = side_pull(
            r_bar[i] * (-1.0 / 6.0), *args_r, smooth, saved_r
        )
        d0 = a0 * (g[0] + p[1]) + x0
        d1 = (b2 * (g[1] + p[2]) - a1 * g[1]) + (x2 - x0) + y2
        d2 = (a2 * (g[2] - p[2]) - b1 * g[2]) + (y0 - y2) - x2
        d3 = b0 * (g[3] - p[3]) - y0
        p2 = pa_l + (d0 - d1)
        p3 = pm_l + pm_r + (d1 - d2)
        p4 = pa_r + (d2 - d3)
        out.append([d0, -d0 - p2, l_bar[i] + (p2 - p3), r_bar[i] + (p3 - p4), p4 - d3, d3])
    return out


def conserved_pull(s, g):
    half_q = 0.5 * (s[1] * s[1] + s[2] * s[2] + s[3] * s[3])
    return [
        g[0] + s[1] * g[1] + s[2] * g[2] + s[3] * g[3] + half_q * g[4],
        s[0] * (g[1] + s[1] * g[4]),
        s[0] * (g[2] + s[2] * g[4]),
        s[0] * (g[3] + s[3] * g[4]),
        2.5 * g[4],
    ]


NEAR_STATE, FAR_STATE = 2, 3
NEAR_COT, FAR_COT = 1, 2
FLAG_ROWS = 3
NEAR = 5 * (NEAR_STATE + NEAR_COT)
FAR = 5 * (FAR_STATE + FAR_COT) + FLAG_ROWS


def views(fields):
    n = fields.shape[0] // 2
    return fields.at[pl.ds(0, n)], fields.at[pl.ds(n, n)]


def pack(ref, rows, first, twin, other, at):
    even = is_even()
    nx = twin.shape[1]
    count = ref.shape[0] // (8 * nx)
    for r in rows:
        for v in range(count):
            low = ref[pl.ds(v * nx * 8 + r, nx, stride=8), :].astype(F32)
            top = ref[pl.ds(v * nx * 8 + 7 - r, nx, stride=8), :].astype(F32)
            i = at + (r - first) * count + v
            twin[i] = jnp.where(even, top, low)
            other[i] = jnp.where(even, low, top)


def near_kernel(flat, order, twin, other):
    del order
    s, g = views(flat)
    pack(s, range(NEAR_STATE), 0, twin, other, 0)
    pack(g, range(NEAR_COT), 0, twin, other, 5 * NEAR_STATE)


def far_kernel(flat, flags, order, twin, other):
    del order
    s, g = views(flat)
    n = flags.shape[0] // 3
    pack(s, range(NEAR_STATE, NEAR_STATE + FAR_STATE), NEAR_STATE, twin, other, 0)
    pack(g, range(NEAR_COT, NEAR_COT + FAR_COT), NEAR_COT, twin, other, 5 * FAR_STATE)
    pack(flags.at[pl.ds(n, n)], range(FLAG_ROWS), 0, twin, other, FAR - FLAG_ROWS)


def from_rims(near_twin, near_other, far_twin=None, far_other=None):
    even = is_even()

    def pick(twin, other, i, below):
        if below:
            return jnp.where(even, other[i], twin[i])
        return jnp.where(even, twin[i], other[i])

    def read(row, near, near_at, far_at, v):
        below = row < 0
        r = -1 - row if below else row - 8
        if r < near:
            return pick(near_twin, near_other, near_at + r * 5 + v, below)
        return pick(far_twin, far_other, far_at + (r - near) * 5 + v, below)

    def state(row, v):
        return read(row, NEAR_STATE, 0, 0, v)

    def cot(row, v):
        return read(row, NEAR_COT, 5 * NEAR_STATE, 5 * FAR_STATE, v)

    def flags(row):
        below = row < 0
        r = -1 - row if below else row - 8
        return pick(far_twin, far_other, FAR - FLAG_ROWS + r, below).astype(jnp.int32)

    return state, cot, flags


def x_faces(fields, flags, out, pad, gpad, acc):
    state, cot = views(fields)
    nx = state.shape[1]
    for v in range(5):
        pad[v, pl.ds(2, nx)] = state[v]
        pad[v, pl.ds(0, 2)] = state[v, pl.ds(nx - 2, 2)]
        pad[v, pl.ds(nx + 2, 3)] = state[v, pl.ds(0, 3)]
        gpad[v, pl.ds(0, nx)] = cot[v]
        gpad[v, pl.ds(nx, 1)] = cot[v, pl.ds(0, 1)]
    acc[...] = jnp.zeros_like(acc)

    def step(i, carry):
        x = i * SLABS
        cells = [[pad[v, pl.ds(x + k, SLABS)] for k in range(6)] for v in range(5)]
        g = [gpad[v, pl.ds(x, SLABS)] for v in range(5)]
        face = [STEP * (gpad[v, pl.ds(x + 1, SLABS)] - g[v]) for v in range(5)]
        terms = face_pull(cells, face, flags[0, pl.ds(x, SLABS)], 0)
        own = conserved_pull([cells[v][2] for v in range(5)], g)
        for v in range(5):
            terms[v][2] = terms[v][2] + own[v]
            for s in range(SLABS + 5):
                total = None
                for k in range(6):
                    if 0 <= s - k < SLABS:
                        part = terms[v][k][s - k]
                        total = part if total is None else total + part
                acc[v, x + s] = acc[v, x + s] + total
        return carry

    lax.fori_loop(0, nx // SLABS, step, 0)
    for v in range(5):
        acc[v, pl.ds(nx, 2)] = acc[v, pl.ds(nx, 2)] + acc[v, pl.ds(0, 2)]
        acc[v, pl.ds(2, 3)] = acc[v, pl.ds(2, 3)] + acc[v, pl.ds(nx + 2, 3)]

    for v in range(5):
        out[v] = acc[v, pl.ds(2, nx)]


def x_early_kernel(fields, flags, out, *scratch):
    @pl.when(lax.axis_index("gy") == 0)
    def _():
        x_faces(fields, flags, out, *scratch)


def x_late_kernel(fields, flags, early, order, out, *scratch):
    del order
    first = lax.axis_index("gy") == 0

    @pl.when(first)
    def _():
        out[...] = early[...]

    @pl.when(jnp.logical_not(first))
    def _():
        x_faces(fields, flags, out, *scratch)


def z_faces(state, cot, flags, x):
    cells, face = [], []
    for v in range(5):
        mid = state[v, pl.ds(x, SLABS)]
        cells.append([mid if k == 0 else pltpu.roll(mid, (-k) % 128, 2) for k in range(-2, 4)])
        g = cot[v, pl.ds(x, SLABS)]
        face.append(STEP * (pltpu.roll(g, 127, 2) - g))
    terms = face_pull(cells, face, flags[2, pl.ds(x, SLABS)], 2)
    total = []
    for v in range(5):
        t = terms[v][2]
        for k in (-2, -1, 1, 2, 3):
            t = t + pltpu.roll(terms[v][k + 2], k % 128, 2)
        total.append(t)
    return total


def e_kernel(flat, near_twin, near_other, far_twin, far_other, order, out):
    del order
    state, cot = views(flat)
    nx = out.shape[0] // 40
    rim_state, rim_cot, rim_flags = from_rims(near_twin, near_other, far_twin, far_other)

    def own(ref, row, v):
        return ref[pl.ds(v * nx * 8 + row, nx, stride=8), :]

    state_rows, cot_rows = {}, {}
    for v in range(5):
        for row in (*range(-5, 3), *range(6, 13)):
            inside = 0 <= row < 8
            state_rows[row, v] = own(state, row, v) if inside else rim_state(row, v)
        for row in (-3, -2, -1, 0, 8, 9, 10):
            inside = 0 <= row < 8
            cot_rows[row, v] = own(cot, row, v) if inside else rim_cot(row, v)
    sums = {}
    for j in (-3, -2, -1, 8, 9):
        cells = [[state_rows[j + k, v] for k in range(-2, 4)] for v in range(5)]
        face = [STEP * (cot_rows[j + 1, v] - cot_rows[j, v]) for v in range(5)]
        terms = face_pull(cells, face, rim_flags(j), 1)
        for v in range(5):
            for k in range(-2, 4):
                if 0 <= j + k < 8:
                    t = terms[v][k + 2]
                    sums[j + k, v] = sums[j + k, v] + t if (j + k, v) in sums else t
    for v in range(5):
        for row in range(8):
            value = sums[row, v] if (row, v) in sums else jnp.zeros((nx, 128), F32)
            out[pl.ds(v * nx * 8 + row, nx, stride=8), :] = value


def yz_kernel(lo, hi, fields, flags, near_twin, near_other, far_twin, far_other, first, before, rim, order, out, halo, ghalo):
    del order
    state, cot = views(fields)
    rims = from_rims(near_twin, near_other, far_twin, far_other)
    rim_state, rim_cot, _ = rims
    nx = out.shape[1]
    for v in range(5):
        for kept in (pl.ds(0, lo), pl.ds(hi, nx - hi)):
            if kept.size:
                out[v, kept] = before[v, kept]
    for v in range(5):
        base = v * nx * 8
        for r in range(ABOVE):
            halo[pl.ds(base + r, nx, stride=8), :] = rim_state(8 + r, v)
        for r in range(BELOW):
            halo[pl.ds(base + 8 - BELOW + r, nx, stride=8), :] = rim_state(r - BELOW, v)
        ghalo[pl.ds(base, nx, stride=8), :] = rim_cot(8, v)
    row = lax.broadcasted_iota(jnp.int32, (SLABS, 8, 128), 1)
    inside = {}
    for k in (-2, -1, 1, 2, 3):
        inside[k] = (row < 8 + k) if k < 0 else (row >= k)

    def step(i, carry):
        x = lo + i * SLABS
        cells, face = [], []
        for v in range(5):
            at = pl.multiple_of((v * nx + x) * 8, 8)
            rim_rows = halo[pl.ds(at, 8 * SLABS), :].reshape(SLABS, 8, 128)
            mid = state[v, pl.ds(x, SLABS)]
            line = []
            for k in range(-2, 4):
                if k == 0:
                    line.append(mid)
                else:
                    line.append(pltpu.roll(jnp.where(inside[k], mid, rim_rows), (-k) % 8, 1))
            cells.append(line)
            g = cot[v, pl.ds(x, SLABS)]
            g_rim = ghalo[pl.ds(at, 8 * SLABS), :].reshape(SLABS, 8, 128)
            face.append(STEP * (pltpu.roll(jnp.where(inside[1], g, g_rim), 7, 1) - g))
        terms = face_pull(cells, face, flags[1, pl.ds(x, SLABS)], 1)
        along_z = z_faces(state, cot, flags, x)
        for v in range(5):
            at = pl.multiple_of((v * nx + x) * 8, 8)
            total = before[v, pl.ds(x, SLABS)] + first[v, pl.ds(x, SLABS)]
            total = total + along_z[v] + terms[v][2]
            total = total + rim[pl.ds(at, 8 * SLABS), :].reshape(SLABS, 8, 128)
            for k in (-2, -1, 1, 2, 3):
                moved = pltpu.roll(terms[v][k + 2], k % 8, 1)
                total = total + jnp.where(inside[k], moved, 0.0)
            out[v, pl.ds(x, SLABS)] = total
        return carry

    lax.fori_loop(0, (hi - lo) // SLABS, step, 0)


def sum_kernel(scale, mine, theirs, k_out, h_out):
    total = (mine[...] + theirs[...]) * scale
    k_out[...] = total[:, : k_out.shape[1]]
    ch = total.shape[0]
    pick = (
        lax.broadcasted_iota(jnp.int32, (8, 128), 1)
        == lax.broadcasted_iota(jnp.int32, (8, 128), 0) + 16
    ).astype(F32)
    heads = lax.dot_general(
        pick,
        total[:, 128:],
        (((1,), (1,)), ((), ())),
        precision=lax.Precision.HIGHEST,
        preferred_element_type=F32,
    )
    h_out[...] = heads[: h_out.shape[0], :ch]


MAIN, RIM = 48, 16
OWN_COLUMNS = 9 * (MAIN + RIM)
COLUMNS = OWN_COLUMNS + 9 * RIM


def split(x):
    hi = x.astype(BF16)
    return hi, (x - hi.astype(F32)).astype(BF16)


def over_lanes(a, b):
    return lax.dot_general(a, b, (((1,), (1,)), ((), ())), preferred_element_type=F32)


def is_even():
    return lax.rem(lax.axis_index("gy"), 2) == 0


def put_patches(high, low, x, rows):
    n = rows.shape[0]
    hi, lo = split(rows)
    hi32, lo32 = hi.astype(F32), lo.astype(F32)
    for q, turn in enumerate((1, 0, 127)):
        at = pl.ds((x + 1) * 3 * n + q * n, n)
        high[at, :] = pltpu.roll(hi32, turn, 1).astype(BF16) if turn else hi
        low[at, :] = pltpu.roll(lo32, turn, 1).astype(BF16) if turn else lo


def wrap_patches(high, low, nx, rows):
    n = 3 * rows
    for ref in (high, low):
        ref[pl.ds(0, n), :] = ref[pl.ds(nx * n, n), :]
        ref[pl.ds((nx + 1) * n, n), :] = ref[pl.ds(n, n), :]


def prepare_kernel(fields, kernel, heads, order, order2, w_rows, w_cols, w_head, bias, t, t_low, wide):
    del order, order2
    state, _ = views(fields)
    nx = state.shape[1]
    for x in range(nx):
        rows = [state[v, x] - (1.0 if v in (0, 4) else 0.0) for v in range(5)]
        mid = jnp.concatenate([*rows, jnp.zeros((8, 128), F32)], axis=0)
        put_patches(t, t_low, x, mid)
    wrap_patches(t, t_low, nx, MAIN)

    ch, taps = kernel.shape
    w = kernel[...]
    hi, lo = split(w)
    wide[...] = jnp.zeros_like(wide)
    wide[pl.ds(0, ch), pl.ds(0, taps)] = hi.astype(F32)
    wide[pl.ds(ch, ch), pl.ds(0, taps)] = lo.astype(F32)
    both = wide[...].astype(BF16)
    kind, tap = columns(COLUMNS)
    base = jnp.dot(both, own_taps(kind, tap), preferred_element_type=F32)
    rim = jnp.dot(both, rim_taps(kind, tap), preferred_element_type=F32)
    n = base.shape[1]
    kind = jnp.broadcast_to(kind[0:1], base.shape)
    main = jnp.where(kind < 3, base, 0.0)
    bands = []
    for y in range(8):
        rows = main
        if y == 0:
            rows = jnp.where(kind == 0, 0.0, rows)
        if y == 7:
            rows = jnp.where(kind == 2, 0.0, rows)
        if y != 1:
            rows = pltpu.roll(rows, (y - 1) % n, 1)
        if y == 0:
            rows = rows + jnp.where(kind == 8, base, 0.0)
        if y == 7:
            rows = rows + jnp.where(kind == 10, base, 0.0)
        bands.append(rows)
    bands.append(jnp.where((kind == 0) | (kind == 8) | (kind == 9), rim, 0.0))
    bands.append(jnp.where((kind == 7) | (kind == 10) | (kind == 11), rim, 0.0))
    full = jnp.concatenate([b[:ch] for b in bands] + [b[ch:] for b in bands], axis=0)
    w_rows[...] = full.astype(BF16)
    kept = full.shape[0] // 2
    cols = jnp.concatenate([full[:kept], full[:kept], full[kept:]], axis=0)
    cols = jnp.concatenate([cols, jnp.zeros((512 - 3 * kept, n), F32)], axis=0)
    own_cols = []
    for q in range(3):
        own_cols += [cols[:, (3 * q + o) * MAIN : (3 * q + o) * MAIN + 40] for o in range(3)]
        own_cols.append(jnp.zeros((512, 8), F32))
    w_cols[...] = jnp.concatenate(own_cols, axis=1).T.astype(BF16)
    total = jnp.sum(w * level_taps(w.shape), axis=1, keepdims=True)
    total = jnp.broadcast_to(total, (ch, 128))
    bias[...] = jnp.concatenate([total] * 10, axis=0)

    h_hi, h_lo = split(STEP * heads[...])
    none = jnp.zeros((3, ch), F32)
    pair = jnp.concatenate([h_hi.astype(F32), none, h_lo.astype(F32), none], axis=0).astype(BF16)
    r = lax.broadcasted_iota(jnp.int32, (kept, ch), 0)
    q = lax.broadcasted_iota(jnp.int32, (kept, ch), 1)
    spread = jnp.where((r & (ch - 1)) == q, 1.0, 0.0).astype(BF16)
    picked = over_lanes(pair, spread)
    y_of = lax.broadcasted_iota(jnp.int32, (8, kept), 0)
    col = lax.broadcasted_iota(jnp.int32, (8, kept), 1)
    same = (col >= y_of * ch) & (col < (y_of + 1) * ch)
    split_heads = []
    for at in (0, 8):
        rows = [
            jnp.where(same, jnp.broadcast_to(picked[at + e : at + e + 1], (8, kept)), 0.0)
            for e in range(5)
        ]
        five = picked[at : at + 8]
        rows.append(jnp.where((col >= 8 * ch) & (col < 9 * ch), five, 0.0))
        rows.append(jnp.where(col >= 9 * ch, five, 0.0))
        rows.append(jnp.zeros((8, kept), F32))
        split_heads.append(jnp.concatenate(rows, axis=0))
    three = jnp.concatenate([split_heads[0], split_heads[1], split_heads[0]], axis=0)
    w_head[...] = three.T.astype(BF16)


def c_kernel(
    fields, near_twin, near_other, kernel, w_rows, w_head, bias, t, t_low,
    parts, d_high, d_low,
    rim, rim_low, outer, outer_low, edge, gedge,
):
    _, cot = views(fields)
    nx = cot.shape[1]
    ch, taps = kernel.shape
    rim_state, rim_cot, _ = from_rims(near_twin, near_other)

    for v in range(5):
        level = 1.0 if v in (0, 4) else 0.0
        for q, row in enumerate((-1, 8, -2, 9)):
            at = q // 2 * RIM + 5 * (q % 2) + v
            edge[pl.ds(at, nx, stride=2 * RIM), :] = rim_state(row, v) - level
        gedge[pl.ds(v, nx, stride=16), :] = rim_cot(-1, v)
        gedge[pl.ds(8 + v, nx, stride=16), :] = rim_cot(8, v)
    none = jnp.zeros((nx, 128), F32)
    for q in range(10, RIM):
        edge[pl.ds(q, nx, stride=2 * RIM), :] = none
        edge[pl.ds(RIM + q, nx, stride=2 * RIM), :] = none
    for q in (5, 6, 7):
        gedge[pl.ds(q, nx, stride=16), :] = none
        gedge[pl.ds(8 + q, nx, stride=16), :] = none
    for x in range(nx):
        put_patches(rim, rim_low, x, edge[pl.ds(2 * x * RIM, RIM), :])
        put_patches(outer, outer_low, x, edge[pl.ds((2 * x + 1) * RIM, RIM), :])
    wrap_patches(rim, rim_low, nx, RIM)
    wrap_patches(outer, outer_low, nx, RIM)

    def gathered(x, *blocks):
        columns = []
        for j in range(WIDE):
            rows = [ref[pl.ds((x + j) * 3 * n, 9 * n), :] for ref, n in blocks]
            columns.append(jnp.concatenate(rows, axis=0) if len(rows) > 1 else rows[0])
        return jnp.concatenate(columns, axis=1)

    kept = 8 * ch
    kg = hg = dsum = None
    zeros8 = jnp.zeros((8, 128 * WIDE), F32)
    for x in range(0, nx, WIDE):
        s_hi = gathered(x, (t, MAIN), (rim, RIM))
        s_lo = gathered(x, (t_low, MAIN), (rim_low, RIM))
        far_hi, far_lo = gathered(x, (outer, RIM)), gathered(x, (outer_low, RIM))
        z2 = jnp.dot(
            w_rows[...], jnp.concatenate([s_hi, far_hi], axis=0), preferred_element_type=F32
        )
        rows = z2.shape[0] // 2
        z3 = jnp.dot(
            w_rows[pl.ds(0, rows), :],
            jnp.concatenate([s_lo, far_lo], axis=0),
            preferred_element_type=F32,
        )
        z = z2[:rows] + (z2[rows:] + z3) + jnp.concatenate([bias[...]] * WIDE, axis=1)
        hidden = jnp.tanh(z)
        g = jnp.concatenate(
            [
                jnp.concatenate(
                    [cot[v, x + j] for v in range(5)] + [gedge[pl.ds((x + j) * 16, 16), :]], axis=0
                )
                for j in range(WIDE)
            ],
            axis=1,
        )
        g_hi, g_lo = split(g)
        g_hi32, g_lo32 = g_hi.astype(F32), g_lo.astype(F32)
        g3 = jnp.concatenate(
            [g_hi32, zeros8, g_hi32, zeros8, g_lo32, zeros8], axis=0
        ).astype(BF16)
        d = (1.0 - hidden * hidden) * jnp.dot(w_head[...], g3, preferred_element_type=F32)
        d_hi, d_lo = split(d)
        d_high[:, pl.ds(128 * x, 128 * WIDE)] = d_hi
        d_low[:, pl.ds(128 * x, 128 * WIDE)] = d_lo
        k2 = over_lanes(
            jnp.concatenate([s_hi, s_lo], axis=0),
            jnp.concatenate([d_hi[:kept], d_lo[:kept]], axis=0),
        )
        k2 = k2[:OWN_COLUMNS, :kept] + (k2[:OWN_COLUMNS, kept:] + k2[OWN_COLUMNS:, :kept])
        kg = k2 if kg is None else kg + k2
        hid2 = jnp.concatenate(split(hidden[:kept]), axis=0)
        g2 = jnp.concatenate([g_hi32[:40], g_lo32[:40]], axis=0).astype(BF16)
        h2 = over_lanes(g2, hid2)
        hg = h2 if hg is None else hg + h2
        for j in range(WIDE):
            level = d[:kept, 128 * j : 128 * (j + 1)]
            dsum = level if dsum is None else dsum + level

    sums = jnp.sum(dsum, axis=1, keepdims=True)
    kg = kg.T
    hg = (hg[:40, :kept] + hg[40:, :kept]) + (hg[:40, kept:] + hg[40:, kept:])
    y_row = lax.broadcasted_iota(jnp.int32, (40, kept), 0) & 7
    y_col = lax.broadcasted_iota(jnp.int32, (40, kept), 1)
    same_y = (y_col >= y_row * ch) & (y_col < (y_row + 1) * ch)
    hg = jnp.where(same_y, hg, 0.0)
    by_eq = jnp.concatenate(
        [jnp.sum(hg[8 * e : 8 * e + 8], axis=0, keepdims=True) for e in range(5)]
        + [jnp.zeros((123, kept), F32)],
        axis=0,
    ).T
    level_sum = jnp.zeros((ch, 1), F32)
    head_sum = jnp.zeros((ch, 128), F32)
    n = kg.shape[1]
    columns_at, tap = columns(n)
    kind = jnp.broadcast_to(columns_at[0:1], (ch, n))
    total = jnp.zeros((ch, n), F32)
    for y in range(8):
        rows = kg[y * ch : (y + 1) * ch]
        moved = rows if y == 1 else pltpu.roll(rows, (1 - y) % n, 1)
        keep = kind < 3
        if y == 0:
            keep = (kind == 1) | (kind == 2)
            total = total + jnp.where(kind == 8, rows, 0.0)
        if y == 7:
            keep = kind < 2
            total = total + jnp.where(kind == 10, rows, 0.0)
        total = total + jnp.where(keep, moved, 0.0)
        level_sum = level_sum + sums[y * ch : (y + 1) * ch]
        head_sum = head_sum + by_eq[y * ch : (y + 1) * ch]
    grads = over_lanes(jnp.concatenate(split(total), axis=0), own_taps(columns_at, tap))
    n_pick = grads.shape[1]
    parts[...] = jnp.zeros_like(parts)
    parts[:, pl.ds(0, n_pick)] = grads[:ch] + grads[ch:]
    parts[:, pl.ds(0, taps)] = parts[:, pl.ds(0, taps)] + level_sum * level_taps((ch, taps))
    parts[:, pl.ds(128, 128)] = parts[:, pl.ds(128, 128)] + pltpu.roll(head_sum * STEP, 16, 1)


def c_back_kernel(w_cols, d_high, d_low, order, own, acc):
    del order
    nx = own.shape[1]
    rows = d_high.shape[0]
    written = set()
    zeros = jnp.zeros((512 - 3 * rows, 128 * WIDE), BF16)
    for x in range(0, nx, WIDE):
        d_hi = d_high[:, pl.ds(128 * x, 128 * WIDE)]
        d_lo = d_low[:, pl.ds(128 * x, 128 * WIDE)]
        back = jnp.dot(
            w_cols[...],
            jnp.concatenate([d_hi, d_lo, d_hi, zeros], axis=0),
            preferred_element_type=F32,
        )
        for m in range(WIDE + 2):
            total = None
            for j in range(WIDE):
                if 0 <= m - j < 3:
                    q = m - j
                    piece = back[q * 128 : q * 128 + 120, 128 * j : 128 * (j + 1)]
                    total = piece if total is None else total + piece
            here = (x + m - 1) % nx
            if here in written:
                total = total + acc[pl.ds(here * 120, 120), :]
            written.add(here)
            acc[pl.ds(here * 120, 120), :] = total
    for x in range(nx):
        at = x * 120
        total = (
            acc[pl.ds(at + 40, 40), :]
            + pltpu.roll(acc[pl.ds(at, 40), :], 127, 1)
            + pltpu.roll(acc[pl.ds(at + 80, 40), :], 1, 1)
        )
        for v in range(5):
            own[v, x] = total[8 * v : 8 * v + 8]


def columns(n):
    lane = lax.broadcasted_iota(jnp.int32, (8, n), 1)
    main = lane < 9 * MAIN
    far = lane >= OWN_COLUMNS
    past = lane - jnp.where(far, OWN_COLUMNS, 9 * MAIN)
    block = sum((lane >= MAIN * i).astype(jnp.int32) for i in range(1, 9))
    o = jnp.where(main, block, past >> 4)
    r = jnp.where(main, lane - MAIN * block, past & (RIM - 1))
    second = (r >= 5).astype(jnp.int32)
    rim = jnp.where(r < 10, 8 + 2 * second + far.astype(jnp.int32), 12)
    kind = jnp.where(main, jnp.where(r < 40, r & 7, 12), rim)
    v = jnp.where(main, r >> 3, r - 5 * second)
    return kind, o * 5 + v


def taps_of(columns_at):
    n = columns_at.shape[1]
    row = lax.broadcasted_iota(jnp.int32, (144, n), 0)
    return jnp.where(row == jnp.broadcast_to(columns_at[0:1], (144, n)), 1.0, 0.0).astype(BF16)


def own_taps(kind, tap):
    at = jnp.where(kind < 3, tap + 45 * kind, 1000)
    at = jnp.where(kind == 8, tap, at)
    return taps_of(jnp.where(kind == 10, tap + 90, at))


def rim_taps(kind, tap):
    first = (kind == 9) | (kind == 7)
    middle = (kind == 8) | (kind == 10)
    last = (kind == 0) | (kind == 11)
    at = jnp.where(first, tap, jnp.where(middle, tap + 45, 1000))
    return taps_of(jnp.where(last, tap + 90, at))


def level_taps(shape):
    t = lax.broadcasted_iota(jnp.int32, shape, 1).astype(F32)
    v = t - 5.0 * jnp.floor((t + 0.5) * 0.2)
    return jnp.where((v < 0.5) | (v > 3.5), 1.0, 0.0)


def call(kernel, outs, scratch, us, n_in, order=0):
    spec = pl.BlockSpec(memory_space=pltpu.VMEM)
    return pl.pallas_call(
        kernel,
        out_shape=outs,
        in_specs=[spec] * n_in + [pl.BlockSpec(memory_space=pl.ANY)] * order,
        scratch_shapes=scratch,
        compiler_params=pltpu.CompilerParams(vmem_limit_bytes=VMEM),
        cost_estimate=pl.CostEstimate(
            flops=int(us * 1.15e9), bytes_accessed=int(us * 3.69e6), transcendentals=0
        ),
    )


def body(state, cot, flags, kernel, heads):
    _, nx, ny, nz = state.shape
    ch, taps = kernel.shape
    count = lax.axis_size("gy")
    cells = nx * ny * nz
    shape = lambda *dims: jax.ShapeDtypeStruct(dims, F32)
    half_shape = lambda *dims: jax.ShapeDtypeStruct(dims, BF16)
    full = shape(5, nx, ny, nz)
    with_twin = [(i, i ^ 1) for i in range(count)]
    with_other = [(i, (i + 1) % count if i % 2 else (i - 1) % count) for i in range(count)]
    vm = pltpu.VMEM
    lines = 5 * nx * ny

    flat = jnp.concatenate([state.reshape(lines, nz), cot.reshape(lines, nz)])
    fields = flat.reshape(10, nx, ny, nz)
    near, far = shape(NEAR, nx, nz), shape(FAR, nx, nz)
    x_scratch = [
        vm((5, nx + 5, ny, nz), F32),
        vm((5, nx + 1, ny, nz), F32),
        vm((5, nx + 5, ny, nz), F32),
    ]
    early = call(x_early_kernel, full, x_scratch, 0.2, 2)(fields, flags)
    near_twin, near_other = call(near_kernel, (near, near), [], 0.2, 1, 1)(flat, early)
    near_rims = (
        lax.ppermute(near_twin, "gy", with_twin),
        lax.ppermute(near_other, "gy", with_other),
    )
    *prepared, patches, patches_low = call(
        prepare_kernel,
        (
            half_shape(20 * ch, COLUMNS),
            half_shape(384, 512),
            half_shape(10 * ch, 192),
            shape(10 * ch, 128),
            half_shape((nx + 2) * 3 * MAIN, nz),
            half_shape((nx + 2) * 3 * MAIN, nz),
        ),
        [vm((2 * ch, 144), F32)],
        1.5,
        3,
        2,
    )(fields, kernel, heads, near_twin, near_other)
    first = call(x_late_kernel, full, x_scratch, 2.8, 3, 1)(fields, flags, early, patches)
    far_twin, far_other = call(far_kernel, (far, far), [], 0.2, 2, 1)(
        flat, flags.reshape(3 * nx * ny, nz), first
    )
    far_rims = (
        lax.ppermute(far_twin, "gy", with_twin),
        lax.ppermute(far_other, "gy", with_other),
    )
    near_rims, patches, first = lax.optimization_barrier((near_rims, patches, first))
    w_rows, w_cols, w_head, bias = prepared
    parts, d_high, d_low = call(
        c_kernel,
        (
            shape(ch, 256),
            half_shape(10 * ch, nx * nz),
            half_shape(10 * ch, nx * nz),
        ),
        [
            *[vm(((nx + 2) * 3 * RIM, nz), BF16)] * 4,
            vm((2 * RIM * nx, nz), F32),
            vm((16 * nx, nz), F32),
        ],
        4.2,
        9,
    )(fields, *near_rims, kernel, w_rows, w_head, bias, patches, patches_low)

    def exchanged(value, bit):
        return lax.ppermute(value, "gy", [(i, i ^ bit) for i in range(count)])

    bits = [1 << b for b in range(count.bit_length() - 1)]
    sums = parts
    for bit in bits[:-4]:
        sums = sums + exchanged(sums, bit)
    third = nx // 6 * 2
    yz = lambda lo, hi, before, order: call(
        functools.partial(yz_kernel, lo, hi), full, [vm((lines, nz), F32)] * 2, 2.2, 9, 1
    )(fields, flags, *near_rims, *far_rims, first, before, rim, order)
    got = exchanged(sums, bits[-4])
    own = call(c_back_kernel, full, [vm((nx * 120, nz), F32)], 1.1, 3, 1)(
        w_cols, d_high, d_low, sums
    )
    got, own = lax.optimization_barrier((got, own))
    sums = sums + got
    got = exchanged(sums, bits[-3])
    rim = call(e_kernel, shape(lines, nz), [], 1.1, 5, 1)(flat, *near_rims, *far_rims, sums)
    total = yz(0, third, own, sums)
    got, total = lax.optimization_barrier((got, total))
    sums = sums + got
    got = exchanged(sums, bits[-2])
    total = yz(third, nx - nx // 8 * 3, total, sums)
    got, total = lax.optimization_barrier((got, total))
    sums = sums + got
    got = exchanged(sums, bits[-1])
    flow = yz(nx - nx // 8 * 3, nx, total, sums)
    got, flow = lax.optimization_barrier((got, flow))
    scale = float(cells * count) ** (-0.5)
    k_out, h_out = call(
        functools.partial(sum_kernel, scale), (shape(ch, taps), shape(5, ch)), [], 0.5, 2
    )(sums, got)
    return flow, k_out, h_out


def solution(mesh):
    split_y = P(None, "ens", "gy", None)
    return jax.shard_map(
        body,
        mesh=mesh,
        in_specs=(split_y, split_y, split_y, P(), P()),
        out_specs=(split_y, P("ens", None), P("ens", None)),
        check_vma=False,
    )
```

```python
import functools

import jax
import jax.numpy as jnp
from jax import lax
from jax.experimental import pallas as pl
from jax.experimental.pallas import tpu as pltpu
from jax.sharding import PartitionSpec as P

STEP = 0.3
FLOOR = 0.01
BELOW, ABOVE = 2, 3
SLABS = 2
WIDE = 4
VMEM = 48 * 1024 * 1024
F32 = jnp.float32
BF16 = jnp.bfloat16


def rcp(x):
    return pl.reciprocal(x, approx=True)


def shared_terms(v):
    p = [v[i + 1] - v[i] for i in range(5)]
    d = [p[i + 1] - p[i] for i in range(4)]
    h = [(4.0 / 3.0) * x for x in d]
    k = [h[i] * d[i] + FLOOR for i in range(4)]
    g = [x + x for x in h]
    t = [d[i + 1] - d[i] for i in range(3)]
    return p, d, k, g, t


def side_value(pa, pm, pm2, ka, kb, kc, m0, m2, td, t1, smooth, c0, c2):
    i0 = rcp(ka + pa * m0)
    i1 = rcp(kb + pa * pm)
    i2 = rcp(kc + pm * m2)
    w0 = i0 * i0
    w1 = 6.0 * (i1 * i1)
    w2 = 3.0 * (i2 * i2)
    r = rcp(w0 + w1 + w2)
    o0 = jnp.where(smooth, w0 * r, c0)
    o2 = jnp.where(smooth, w2 * r, c2)
    u = o0 * td + o2 * t1
    b0 = w0 * i0 * (td - u)
    b1 = w1 * i1 * u
    b2 = w2 * i2 * (t1 - u)
    return (pa + pm2) - u, (b0, b1, b2, r, o0, o2)


def side_pull(mu, pa, pm, m0, m2, smooth, saved):
    b0, b1, b2, r, o0, o2 = saved
    mu2 = mu + mu
    rm = jnp.where(smooth, mu2, 0.0) * r
    s0, s1, s2 = b0 * rm, b1 * rm, b2 * rm
    pa_bar = s0 * (m0 + pa) - s1 * pm + mu
    pm_bar = s2 * (m2 + pm) - s1 * pa + mu2
    return s0, s1, s2, pa_bar, pm_bar, o0 * mu2, o2 * mu


def hllc_pull(left, right, normal, flags, cot):
    region = flags & 3
    is_right = region >= 2
    star = ((region + 1) & 2) != 0
    n_at = 1 + normal
    tang = [1 + i for i in range(3) if i != normal]
    rl, rr_, pl_, pr_, nl, nr = left[0], right[0], left[4], right[4], left[n_at], right[n_at]

    def sound(r, p):
        inv = rcp(r)
        t = 1.4 * p * inv
        inv_c = lax.rsqrt(t)
        return inv, inv_c, t * inv_c

    inv_rl, inv_cl, cl = sound(rl, pl_)
    inv_rr, inv_cr, cr = sound(rr_, pr_)
    c = 0.5 * (cl + cr)
    r2 = rl + rr_
    inv = rcp(r2 * c)
    nm = 0.5 * (nl + nr)
    gap = (pl_ - pr_) * inv
    sm = nm + gap
    sc = jnp.where(is_right, c, -c)
    s = nm + sc
    pick = [jnp.where(is_right, right[i], left[i]) for i in range(5)]
    r, un, u1, u2, p = pick[0], pick[n_at], pick[tang[0]], pick[tang[1]], pick[4]
    a = s - un
    dl = sm - un
    si = jnp.where(star, rcp(sc - gap), 0.0)
    j = s * si
    kap = j * dl
    g0, gn, g1, g2, ge = cot[0], cot[n_at], cot[tang[0]], cot[tang[1]], cot[4]
    w = un + kap
    half_q = 0.5 * (un * un + u1 * u1 + u2 * u2)
    enthalpy = 3.5 * p + r * half_q
    b = g0 + u1 * g1 + u2 * g2 + un * gn
    m = r * b + enthalpy * ge
    n = gn + sm * ge
    rkap = r * kap
    f_kap = m + r * a * n
    f_a = rkap * n
    si2 = si * si
    s_bar = f_a - f_kap * (dl * sm * si2)
    sm_bar = f_kap * (s * a * si2) + rkap * a * ge
    wr = w * r
    k_bar = [None] * 5
    k_bar[0] = w * (b + half_q * ge) + kap * a * n
    k_bar[n_at] = m + wr * (gn + un * ge) - f_kap * j - f_a
    k_bar[tang[0]] = wr * (g1 + u1 * ge)
    k_bar[tang[1]] = wr * (g2 + u2 * ge)
    k_bar[4] = 3.5 * (w * ge) + gn
    e = sm_bar * inv
    eg = e * gap
    c_half = 0.5 * (jnp.where(is_right, s_bar, -s_bar) - eg * r2)
    n_half = 0.5 * (s_bar + sm_bar)
    r_both = -(eg * c)
    xl = c_half * inv_rl
    xr = c_half * inv_rr
    base_l = {0: r_both - 0.5 * (xl * cl), n_at: n_half, 4: 0.7 * (xl * inv_cl) + e}
    base_r = {0: r_both - 0.5 * (xr * cr), n_at: n_half, 4: 0.7 * (xr * inv_cr) - e}
    l_bar, r_bar = [], []
    for i in range(5):
        kr = jnp.where(is_right, k_bar[i], 0.0)
        kl = k_bar[i] - kr
        l_bar.append(base_l[i] + kl if i in base_l else kl)
        r_bar.append(base_r[i] + kr if i in base_r else kr)
    return l_bar, r_bar


def face_pull(cells, cot, flags, normal):
    stencil = flags >> 2
    smooth = stencil == 0
    c0 = jnp.where(stencil == 1, 1.0, 0.0)
    c2 = jnp.where(stencil == 3, 1.0, 0.0)
    left, right, kept = [], [], []
    for v in cells:
        p, d, k, g, t = shared_terms(v)
        pm2 = p[2] + p[2]
        args_l = (p[1], p[2], p[1] + d[0], p[2] - d[2], t[0] + t[0], t[1])
        args_r = (p[3], p[2], p[3] - d[3], p[2] + d[1], t[2] + t[2], t[1])
        hl, saved_l = side_value(
            p[1], p[2], pm2, k[0], k[1], k[2], *args_l[2:], smooth, c0, c2
        )
        hr, saved_r = side_value(
            p[3], p[2], pm2, k[3], k[2], k[1], *args_r[2:], smooth, c0, c2
        )
        left.append(v[2] + hl * (1.0 / 6.0))
        right.append(v[3] - hr * (1.0 / 6.0))
        kept.append((p, g, args_l[:4], args_r[:4], saved_l, saved_r))
    l_bar, r_bar = hllc_pull(left, right, normal, flags, cot)
    out = []
    for i in range(5):
        p, g, args_l, args_r, saved_l, saved_r = kept[i]
        a0, a1, a2, pa_l, pm_l, x0, x2 = side_pull(
            l_bar[i] * (1.0 / 6.0), *args_l, smooth, saved_l
        )
        b0, b1, b2, pa_r, pm_r, y0, y2 = side_pull(
            r_bar[i] * (-1.0 / 6.0), *args_r, smooth, saved_r
        )
        d0 = a0 * (g[0] + p[1]) + x0
        d1 = (b2 * (g[1] + p[2]) - a1 * g[1]) + (x2 - x0) + y2
        d2 = (a2 * (g[2] - p[2]) - b1 * g[2]) + (y0 - y2) - x2
        d3 = b0 * (g[3] - p[3]) - y0
        p2 = pa_l + (d0 - d1)
        p3 = pm_l + pm_r + (d1 - d2)
        p4 = pa_r + (d2 - d3)
        out.append([d0, -d0 - p2, l_bar[i] + (p2 - p3), r_bar[i] + (p3 - p4), p4 - d3, d3])
    return out


def conserved_pull(s, g):
    half_q = 0.5 * (s[1] * s[1] + s[2] * s[2] + s[3] * s[3])
    return [
        g[0] + s[1] * g[1] + s[2] * g[2] + s[3] * g[3] + half_q * g[4],
        s[0] * (g[1] + s[1] * g[4]),
        s[0] * (g[2] + s[2] * g[4]),
        s[0] * (g[3] + s[3] * g[4]),
        2.5 * g[4],
    ]


NEAR_STATE, FAR_STATE = 2, 3
NEAR_COT, FAR_COT = 1, 2
FLAG_ROWS = 3
NEAR = 5 * (NEAR_STATE + NEAR_COT)
FAR = 5 * (FAR_STATE + FAR_COT) + FLAG_ROWS


def views(fields):
    n = fields.shape[0] // 2
    return fields.at[pl.ds(0, n)], fields.at[pl.ds(n, n)]


def pack(ref, rows, first, twin, other, at):
    even = is_even()
    nx = twin.shape[1]
    count = ref.shape[0] // (8 * nx)
    for r in rows:
        for v in range(count):
            low = ref[pl.ds(v * nx * 8 + r, nx, stride=8), :].astype(F32)
            top = ref[pl.ds(v * nx * 8 + 7 - r, nx, stride=8), :].astype(F32)
            i = at + (r - first) * count + v
            twin[i] = jnp.where(even, top, low)
            other[i] = jnp.where(even, low, top)


def near_kernel(flat, order, twin, other):
    del order
    s, g = views(flat)
    pack(s, range(NEAR_STATE), 0, twin, other, 0)
    pack(g, range(NEAR_COT), 0, twin, other, 5 * NEAR_STATE)


def far_kernel(flat, flags, order, twin, other):
    del order
    s, g = views(flat)
    n = flags.shape[0] // 3
    pack(s, range(NEAR_STATE, NEAR_STATE + FAR_STATE), NEAR_STATE, twin, other, 0)
    pack(g, range(NEAR_COT, NEAR_COT + FAR_COT), NEAR_COT, twin, other, 5 * FAR_STATE)
    pack(flags.at[pl.ds(n, n)], range(FLAG_ROWS), 0, twin, other, FAR - FLAG_ROWS)


def from_rims(near_twin, near_other, far_twin=None, far_other=None):
    even = is_even()

    def pick(twin, other, i, below):
        if below:
            return jnp.where(even, other[i], twin[i])
        return jnp.where(even, twin[i], other[i])

    def read(row, near, near_at, far_at, v):
        below = row < 0
        r = -1 - row if below else row - 8
        if r < near:
            return pick(near_twin, near_other, near_at + r * 5 + v, below)
        return pick(far_twin, far_other, far_at + (r - near) * 5 + v, below)

    def state(row, v):
        return read(row, NEAR_STATE, 0, 0, v)

    def cot(row, v):
        return read(row, NEAR_COT, 5 * NEAR_STATE, 5 * FAR_STATE, v)

    def flags(row):
        below = row < 0
        r = -1 - row if below else row - 8
        return pick(far_twin, far_other, FAR - FLAG_ROWS + r, below).astype(jnp.int32)

    return state, cot, flags


def x_faces(lo, hi, fields, flags, acc, pad, gpad):
    state, cot = views(fields)
    nx = state.shape[1]
    for v in range(5):
        pad[v, pl.ds(2, nx)] = state[v]
        pad[v, pl.ds(0, 2)] = state[v, pl.ds(nx - 2, 2)]
        pad[v, pl.ds(nx + 2, 3)] = state[v, pl.ds(0, 3)]
        gpad[v, pl.ds(0, nx)] = cot[v]
        gpad[v, pl.ds(nx, 1)] = cot[v, pl.ds(0, 1)]

    def step(i, carry):
        x = lo + i * SLABS
        cells = [[pad[v, pl.ds(x + k, SLABS)] for k in range(6)] for v in range(5)]
        g = [gpad[v, pl.ds(x, SLABS)] for v in range(5)]
        face = [STEP * (gpad[v, pl.ds(x + 1, SLABS)] - g[v]) for v in range(5)]
        terms = face_pull(cells, face, flags[0, pl.ds(x, SLABS)], 0)
        own = conserved_pull([cells[v][2] for v in range(5)], g)
        for v in range(5):
            terms[v][2] = terms[v][2] + own[v]
            for s in range(SLABS + 5):
                total = None
                for k in range(6):
                    if 0 <= s - k < SLABS:
                        part = terms[v][k][s - k]
                        total = part if total is None else total + part
                acc[v, x + s] = acc[v, x + s] + total
        return carry

    lax.fori_loop(0, (hi - lo) // SLABS, step, 0)


def fold_rim(acc, out):
    nx = out.shape[1]
    for v in range(5):
        acc[v, pl.ds(nx, 2)] = acc[v, pl.ds(nx, 2)] + acc[v, pl.ds(0, 2)]
        acc[v, pl.ds(2, 3)] = acc[v, pl.ds(2, 3)] + acc[v, pl.ds(nx + 2, 3)]
        out[v] = acc[v, pl.ds(2, nx)]


def x_early_kernel(fields, flags, out, pad, gpad, acc):
    @pl.when(lax.axis_index("gy") == 0)
    def _():
        acc[...] = jnp.zeros_like(acc)
        x_faces(0, out.shape[1], fields, flags, acc, pad, gpad)
        fold_rim(acc, out)


def x_late_kernel(fields, flags, order, acc, pad, gpad):
    del order

    @pl.when(lax.axis_index("gy") != 0)
    def _():
        acc[...] = jnp.zeros_like(acc)
        x_faces(0, flags.shape[1] // 2, fields, flags, acc, pad, gpad)


def x_last_kernel(fields, flags, early, begun, order, out, pad, gpad, acc):
    del order
    nx = out.shape[1]
    first = lax.axis_index("gy") == 0

    @pl.when(first)
    def _():
        out[...] = early[...]

    @pl.when(jnp.logical_not(first))
    def _():
        acc[...] = begun[...]
        x_faces(nx // 2, nx, fields, flags, acc, pad, gpad)
        fold_rim(acc, out)


def z_faces(state, cot, flags, x):
    cells, face = [], []
    for v in range(5):
        mid = state[v, pl.ds(x, SLABS)]
        cells.append([mid if k == 0 else pltpu.roll(mid, (-k) % 128, 2) for k in range(-2, 4)])
        g = cot[v, pl.ds(x, SLABS)]
        face.append(STEP * (pltpu.roll(g, 127, 2) - g))
    terms = face_pull(cells, face, flags[2, pl.ds(x, SLABS)], 2)
    total = []
    for v in range(5):
        t = terms[v][2]
        for k in (-2, -1, 1, 2, 3):
            t = t + pltpu.roll(terms[v][k + 2], k % 128, 2)
        total.append(t)
    return total


def e_kernel(flat, near_twin, near_other, far_twin, far_other, order, out):
    del order
    state, cot = views(flat)
    nx = out.shape[0] // 40
    rim_state, rim_cot, rim_flags = from_rims(near_twin, near_other, far_twin, far_other)

    def own(ref, row, v):
        return ref[pl.ds(v * nx * 8 + row, nx, stride=8), :]

    state_rows, cot_rows = {}, {}
    for v in range(5):
        for row in (*range(-5, 3), *range(6, 13)):
            inside = 0 <= row < 8
            state_rows[row, v] = own(state, row, v) if inside else rim_state(row, v)
        for row in (-3, -2, -1, 0, 8, 9, 10):
            inside = 0 <= row < 8
            cot_rows[row, v] = own(cot, row, v) if inside else rim_cot(row, v)
    sums = {}
    for j in (-3, -2, -1, 8, 9):
        cells = [[state_rows[j + k, v] for k in range(-2, 4)] for v in range(5)]
        face = [STEP * (cot_rows[j + 1, v] - cot_rows[j, v]) for v in range(5)]
        terms = face_pull(cells, face, rim_flags(j), 1)
        for v in range(5):
            for k in range(-2, 4):
                if 0 <= j + k < 8:
                    t = terms[v][k + 2]
                    sums[j + k, v] = sums[j + k, v] + t if (j + k, v) in sums else t
    for v in range(5):
        for row in range(8):
            value = sums[row, v] if (row, v) in sums else jnp.zeros((nx, 128), F32)
            out[pl.ds(v * nx * 8 + row, nx, stride=8), :] = value


def yz_kernel(lo, hi, fields, flags, near_twin, near_other, far_twin, far_other, first, before, rim, order, out, halo, ghalo):
    del order
    state, cot = views(fields)
    rims = from_rims(near_twin, near_other, far_twin, far_other)
    rim_state, rim_cot, _ = rims
    nx = out.shape[1]
    for v in range(5):
        for kept in (pl.ds(0, lo), pl.ds(hi, nx - hi)):
            if kept.size:
                out[v, kept] = before[v, kept]
    for v in range(5):
        base = v * nx * 8
        for r in range(ABOVE):
            halo[pl.ds(base + r, nx, stride=8), :] = rim_state(8 + r, v)
        for r in range(BELOW):
            halo[pl.ds(base + 8 - BELOW + r, nx, stride=8), :] = rim_state(r - BELOW, v)
        ghalo[pl.ds(base, nx, stride=8), :] = rim_cot(8, v)
    row = lax.broadcasted_iota(jnp.int32, (SLABS, 8, 128), 1)
    inside = {}
    for k in (-2, -1, 1, 2, 3):
        inside[k] = (row < 8 + k) if k < 0 else (row >= k)

    def step(i, carry):
        x = lo + i * SLABS
        cells, face = [], []
        for v in range(5):
            at = pl.multiple_of((v * nx + x) * 8, 8)
            rim_rows = halo[pl.ds(at, 8 * SLABS), :].reshape(SLABS, 8, 128)
            mid = state[v, pl.ds(x, SLABS)]
            line = []
            for k in range(-2, 4):
                if k == 0:
                    line.append(mid)
                else:
                    line.append(pltpu.roll(jnp.where(inside[k], mid, rim_rows), (-k) % 8, 1))
            cells.append(line)
            g = cot[v, pl.ds(x, SLABS)]
            g_rim = ghalo[pl.ds(at, 8 * SLABS), :].reshape(SLABS, 8, 128)
            face.append(STEP * (pltpu.roll(jnp.where(inside[1], g, g_rim), 7, 1) - g))
        terms = face_pull(cells, face, flags[1, pl.ds(x, SLABS)], 1)
        along_z = z_faces(state, cot, flags, x)
        for v in range(5):
            at = pl.multiple_of((v * nx + x) * 8, 8)
            total = before[v, pl.ds(x, SLABS)] + first[v, pl.ds(x, SLABS)]
            total = total + along_z[v] + terms[v][2]
            total = total + rim[pl.ds(at, 8 * SLABS), :].reshape(SLABS, 8, 128)
            for k in (-2, -1, 1, 2, 3):
                moved = pltpu.roll(terms[v][k + 2], k % 8, 1)
                total = total + jnp.where(inside[k], moved, 0.0)
            out[v, pl.ds(x, SLABS)] = total
        return carry

    lax.fori_loop(0, (hi - lo) // SLABS, step, 0)


def sum_kernel(scale, mine, theirs, k_out, h_out):
    total = (mine[...] + theirs[...]) * scale
    k_out[...] = total[:, : k_out.shape[1]]
    ch = total.shape[0]
    pick = (
        lax.broadcasted_iota(jnp.int32, (8, 128), 1)
        == lax.broadcasted_iota(jnp.int32, (8, 128), 0) + 16
    ).astype(F32)
    heads = lax.dot_general(
        pick,
        total[:, 128:],
        (((1,), (1,)), ((), ())),
        precision=lax.Precision.HIGHEST,
        preferred_element_type=F32,
    )
    h_out[...] = heads[: h_out.shape[0], :ch]


MAIN, RIM = 48, 16
OWN_COLUMNS = 9 * (MAIN + RIM)
COLUMNS = OWN_COLUMNS + 9 * RIM


def split(x):
    hi = x.astype(BF16)
    return hi, (x - hi.astype(F32)).astype(BF16)


def over_lanes(a, b):
    return lax.dot_general(a, b, (((1,), (1,)), ((), ())), preferred_element_type=F32)


def is_even():
    return lax.rem(lax.axis_index("gy"), 2) == 0


def put_patches(high, low, x, rows):
    n = rows.shape[0]
    hi, lo = split(rows)
    hi32, lo32 = hi.astype(F32), lo.astype(F32)
    for q, turn in enumerate((1, 0, 127)):
        at = pl.ds((x + 1) * 3 * n + q * n, n)
        high[at, :] = pltpu.roll(hi32, turn, 1).astype(BF16) if turn else hi
        low[at, :] = pltpu.roll(lo32, turn, 1).astype(BF16) if turn else lo


def wrap_patches(high, low, nx, rows):
    n = 3 * rows
    for ref in (high, low):
        ref[pl.ds(0, n), :] = ref[pl.ds(nx * n, n), :]
        ref[pl.ds((nx + 1) * n, n), :] = ref[pl.ds(n, n), :]


def prepare_kernel(fields, kernel, heads, order, order2, w_rows, w_cols, w_head, bias, t, t_low, wide):
    del order, order2
    state, _ = views(fields)
    nx = state.shape[1]
    for x in range(nx):
        rows = [state[v, x] - (1.0 if v in (0, 4) else 0.0) for v in range(5)]
        mid = jnp.concatenate([*rows, jnp.zeros((8, 128), F32)], axis=0)
        put_patches(t, t_low, x, mid)
    wrap_patches(t, t_low, nx, MAIN)

    ch, taps = kernel.shape
    w = kernel[...]
    hi, lo = split(w)
    wide[...] = jnp.zeros_like(wide)
    wide[pl.ds(0, ch), pl.ds(0, taps)] = hi.astype(F32)
    wide[pl.ds(ch, ch), pl.ds(0, taps)] = lo.astype(F32)
    both = wide[...].astype(BF16)
    kind, tap = columns(COLUMNS)
    base = jnp.dot(both, own_taps(kind, tap), preferred_element_type=F32)
    rim = jnp.dot(both, rim_taps(kind, tap), preferred_element_type=F32)
    n = base.shape[1]
    kind = jnp.broadcast_to(kind[0:1], base.shape)
    main = jnp.where(kind < 3, base, 0.0)
    bands = []
    for y in range(8):
        rows = main
        if y == 0:
            rows = jnp.where(kind == 0, 0.0, rows)
        if y == 7:
            rows = jnp.where(kind == 2, 0.0, rows)
        if y != 1:
            rows = pltpu.roll(rows, (y - 1) % n, 1)
        if y == 0:
            rows = rows + jnp.where(kind == 8, base, 0.0)
        if y == 7:
            rows = rows + jnp.where(kind == 10, base, 0.0)
        bands.append(rows)
    bands.append(jnp.where((kind == 0) | (kind == 8) | (kind == 9), rim, 0.0))
    bands.append(jnp.where((kind == 7) | (kind == 10) | (kind == 11), rim, 0.0))
    full = jnp.concatenate([b[:ch] for b in bands] + [b[ch:] for b in bands], axis=0)
    w_rows[...] = full.astype(BF16)
    kept = full.shape[0] // 2
    cols = jnp.concatenate([full[:kept], full[:kept], full[kept:]], axis=0)
    cols = jnp.concatenate([cols, jnp.zeros((512 - 3 * kept, n), F32)], axis=0)
    own_cols = []
    for q in range(3):
        own_cols += [cols[:, (3 * q + o) * MAIN : (3 * q + o) * MAIN + 40] for o in range(3)]
        own_cols.append(jnp.zeros((512, 8), F32))
    w_cols[...] = jnp.concatenate(own_cols, axis=1).T.astype(BF16)
    total = jnp.sum(w * level_taps(w.shape), axis=1, keepdims=True)
    total = jnp.broadcast_to(total, (ch, 128))
    bias[...] = jnp.concatenate([total] * 10, axis=0)

    h_hi, h_lo = split(STEP * heads[...])
    none = jnp.zeros((3, ch), F32)
    pair = jnp.concatenate([h_hi.astype(F32), none, h_lo.astype(F32), none], axis=0).astype(BF16)
    r = lax.broadcasted_iota(jnp.int32, (kept, ch), 0)
    q = lax.broadcasted_iota(jnp.int32, (kept, ch), 1)
    spread = jnp.where((r & (ch - 1)) == q, 1.0, 0.0).astype(BF16)
    picked = over_lanes(pair, spread)
    y_of = lax.broadcasted_iota(jnp.int32, (8, kept), 0)
    col = lax.broadcasted_iota(jnp.int32, (8, kept), 1)
    same = (col >= y_of * ch) & (col < (y_of + 1) * ch)
    split_heads = []
    for at in (0, 8):
        rows = [
            jnp.where(same, jnp.broadcast_to(picked[at + e : at + e + 1], (8, kept)), 0.0)
            for e in range(5)
        ]
        five = picked[at : at + 8]
        rows.append(jnp.where((col >= 8 * ch) & (col < 9 * ch), five, 0.0))
        rows.append(jnp.where(col >= 9 * ch, five, 0.0))
        rows.append(jnp.zeros((8, kept), F32))
        split_heads.append(jnp.concatenate(rows, axis=0))
    three = jnp.concatenate([split_heads[0], split_heads[1], split_heads[0]], axis=0)
    w_head[...] = three.T.astype(BF16)


def c_kernel(
    fields, near_twin, near_other, kernel, w_rows, w_head, bias, t, t_low,
    parts, d_high, d_low,
    rim, rim_low, outer, outer_low, edge, gedge,
):
    _, cot = views(fields)
    nx = cot.shape[1]
    ch, taps = kernel.shape
    rim_state, rim_cot, _ = from_rims(near_twin, near_other)

    for v in range(5):
        level = 1.0 if v in (0, 4) else 0.0
        for q, row in enumerate((-1, 8, -2, 9)):
            at = q // 2 * RIM + 5 * (q % 2) + v
            edge[pl.ds(at, nx, stride=2 * RIM), :] = rim_state(row, v) - level
        gedge[pl.ds(v, nx, stride=16), :] = rim_cot(-1, v)
        gedge[pl.ds(8 + v, nx, stride=16), :] = rim_cot(8, v)
    none = jnp.zeros((nx, 128), F32)
    for q in range(10, RIM):
        edge[pl.ds(q, nx, stride=2 * RIM), :] = none
        edge[pl.ds(RIM + q, nx, stride=2 * RIM), :] = none
    for q in (5, 6, 7):
        gedge[pl.ds(q, nx, stride=16), :] = none
        gedge[pl.ds(8 + q, nx, stride=16), :] = none
    for x in range(nx):
        put_patches(rim, rim_low, x, edge[pl.ds(2 * x * RIM, RIM), :])
        put_patches(outer, outer_low, x, edge[pl.ds((2 * x + 1) * RIM, RIM), :])
    wrap_patches(rim, rim_low, nx, RIM)
    wrap_patches(outer, outer_low, nx, RIM)

    def gathered(x, *blocks):
        columns = []
        for j in range(WIDE):
            rows = [ref[pl.ds((x + j) * 3 * n, 9 * n), :] for ref, n in blocks]
            columns.append(jnp.concatenate(rows, axis=0) if len(rows) > 1 else rows[0])
        return jnp.concatenate(columns, axis=1)

    kept = 8 * ch
    kg = hg = dsum = None
    zeros8 = jnp.zeros((8, 128 * WIDE), F32)
    for x in range(0, nx, WIDE):
        s_hi = gathered(x, (t, MAIN), (rim, RIM))
        s_lo = gathered(x, (t_low, MAIN), (rim_low, RIM))
        far_hi, far_lo = gathered(x, (outer, RIM)), gathered(x, (outer_low, RIM))
        z2 = jnp.dot(
            w_rows[...], jnp.concatenate([s_hi, far_hi], axis=0), preferred_element_type=F32
        )
        rows = z2.shape[0] // 2
        z3 = jnp.dot(
            w_rows[pl.ds(0, rows), :],
            jnp.concatenate([s_lo, far_lo], axis=0),
            preferred_element_type=F32,
        )
        z = z2[:rows] + (z2[rows:] + z3) + jnp.concatenate([bias[...]] * WIDE, axis=1)
        hidden = jnp.tanh(z)
        g = jnp.concatenate(
            [
                jnp.concatenate(
                    [cot[v, x + j] for v in range(5)] + [gedge[pl.ds((x + j) * 16, 16), :]], axis=0
                )
                for j in range(WIDE)
            ],
            axis=1,
        )
        g_hi, g_lo = split(g)
        g_hi32, g_lo32 = g_hi.astype(F32), g_lo.astype(F32)
        g3 = jnp.concatenate(
            [g_hi32, zeros8, g_hi32, zeros8, g_lo32, zeros8], axis=0
        ).astype(BF16)
        d = (1.0 - hidden * hidden) * jnp.dot(w_head[...], g3, preferred_element_type=F32)
        d_hi, d_lo = split(d)
        d_high[:, pl.ds(128 * x, 128 * WIDE)] = d_hi
        d_low[:, pl.ds(128 * x, 128 * WIDE)] = d_lo
        k2 = over_lanes(
            jnp.concatenate([s_hi, s_lo], axis=0),
            jnp.concatenate([d_hi[:kept], d_lo[:kept]], axis=0),
        )
        k2 = k2[:OWN_COLUMNS, :kept] + (k2[:OWN_COLUMNS, kept:] + k2[OWN_COLUMNS:, :kept])
        kg = k2 if kg is None else kg + k2
        hid2 = jnp.concatenate(split(hidden[:kept]), axis=0)
        g2 = jnp.concatenate([g_hi32[:40], g_lo32[:40]], axis=0).astype(BF16)
        h2 = over_lanes(g2, hid2)
        hg = h2 if hg is None else hg + h2
        for j in range(WIDE):
            level = d[:kept, 128 * j : 128 * (j + 1)]
            dsum = level if dsum is None else dsum + level

    sums = jnp.sum(dsum, axis=1, keepdims=True)
    kg = kg.T
    hg = (hg[:40, :kept] + hg[40:, :kept]) + (hg[:40, kept:] + hg[40:, kept:])
    y_row = lax.broadcasted_iota(jnp.int32, (40, kept), 0) & 7
    y_col = lax.broadcasted_iota(jnp.int32, (40, kept), 1)
    same_y = (y_col >= y_row * ch) & (y_col < (y_row + 1) * ch)
    hg = jnp.where(same_y, hg, 0.0)
    by_eq = jnp.concatenate(
        [jnp.sum(hg[8 * e : 8 * e + 8], axis=0, keepdims=True) for e in range(5)]
        + [jnp.zeros((123, kept), F32)],
        axis=0,
    ).T
    level_sum = jnp.zeros((ch, 1), F32)
    head_sum = jnp.zeros((ch, 128), F32)
    n = kg.shape[1]
    columns_at, tap = columns(n)
    kind = jnp.broadcast_to(columns_at[0:1], (ch, n))
    total = jnp.zeros((ch, n), F32)
    for y in range(8):
        rows = kg[y * ch : (y + 1) * ch]
        moved = rows if y == 1 else pltpu.roll(rows, (1 - y) % n, 1)
        keep = kind < 3
        if y == 0:
            keep = (kind == 1) | (kind == 2)
            total = total + jnp.where(kind == 8, rows, 0.0)
        if y == 7:
            keep = kind < 2
            total = total + jnp.where(kind == 10, rows, 0.0)
        total = total + jnp.where(keep, moved, 0.0)
        level_sum = level_sum + sums[y * ch : (y + 1) * ch]
        head_sum = head_sum + by_eq[y * ch : (y + 1) * ch]
    grads = over_lanes(jnp.concatenate(split(total), axis=0), own_taps(columns_at, tap))
    n_pick = grads.shape[1]
    parts[...] = jnp.zeros_like(parts)
    parts[:, pl.ds(0, n_pick)] = grads[:ch] + grads[ch:]
    parts[:, pl.ds(0, taps)] = parts[:, pl.ds(0, taps)] + level_sum * level_taps((ch, taps))
    parts[:, pl.ds(128, 128)] = parts[:, pl.ds(128, 128)] + pltpu.roll(head_sum * STEP, 16, 1)


def c_back_kernel(w_cols, d_high, d_low, order, own, acc):
    del order
    nx = own.shape[1]
    rows = d_high.shape[0]
    written = set()
    zeros = jnp.zeros((512 - 3 * rows, 128 * WIDE), BF16)
    for x in range(0, nx, WIDE):
        d_hi = d_high[:, pl.ds(128 * x, 128 * WIDE)]
        d_lo = d_low[:, pl.ds(128 * x, 128 * WIDE)]
        back = jnp.dot(
            w_cols[...],
            jnp.concatenate([d_hi, d_lo, d_hi, zeros], axis=0),
            preferred_element_type=F32,
        )
        for m in range(WIDE + 2):
            total = None
            for j in range(WIDE):
                if 0 <= m - j < 3:
                    q = m - j
                    piece = back[q * 128 : q * 128 + 120, 128 * j : 128 * (j + 1)]
                    total = piece if total is None else total + piece
            here = (x + m - 1) % nx
            if here in written:
                total = total + acc[pl.ds(here * 120, 120), :]
            written.add(here)
            acc[pl.ds(here * 120, 120), :] = total
    for x in range(nx):
        at = x * 120
        total = (
            acc[pl.ds(at + 40, 40), :]
            + pltpu.roll(acc[pl.ds(at, 40), :], 127, 1)
            + pltpu.roll(acc[pl.ds(at + 80, 40), :], 1, 1)
        )
        for v in range(5):
            own[v, x] = total[8 * v : 8 * v + 8]


def columns(n):
    lane = lax.broadcasted_iota(jnp.int32, (8, n), 1)
    main = lane < 9 * MAIN
    far = lane >= OWN_COLUMNS
    past = lane - jnp.where(far, OWN_COLUMNS, 9 * MAIN)
    block = sum((lane >= MAIN * i).astype(jnp.int32) for i in range(1, 9))
    o = jnp.where(main, block, past >> 4)
    r = jnp.where(main, lane - MAIN * block, past & (RIM - 1))
    second = (r >= 5).astype(jnp.int32)
    rim = jnp.where(r < 10, 8 + 2 * second + far.astype(jnp.int32), 12)
    kind = jnp.where(main, jnp.where(r < 40, r & 7, 12), rim)
    v = jnp.where(main, r >> 3, r - 5 * second)
    return kind, o * 5 + v


def taps_of(columns_at):
    n = columns_at.shape[1]
    row = lax.broadcasted_iota(jnp.int32, (144, n), 0)
    return jnp.where(row == jnp.broadcast_to(columns_at[0:1], (144, n)), 1.0, 0.0).astype(BF16)


def own_taps(kind, tap):
    at = jnp.where(kind < 3, tap + 45 * kind, 1000)
    at = jnp.where(kind == 8, tap, at)
    return taps_of(jnp.where(kind == 10, tap + 90, at))


def rim_taps(kind, tap):
    first = (kind == 9) | (kind == 7)
    middle = (kind == 8) | (kind == 10)
    last = (kind == 0) | (kind == 11)
    at = jnp.where(first, tap, jnp.where(middle, tap + 45, 1000))
    return taps_of(jnp.where(last, tap + 90, at))


def level_taps(shape):
    t = lax.broadcasted_iota(jnp.int32, shape, 1).astype(F32)
    v = t - 5.0 * jnp.floor((t + 0.5) * 0.2)
    return jnp.where((v < 0.5) | (v > 3.5), 1.0, 0.0)


def call(kernel, outs, scratch, us, n_in, order=0):
    spec = pl.BlockSpec(memory_space=pltpu.VMEM)
    return pl.pallas_call(
        kernel,
        out_shape=outs,
        in_specs=[spec] * n_in + [pl.BlockSpec(memory_space=pl.ANY)] * order,
        scratch_shapes=scratch,
        compiler_params=pltpu.CompilerParams(vmem_limit_bytes=VMEM),
        cost_estimate=pl.CostEstimate(
            flops=int(us * 1.15e9), bytes_accessed=int(us * 3.69e6), transcendentals=0
        ),
    )


def body(state, cot, flags, kernel, heads):
    _, nx, ny, nz = state.shape
    ch, taps = kernel.shape
    count = lax.axis_size("gy")
    cells = nx * ny * nz
    shape = lambda *dims: jax.ShapeDtypeStruct(dims, F32)
    half_shape = lambda *dims: jax.ShapeDtypeStruct(dims, BF16)
    full = shape(5, nx, ny, nz)
    with_twin = [(i, i ^ 1) for i in range(count)]
    with_other = [(i, (i + 1) % count if i % 2 else (i - 1) % count) for i in range(count)]
    vm = pltpu.VMEM
    lines = 5 * nx * ny

    flat = jnp.concatenate([state.reshape(lines, nz), cot.reshape(lines, nz)])
    fields = flat.reshape(10, nx, ny, nz)
    near, far = shape(NEAR, nx, nz), shape(FAR, nx, nz)
    x_scratch = [
        vm((5, nx + 5, ny, nz), F32),
        vm((5, nx + 1, ny, nz), F32),
        vm((5, nx + 5, ny, nz), F32),
    ]
    early = call(x_early_kernel, full, x_scratch, 0.2, 2)(fields, flags)
    near_twin, near_other = call(near_kernel, (near, near), [], 0.2, 1, 1)(flat, early)
    near_rims = (
        lax.ppermute(near_twin, "gy", with_twin),
        lax.ppermute(near_other, "gy", with_other),
    )
    *prepared, patches, patches_low = call(
        prepare_kernel,
        (
            half_shape(20 * ch, COLUMNS),
            half_shape(384, 512),
            half_shape(10 * ch, 192),
            shape(10 * ch, 128),
            half_shape((nx + 2) * 3 * MAIN, nz),
            half_shape((nx + 2) * 3 * MAIN, nz),
        ),
        [vm((2 * ch, 144), F32)],
        1.5,
        3,
        2,
    )(fields, kernel, heads, near_twin, near_other)
    begun = call(x_late_kernel, shape(5, nx + 5, ny, nz), x_scratch[:2], 1.5, 2, 1)(
        fields, flags, patches
    )
    far_twin, far_other = call(far_kernel, (far, far), [], 0.2, 2, 1)(
        flat, flags.reshape(3 * nx * ny, nz), begun
    )
    first = call(x_last_kernel, full, x_scratch, 1.5, 4, 1)(
        fields, flags, early, begun, far_other
    )
    far_rims = (
        lax.ppermute(far_twin, "gy", with_twin),
        lax.ppermute(far_other, "gy", with_other),
    )
    near_rims, patches, first = lax.optimization_barrier((near_rims, patches, first))
    w_rows, w_cols, w_head, bias = prepared
    parts, d_high, d_low = call(
        c_kernel,
        (
            shape(ch, 256),
            half_shape(10 * ch, nx * nz),
            half_shape(10 * ch, nx * nz),
        ),
        [
            *[vm(((nx + 2) * 3 * RIM, nz), BF16)] * 4,
            vm((2 * RIM * nx, nz), F32),
            vm((16 * nx, nz), F32),
        ],
        4.2,
        9,
    )(fields, *near_rims, kernel, w_rows, w_head, bias, patches, patches_low)

    def exchanged(value, bit):
        return lax.ppermute(value, "gy", [(i, i ^ bit) for i in range(count)])

    bits = [1 << b for b in range(count.bit_length() - 1)]
    sums = parts
    for bit in bits[:-4]:
        sums = sums + exchanged(sums, bit)
    third = nx // 6 * 2
    yz = lambda lo, hi, before, order: call(
        functools.partial(yz_kernel, lo, hi), full, [vm((lines, nz), F32)] * 2, 2.2, 9, 1
    )(fields, flags, *near_rims, *far_rims, first, before, rim, order)
    got = exchanged(sums, bits[-4])
    own = call(c_back_kernel, full, [vm((nx * 120, nz), F32)], 1.1, 3, 1)(
        w_cols, d_high, d_low, sums
    )
    got, own = lax.optimization_barrier((got, own))
    sums = sums + got
    got = exchanged(sums, bits[-3])
    rim = call(e_kernel, shape(lines, nz), [], 1.1, 5, 1)(flat, *near_rims, *far_rims, sums)
    total = yz(0, third, own, sums)
    got, total = lax.optimization_barrier((got, total))
    sums = sums + got
    got = exchanged(sums, bits[-2])
    total = yz(third, nx - nx // 8 * 3, total, sums)
    got, total = lax.optimization_barrier((got, total))
    sums = sums + got
    got = exchanged(sums, bits[-1])
    flow = yz(nx - nx // 8 * 3, nx, total, sums)
    got, flow = lax.optimization_barrier((got, flow))
    scale = float(cells * count) ** (-0.5)
    k_out, h_out = call(
        functools.partial(sum_kernel, scale), (shape(ch, taps), shape(5, ch)), [], 0.5, 2
    )(sums, got)
    return flow, k_out, h_out


def solution(mesh):
    split_y = P(None, "ens", "gy", None)
    return jax.shard_map(
        body,
        mesh=mesh,
        in_specs=(split_y, split_y, split_y, P(), P()),
        out_specs=(split_y, P("ens", None), P("ens", None)),
        check_vma=False,
    )
```

```python
import functools

import jax
import jax.numpy as jnp
from jax import lax
from jax.experimental import pallas as pl
from jax.experimental.pallas import tpu as pltpu
from jax.sharding import PartitionSpec as P

STEP = 0.3
FLOOR = 0.01
BELOW, ABOVE = 2, 3
SLABS = 2
WIDE = 4
VMEM = 48 * 1024 * 1024
F32 = jnp.float32
BF16 = jnp.bfloat16


def rcp(x):
    return pl.reciprocal(x, approx=True)


def shared_terms(v):
    p = [v[i + 1] - v[i] for i in range(5)]
    d = [p[i + 1] - p[i] for i in range(4)]
    h = [(4.0 / 3.0) * x for x in d]
    k = [h[i] * d[i] + FLOOR for i in range(4)]
    g = [x + x for x in h]
    t = [d[i + 1] - d[i] for i in range(3)]
    return p, d, k, g, t


def side_value(pa, pm, pm2, ka, kb, kc, m0, m2, td, t1, smooth, c0, c2):
    i0 = rcp(ka + pa * m0)
    i1 = rcp(kb + pa * pm)
    i2 = rcp(kc + pm * m2)
    w0 = i0 * i0
    w1 = 6.0 * (i1 * i1)
    w2 = 3.0 * (i2 * i2)
    r = rcp(w0 + w1 + w2)
    o0 = jnp.where(smooth, w0 * r, c0)
    o2 = jnp.where(smooth, w2 * r, c2)
    u = o0 * td + o2 * t1
    b0 = w0 * i0 * (td - u)
    b1 = w1 * i1 * u
    b2 = w2 * i2 * (t1 - u)
    return (pa + pm2) - u, (b0, b1, b2, r, o0, o2)


def side_pull(mu, pa, pm, m0, m2, smooth, saved):
    b0, b1, b2, r, o0, o2 = saved
    mu2 = mu + mu
    rm = jnp.where(smooth, mu2, 0.0) * r
    s0, s1, s2 = b0 * rm, b1 * rm, b2 * rm
    pa_bar = s0 * (m0 + pa) - s1 * pm + mu
    pm_bar = s2 * (m2 + pm) - s1 * pa + mu2
    return s0, s1, s2, pa_bar, pm_bar, o0 * mu2, o2 * mu


def hllc_pull(left, right, normal, flags, cot):
    region = flags & 3
    is_right = region >= 2
    star = ((region + 1) & 2) != 0
    n_at = 1 + normal
    tang = [1 + i for i in range(3) if i != normal]
    rl, rr_, pl_, pr_, nl, nr = left[0], right[0], left[4], right[4], left[n_at], right[n_at]

    def sound(r, p):
        inv = rcp(r)
        t = 1.4 * p * inv
        inv_c = lax.rsqrt(t)
        return inv, inv_c, t * inv_c

    inv_rl, inv_cl, cl = sound(rl, pl_)
    inv_rr, inv_cr, cr = sound(rr_, pr_)
    c = 0.5 * (cl + cr)
    r2 = rl + rr_
    inv = rcp(r2 * c)
    nm = 0.5 * (nl + nr)
    gap = (pl_ - pr_) * inv
    sm = nm + gap
    sc = jnp.where(is_right, c, -c)
    s = nm + sc
    pick = [jnp.where(is_right, right[i], left[i]) for i in range(5)]
    r, un, u1, u2, p = pick[0], pick[n_at], pick[tang[0]], pick[tang[1]], pick[4]
    a = s - un
    dl = sm - un
    si = jnp.where(star, rcp(sc - gap), 0.0)
    j = s * si
    kap = j * dl
    g0, gn, g1, g2, ge = cot[0], cot[n_at], cot[tang[0]], cot[tang[1]], cot[4]
    w = un + kap
    half_q = 0.5 * (un * un + u1 * u1 + u2 * u2)
    enthalpy = 3.5 * p + r * half_q
    b = g0 + u1 * g1 + u2 * g2 + un * gn
    m = r * b + enthalpy * ge
    n = gn + sm * ge
    rkap = r * kap
    f_kap = m + r * a * n
    f_a = rkap * n
    si2 = si * si
    s_bar = f_a - f_kap * (dl * sm * si2)
    sm_bar = f_kap * (s * a * si2) + rkap * a * ge
    wr = w * r
    k_bar = [None] * 5
    k_bar[0] = w * (b + half_q * ge) + kap * a * n
    k_bar[n_at] = m + wr * (gn + un * ge) - f_kap * j - f_a
    k_bar[tang[0]] = wr * (g1 + u1 * ge)
    k_bar[tang[1]] = wr * (g2 + u2 * ge)
    k_bar[4] = 3.5 * (w * ge) + gn
    e = sm_bar * inv
    eg = e * gap
    c_half = 0.5 * (jnp.where(is_right, s_bar, -s_bar) - eg * r2)
    n_half = 0.5 * (s_bar + sm_bar)
    r_both = -(eg * c)
    xl = c_half * inv_rl
    xr = c_half * inv_rr
    base_l = {0: r_both - 0.5 * (xl * cl), n_at: n_half, 4: 0.7 * (xl * inv_cl) + e}
    base_r = {0: r_both - 0.5 * (xr * cr), n_at: n_half, 4: 0.7 * (xr * inv_cr) - e}
    l_bar, r_bar = [], []
    for i in range(5):
        kr = jnp.where(is_right, k_bar[i], 0.0)
        kl = k_bar[i] - kr
        l_bar.append(base_l[i] + kl if i in base_l else kl)
        r_bar.append(base_r[i] + kr if i in base_r else kr)
    return l_bar, r_bar


def face_pull(cells, cot, flags, normal):
    stencil = flags >> 2
    smooth = stencil == 0
    c0 = jnp.where(stencil == 1, 1.0, 0.0)
    c2 = jnp.where(stencil == 3, 1.0, 0.0)
    left, right, kept = [], [], []
    for v in cells:
        p, d, k, g, t = shared_terms(v)
        pm2 = p[2] + p[2]
        args_l = (p[1], p[2], p[1] + d[0], p[2] - d[2], t[0] + t[0], t[1])
        args_r = (p[3], p[2], p[3] - d[3], p[2] + d[1], t[2] + t[2], t[1])
        hl, saved_l = side_value(
            p[1], p[2], pm2, k[0], k[1], k[2], *args_l[2:], smooth, c0, c2
        )
        hr, saved_r = side_value(
            p[3], p[2], pm2, k[3], k[2], k[1], *args_r[2:], smooth, c0, c2
        )
        left.append(v[2] + hl * (1.0 / 6.0))
        right.append(v[3] - hr * (1.0 / 6.0))
        kept.append((p, g, args_l[:4], args_r[:4], saved_l, saved_r))
    l_bar, r_bar = hllc_pull(left, right, normal, flags, cot)
    out = []
    for i in range(5):
        p, g, args_l, args_r, saved_l, saved_r = kept[i]
        a0, a1, a2, pa_l, pm_l, x0, x2 = side_pull(
            l_bar[i] * (1.0 / 6.0), *args_l, smooth, saved_l
        )
        b0, b1, b2, pa_r, pm_r, y0, y2 = side_pull(
            r_bar[i] * (-1.0 / 6.0), *args_r, smooth, saved_r
        )
        d0 = a0 * (g[0] + p[1]) + x0
        d1 = (b2 * (g[1] + p[2]) - a1 * g[1]) + (x2 - x0) + y2
        d2 = (a2 * (g[2] - p[2]) - b1 * g[2]) + (y0 - y2) - x2
        d3 = b0 * (g[3] - p[3]) - y0
        p2 = pa_l + (d0 - d1)
        p3 = pm_l + pm_r + (d1 - d2)
        p4 = pa_r + (d2 - d3)
        out.append([d0, -d0 - p2, l_bar[i] + (p2 - p3), r_bar[i] + (p3 - p4), p4 - d3, d3])
    return out


def conserved_pull(s, g):
    half_q = 0.5 * (s[1] * s[1] + s[2] * s[2] + s[3] * s[3])
    return [
        g[0] + s[1] * g[1] + s[2] * g[2] + s[3] * g[3] + half_q * g[4],
        s[0] * (g[1] + s[1] * g[4]),
        s[0] * (g[2] + s[2] * g[4]),
        s[0] * (g[3] + s[3] * g[4]),
        2.5 * g[4],
    ]


NEAR_STATE, FAR_STATE = 2, 3
NEAR_COT, FAR_COT = 1, 2
FLAG_ROWS = 3
NEAR = 5 * (NEAR_STATE + NEAR_COT)
FAR = 5 * (FAR_STATE + FAR_COT) + FLAG_ROWS


def views(fields):
    n = fields.shape[0] // 2
    return fields.at[pl.ds(0, n)], fields.at[pl.ds(n, n)]


def pack(ref, rows, first, twin, other, at):
    even = is_even()
    nx = twin.shape[1]
    count = ref.shape[0] // (8 * nx)
    for r in rows:
        for v in range(count):
            low = ref[pl.ds(v * nx * 8 + r, nx, stride=8), :].astype(F32)
            top = ref[pl.ds(v * nx * 8 + 7 - r, nx, stride=8), :].astype(F32)
            i = at + (r - first) * count + v
            twin[i] = jnp.where(even, top, low)
            other[i] = jnp.where(even, low, top)


def near_kernel(flat, order, twin, other):
    del order
    s, g = views(flat)
    pack(s, range(NEAR_STATE), 0, twin, other, 0)
    pack(g, range(NEAR_COT), 0, twin, other, 5 * NEAR_STATE)


def far_kernel(flat, flags, order, twin, other):
    del order
    s, g = views(flat)
    n = flags.shape[0] // 3
    pack(s, range(NEAR_STATE, NEAR_STATE + FAR_STATE), NEAR_STATE, twin, other, 0)
    pack(g, range(NEAR_COT, NEAR_COT + FAR_COT), NEAR_COT, twin, other, 5 * FAR_STATE)
    pack(flags.at[pl.ds(n, n)], range(FLAG_ROWS), 0, twin, other, FAR - FLAG_ROWS)


def from_rims(near_twin, near_other, far_twin=None, far_other=None):
    even = is_even()

    def pick(twin, other, i, below):
        if below:
            return jnp.where(even, other[i], twin[i])
        return jnp.where(even, twin[i], other[i])

    def read(row, near, near_at, far_at, v):
        below = row < 0
        r = -1 - row if below else row - 8
        if r < near:
            return pick(near_twin, near_other, near_at + r * 5 + v, below)
        return pick(far_twin, far_other, far_at + (r - near) * 5 + v, below)

    def state(row, v):
        return read(row, NEAR_STATE, 0, 0, v)

    def cot(row, v):
        return read(row, NEAR_COT, 5 * NEAR_STATE, 5 * FAR_STATE, v)

    def flags(row):
        below = row < 0
        r = -1 - row if below else row - 8
        return pick(far_twin, far_other, FAR - FLAG_ROWS + r, below).astype(jnp.int32)

    return state, cot, flags


def x_faces(lo, hi, fields, flags, acc, pad, gpad):
    state, cot = views(fields)
    nx = state.shape[1]
    for v in range(5):
        pad[v, pl.ds(2, nx)] = state[v]
        pad[v, pl.ds(0, 2)] = state[v, pl.ds(nx - 2, 2)]
        pad[v, pl.ds(nx + 2, 3)] = state[v, pl.ds(0, 3)]
        gpad[v, pl.ds(0, nx)] = cot[v]
        gpad[v, pl.ds(nx, 1)] = cot[v, pl.ds(0, 1)]

    def step(i, carry):
        x = lo + i * SLABS
        cells = [[pad[v, pl.ds(x + k, SLABS)] for k in range(6)] for v in range(5)]
        g = [gpad[v, pl.ds(x, SLABS)] for v in range(5)]
        face = [STEP * (gpad[v, pl.ds(x + 1, SLABS)] - g[v]) for v in range(5)]
        terms = face_pull(cells, face, flags[0, pl.ds(x, SLABS)], 0)
        own = conserved_pull([cells[v][2] for v in range(5)], g)
        for v in range(5):
            terms[v][2] = terms[v][2] + own[v]
            for s in range(SLABS + 5):
                total = None
                for k in range(6):
                    if 0 <= s - k < SLABS:
                        part = terms[v][k][s - k]
                        total = part if total is None else total + part
                acc[v, x + s] = acc[v, x + s] + total
        return carry

    lax.fori_loop(0, (hi - lo) // SLABS, step, 0)


def fold_rim(acc, out):
    nx = out.shape[1]
    for v in range(5):
        acc[v, pl.ds(nx, 2)] = acc[v, pl.ds(nx, 2)] + acc[v, pl.ds(0, 2)]
        acc[v, pl.ds(2, 3)] = acc[v, pl.ds(2, 3)] + acc[v, pl.ds(nx + 2, 3)]
        out[v] = acc[v, pl.ds(2, nx)]


def x_early_kernel(fields, flags, out, pad, gpad, acc):
    @pl.when(lax.axis_index("gy") == 0)
    def _():
        acc[...] = jnp.zeros_like(acc)
        x_faces(0, out.shape[1], fields, flags, acc, pad, gpad)
        fold_rim(acc, out)


def x_late_kernel(fields, flags, order, acc, pad, gpad):
    del order

    @pl.when(lax.axis_index("gy") != 0)
    def _():
        acc[...] = jnp.zeros_like(acc)
        x_faces(0, flags.shape[1] // 2, fields, flags, acc, pad, gpad)


def x_last_kernel(fields, flags, early, begun, order, out, pad, gpad, acc):
    del order
    nx = out.shape[1]
    first = lax.axis_index("gy") == 0

    @pl.when(first)
    def _():
        out[...] = early[...]

    @pl.when(jnp.logical_not(first))
    def _():
        acc[...] = begun[...]
        x_faces(nx // 2, nx, fields, flags, acc, pad, gpad)
        fold_rim(acc, out)


def z_faces(state, cot, flags, x):
    cells, face = [], []
    for v in range(5):
        mid = state[v, pl.ds(x, SLABS)]
        cells.append([mid if k == 0 else pltpu.roll(mid, (-k) % 128, 2) for k in range(-2, 4)])
        g = cot[v, pl.ds(x, SLABS)]
        face.append(STEP * (pltpu.roll(g, 127, 2) - g))
    terms = face_pull(cells, face, flags[2, pl.ds(x, SLABS)], 2)
    total = []
    for v in range(5):
        t = terms[v][2]
        for k in (-2, -1, 1, 2, 3):
            t = t + pltpu.roll(terms[v][k + 2], k % 128, 2)
        total.append(t)
    return total


def e_kernel(flat, near_twin, near_other, far_twin, far_other, order, out):
    del order
    state, cot = views(flat)
    nx = out.shape[0] // 40
    rim_state, rim_cot, rim_flags = from_rims(near_twin, near_other, far_twin, far_other)

    def own(ref, row, v):
        return ref[pl.ds(v * nx * 8 + row, nx, stride=8), :]

    state_rows, cot_rows = {}, {}
    for v in range(5):
        for row in (*range(-5, 3), *range(6, 13)):
            inside = 0 <= row < 8
            state_rows[row, v] = own(state, row, v) if inside else rim_state(row, v)
        for row in (-3, -2, -1, 0, 8, 9, 10):
            inside = 0 <= row < 8
            cot_rows[row, v] = own(cot, row, v) if inside else rim_cot(row, v)
    sums = {}
    for j in (-3, -2, -1, 8, 9):
        cells = [[state_rows[j + k, v] for k in range(-2, 4)] for v in range(5)]
        face = [STEP * (cot_rows[j + 1, v] - cot_rows[j, v]) for v in range(5)]
        terms = face_pull(cells, face, rim_flags(j), 1)
        for v in range(5):
            for k in range(-2, 4):
                if 0 <= j + k < 8:
                    t = terms[v][k + 2]
                    sums[j + k, v] = sums[j + k, v] + t if (j + k, v) in sums else t
    for v in range(5):
        for row in range(8):
            value = sums[row, v] if (row, v) in sums else jnp.zeros((nx, 128), F32)
            out[pl.ds(v * nx * 8 + row, nx, stride=8), :] = value


def yz_kernel(lo, hi, fields, flags, near_twin, near_other, far_twin, far_other, first, before, rim, order, out, halo, ghalo):
    del order
    state, cot = views(fields)
    rims = from_rims(near_twin, near_other, far_twin, far_other)
    rim_state, rim_cot, _ = rims
    nx = out.shape[1]
    for v in range(5):
        for kept in (pl.ds(0, lo), pl.ds(hi, nx - hi)):
            if kept.size:
                out[v, kept] = before[v, kept]
    for v in range(5):
        base = v * nx * 8
        for r in range(ABOVE):
            halo[pl.ds(base + r, nx, stride=8), :] = rim_state(8 + r, v)
        for r in range(BELOW):
            halo[pl.ds(base + 8 - BELOW + r, nx, stride=8), :] = rim_state(r - BELOW, v)
        ghalo[pl.ds(base, nx, stride=8), :] = rim_cot(8, v)
    row = lax.broadcasted_iota(jnp.int32, (SLABS, 8, 128), 1)
    inside = {}
    for k in (-2, -1, 1, 2, 3):
        inside[k] = (row < 8 + k) if k < 0 else (row >= k)

    def step(i, carry):
        x = lo + i * SLABS
        cells, face = [], []
        for v in range(5):
            at = pl.multiple_of((v * nx + x) * 8, 8)
            rim_rows = halo[pl.ds(at, 8 * SLABS), :].reshape(SLABS, 8, 128)
            mid = state[v, pl.ds(x, SLABS)]
            line = []
            for k in range(-2, 4):
                if k == 0:
                    line.append(mid)
                else:
                    line.append(pltpu.roll(jnp.where(inside[k], mid, rim_rows), (-k) % 8, 1))
            cells.append(line)
            g = cot[v, pl.ds(x, SLABS)]
            g_rim = ghalo[pl.ds(at, 8 * SLABS), :].reshape(SLABS, 8, 128)
            face.append(STEP * (pltpu.roll(jnp.where(inside[1], g, g_rim), 7, 1) - g))
        terms = face_pull(cells, face, flags[1, pl.ds(x, SLABS)], 1)
        along_z = z_faces(state, cot, flags, x)
        for v in range(5):
            at = pl.multiple_of((v * nx + x) * 8, 8)
            total = before[v, pl.ds(x, SLABS)] + first[v, pl.ds(x, SLABS)]
            total = total + along_z[v] + terms[v][2]
            total = total + rim[pl.ds(at, 8 * SLABS), :].reshape(SLABS, 8, 128)
            for k in (-2, -1, 1, 2, 3):
                moved = pltpu.roll(terms[v][k + 2], k % 8, 1)
                total = total + jnp.where(inside[k], moved, 0.0)
            out[v, pl.ds(x, SLABS)] = total
        return carry

    lax.fori_loop(0, (hi - lo) // SLABS, step, 0)


def sum_kernel(scale, mine, theirs, k_out, h_out):
    total = (mine[...] + theirs[...]) * scale
    k_out[...] = total[:, : k_out.shape[1]]
    ch = total.shape[0]
    pick = (
        lax.broadcasted_iota(jnp.int32, (8, 128), 1)
        == lax.broadcasted_iota(jnp.int32, (8, 128), 0) + 16
    ).astype(F32)
    heads = lax.dot_general(
        pick,
        total[:, 128:],
        (((1,), (1,)), ((), ())),
        precision=lax.Precision.HIGHEST,
        preferred_element_type=F32,
    )
    h_out[...] = heads[: h_out.shape[0], :ch]


MAIN, RIM = 48, 16
OWN_COLUMNS = 9 * (MAIN + RIM)
COLUMNS = OWN_COLUMNS + 9 * RIM


def split(x):
    hi = x.astype(BF16)
    return hi, (x - hi.astype(F32)).astype(BF16)


def over_lanes(a, b):
    return lax.dot_general(a, b, (((1,), (1,)), ((), ())), preferred_element_type=F32)


def is_even():
    return lax.rem(lax.axis_index("gy"), 2) == 0


def put_patches(high, low, x, rows):
    n = rows.shape[0]
    hi, lo = split(rows)
    hi32, lo32 = hi.astype(F32), lo.astype(F32)
    for q, turn in enumerate((1, 0, 127)):
        at = pl.ds((x + 1) * 3 * n + q * n, n)
        high[at, :] = pltpu.roll(hi32, turn, 1).astype(BF16) if turn else hi
        low[at, :] = pltpu.roll(lo32, turn, 1).astype(BF16) if turn else lo


def wrap_patches(high, low, nx, rows):
    n = 3 * rows
    for ref in (high, low):
        ref[pl.ds(0, n), :] = ref[pl.ds(nx * n, n), :]
        ref[pl.ds((nx + 1) * n, n), :] = ref[pl.ds(n, n), :]


def prepare_kernel(fields, kernel, heads, order, order2, w_rows, w_cols, w_head, bias, t, t_low, wide):
    del order, order2
    state, _ = views(fields)
    nx = state.shape[1]
    for x in range(nx):
        rows = [state[v, x] - (1.0 if v in (0, 4) else 0.0) for v in range(5)]
        mid = jnp.concatenate([*rows, jnp.zeros((8, 128), F32)], axis=0)
        put_patches(t, t_low, x, mid)
    wrap_patches(t, t_low, nx, MAIN)

    ch, taps = kernel.shape
    w = kernel[...]
    hi, lo = split(w)
    wide[...] = jnp.zeros_like(wide)
    wide[pl.ds(0, ch), pl.ds(0, taps)] = hi.astype(F32)
    wide[pl.ds(ch, ch), pl.ds(0, taps)] = lo.astype(F32)
    both = wide[...].astype(BF16)
    kind, tap = columns(COLUMNS)
    base = jnp.dot(both, own_taps(kind, tap), preferred_element_type=F32)
    rim = jnp.dot(both, rim_taps(kind, tap), preferred_element_type=F32)
    n = base.shape[1]
    kind = jnp.broadcast_to(kind[0:1], base.shape)
    main = jnp.where(kind < 3, base, 0.0)
    bands = []
    for y in range(8):
        rows = main
        if y == 0:
            rows = jnp.where(kind == 0, 0.0, rows)
        if y == 7:
            rows = jnp.where(kind == 2, 0.0, rows)
        if y != 1:
            rows = pltpu.roll(rows, (y - 1) % n, 1)
        if y == 0:
            rows = rows + jnp.where(kind == 8, base, 0.0)
        if y == 7:
            rows = rows + jnp.where(kind == 10, base, 0.0)
        bands.append(rows)
    bands.append(jnp.where((kind == 0) | (kind == 8) | (kind == 9), rim, 0.0))
    bands.append(jnp.where((kind == 7) | (kind == 10) | (kind == 11), rim, 0.0))
    full = jnp.concatenate([b[:ch] for b in bands] + [b[ch:] for b in bands], axis=0)
    w_rows[...] = full.astype(BF16)
    kept = full.shape[0] // 2
    cols = jnp.concatenate([full[:kept], full[:kept], full[kept:]], axis=0)
    cols = jnp.concatenate([cols, jnp.zeros((512 - 3 * kept, n), F32)], axis=0)
    own_cols = []
    for q in range(3):
        own_cols += [cols[:, (3 * q + o) * MAIN : (3 * q + o) * MAIN + 40] for o in range(3)]
        own_cols.append(jnp.zeros((512, 8), F32))
    w_cols[...] = jnp.concatenate(own_cols, axis=1).T.astype(BF16)
    total = jnp.sum(w * level_taps(w.shape), axis=1, keepdims=True)
    total = jnp.broadcast_to(total, (ch, 128))
    bias[...] = jnp.concatenate([total] * 10, axis=0)

    h_hi, h_lo = split(STEP * heads[...])
    none = jnp.zeros((3, ch), F32)
    pair = jnp.concatenate([h_hi.astype(F32), none, h_lo.astype(F32), none], axis=0).astype(BF16)
    r = lax.broadcasted_iota(jnp.int32, (kept, ch), 0)
    q = lax.broadcasted_iota(jnp.int32, (kept, ch), 1)
    spread = jnp.where((r & (ch - 1)) == q, 1.0, 0.0).astype(BF16)
    picked = over_lanes(pair, spread)
    y_of = lax.broadcasted_iota(jnp.int32, (8, kept), 0)
    col = lax.broadcasted_iota(jnp.int32, (8, kept), 1)
    same = (col >= y_of * ch) & (col < (y_of + 1) * ch)
    split_heads = []
    for at in (0, 8):
        rows = [
            jnp.where(same, jnp.broadcast_to(picked[at + e : at + e + 1], (8, kept)), 0.0)
            for e in range(5)
        ]
        five = picked[at : at + 8]
        rows.append(jnp.where((col >= 8 * ch) & (col < 9 * ch), five, 0.0))
        rows.append(jnp.where(col >= 9 * ch, five, 0.0))
        rows.append(jnp.zeros((8, kept), F32))
        split_heads.append(jnp.concatenate(rows, axis=0))
    three = jnp.concatenate([split_heads[0], split_heads[1], split_heads[0]], axis=0)
    w_head[...] = three.T.astype(BF16)


def c_kernel(
    fields, near_twin, near_other, kernel, w_rows, w_head, bias, t, t_low,
    parts, d_high, d_low,
    rim, rim_low, outer, outer_low, edge, gedge,
):
    _, cot = views(fields)
    nx = cot.shape[1]
    ch, taps = kernel.shape
    rim_state, rim_cot, _ = from_rims(near_twin, near_other)

    for v in range(5):
        level = 1.0 if v in (0, 4) else 0.0
        for q, row in enumerate((-1, 8, -2, 9)):
            at = q // 2 * RIM + 5 * (q % 2) + v
            edge[pl.ds(at, nx, stride=2 * RIM), :] = rim_state(row, v) - level
        gedge[pl.ds(v, nx, stride=16), :] = rim_cot(-1, v)
        gedge[pl.ds(8 + v, nx, stride=16), :] = rim_cot(8, v)
    none = jnp.zeros((nx, 128), F32)
    for q in range(10, RIM):
        edge[pl.ds(q, nx, stride=2 * RIM), :] = none
        edge[pl.ds(RIM + q, nx, stride=2 * RIM), :] = none
    for q in (5, 6, 7):
        gedge[pl.ds(q, nx, stride=16), :] = none
        gedge[pl.ds(8 + q, nx, stride=16), :] = none
    for x in range(nx):
        put_patches(rim, rim_low, x, edge[pl.ds(2 * x * RIM, RIM), :])
        put_patches(outer, outer_low, x, edge[pl.ds((2 * x + 1) * RIM, RIM), :])
    wrap_patches(rim, rim_low, nx, RIM)
    wrap_patches(outer, outer_low, nx, RIM)

    def gathered(x, *blocks):
        columns = []
        for j in range(WIDE):
            rows = [ref[pl.ds((x + j) * 3 * n, 9 * n), :] for ref, n in blocks]
            columns.append(jnp.concatenate(rows, axis=0) if len(rows) > 1 else rows[0])
        return jnp.concatenate(columns, axis=1)

    kept = 8 * ch
    kg = hg = dsum = None
    zeros8 = jnp.zeros((8, 128 * WIDE), F32)
    for x in range(0, nx, WIDE):
        s_hi = gathered(x, (t, MAIN), (rim, RIM))
        s_lo = gathered(x, (t_low, MAIN), (rim_low, RIM))
        far_hi, far_lo = gathered(x, (outer, RIM)), gathered(x, (outer_low, RIM))
        z2 = jnp.dot(
            w_rows[...], jnp.concatenate([s_hi, far_hi], axis=0), preferred_element_type=F32
        )
        rows = z2.shape[0] // 2
        z3 = jnp.dot(
            w_rows[pl.ds(0, rows), :],
            jnp.concatenate([s_lo, far_lo], axis=0),
            preferred_element_type=F32,
        )
        z = z2[:rows] + (z2[rows:] + z3) + jnp.concatenate([bias[...]] * WIDE, axis=1)
        hidden = jnp.tanh(z)
        g = jnp.concatenate(
            [
                jnp.concatenate(
                    [cot[v, x + j] for v in range(5)] + [gedge[pl.ds((x + j) * 16, 16), :]], axis=0
                )
                for j in range(WIDE)
            ],
            axis=1,
        )
        g_hi, g_lo = split(g)
        g_hi32, g_lo32 = g_hi.astype(F32), g_lo.astype(F32)
        g3 = jnp.concatenate(
            [g_hi32, zeros8, g_hi32, zeros8, g_lo32, zeros8], axis=0
        ).astype(BF16)
        d = (1.0 - hidden * hidden) * jnp.dot(w_head[...], g3, preferred_element_type=F32)
        d_hi, d_lo = split(d)
        d_high[:, pl.ds(128 * x, 128 * WIDE)] = d_hi
        d_low[:, pl.ds(128 * x, 128 * WIDE)] = d_lo
        k2 = over_lanes(
            jnp.concatenate([s_hi, s_lo], axis=0),
            jnp.concatenate([d_hi[:kept], d_lo[:kept]], axis=0),
        )
        k2 = k2[:OWN_COLUMNS, :kept] + (k2[:OWN_COLUMNS, kept:] + k2[OWN_COLUMNS:, :kept])
        kg = k2 if kg is None else kg + k2
        hid2 = jnp.concatenate(split(hidden[:kept]), axis=0)
        g2 = jnp.concatenate([g_hi32[:40], g_lo32[:40]], axis=0).astype(BF16)
        h2 = over_lanes(g2, hid2)
        hg = h2 if hg is None else hg + h2
        for j in range(WIDE):
            level = d[:kept, 128 * j : 128 * (j + 1)]
            dsum = level if dsum is None else dsum + level

    sums = jnp.sum(dsum, axis=1, keepdims=True)
    kg = kg.T
    hg = (hg[:40, :kept] + hg[40:, :kept]) + (hg[:40, kept:] + hg[40:, kept:])
    y_row = lax.broadcasted_iota(jnp.int32, (40, kept), 0) & 7
    y_col = lax.broadcasted_iota(jnp.int32, (40, kept), 1)
    same_y = (y_col >= y_row * ch) & (y_col < (y_row + 1) * ch)
    hg = jnp.where(same_y, hg, 0.0)
    by_eq = jnp.concatenate(
        [jnp.sum(hg[8 * e : 8 * e + 8], axis=0, keepdims=True) for e in range(5)]
        + [jnp.zeros((123, kept), F32)],
        axis=0,
    ).T
    level_sum = jnp.zeros((ch, 1), F32)
    head_sum = jnp.zeros((ch, 128), F32)
    n = kg.shape[1]
    columns_at, tap = columns(n)
    kind = jnp.broadcast_to(columns_at[0:1], (ch, n))
    total = jnp.zeros((ch, n), F32)
    for y in range(8):
        rows = kg[y * ch : (y + 1) * ch]
        moved = rows if y == 1 else pltpu.roll(rows, (1 - y) % n, 1)
        keep = kind < 3
        if y == 0:
            keep = (kind == 1) | (kind == 2)
            total = total + jnp.where(kind == 8, rows, 0.0)
        if y == 7:
            keep = kind < 2
            total = total + jnp.where(kind == 10, rows, 0.0)
        total = total + jnp.where(keep, moved, 0.0)
        level_sum = level_sum + sums[y * ch : (y + 1) * ch]
        head_sum = head_sum + by_eq[y * ch : (y + 1) * ch]
    grads = over_lanes(jnp.concatenate(split(total), axis=0), own_taps(columns_at, tap))
    n_pick = grads.shape[1]
    parts[...] = jnp.zeros_like(parts)
    parts[:, pl.ds(0, n_pick)] = grads[:ch] + grads[ch:]
    parts[:, pl.ds(0, taps)] = parts[:, pl.ds(0, taps)] + level_sum * level_taps((ch, taps))
    parts[:, pl.ds(128, 128)] = parts[:, pl.ds(128, 128)] + pltpu.roll(head_sum * STEP, 16, 1)


def c_back_kernel(w_cols, d_high, d_low, order, own, acc):
    del order
    nx = own.shape[1]
    rows = d_high.shape[0]
    written = set()
    zeros = jnp.zeros((512 - 3 * rows, 128 * WIDE), BF16)
    for x in range(0, nx, WIDE):
        d_hi = d_high[:, pl.ds(128 * x, 128 * WIDE)]
        d_lo = d_low[:, pl.ds(128 * x, 128 * WIDE)]
        back = jnp.dot(
            w_cols[...],
            jnp.concatenate([d_hi, d_lo, d_hi, zeros], axis=0),
            preferred_element_type=F32,
        )
        for m in range(WIDE + 2):
            total = None
            for j in range(WIDE):
                if 0 <= m - j < 3:
                    q = m - j
                    piece = back[q * 128 : q * 128 + 120, 128 * j : 128 * (j + 1)]
                    total = piece if total is None else total + piece
            here = (x + m - 1) % nx
            if here in written:
                total = total + acc[pl.ds(here * 120, 120), :]
            written.add(here)
            acc[pl.ds(here * 120, 120), :] = total
    for x in range(nx):
        at = x * 120
        total = (
            acc[pl.ds(at + 40, 40), :]
            + pltpu.roll(acc[pl.ds(at, 40), :], 127, 1)
            + pltpu.roll(acc[pl.ds(at + 80, 40), :], 1, 1)
        )
        for v in range(5):
            own[v, x] = total[8 * v : 8 * v + 8]


def columns(n):
    lane = lax.broadcasted_iota(jnp.int32, (8, n), 1)
    main = lane < 9 * MAIN
    far = lane >= OWN_COLUMNS
    past = lane - jnp.where(far, OWN_COLUMNS, 9 * MAIN)
    block = sum((lane >= MAIN * i).astype(jnp.int32) for i in range(1, 9))
    o = jnp.where(main, block, past >> 4)
    r = jnp.where(main, lane - MAIN * block, past & (RIM - 1))
    second = (r >= 5).astype(jnp.int32)
    rim = jnp.where(r < 10, 8 + 2 * second + far.astype(jnp.int32), 12)
    kind = jnp.where(main, jnp.where(r < 40, r & 7, 12), rim)
    v = jnp.where(main, r >> 3, r - 5 * second)
    return kind, o * 5 + v


def taps_of(columns_at):
    n = columns_at.shape[1]
    row = lax.broadcasted_iota(jnp.int32, (144, n), 0)
    return jnp.where(row == jnp.broadcast_to(columns_at[0:1], (144, n)), 1.0, 0.0).astype(BF16)


def own_taps(kind, tap):
    at = jnp.where(kind < 3, tap + 45 * kind, 1000)
    at = jnp.where(kind == 8, tap, at)
    return taps_of(jnp.where(kind == 10, tap + 90, at))


def rim_taps(kind, tap):
    first = (kind == 9) | (kind == 7)
    middle = (kind == 8) | (kind == 10)
    last = (kind == 0) | (kind == 11)
    at = jnp.where(first, tap, jnp.where(middle, tap + 45, 1000))
    return taps_of(jnp.where(last, tap + 90, at))


def level_taps(shape):
    t = lax.broadcasted_iota(jnp.int32, shape, 1).astype(F32)
    v = t - 5.0 * jnp.floor((t + 0.5) * 0.2)
    return jnp.where((v < 0.5) | (v > 3.5), 1.0, 0.0)


def call(kernel, outs, scratch, us, n_in, order=0):
    spec = pl.BlockSpec(memory_space=pltpu.VMEM)
    return pl.pallas_call(
        kernel,
        out_shape=outs,
        in_specs=[spec] * n_in + [pl.BlockSpec(memory_space=pl.ANY)] * order,
        scratch_shapes=scratch,
        compiler_params=pltpu.CompilerParams(vmem_limit_bytes=VMEM),
        cost_estimate=pl.CostEstimate(
            flops=int(us * 1.15e9), bytes_accessed=int(us * 3.69e6), transcendentals=0
        ),
    )


def body(state, cot, flags, kernel, heads):
    _, nx, ny, nz = state.shape
    ch, taps = kernel.shape
    count = lax.axis_size("gy")
    cells = nx * ny * nz
    shape = lambda *dims: jax.ShapeDtypeStruct(dims, F32)
    half_shape = lambda *dims: jax.ShapeDtypeStruct(dims, BF16)
    full = shape(5, nx, ny, nz)
    with_twin = [(i, i ^ 1) for i in range(count)]
    with_other = [(i, (i + 1) % count if i % 2 else (i - 1) % count) for i in range(count)]
    vm = pltpu.VMEM
    lines = 5 * nx * ny

    flat = jnp.concatenate([state.reshape(lines, nz), cot.reshape(lines, nz)])
    fields = flat.reshape(10, nx, ny, nz)
    near, far = shape(NEAR, nx, nz), shape(FAR, nx, nz)
    x_scratch = [
        vm((5, nx + 5, ny, nz), F32),
        vm((5, nx + 1, ny, nz), F32),
        vm((5, nx + 5, ny, nz), F32),
    ]
    early = call(x_early_kernel, full, x_scratch, 0.2, 2)(fields, flags)
    near_twin, near_other = call(near_kernel, (near, near), [], 0.2, 1, 1)(flat, early)
    near_rims = (
        lax.ppermute(near_twin, "gy", with_twin),
        lax.ppermute(near_other, "gy", with_other),
    )
    *prepared, patches, patches_low = call(
        prepare_kernel,
        (
            half_shape(20 * ch, COLUMNS),
            half_shape(384, 512),
            half_shape(10 * ch, 192),
            shape(10 * ch, 128),
            half_shape((nx + 2) * 3 * MAIN, nz),
            half_shape((nx + 2) * 3 * MAIN, nz),
        ),
        [vm((2 * ch, 144), F32)],
        1.5,
        3,
        2,
    )(fields, kernel, heads, near_twin, near_other)
    begun = call(x_late_kernel, shape(5, nx + 5, ny, nz), x_scratch[:2], 1.5, 2, 1)(
        fields, flags, patches
    )
    far_twin, far_other = call(far_kernel, (far, far), [], 0.2, 2, 1)(
        flat, flags.reshape(3 * nx * ny, nz), begun
    )
    first = call(x_last_kernel, full, x_scratch, 1.5, 4, 1)(
        fields, flags, early, begun, far_other
    )
    far_rims = (
        lax.ppermute(far_twin, "gy", with_twin),
        lax.ppermute(far_other, "gy", with_other),
    )
    near_rims, patches, first = lax.optimization_barrier((near_rims, patches, first))
    w_rows, w_cols, w_head, bias = prepared
    parts, d_high, d_low = call(
        c_kernel,
        (
            shape(ch, 256),
            half_shape(10 * ch, nx * nz),
            half_shape(10 * ch, nx * nz),
        ),
        [
            *[vm(((nx + 2) * 3 * RIM, nz), BF16)] * 4,
            vm((2 * RIM * nx, nz), F32),
            vm((16 * nx, nz), F32),
        ],
        4.2,
        9,
    )(fields, *near_rims, kernel, w_rows, w_head, bias, patches, patches_low)

    def exchanged(value, bit):
        return lax.ppermute(value, "gy", [(i, i ^ bit) for i in range(count)])

    bits = [1 << b for b in range(count.bit_length() - 1)]
    sums = parts
    for bit in bits[:-4]:
        sums = sums + exchanged(sums, bit)
    third = nx // 6 * 2
    yz = lambda lo, hi, before, order: call(
        functools.partial(yz_kernel, lo, hi), full, [vm((lines, nz), F32)] * 2, 2.2, 9, 1
    )(fields, flags, *near_rims, *far_rims, first, before, rim, order)
    got = exchanged(sums, bits[-4])
    own = call(c_back_kernel, full, [vm((nx * 120, nz), F32)], 1.1, 3, 1)(
        w_cols, d_high, d_low, sums
    )
    got, own = lax.optimization_barrier((got, own))
    sums = sums + got
    got = exchanged(sums, bits[-3])
    rim = call(e_kernel, shape(lines, nz), [], 1.1, 5, 1)(flat, *near_rims, *far_rims, sums)
    total = yz(0, third, own, sums)
    got, total = lax.optimization_barrier((got, total))
    sums = sums + got
    got = exchanged(sums, bits[-2])
    total = yz(third, nx - nx // 4, total, sums)
    got, total = lax.optimization_barrier((got, total))
    sums = sums + got
    got = exchanged(sums, bits[-1])
    flow = yz(nx - nx // 4, nx, total, sums)
    got, flow = lax.optimization_barrier((got, flow))
    scale = float(cells * count) ** (-0.5)
    k_out, h_out = call(
        functools.partial(sum_kernel, scale), (shape(ch, taps), shape(5, ch)), [], 0.5, 2
    )(sums, got)
    return flow, k_out, h_out


def solution(mesh):
    split_y = P(None, "ens", "gy", None)
    return jax.shard_map(
        body,
        mesh=mesh,
        in_specs=(split_y, split_y, split_y, P(), P()),
        out_specs=(split_y, P("ens", None), P("ens", None)),
        check_vma=False,
    )
```
